32 devices in a mesh: wide: 8 (over z, x), grid: 4 (over y, core).
Axes of the slice: x: 2, y: 2, z: 4, core: 2. Of those that a mesh axis runs over, the one named last changes fastest.
Arguments:
- tokens: bfloat16 [4096, 2048], P('wide', 'grid'), may hold values from -6 to 6
- segment_ids: int32 [4096], replicated, may hold values from 0 to 3, never falling along the last dimension, each value on 1 to 2000 neighbouring positions
- attention_routes: int32 [4096, 2], P('wide'), may hold values from 0 to 3, all different within a row; in each aligned block of 512 rows (0 to 511, 512 to 1023, ...) at most 320 rows name the same one
- expert_routes: int32 [4096, 2], P('wide'), may hold values from 0 to 3, all different within a row; in each aligned block of 512 rows (0 to 511, 512 to 1023, ...) at most 320 rows name the same one
- attention_gain: bfloat16 [2048], P('wide'), may hold values from 0.099609375 to 1.8984375
- attention_kv: bfloat16 [2048, 16, 2, 128], P('wide', 'grid'), may hold values from -0.125 to 0.125
- attention_query: bfloat16 [4, 2048, 16, 128], P(None, 'wide', 'grid'), may hold values from -0.125 to 0.125
- attention_out: bfloat16 [4, 16, 128, 2048], P(None, 'grid', None, 'wide'), may hold values from -1 to 1
- attention_router: bfloat16 [2048, 4], P('wide'), may hold values from -0.09375 to 0.09375
- feedforward_gain: bfloat16 [2048], P('wide'), may hold values from 0.099609375 to 1.8984375
- feedforward_router: bfloat16 [2048, 4], P('wide'), may hold values from -0.09375 to 0.09375
- expert_gate_up: bfloat16 [4, 2048, 2, 5632], P(None, 'wide', None, 'grid'), may hold values from -0.125 to 0.125
- expert_down: bfloat16 [4, 5632, 2048], P(None, 'grid', 'wide'), may hold values from -0.078125 to 0.078125
- output_grad: bfloat16 [4096, 2048], P('wide', 'grid'), may hold values from -6 to 6
Outputs:
- layer_output: bfloat16 [4096, 2048], P('wide', 'grid')
- input_grad: bfloat16 [4096, 2048], P('wide', 'grid')
- attention_gain_grad: float32 [2048], P('wide')
- attention_kv_grad: float32 [2048, 16, 2, 128], P('wide', 'grid')
- attention_query_grad: float32 [4, 2048, 16, 128], P(None, 'wide', 'grid')
- attention_out_grad: float32 [4, 16, 128, 2048], P(None, 'grid', None, 'wide')
- attention_router_grad: float32 [2048, 4], P('wide')
- feedforward_gain_grad: float32 [2048], P('wide')
- feedforward_router_grad: float32 [2048, 4], P('wide')
- expert_gate_up_grad: float32 [4, 2048, 2, 5632], P(None, 'wide', None, 'grid')
- expert_down_grad: float32 [4, 5632, 2048], P(None, 'grid', 'wide')
The draws below stay inside these ranges and needn't reach their ends.
Inputs may be any that keep to these rules, and one draw needn't show every extreme that they name: `segment_ids`: segment numbers never fall along the tokens; every document holds 1 to 2000 tokens and one holds exactly 2000. `attention_routes`: each token names two different experts; in the rows of one index of wide no expert is named by more than 320 tokens, and in every draw some expert is named by exactly 320 tokens of one such block. `expert_routes`: each token names two different experts; in the rows of one index of wide no expert is named by more than 320 tokens, and in every draw some expert is named by exactly 320 tokens of one such block.
All inputs are finite; a program needn't handle non-finite values.
Results may differ from the reference program's by a relative error of at most 0.028.
Values may be sent and summed in bfloat16 or wider, within the bound.
A program may use at most 512 MiB of HBM per device.

```python
import math
import jax
import jax.numpy as jnp
import numpy as np
from jax import lax

MODEL_DIMENSION = 2048
HEADS = 16
HEAD_DIM = 128
FF = 5632
EXPERTS = 4
TOK_DEV = 512
LENGTH = 4096
DOC_MOST = 2000
CAP = 320
TOKENS = 4096
NDOCS = 4


def block_scale(key, shape, cuts, low, high):
    def one(dim, shards_of):
        heights = jax.random.uniform(jax.random.fold_in(jax.random.fold_in(key, 6), dim), (shards_of,), jnp.float32, low / len(cuts), high / len(cuts))
        return jnp.repeat(jnp.exp(heights), shape[dim] // shards_of).reshape((-1,) + (1,) * (len(shape) - dim - 1))

    factor_of = one(*cuts[0])
    for cut in cuts[1:]:
        factor_of = factor_of * one(*cut)
    return factor_of


def profile(amount, total, bound, slope):
    portions = [(1 << 20) // math.isqrt(grade ** slope) + 1 for grade in range(2, amount + 1)]
    surplus, given = total - bound - (amount - 1), [1] * (amount - 1)
    while surplus > 0:
        candidates = [i for i in range(amount - 1) if given[i] < bound]
        mass, remaining = sum([portions[i] for i in candidates]), surplus
        for i in candidates:
            addition = min(bound - given[i], max(1, remaining * portions[i] // mass), surplus)
            given[i] = given[i] + addition
            surplus = surplus - addition
    return np.array([bound] + given)


def ragged(own_key, number_of, total, limit, skew):
    if number_of == 2:
        one = jax.random.randint(own_key, (), max(1, total - limit), min(limit, total - 1) + 1)
        return jnp.stack([one, total - one])
    lengths = jnp.asarray(profile(number_of, total, limit, skew), jnp.int32)
    pairs = (number_of - 1) // 2
    source_of, receiver = lengths[1:1 + 2 * pairs:2], lengths[2:2 + 2 * pairs:2]
    room = jnp.minimum(source_of - 1, limit - receiver)
    shifted = jax.random.randint(jax.random.fold_in(own_key, 1), (pairs,), 0, 1 << 20) % (room + 1)
    lengths = lengths.at[1:1 + 2 * pairs:2].set(source_of - shifted).at[2:2 + 2 * pairs:2].set(receiver + shifted)
    return lengths[jax.random.permutation(jax.random.fold_in(own_key, 2), number_of)]


def shared_out(stream_key, own, number, rows, amount, top, limit, slope):
    sequence = jax.random.permutation(stream_key, amount)
    crowded, common = portions_of(amount, rows * top, limit, slope, True), portions_of(amount, rows * top, limit, slope, False)
    places = jnp.arange(amount)

    def named(lengths, offset_by):
        used = int((lengths > 0).sum())
        fixed = max(1, used // 4)
        shifted = fixed + (places - fixed + offset_by * (used - fixed)) % max(1, amount - fixed)
        return jnp.zeros((amount,), jnp.int32).at[sequence[jnp.where(places < fixed, places, shifted)]].set(jnp.asarray(lengths, jnp.int32))

    lengths = jnp.where(number % 4 == 0, named(crowded, number // 4), named(common, number - number // 4 - 1))
    mixed = jax.random.permutation(jax.random.fold_in(own, 3), amount)
    donor, receiver = mixed[0:amount // 2 * 2:2], mixed[1:amount // 2 * 2:2]
    slack = jnp.minimum(lengths[donor] - 1, limit - lengths[receiver]) // 2
    slack = jnp.where((donor == sequence[0]) | (receiver == sequence[0]) | (lengths[receiver] == 0), 0, jnp.maximum(slack, 0))
    shifted = jax.random.randint(jax.random.fold_in(own, 4), (amount // 2,), 0, 1 << 20) % (slack + 1)
    lengths = lengths.at[donor].add(-shifted).at[receiver].add(shifted)
    items = jnp.searchsorted(jnp.cumsum(lengths), jnp.arange(rows * top), side="right").astype(jnp.int32)
    grid = items.reshape(top, rows).T
    grid = grid[jax.random.permutation(jax.random.fold_in(own, 1), rows)]
    offset_by = jax.random.randint(jax.random.fold_in(own, 2), (rows, 1), 0, top)
    return jnp.take_along_axis(grid, (jnp.arange(top)[None, :] + offset_by) % top, axis=1)


def portions_of(number_of, total, bound, lean, full):
    portions = [(1 << 20) // math.isqrt(rank ** lean) + 1 for rank in range(1, number_of + 1)]
    largest = bound if full else min(bound, max(-(-total // number_of), total * portions[0] // sum(portions)))
    least = 1 if total - largest >= number_of - 1 else 0
    counts, surplus = [largest] + [least] * (number_of - 1), total - largest - least * (number_of - 1)
    while surplus > 0:
        movable = [i for i in range(1, number_of) if counts[i] < largest] or [i for i in range(1, number_of) if counts[i] < bound]
        whole, budget = sum([portions[i] for i in movable]), surplus
        for i in movable:
            addition = min(bound - counts[i], max(1, budget * portions[i] // whole), surplus)
            counts[i] = counts[i] + addition
            surplus = surplus - addition
    return np.array(counts)


def normal_values(rng, shape, spread, bound, shards=(), kind=jnp.bfloat16):
    array = jax.random.normal(rng, shape, jnp.float32) * spread
    if len(shards) > 0:
        array = block_scale(rng, shape, shards, -0.22, 0.18) * array
    return jnp.clip(array, min=-bound, max=bound).astype(kind)


def setup_inputs(seed: int = 0) -> dict:
    key_of = jax.random.split(jax.random.key(seed), 15)
    tokens = normal_values(key_of[0], (TOKENS, MODEL_DIMENSION), 1.0, 6.0, ((0, 8), (1, 4)))
    segment_ids = jnp.searchsorted(jnp.cumsum(ragged(key_of[1], NDOCS, TOKENS, DOC_MOST, 0)), jnp.arange(TOKENS), side="right").astype(jnp.int32)
    attention_routes_keys = jax.random.split(jax.random.fold_in(key_of[2], 1), TOKENS // TOK_DEV)
    attention_routes_turns = jax.random.permutation(jax.random.fold_in(key_of[2], 3), TOKENS // TOK_DEV)
    attention_routes = jax.vmap(lambda own, number: shared_out(jax.random.fold_in(key_of[2], 2), own, number, TOK_DEV, EXPERTS, 2, CAP, 1))(attention_routes_keys, attention_routes_turns).reshape((TOKENS, 2))
    expert_routes_keys = jax.random.split(jax.random.fold_in(key_of[3], 1), TOKENS // TOK_DEV)
    expert_routes_turns = jax.random.permutation(jax.random.fold_in(key_of[3], 3), TOKENS // TOK_DEV)
    expert_routes = jax.vmap(lambda own, number: shared_out(jax.random.fold_in(key_of[3], 2), own, number, TOK_DEV, EXPERTS, 2, CAP, 1))(expert_routes_keys, expert_routes_turns).reshape((TOKENS, 2))
    attention_gain = jnp.clip(1.0 + 0.18 * jax.random.normal(key_of[4], (MODEL_DIMENSION,), jnp.float32), 0.099609375, 1.8984375).astype(jnp.bfloat16)
    attention_kv = normal_values(key_of[5], (MODEL_DIMENSION, HEADS, 2, HEAD_DIM), MODEL_DIMENSION ** -0.5, 0.125, ((0, 8), (1, 4)))
    attention_query = normal_values(key_of[6], (EXPERTS, MODEL_DIMENSION, HEADS, HEAD_DIM), MODEL_DIMENSION ** -0.5, 0.125, ((1, 8), (2, 4)))
    attention_out = normal_values(key_of[7], (EXPERTS, HEADS, HEAD_DIM, MODEL_DIMENSION), (HEADS * HEAD_DIM // 64) ** -0.5, 1.0, ((1, 4), (3, 8)))
    attention_router = normal_values(key_of[8], (MODEL_DIMENSION, EXPERTS), (2 * MODEL_DIMENSION) ** -0.5, 0.09375, ((0, 8),))
    feedforward_gain = jnp.clip(1.0 + 0.18 * jax.random.normal(key_of[9], (MODEL_DIMENSION,), jnp.float32), 0.099609375, 1.8984375).astype(jnp.bfloat16)
    feedforward_router = normal_values(key_of[10], (MODEL_DIMENSION, EXPERTS), (2 * MODEL_DIMENSION) ** -0.5, 0.09375, ((0, 8),))
    expert_gate_up = normal_values(key_of[11], (EXPERTS, MODEL_DIMENSION, 2, FF), MODEL_DIMENSION ** -0.5, 0.125, ((1, 8), (3, 4)))
    expert_down = normal_values(key_of[12], (EXPERTS, FF, MODEL_DIMENSION), FF ** -0.5, 0.078125, ((1, 4), (2, 8)))
    output_grad = normal_values(key_of[13], (TOKENS, MODEL_DIMENSION), 1.0, 6.0, ((0, 8), (1, 4)))
    return dict(tokens=tokens, segment_ids=segment_ids, attention_routes=attention_routes, expert_routes=expert_routes, attention_gain=attention_gain, attention_kv=attention_kv, attention_query=attention_query, attention_out=attention_out, attention_router=attention_router, feedforward_gain=feedforward_gain, feedforward_router=feedforward_router, expert_gate_up=expert_gate_up, expert_down=expert_down, output_grad=output_grad)


EPSILON = 1e-05
ROPE_BASE = 10000.0
NEGATIVE = -1e+30
FULL_PRECISION = lax.Precision.HIGHEST

@jax.custom_vjp
def low(v):
    return lax.optimization_barrier(v.astype(jnp.bfloat16)).astype(jnp.float32)

@jax.custom_vjp
def reduced_backward(v):
    return v

def low_keep(v):
    return (low(v), None)

def low_pass(kept, grad):
    return (grad,)

def back_keep(v):
    return (v, None)

def back_low(kept, grad):
    return (low(grad),)
low.defvjp(low_keep, low_pass)
reduced_backward.defvjp(back_keep, back_low)

def rope_tables(positions, table_width):
    half_width = table_width // 2
    frequency = ROPE_BASE ** (-jnp.arange(half_width, dtype=jnp.float32) / half_width)
    angles = positions.astype(jnp.float32)[:, None] * frequency[None, :]
    return (jnp.cos(angles), jnp.sin(angles))

def rotate(values, cosine, sine_table):
    half_width = values.shape[-1] // 2
    leading = values[..., :half_width]
    trailing = values[..., half_width:]
    return jnp.concatenate([leading * cosine - trailing * sine_table, trailing * cosine + leading * sine_table], axis=-1)

def normalize(values, gain_row):
    inverse = lax.rsqrt(lax.optimization_barrier(jnp.mean(values * values, axis=-1, keepdims=True)) + EPSILON)
    return values * inverse * gain_row

def route_gates(hidden, router, routes):
    logits = jnp.dot(hidden, router, precision=FULL_PRECISION)
    picked = jnp.take_along_axis(logits, routes, axis=1)
    return jax.nn.softmax(picked, axis=-1)

def reference(tokens, segment_ids, attention_routes, expert_routes, attention_gain, attention_kv, attention_query, attention_out, attention_router, feedforward_gain, feedforward_router, expert_gate_up, expert_down, output_grad):
    seq_length = min(LENGTH, TOKENS)
    block_rows = min(512, seq_length)
    positions = jnp.arange(TOKENS, dtype=jnp.int32)
    cosine, sine_table = rope_tables(positions % seq_length, HEAD_DIM)
    score_scaling = 1.0 / math.sqrt(HEAD_DIM)
    expert_index = jnp.arange(EXPERTS, dtype=jnp.int32)

    def attention(queries, keys, values):

        def attend_block(index):
            first_row = (index * block_rows).astype(jnp.int32)
            seq_start = (first_row // seq_length * seq_length).astype(jnp.int32)
            query_block_rows = lax.dynamic_slice_in_dim(queries, first_row, block_rows, 0)
            sequence_keys = lax.dynamic_slice_in_dim(keys, seq_start, seq_length, 0)
            sequence_values = lax.dynamic_slice_in_dim(values, seq_start, seq_length, 0)
            query_position = first_row + jnp.arange(block_rows, dtype=jnp.int32)
            key_position = seq_start + jnp.arange(seq_length, dtype=jnp.int32)
            query_segment = lax.dynamic_slice_in_dim(segment_ids, first_row, block_rows, 0)
            key_segment = lax.dynamic_slice_in_dim(segment_ids, seq_start, seq_length, 0)
            allowed = (key_segment[None, :] == query_segment[:, None]) & (key_position[None, :] <= query_position[:, None])
            score_matrix = reduced_backward(jnp.einsum('jfeu,geu->fejg', query_block_rows, sequence_keys, precision=FULL_PRECISION) * score_scaling)
            score_matrix = jnp.where(allowed[None, None], score_matrix, NEGATIVE)
            largest = lax.optimization_barrier(jnp.max(score_matrix, axis=-1, keepdims=True))
            weights = jnp.exp(score_matrix - largest)
            attention_probabilities = low(weights / lax.optimization_barrier(jnp.sum(weights, axis=-1, keepdims=True)))
            return jnp.einsum('jegf,feq->gjeq', attention_probabilities, sequence_values, precision=FULL_PRECISION)
        blocks = lax.map(jax.checkpoint(attend_block), jnp.arange(TOKENS // block_rows, dtype=jnp.int32))
        return blocks.reshape(TOKENS, 2, HEADS, HEAD_DIM)

    def forward(inputs, gain_first, kv_weight, query_weight, out_weight, router_first, gain_second, router_second, gate_up_weight, down_weight):
        hidden_first = low(normalize(inputs, gain_first))
        gates_first = route_gates(hidden_first, router_first, attention_routes)
        kv_rows = reduced_backward(jnp.dot(hidden_first, kv_weight.reshape(MODEL_DIMENSION, -1), precision=FULL_PRECISION)).reshape(TOKENS, HEADS, 2, HEAD_DIM)
        keys = low(rotate(kv_rows[:, :, 0], cosine[:, None, :], sine_table[:, None, :]))
        values = low(kv_rows[:, :, 1])

        def query_step(running, pieces):
            weight_matrix, expert = pieces
            matrix_product = jnp.dot(hidden_first, weight_matrix.reshape(MODEL_DIMENSION, -1), precision=FULL_PRECISION)
            chosen = (attention_routes == expert).astype(jnp.float32)
            return (running + chosen[:, :, None] * matrix_product[:, None, :], None)
        query_sum = lax.scan(jax.checkpoint(query_step), jnp.zeros((TOKENS, 2, HEADS * HEAD_DIM), jnp.float32), (query_weight, expert_index))[0]
        query_pre = reduced_backward(query_sum).reshape(TOKENS, 2, HEADS, HEAD_DIM)
        queries = low(rotate(query_pre, cosine[:, None, None, :], sine_table[:, None, None, :]))
        attended_output = low(reduced_backward(attention(queries, keys, values))).reshape(TOKENS, 2, HEADS * HEAD_DIM)

        def out_step(running, pieces):
            weight_matrix, expert = pieces
            matrix_product = jnp.einsum('apk,kb->apb', attended_output, weight_matrix.reshape(-1, MODEL_DIMENSION), precision=FULL_PRECISION)
            chosen = (attention_routes == expert).astype(jnp.float32)
            return (running + chosen[:, :, None] * matrix_product, None)
        branch_first = reduced_backward(lax.scan(jax.checkpoint(out_step), jnp.zeros((TOKENS, 2, MODEL_DIMENSION), jnp.float32), (out_weight, expert_index))[0])
        residual = inputs + lax.optimization_barrier(jnp.sum(gates_first[:, :, None] * branch_first, axis=1))
        hidden_second = low(normalize(residual, gain_second))
        gates_second = route_gates(hidden_second, router_second, expert_routes)

        def expert_step(running, pieces):
            gate_up_matrix, down_matrix, expert = pieces
            gate_up = reduced_backward(jnp.dot(hidden_second, gate_up_matrix.reshape(MODEL_DIMENSION, -1), precision=FULL_PRECISION)).reshape(TOKENS, 2, FF)
            hidden = low(jax.nn.silu(gate_up[:, 0]) * gate_up[:, 1])
            result = jnp.dot(hidden, down_matrix, precision=FULL_PRECISION)
            chosen = (expert_routes == expert).astype(jnp.float32)
            return (running + chosen[:, :, None] * result[:, None, :], None)
        branch_second = reduced_backward(lax.scan(jax.checkpoint(expert_step), jnp.zeros((TOKENS, 2, MODEL_DIMENSION), jnp.float32), (gate_up_weight, down_weight, expert_index))[0])
        return residual + lax.optimization_barrier(jnp.sum(gates_second[:, :, None] * branch_second, axis=1))
    layer_output, pullback = jax.vjp(forward, tokens.astype(jnp.float32), attention_gain.astype(jnp.float32), attention_kv.astype(jnp.float32), attention_query.astype(jnp.float32), attention_out.astype(jnp.float32), attention_router.astype(jnp.float32), feedforward_gain.astype(jnp.float32), feedforward_router.astype(jnp.float32), expert_gate_up.astype(jnp.float32), expert_down.astype(jnp.float32))
    gradients = pullback(output_grad.astype(jnp.float32))
    return (layer_output.astype(jnp.bfloat16), gradients[0].astype(jnp.bfloat16), gradients[1], gradients[2], gradients[3], gradients[4], gradients[5], gradients[6], gradients[7], gradients[8], gradients[9])
```

```python
import functools
import math

import jax
import jax.numpy as jnp
from jax import lax
from jax.experimental import pallas as pl
from jax.experimental.pallas import tpu as pltpu
from jax.sharding import Mesh, PartitionSpec as P

CAP = 320
PLANES = 4
HALVES = 2
BLOCKS = PLANES * HALVES
EPSILON = 1e-05
ROPE_BASE = 10000.0
NEGATIVE = -1e30
BF16 = jnp.bfloat16
F32 = jnp.float32
PLACES = ("z", "x")
VMEM_BYTES = 56 * 1024 * 1024


def rope_tables(positions, table_width):
    half_width = table_width // 2
    frequency = ROPE_BASE ** (-jnp.arange(half_width, dtype=F32) / half_width)
    angles = positions.astype(F32)[:, None] * frequency[None, :]
    return (jnp.cos(angles), jnp.sin(angles))


def rotate(values, cosine, sine_table):
    half_width = values.shape[-1] // 2
    leading = values[..., :half_width]
    trailing = values[..., half_width:]
    return jnp.concatenate(
        [leading * cosine - trailing * sine_table, trailing * cosine + leading * sine_table],
        axis=-1,
    )


def dot(left, right):
    return jnp.dot(left, right, preferred_element_type=F32)


def contract_first(left, right):
    return lax.dot_general(left, right, (((0,), (0,)), ((), ())), preferred_element_type=F32)


def contract_last(left, right):
    return lax.dot_general(left, right, (((1,), (1,)), ((), ())), preferred_element_type=F32)


def exact(left, right):
    return jnp.dot(left, right, precision=lax.Precision.HIGHEST)


def first_of(position_ref, index):
    return position_ref[index]


def attention_scores(q, k_ref, low_bound, high_bound, tile, tile_rows, scaling):
    rows = pl.ds(pl.multiple_of(tile * tile_rows, tile_rows), tile_rows)
    keys = k_ref[rows, :]
    scores = contract_last(q, keys) * scaling
    column = tile * tile_rows + lax.broadcasted_iota(jnp.int32, scores.shape, 1)
    allowed = (column >= low_bound) & (column <= high_bound)
    return rows, keys, scores, allowed


def attention_forward_kernel(
    begin_ref, q_ref, k_ref, v_ref, rank_ref, low_ref, high_ref, out_ref, lse_ref, *, scaling
):
    block = pl.program_id(1)
    cap, width = out_ref.shape
    tile_rows = q_ref.shape[0]
    pick = (lax.broadcasted_iota(jnp.int32, (cap, tile_rows), 0) == rank_ref[0]).astype(BF16)
    q = dot(pick, q_ref[...]).astype(BF16)
    low_bound, high_bound = low_ref[...], high_ref[...]

    def step(tile, carried):
        largest, total, summed = carried
        rows, _, scores, allowed = attention_scores(
            q, k_ref, low_bound, high_bound, tile, tile_rows, scaling
        )
        scores = jnp.where(allowed, scores, NEGATIVE)
        new_largest = jnp.maximum(largest, jnp.max(scores, axis=1, keepdims=True))
        weights = jnp.where(allowed, jnp.exp(scores - new_largest), 0.0)
        shrink = jnp.exp(largest - new_largest)
        return (
            new_largest,
            total * shrink + jnp.sum(weights, axis=1, keepdims=True),
            summed * shrink + dot(weights.astype(BF16), v_ref[rows, :]),
        )

    largest, total, summed = lax.fori_loop(
        begin_ref[block],
        block + 1,
        step,
        (jnp.full((cap, 1), NEGATIVE, F32), jnp.zeros((cap, 1), F32), jnp.zeros((cap, width), F32)),
    )
    out_ref[...] = (summed / total).astype(BF16)
    lse_ref[0] = largest + jnp.log(total)


def attention_backward_kernel(
    begin_ref, q_ref, k_ref, v_ref, rank_ref, low_ref, high_ref, out_ref, lse_ref, grad_ref,
    dq_ref, dk_ref, dv_ref, *, scaling
):
    block = pl.program_id(1)
    cap, width = out_ref.shape
    tile_rows = q_ref.shape[0]
    pick = (lax.broadcasted_iota(jnp.int32, (cap, tile_rows), 0) == rank_ref[0]).astype(BF16)
    q = dot(pick, q_ref[...]).astype(BF16)
    low_bound, high_bound = low_ref[...], high_ref[...]
    grad = grad_ref[...]
    delta = jnp.sum(grad.astype(F32) * out_ref[...].astype(F32), axis=1, keepdims=True)
    lse = lse_ref[0]

    @pl.when(block == 0)
    def _():
        dk_ref[...] = jnp.zeros_like(dk_ref)
        dv_ref[...] = jnp.zeros_like(dv_ref)

    def step(tile, dq):
        rows, keys, scores, allowed = attention_scores(
            q, k_ref, low_bound, high_bound, tile, tile_rows, scaling
        )
        chances = jnp.where(allowed, jnp.exp(scores - lse), 0.0)
        dv_ref[rows, :] += contract_first(chances.astype(BF16), grad)
        grad_chances = contract_last(grad, v_ref[rows, :])
        grad_scores = (chances * (grad_chances - delta)).astype(BF16)
        dk_ref[rows, :] += contract_first(grad_scores, q) * scaling
        return dq + dot(grad_scores, keys)

    dq = lax.fori_loop(begin_ref[block], block + 1, step, jnp.zeros((cap, width), F32))
    dq_ref[...] = dq * scaling


def attention_specs(row_count, token_count, width):
    return dict(
        q=pl.BlockSpec((row_count, width), lambda h, b, s: (b, h)),
        k=pl.BlockSpec((token_count, width), lambda h, b, s: (0, h)),
        rank=pl.BlockSpec((1, 1, row_count), lambda h, b, s: (b, 0, 0)),
        bound=pl.BlockSpec((CAP, 1), lambda h, b, s: (b, 0)),
        slots=pl.BlockSpec((CAP, width), lambda h, b, s: (b, h)),
        lse=pl.BlockSpec((1, CAP, 1), lambda h, b, s: (h, b, 0)),
    )


def attention_forward(begin, q, k, v, rank, low_bound, high_bound, width):
    token_count, heads = q.shape[0], q.shape[1] // width
    row_count = token_count // BLOCKS
    s = attention_specs(row_count, token_count, width)
    return pl.pallas_call(
        functools.partial(attention_forward_kernel, scaling=1.0 / math.sqrt(width)),
        grid_spec=pltpu.PrefetchScalarGridSpec(
            num_scalar_prefetch=1,
            grid=(heads, BLOCKS),
            in_specs=[s["q"], s["k"], s["k"], s["rank"], s["bound"], s["bound"]],
            out_specs=[s["slots"], s["lse"]],
        ),
        out_shape=[
            jax.ShapeDtypeStruct((BLOCKS * CAP, heads * width), BF16),
            jax.ShapeDtypeStruct((heads, BLOCKS * CAP, 1), F32),
        ],
        compiler_params=pltpu.CompilerParams(vmem_limit_bytes=VMEM_BYTES),
        cost_estimate=pl.CostEstimate(
            flops=10_000_000_000, bytes_accessed=8_000_000, transcendentals=8_000_000
        ),
        name="attention_forward",
    )(begin, q, k, v, rank, low_bound, high_bound)


def attention_backward(begin, q, k, v, rank, low_bound, high_bound, out, lse, grad, width):
    token_count, heads = q.shape[0], q.shape[1] // width
    row_count = token_count // BLOCKS
    s = attention_specs(row_count, token_count, width)
    return pl.pallas_call(
        functools.partial(attention_backward_kernel, scaling=1.0 / math.sqrt(width)),
        grid_spec=pltpu.PrefetchScalarGridSpec(
            num_scalar_prefetch=1,
            grid=(heads, BLOCKS),
            in_specs=[
                s["q"], s["k"], s["k"], s["rank"], s["bound"], s["bound"],
                s["slots"], s["lse"], s["slots"],
            ],
            out_specs=[s["slots"], s["k"], s["k"]],
        ),
        out_shape=[
            jax.ShapeDtypeStruct((BLOCKS * CAP, heads * width), F32),
            jax.ShapeDtypeStruct((token_count, heads * width), F32),
            jax.ShapeDtypeStruct((token_count, heads * width), F32),
        ],
        compiler_params=pltpu.CompilerParams(vmem_limit_bytes=VMEM_BYTES),
        cost_estimate=pl.CostEstimate(
            flops=20_000_000_000, bytes_accessed=16_000_000, transcendentals=8_000_000
        ),
        name="attention_backward",
    )(begin, q, k, v, rank, low_bound, high_bound, out, lse, grad)


def exchanged(pieces):
    return lax.all_to_all(pieces, PLACES, 0, 0, tiled=True)


def spread_weights(pieces):
    return lax.all_gather(exchanged(pieces), "t", axis=0, tiled=False)


def return_gradients(pieces):
    return exchanged(lax.psum_scatter(pieces, "t", scatter_dimension=0, tiled=False))


def to_plane(slots):
    arrived = lax.all_to_all(slots, "z", 0, 0, tiled=True)
    gathered = lax.all_gather(arrived, ("x", "grid"), axis=0, tiled=False)
    planes, cap, width = arrived.shape
    gathered = gathered.reshape(HALVES, -1, planes, cap, width)
    return gathered.transpose(2, 0, 3, 1, 4).reshape(BLOCKS * cap, -1)


def from_plane(partial, grid_count):
    pieces = partial.reshape(PLANES, HALVES, CAP, grid_count, -1).transpose(1, 3, 0, 2, 4)
    pieces = pieces.reshape((HALVES * grid_count,) + pieces.shape[2:])
    summed = lax.psum_scatter(pieces, ("x", "grid"), scatter_dimension=0, tiled=False)
    return lax.all_to_all(summed, "z", 0, 0, tiled=True)


def grid_sum(values):
    shape = values.shape
    return lax.all_gather(values.reshape(-1, 128), "grid", axis=0).sum(axis=0).reshape(shape)


def ranks(member):
    counted = member.astype(jnp.int32)
    before = jnp.cumsum(counted, axis=-1) - counted
    return jnp.where(member, before, -1)


def picks(rank):
    return jnp.arange(CAP, dtype=jnp.int32)[:, None] == rank[..., None, :]


def routed(routes):
    return routes[:, None, :] == jnp.arange(PLANES, dtype=jnp.int32)[None, :, None]


def route_gates(logits, member):
    shown = jnp.where(member, logits, NEGATIVE)
    weights = jnp.where(member, jnp.exp(shown - jnp.max(shown, axis=1, keepdims=True)), 0.0)
    return weights / jnp.sum(weights, axis=1, keepdims=True)


def logits_grad(gates, grad_gates):
    return gates * (grad_gates - jnp.sum(gates * grad_gates, axis=1, keepdims=True))


def per_device(
    tokens, segment_ids, attention_routes, expert_routes, attention_gain, attention_kv,
    attention_query, attention_out, attention_router, feedforward_gain, feedforward_router,
    expert_gate_up, expert_down, output_grad,
):
    groups = lax.axis_size("t")
    grid_count = lax.axis_size("grid")
    group = lax.axis_index("t")
    plane = lax.axis_index("z")
    place = plane * HALVES + lax.axis_index("x")
    column = lax.axis_index("grid")
    rows, features = tokens.shape
    width_all = features * grid_count
    token_count = BLOCKS * rows
    own_rows = attention_gain.shape[0]
    head_width = attention_kv.shape[3]
    head_pair = attention_kv.shape[1] // HALVES
    span = head_pair * head_width
    hidden_units = expert_gate_up.shape[3] // HALVES

    def mine(array, axis=0):
        return lax.dynamic_slice_in_dim(array, column * features, features, axis)

    def own(array):
        return lax.dynamic_slice_in_dim(array, place * rows, rows, 0)

    query_pieces = attention_query.reshape(PLANES, own_rows, HALVES, span).transpose(0, 2, 1, 3)
    kv_pieces = attention_kv.reshape(own_rows, HALVES, head_pair, 2, head_width)
    kv_pieces = kv_pieces.transpose(1, 0, 3, 2, 4).reshape(1, HALVES, own_rows, 2 * span)
    kv_pieces = jnp.broadcast_to(kv_pieces, (PLANES,) + kv_pieces.shape[1:])
    qkv_pieces = jnp.concatenate([query_pieces, kv_pieces], axis=-1)
    qkv_weight = spread_weights(qkv_pieces.reshape(BLOCKS, own_rows, 3 * span))
    qkv_weight = qkv_weight.reshape(width_all, 3 * span)
    out_pieces = attention_out.reshape(BLOCKS, span, own_rows)
    out_weight = spread_weights(out_pieces).transpose(2, 0, 1, 3).reshape(span, width_all)
    up_pieces = expert_gate_up.reshape(PLANES, own_rows, 2, HALVES, hidden_units)
    up_pieces = up_pieces.transpose(0, 3, 1, 2, 4).reshape(BLOCKS, own_rows, 2 * hidden_units)
    up_weight = spread_weights(up_pieces).reshape(width_all, 2 * hidden_units)
    down_pieces = expert_down.reshape(BLOCKS, hidden_units, own_rows)
    down_weight = spread_weights(down_pieces).transpose(2, 0, 1, 3).reshape(hidden_units, width_all)

    small = jnp.concatenate(
        [attention_gain[:, None], feedforward_gain[:, None], attention_router, feedforward_router],
        axis=1,
    )
    small = lax.all_gather(small.T, ("t", "z", "x"), axis=1, tiled=True)
    gain_first, gain_second = small[0].astype(F32), small[1].astype(F32)
    router_first, router_second = small[2:6].T, small[6:10].T

    own_routes = jnp.concatenate([attention_routes, expert_routes], axis=1)
    all_routes = lax.all_gather(own_routes, PLACES, axis=0, tiled=True)
    member_first = jnp.any(routed(all_routes[:, :2]), axis=2)
    member_second = jnp.any(routed(all_routes[:, 2:]), axis=2)

    def plane_rank(member):
        shown = lax.dynamic_index_in_dim(member, plane, 1, keepdims=False)
        return ranks(shown.reshape(BLOCKS, rows))

    rank_first, rank_second = plane_rank(member_first), plane_rank(member_second)
    own_member_first, own_member_second = own(member_first), own(member_second)
    own_pick_first = picks(ranks(own_member_first.T)).astype(BF16)
    own_pick_second = picks(ranks(own_member_second.T)).astype(BF16)

    def to_slots(values, pick):
        return jnp.einsum("est,tf->esf", pick, values, preferred_element_type=F32).astype(BF16)

    def to_tokens(slots, pick):
        return jnp.einsum("est,esf->etf", pick, slots, preferred_element_type=F32)

    grad_out = output_grad.astype(F32)
    grad_slots_second = to_plane(to_slots(output_grad, own_pick_second))

    inputs = lax.all_gather(tokens, "grid", axis=1, tiled=True)
    inputs = lax.all_gather(inputs, PLACES, axis=0, tiled=True).astype(F32)
    inverse_first = lax.rsqrt(jnp.mean(inputs * inputs, axis=-1, keepdims=True) + EPSILON)
    hidden_first = (inputs * inverse_first * gain_first).astype(BF16)
    gates_first = route_gates(dot(hidden_first, router_first), member_first)
    position = jnp.arange(token_count, dtype=jnp.int32)
    cosine, sine_table = rope_tables(position, head_width)
    cosine, sine_table = cosine[:, None, :], sine_table[:, None, :]
    qkv = dot(hidden_first, qkv_weight)

    def turned(values, sine):
        split = values.reshape(values.shape[0], -1, head_width)
        return rotate(split, cosine, sine).reshape(values.shape).astype(BF16)

    queries = turned(qkv[:, :span], sine_table)
    keys = turned(qkv[:, span : 2 * span], sine_table)
    values = qkv[:, 2 * span :].astype(BF16)
    segment = lax.dynamic_slice_in_dim(segment_ids, group * token_count, token_count, 0)
    opens = jnp.concatenate([jnp.ones((1,), jnp.bool_), segment[1:] != segment[:-1]])
    document_start = lax.cummax(jnp.where(opens, position, 0))
    begin = document_start.reshape(BLOCKS, rows)[:, 0] // rows
    slot_pick = picks(rank_first)

    def slot_values(per_token):
        shown = jnp.where(slot_pick, per_token.reshape(BLOCKS, 1, rows), 0)
        return jnp.sum(shown, axis=-1).reshape(-1, 1)

    block_first = jnp.repeat(jnp.arange(BLOCKS, dtype=jnp.int32) * rows, CAP)[:, None]
    filled = slot_values(jnp.ones((token_count,), jnp.int32)) > 0
    low_bound = jnp.where(filled, slot_values(document_start), block_first)
    high_bound = jnp.where(filled, slot_values(position), block_first)
    attention_args = (begin, queries, keys, values, rank_first[:, None, :], low_bound, high_bound)
    attended, lse = attention_forward(*attention_args, head_width)
    gate_first = lax.dynamic_index_in_dim(gates_first, plane, 1, keepdims=False)
    gate_slots_first = slot_values(gate_first)
    branch_slots = from_plane(dot(attended, out_weight).astype(BF16), grid_count)
    branch_first = to_tokens(branch_slots, own_pick_first)
    own_gates_first = own(gates_first)
    residual = tokens.astype(F32) + jnp.sum(own_gates_first.T[:, :, None] * branch_first, axis=0)

    square = grid_sum(jnp.sum(residual * residual, axis=1))
    inverse_second = lax.rsqrt(square / width_all + EPSILON)[:, None]
    normed_second = residual * inverse_second
    hidden_second = (normed_second * mine(gain_second)).astype(BF16)
    slots_second = to_plane(to_slots(hidden_second, own_pick_second))
    plane_gates = dot(slots_second, router_second)
    slot_member = jnp.stack(
        [slot_values(member_second[:, e].astype(jnp.int32))[:, 0] for e in range(PLANES)], axis=1
    )
    rank_pick = picks(rank_second)

    def slot_values_second(per_token):
        shown = jnp.where(rank_pick, per_token.reshape(BLOCKS, 1, rows), 0)
        return jnp.sum(shown, axis=-1).reshape(-1)

    slot_member = jnp.stack(
        [slot_values_second(member_second[:, e].astype(jnp.int32)) for e in range(PLANES)], axis=1
    )
    filled_second = slot_values_second(jnp.ones((token_count,), jnp.int32))[:, None] > 0
    slot_gates = route_gates(plane_gates, (slot_member > 0) | ~filled_second)
    gate_slots_second = lax.dynamic_index_in_dim(slot_gates, plane, 1, keepdims=True)
    gate_up = dot(slots_second, up_weight)
    gate_pre, up_pre = gate_up[:, :hidden_units], gate_up[:, hidden_units:]
    sigmoid_gate = jax.nn.sigmoid(gate_pre)
    silu_gate = gate_pre * sigmoid_gate
    inner = silu_gate * up_pre
    result_slots = from_plane(dot(inner.astype(BF16), down_weight).astype(BF16), grid_count)
    own_logits = grid_sum(dot(hidden_second, mine(router_second)))
    own_gates_second = route_gates(own_logits, own_member_second)
    branch_second = to_tokens(result_slots, own_pick_second)
    layer_output = residual + jnp.sum(own_gates_second.T[:, :, None] * branch_second, axis=0)
    layer_output = layer_output.astype(BF16)

    grad_inner = gate_slots_second * contract_last(grad_slots_second, down_weight)
    grad_gate = grad_inner * up_pre * sigmoid_gate * (1.0 + gate_pre * (1.0 - sigmoid_gate))
    grad_gate_up = jnp.concatenate([grad_gate, grad_inner * silu_gate], axis=1).astype(BF16)
    grad_rows = from_plane(contract_last(grad_gate_up, up_weight).astype(BF16), grid_count)
    grad_up_weight = contract_first(slots_second, grad_gate_up).astype(BF16)
    grad_up_weight = return_gradients(
        grad_up_weight.reshape(groups, BLOCKS, own_rows, 2 * hidden_units)
    )
    grad_down = contract_first((gate_slots_second * inner).astype(BF16), grad_slots_second)
    grad_down = grad_down.astype(BF16).reshape(hidden_units, groups, BLOCKS, own_rows)
    grad_down = return_gradients(grad_down.transpose(1, 2, 0, 3))
    expert_gate_up_grad = grad_up_weight.reshape(PLANES, HALVES, own_rows, 2, hidden_units)
    expert_gate_up_grad = expert_gate_up_grad.transpose(0, 2, 3, 1, 4).reshape(expert_gate_up.shape)
    expert_down_grad = grad_down.reshape(expert_down.shape)

    grad_gates_second = grid_sum(jnp.sum(branch_second * grad_out[None], axis=2).T)
    grad_logits_second = logits_grad(own_gates_second, grad_gates_second)
    grad_hidden_second = jnp.sum(to_tokens(grad_rows, own_pick_second), axis=0)
    grad_hidden_second = grad_hidden_second + exact(
        grad_logits_second, mine(router_second).astype(F32).T
    )
    grad_router_second = exact(hidden_second.astype(F32).T, grad_logits_second)
    grad_gain_second = jnp.sum(grad_hidden_second * normed_second, axis=0)
    grad_normed = grad_hidden_second * mine(gain_second)
    inner_mean = grid_sum(jnp.sum(grad_normed * normed_second, axis=1))[:, None] / width_all
    grad_residual = grad_out + inverse_second * (grad_normed - normed_second * inner_mean)

    grad_slots_first = to_plane(to_slots(grad_residual.astype(BF16), own_pick_first))
    grad_attended = gate_slots_first * contract_last(grad_slots_first, out_weight)
    grad_attended = grad_attended.astype(BF16)
    grad_out_weight = contract_first(
        (gate_slots_first * attended.astype(F32)).astype(BF16), grad_slots_first
    )
    grad_out_weight = grad_out_weight.astype(BF16).reshape(span, groups, BLOCKS, own_rows)
    grad_out_weight = return_gradients(grad_out_weight.transpose(1, 2, 0, 3))
    attention_out_grad = grad_out_weight.reshape(attention_out.shape)
    grad_query, grad_keys, grad_values = attention_backward(
        *attention_args, attended, lse, grad_attended, head_width
    )
    grad_query = jnp.einsum(
        "bst,bsf->btf",
        slot_pick.astype(BF16),
        turned_slots(grad_query, high_bound, head_width).reshape(BLOCKS, CAP, span),
        preferred_element_type=F32,
    )
    grad_qkv = jnp.concatenate(
        [
            grad_query.reshape(token_count, span).astype(BF16),
            turned(grad_keys, -sine_table),
            grad_values.astype(BF16),
        ],
        axis=1,
    )
    grad_hidden = contract_last(grad_qkv, qkv_weight).astype(BF16)
    grad_hidden = lax.psum_scatter(grad_hidden, "grid", scatter_dimension=1, tiled=True)
    grad_hidden = lax.psum_scatter(grad_hidden, PLACES, scatter_dimension=0, tiled=True)
    grad_qkv_weight = contract_first(hidden_first, grad_qkv).astype(BF16)
    grad_qkv_weight = return_gradients(
        grad_qkv_weight.reshape(groups, BLOCKS, own_rows, 3 * span)
    ).astype(F32)
    attention_query_grad = grad_qkv_weight[..., :span].reshape(PLANES, HALVES, own_rows, span)
    attention_query_grad = attention_query_grad.transpose(0, 2, 1, 3).reshape(attention_query.shape)
    grad_kv_weight = grad_qkv_weight[..., span:].reshape(
        PLANES, HALVES, own_rows, 2, head_pair, head_width
    )
    attention_kv_grad = grad_kv_weight.sum(axis=0).transpose(1, 0, 3, 2, 4)
    attention_kv_grad = attention_kv_grad.reshape(attention_kv.shape)

    own_normed = tokens.astype(F32) * own(inverse_first)
    own_hidden = (own_normed * mine(gain_first)).astype(BF16)
    grad_gates_first = grid_sum(jnp.sum(branch_first * grad_residual[None], axis=2).T)
    grad_logits_first = logits_grad(own_gates_first, grad_gates_first)
    grad_hidden_first = grad_hidden.astype(F32) + exact(
        grad_logits_first, mine(router_first).astype(F32).T
    )
    grad_router_first = exact(own_hidden.astype(F32).T, grad_logits_first)
    grad_gain_first = jnp.sum(grad_hidden_first * own_normed, axis=0)
    grad_normed = grad_hidden_first * mine(gain_first)
    inner_mean = grid_sum(jnp.sum(grad_normed * own_normed, axis=1))[:, None] / width_all
    input_grad = grad_residual + own(inverse_first) * (grad_normed - own_normed * inner_mean)

    small_grads = jnp.concatenate(
        [grad_gain_first[None], grad_gain_second[None], grad_router_first.T, grad_router_second.T],
        axis=0,
    )
    small_grads = lax.all_gather(small_grads, "grid", axis=1, tiled=True)
    small_grads = small_grads.reshape(-1, groups * BLOCKS, own_rows).transpose(1, 0, 2)
    small_grads = lax.psum_scatter(
        small_grads, ("t",) + PLACES, scatter_dimension=0, tiled=False
    )
    return (
        layer_output,
        input_grad.astype(BF16),
        small_grads[0],
        attention_kv_grad,
        attention_query_grad,
        attention_out_grad.astype(F32),
        small_grads[2:6].T,
        small_grads[1],
        small_grads[6:10].T,
        expert_gate_up_grad.astype(F32),
        expert_down_grad.astype(F32),
    )


def turned_slots(values, positions, head_width):
    cosine, sine_table = rope_tables(positions[:, 0], head_width)
    split = values.reshape(values.shape[0], -1, head_width)
    turned = rotate(split, cosine[:, None, :], -sine_table[:, None, :])
    return turned.reshape(values.shape).astype(BF16)


def solution(mesh):
    groups = mesh.shape["wide"] // BLOCKS
    shape = (groups, PLANES, HALVES, mesh.shape["grid"])
    inner_mesh = Mesh(mesh.devices.reshape(shape), ("t", "z", "x", "grid"))
    wide = ("t", "z", "x")
    in_specs = (
        P(wide, "grid"),
        P(),
        P(wide, None),
        P(wide, None),
        P(wide),
        P(wide, "grid", None, None),
        P(None, wide, "grid", None),
        P(None, "grid", None, wide),
        P(wide, None),
        P(wide),
        P(wide, None),
        P(None, wide, None, "grid"),
        P(None, "grid", wide),
        P(wide, "grid"),
    )
    out_specs = (
        P(wide, "grid"),
        P(wide, "grid"),
        P(wide),
        P(wide, "grid", None, None),
        P(None, wide, "grid", None),
        P(None, "grid", None, wide),
        P(wide, None),
        P(wide),
        P(wide, None),
        P(None, wide, None, "grid"),
        P(None, "grid", wide),
    )
    return jax.shard_map(
        per_device, mesh=inner_mesh, in_specs=in_specs, out_specs=out_specs, check_vma=False
    )
```

```python
import functools
import math

import jax
import jax.numpy as jnp
from jax import lax
from jax.experimental import pallas as pl
from jax.experimental.pallas import tpu as pltpu
from jax.sharding import Mesh, PartitionSpec as P

CAP = 320
PLANES = 4
HALVES = 2
BLOCKS = PLANES * HALVES
EPSILON = 1e-05
ROPE_BASE = 10000.0
NEGATIVE = -1e30
BF16 = jnp.bfloat16
F32 = jnp.float32
PLACES = ("z", "x")
MESH = pl.DeviceIdType.MESH
VMEM_BYTES = 56 * 1024 * 1024


def rope_tables(positions, table_width):
    half_width = table_width // 2
    frequency = ROPE_BASE ** (-jnp.arange(half_width, dtype=F32) / half_width)
    angles = positions.astype(F32)[:, None] * frequency[None, :]
    return (jnp.cos(angles), jnp.sin(angles))


def rotate(values, cosine, sine_table):
    half_width = values.shape[-1] // 2
    leading = values[..., :half_width]
    trailing = values[..., half_width:]
    return jnp.concatenate(
        [leading * cosine - trailing * sine_table, trailing * cosine + leading * sine_table],
        axis=-1,
    )


def dot(left, right):
    return jnp.dot(left, right, preferred_element_type=F32)


def contract_first(left, right):
    return lax.dot_general(left, right, (((0,), (0,)), ((), ())), preferred_element_type=F32)


def contract_last(left, right):
    return lax.dot_general(left, right, (((1,), (1,)), ((), ())), preferred_element_type=F32)


def exact(left, right):
    return jnp.dot(left, right, precision=lax.Precision.HIGHEST)


def first_of(position_ref, index):
    return position_ref[index]


def attention_scores(q, k_ref, low_bound, high_bound, tile, tile_rows, scaling):
    rows = pl.ds(pl.multiple_of(tile * tile_rows, tile_rows), tile_rows)
    keys = k_ref[rows, :]
    scores = contract_last(q, keys) * scaling
    column = tile * tile_rows + lax.broadcasted_iota(jnp.int32, scores.shape, 1)
    allowed = (column >= low_bound) & (column <= high_bound)
    return rows, keys, scores, allowed


def attention_forward_kernel(
    begin_ref, q_ref, k_ref, v_ref, rank_ref, low_ref, high_ref, out_ref, lse_ref, *, scaling
):
    block = pl.program_id(1)
    cap, width = out_ref.shape
    tile_rows = q_ref.shape[0]
    pick = (lax.broadcasted_iota(jnp.int32, (cap, tile_rows), 0) == rank_ref[0]).astype(BF16)
    q = dot(pick, q_ref[...]).astype(BF16)
    low_bound, high_bound = low_ref[...], high_ref[...]

    def step(tile, carried):
        largest, total, summed = carried
        rows, _, scores, allowed = attention_scores(
            q, k_ref, low_bound, high_bound, tile, tile_rows, scaling
        )
        scores = jnp.where(allowed, scores, NEGATIVE)
        new_largest = jnp.maximum(largest, jnp.max(scores, axis=1, keepdims=True))
        weights = jnp.where(allowed, jnp.exp(scores - new_largest), 0.0)
        shrink = jnp.exp(largest - new_largest)
        return (
            new_largest,
            total * shrink + jnp.sum(weights, axis=1, keepdims=True),
            summed * shrink + dot(weights.astype(BF16), v_ref[rows, :]),
        )

    largest, total, summed = lax.fori_loop(
        begin_ref[block],
        block + 1,
        step,
        (jnp.full((cap, 1), NEGATIVE, F32), jnp.zeros((cap, 1), F32), jnp.zeros((cap, width), F32)),
    )
    out_ref[...] = (summed / total).astype(BF16)
    lse_ref[0] = largest + jnp.log(total)


def attention_backward_kernel(
    begin_ref, q_ref, k_ref, v_ref, rank_ref, low_ref, high_ref, out_ref, lse_ref, grad_ref,
    dq_ref, dk_ref, dv_ref, *, scaling
):
    block = pl.program_id(1)
    cap, width = out_ref.shape
    tile_rows = q_ref.shape[0]
    pick = (lax.broadcasted_iota(jnp.int32, (cap, tile_rows), 0) == rank_ref[0]).astype(BF16)
    q = dot(pick, q_ref[...]).astype(BF16)
    low_bound, high_bound = low_ref[...], high_ref[...]
    grad = grad_ref[...]
    delta = jnp.sum(grad.astype(F32) * out_ref[...].astype(F32), axis=1, keepdims=True)
    lse = lse_ref[0]

    @pl.when(block == 0)
    def _():
        dk_ref[...] = jnp.zeros_like(dk_ref)
        dv_ref[...] = jnp.zeros_like(dv_ref)

    def step(tile, dq):
        rows, keys, scores, allowed = attention_scores(
            q, k_ref, low_bound, high_bound, tile, tile_rows, scaling
        )
        chances = jnp.where(allowed, jnp.exp(scores - lse), 0.0)
        dv_ref[rows, :] += contract_first(chances.astype(BF16), grad)
        grad_chances = contract_last(grad, v_ref[rows, :])
        grad_scores = (chances * (grad_chances - delta)).astype(BF16)
        dk_ref[rows, :] += contract_first(grad_scores, q) * scaling
        return dq + dot(grad_scores, keys)

    dq = lax.fori_loop(begin_ref[block], block + 1, step, jnp.zeros((cap, width), F32))
    dq_ref[...] = dq * scaling


def attention_specs(row_count, token_count, width):
    return dict(
        q=pl.BlockSpec((row_count, width), lambda h, b, s: (b, h)),
        k=pl.BlockSpec((token_count, width), lambda h, b, s: (0, h)),
        rank=pl.BlockSpec((1, 1, row_count), lambda h, b, s: (b, 0, 0)),
        bound=pl.BlockSpec((CAP, 1), lambda h, b, s: (b, 0)),
        slots=pl.BlockSpec((CAP, width), lambda h, b, s: (b, h)),
        lse=pl.BlockSpec((1, CAP, 1), lambda h, b, s: (h, b, 0)),
    )


def attention_forward(begin, q, k, v, rank, low_bound, high_bound, width):
    token_count, heads = q.shape[0], q.shape[1] // width
    row_count = token_count // BLOCKS
    s = attention_specs(row_count, token_count, width)
    return pl.pallas_call(
        functools.partial(attention_forward_kernel, scaling=1.0 / math.sqrt(width)),
        grid_spec=pltpu.PrefetchScalarGridSpec(
            num_scalar_prefetch=1,
            grid=(heads, BLOCKS),
            in_specs=[s["q"], s["k"], s["k"], s["rank"], s["bound"], s["bound"]],
            out_specs=[s["slots"], s["lse"]],
        ),
        out_shape=[
            jax.ShapeDtypeStruct((BLOCKS * CAP, heads * width), BF16),
            jax.ShapeDtypeStruct((heads, BLOCKS * CAP, 1), F32),
        ],
        compiler_params=pltpu.CompilerParams(vmem_limit_bytes=VMEM_BYTES),
        cost_estimate=pl.CostEstimate(
            flops=10_000_000_000, bytes_accessed=8_000_000, transcendentals=8_000_000
        ),
        name="attention_forward",
    )(begin, q, k, v, rank, low_bound, high_bound)


def attention_backward(begin, q, k, v, rank, low_bound, high_bound, out, lse, grad, width):
    token_count, heads = q.shape[0], q.shape[1] // width
    row_count = token_count // BLOCKS
    s = attention_specs(row_count, token_count, width)
    return pl.pallas_call(
        functools.partial(attention_backward_kernel, scaling=1.0 / math.sqrt(width)),
        grid_spec=pltpu.PrefetchScalarGridSpec(
            num_scalar_prefetch=1,
            grid=(heads, BLOCKS),
            in_specs=[
                s["q"], s["k"], s["k"], s["rank"], s["bound"], s["bound"],
                s["slots"], s["lse"], s["slots"],
            ],
            out_specs=[s["slots"], s["k"], s["k"]],
        ),
        out_shape=[
            jax.ShapeDtypeStruct((BLOCKS * CAP, heads * width), F32),
            jax.ShapeDtypeStruct((token_count, heads * width), F32),
            jax.ShapeDtypeStruct((token_count, heads * width), F32),
        ],
        compiler_params=pltpu.CompilerParams(vmem_limit_bytes=VMEM_BYTES),
        cost_estimate=pl.CostEstimate(
            flops=20_000_000_000, bytes_accessed=16_000_000, transcendentals=8_000_000
        ),
        name="attention_backward",
    )(begin, q, k, v, rank, low_bound, high_bound, out, lse, grad)


def exchanged(pieces):
    return lax.all_to_all(pieces, PLACES, 0, 0, tiled=True)


def spread_weights(pieces):
    return lax.all_gather(exchanged(pieces), "t", axis=0, tiled=False)


def return_gradients(pieces):
    return exchanged(lax.psum_scatter(pieces, "t", scatter_dimension=0, tiled=False))


def other_core(column):
    return column + 1 - 2 * (column % 2)


def meet(peers):
    barrier = pltpu.get_barrier_semaphore()
    for peer in peers:
        pl.semaphore_signal(barrier, inc=1, device_id=peer, device_id_type=MESH)
    pl.semaphore_wait(barrier, len(peers))


def partners():
    plane, half, column = lax.axis_index("z"), lax.axis_index("x"), lax.axis_index("grid")
    planes = [{"z": (plane + j) % PLANES} for j in range(PLANES)]
    along_x, along_y = {"x": 1 - half}, {"grid": (column + 2) % 4}
    core = {"grid": other_core(column)}
    return plane, half, column, planes, along_x, along_y, core


def gather_kernel(slots_ref, out_ref, send, recv, local, *, same):
    plane, half, column, planes, along_x, along_y, core = partners()
    cap, width = slots_ref.shape[-2:]
    middle = cap // 2
    meet(planes[1:] + [along_x, along_y, core])

    def piece(source, at_half, at_column, first=0, count=cap):
        columns = pl.ds(pl.multiple_of(at_column * width, width), width)
        return out_ref.at[source, at_half, pl.ds(first, count), columns]

    def source_of(j):
        return (plane - j + PLANES) % PLANES

    def slots_for(j):
        return slots_ref if same else slots_ref.at[(plane + j) % PLANES]

    started = []

    def copy(index, source, target, peer):
        made = pltpu.make_async_remote_copy(
            src_ref=source, dst_ref=target, send_sem=send.at[index], recv_sem=recv.at[index],
            device_id=peer, device_id_type=MESH,
        )
        made.start()
        started.append(made)

    def arrived(index, target, peer):
        pltpu.make_async_remote_copy(
            src_ref=target, dst_ref=target, send_sem=send.at[index], recv_sem=recv.at[index],
            device_id=peer, device_id_type=MESH,
        ).wait_recv()

    y_column, core_column = (column + 2) % 4, other_core(column)
    core_y = (core_column + 2) % 4
    for j in (2, 1, 3):
        copy(j, slots_for(j), piece(plane, half, column), planes[j])
    keep = pltpu.make_async_copy(slots_for(0), piece(plane, half, column), local)
    keep.start()

    def spread(j):
        place = piece(source_of(j), half, column)
        if j:
            arrived(j, place, planes[(PLANES - j) % PLANES])
        source = place if j else slots_for(0)
        copy(4 + j, source, place, along_x)
        copy(8 + j, source, place, along_y)
        copy(12 + j, source, place, core)

    def forward(j):
        source = source_of(j)
        from_x = piece(source, 1 - half, column)
        arrived(4 + j, from_x, along_x)
        part = piece(source, 1 - half, column, 0, middle)
        copy(16 + j, part, part, along_y)
        copy(20 + j, from_x, from_x, core)
        from_y = piece(source, half, y_column)
        arrived(8 + j, from_y, along_y)
        part = piece(source, half, y_column, middle, cap - middle)
        copy(24 + j, part, part, along_x)
        copy(28 + j, from_y, from_y, core)

    def cross(j):
        source = source_of(j)
        arrived(16 + j, piece(source, 1 - half, y_column, 0, middle), along_y)
        arrived(24 + j, piece(source, 1 - half, y_column, middle, cap - middle), along_x)
        place = piece(source, 1 - half, y_column)
        copy(32 + j, place, place, core)

    def from_core(j):
        source = source_of(j)
        arrived(12 + j, piece(source, half, core_column), core)
        arrived(20 + j, piece(source, 1 - half, core_column), core)
        arrived(28 + j, piece(source, half, core_y), core)
        arrived(32 + j, piece(source, 1 - half, core_y), core)

    order = (0, 1, 3, 2)
    for step in range(len(order) + 2):
        if step < len(order):
            spread(order[step])
        if 0 <= step - 1 < len(order):
            forward(order[step - 1])
        if 0 <= step - 2 < len(order):
            cross(order[step - 2])
    for j in order:
        from_core(j)
    for made in started:
        made.wait_send()
    keep.wait()


def gathered(slots, collective_id):
    rows, width = slots.shape[-2:]
    out = pl.pallas_call(
        functools.partial(gather_kernel, same=slots.ndim == 2),
        out_shape=jax.ShapeDtypeStruct((PLANES, HALVES, rows, 4 * width), BF16),
        in_specs=[pl.BlockSpec(memory_space=pl.ANY)],
        out_specs=pl.BlockSpec(memory_space=pl.ANY),
        scratch_shapes=[
            pltpu.SemaphoreType.DMA((36,)),
            pltpu.SemaphoreType.DMA((36,)),
            pltpu.SemaphoreType.DMA,
        ],
        compiler_params=pltpu.CompilerParams(collective_id=collective_id, has_side_effects=True),
        cost_estimate=pl.CostEstimate(flops=0, bytes_accessed=200_000_000, transcendentals=0),
        name="gather_rows",
    )(slots)
    return out.reshape(BLOCKS * rows, 4 * width)


def scatter_kernel(partial_ref, out_ref, own, other, crossing, side, send, recv, load):
    plane, half, column, planes, along_x, along_y, core = partners()
    cap, width = out_ref.shape[-2:]
    middle = cap // 2
    chunk = 32
    meet(planes[1:] + [along_x, along_y, core])
    y_column, core_column = (column + 2) % 4, other_core(column)
    core_y = (core_column + 2) % 4
    halves = (half, 1 - half, half, 1 - half)
    own_columns = (column, column, y_column, y_column)
    core_columns = (core_column, core_column, core_y, core_y)
    started = []

    def copy(index, source, target, peer):
        made = pltpu.make_async_remote_copy(
            src_ref=source, dst_ref=target, send_sem=send.at[index], recv_sem=recv.at[index],
            device_id=peer, device_id_type=MESH,
        )
        made.start()
        started.append(made)

    def arrived(index, target, peer):
        pltpu.make_async_remote_copy(
            src_ref=target, dst_ref=target, send_sem=send.at[index], recv_sem=recv.at[index],
            device_id=peer, device_id_type=MESH,
        ).wait_recv()

    def part(j, q, at_columns):
        columns = pl.ds(pl.multiple_of(at_columns[q] * width, width), width)
        return partial_ref.at[(plane + j) % PLANES, halves[q], :, columns]

    def loading(j, q):
        return pltpu.make_async_copy(part(j, q, own_columns), own.at[j, q], load.at[4 * j + q])

    order = (2, 1, 3, 0)
    for j in order:
        for q in (3, 2, 1, 0):
            copy(4 * j + q, part(j, q, core_columns), other.at[j, q], core)
            loading(j, q).start()

    def add(j, q, first, count, terms):
        def step(i, nothing):
            rows = pl.ds(pl.multiple_of(first + i * chunk, chunk), chunk)
            total = own[j, q, rows, :].astype(F32)
            for ref, index in terms:
                total = total + ref[index + (rows, slice(None))].astype(F32)
            own[j, q, rows, :] = total.astype(BF16)
            return nothing

        lax.fori_loop(0, count // chunk, step, 0)

    def chip_sum(j, q):
        arrived(4 * j + q, other.at[j, q], core)
        loading(j, q).wait()
        add(j, q, 0, cap, [(other, (j, q))])

    def stage_one(j):
        chip_sum(j, 3)
        first, last = pl.ds(0, middle), pl.ds(middle, cap - middle)
        copy(16 + j, own.at[j, 3, first], crossing.at[j, first], along_x)
        copy(20 + j, own.at[j, 3, last], crossing.at[j, last], along_y)
        chip_sum(j, 2)
        chip_sum(j, 1)
        chip_sum(j, 0)

    def stage_two(j):
        arrived(16 + j, crossing.at[j, pl.ds(0, middle)], along_x)
        add(j, 2, 0, middle, [(crossing, (j,))])
        copy(24 + j, own.at[j, 2], side.at[j, 1], along_y)
        arrived(20 + j, crossing.at[j, pl.ds(middle, cap - middle)], along_y)
        add(j, 1, middle, cap - middle, [(crossing, (j,))])
        copy(28 + j, own.at[j, 1], side.at[j, 0], along_x)

    def stage_three(j):
        arrived(24 + j, side.at[j, 1], along_y)
        arrived(28 + j, side.at[j, 0], along_x)
        add(j, 0, 0, cap, [(side, (j, 0)), (side, (j, 1))])
        if j:
            copy(32 + j, own.at[j, 0], out_ref.at[plane], planes[j])

    for step in range(len(order) + 2):
        if step < len(order):
            stage_one(order[step])
        if 0 <= step - 1 < len(order):
            stage_two(order[step - 1])
        if 0 <= step - 2 < len(order):
            stage_three(order[step - 2])
    keep = pltpu.make_async_copy(own.at[0, 0], out_ref.at[plane], load.at[16])
    keep.start()
    for j in range(1, PLANES):
        arrived(32 + j, out_ref.at[(plane - j + PLANES) % PLANES], planes[PLANES - j])
    for made in started:
        made.wait_send()
    keep.wait()


def scattered(partial, rows, collective_id):
    width = partial.shape[1] // 4
    return pl.pallas_call(
        scatter_kernel,
        out_shape=jax.ShapeDtypeStruct((PLANES, rows, width), BF16),
        in_specs=[pl.BlockSpec(memory_space=pl.ANY)],
        out_specs=pl.BlockSpec(memory_space=pl.ANY),
        scratch_shapes=[
            pltpu.VMEM((PLANES, 4, rows, width), BF16),
            pltpu.VMEM((PLANES, 4, rows, width), BF16),
            pltpu.VMEM((PLANES, rows, width), BF16),
            pltpu.VMEM((PLANES, 2, rows, width), BF16),
            pltpu.SemaphoreType.DMA((36,)),
            pltpu.SemaphoreType.DMA((36,)),
            pltpu.SemaphoreType.DMA((17,)),
        ],
        compiler_params=pltpu.CompilerParams(
            collective_id=collective_id, has_side_effects=True, vmem_limit_bytes=VMEM_BYTES
        ),
        cost_estimate=pl.CostEstimate(flops=0, bytes_accessed=200_000_000, transcendentals=0),
        name="scatter_rows",
    )(partial.reshape(PLANES, HALVES, rows, 4 * width))


def grid_sum(values):
    shape = values.shape
    return lax.all_gather(values.reshape(-1, 128), "grid", axis=0).sum(axis=0).reshape(shape)


def ranks(member):
    counted = member.astype(jnp.int32)
    before = jnp.cumsum(counted, axis=-1) - counted
    return jnp.where(member, before, -1)


def picks(rank):
    return jnp.arange(CAP, dtype=jnp.int32)[:, None] == rank[..., None, :]


def routed(routes):
    return routes[:, None, :] == jnp.arange(PLANES, dtype=jnp.int32)[None, :, None]


def route_gates(logits, member):
    shown = jnp.where(member, logits, NEGATIVE)
    weights = jnp.where(member, jnp.exp(shown - jnp.max(shown, axis=1, keepdims=True)), 0.0)
    return weights / jnp.sum(weights, axis=1, keepdims=True)


def logits_grad(gates, grad_gates):
    return gates * (grad_gates - jnp.sum(gates * grad_gates, axis=1, keepdims=True))


def per_device(
    tokens, segment_ids, attention_routes, expert_routes, attention_gain, attention_kv,
    attention_query, attention_out, attention_router, feedforward_gain, feedforward_router,
    expert_gate_up, expert_down, output_grad,
):
    groups = lax.axis_size("t")
    grid_count = lax.axis_size("grid")
    group = lax.axis_index("t")
    plane = lax.axis_index("z")
    place = plane * HALVES + lax.axis_index("x")
    column = lax.axis_index("grid")
    rows, features = tokens.shape
    width_all = features * grid_count
    token_count = BLOCKS * rows
    own_rows = attention_gain.shape[0]
    head_width = attention_kv.shape[3]
    head_pair = attention_kv.shape[1] // HALVES
    span = head_pair * head_width
    hidden_units = expert_gate_up.shape[3] // HALVES

    def mine(array, axis=0):
        return lax.dynamic_slice_in_dim(array, column * features, features, axis)

    def own(array):
        return lax.dynamic_slice_in_dim(array, place * rows, rows, 0)

    query_pieces = attention_query.reshape(PLANES, own_rows, HALVES, span).transpose(0, 2, 1, 3)
    kv_pieces = attention_kv.reshape(own_rows, HALVES, head_pair, 2, head_width)
    kv_pieces = kv_pieces.transpose(1, 0, 3, 2, 4).reshape(1, HALVES, own_rows, 2 * span)
    kv_pieces = jnp.broadcast_to(kv_pieces, (PLANES,) + kv_pieces.shape[1:])
    qkv_pieces = jnp.concatenate([query_pieces, kv_pieces], axis=-1)
    out_pieces = attention_out.reshape(BLOCKS, span, own_rows).swapaxes(1, 2)
    first_pieces = jnp.concatenate([qkv_pieces.reshape(BLOCKS, own_rows, 3 * span), out_pieces], axis=2)
    first_weight = spread_weights(first_pieces).reshape(width_all, 4 * span)
    qkv_weight, out_weight = first_weight[:, : 3 * span], first_weight[:, 3 * span :]
    up_pieces = expert_gate_up.reshape(PLANES, own_rows, 2, HALVES, hidden_units)
    up_pieces = up_pieces.transpose(0, 3, 1, 2, 4).reshape(BLOCKS, own_rows, 2 * hidden_units)
    down_pieces = expert_down.reshape(BLOCKS, hidden_units, own_rows).swapaxes(1, 2)
    second_pieces = jnp.concatenate([up_pieces, down_pieces], axis=2)
    second_weight = spread_weights(second_pieces).reshape(width_all, 3 * hidden_units)
    up_weight, down_weight = second_weight[:, : 2 * hidden_units], second_weight[:, 2 * hidden_units :]

    small = jnp.concatenate(
        [attention_gain[:, None], feedforward_gain[:, None], attention_router, feedforward_router],
        axis=1,
    )
    small = lax.all_gather(small.T, ("t", "z", "x"), axis=1, tiled=True)
    gain_first, gain_second = small[0].astype(F32), small[1].astype(F32)
    router_first, router_second = small[2:6].T, small[6:10].T

    own_routes = jnp.concatenate([attention_routes, expert_routes], axis=1)
    all_routes = lax.all_gather(own_routes, PLACES, axis=0, tiled=True)
    member_first = jnp.any(routed(all_routes[:, :2]), axis=2)
    member_second = jnp.any(routed(all_routes[:, 2:]), axis=2)

    def plane_rank(member):
        shown = lax.dynamic_index_in_dim(member, plane, 1, keepdims=False)
        return ranks(shown.reshape(BLOCKS, rows))

    rank_first, rank_second = plane_rank(member_first), plane_rank(member_second)
    own_member_first, own_member_second = own(member_first), own(member_second)
    own_pick_first = picks(ranks(own_member_first.T)).astype(BF16)
    own_pick_second = picks(ranks(own_member_second.T)).astype(BF16)

    def to_slots(values, pick):
        return jnp.einsum("est,tf->esf", pick, values, preferred_element_type=F32).astype(BF16)

    def to_tokens(slots, pick):
        return jnp.einsum("est,esf->etf", pick, slots, preferred_element_type=F32)

    grad_out = output_grad.astype(F32)
    grad_slots_second = gathered(to_slots(output_grad, own_pick_second), 1)

    inputs = gathered(tokens, 0).astype(F32)
    inverse_first = lax.rsqrt(jnp.mean(inputs * inputs, axis=-1, keepdims=True) + EPSILON)
    hidden_first = (inputs * inverse_first * gain_first).astype(BF16)
    gates_first = route_gates(dot(hidden_first, router_first), member_first)
    position = jnp.arange(token_count, dtype=jnp.int32)
    cosine, sine_table = rope_tables(position, head_width)
    cosine, sine_table = cosine[:, None, :], sine_table[:, None, :]
    qkv = dot(hidden_first, qkv_weight)

    def turned(values, sine):
        split = values.reshape(values.shape[0], -1, head_width)
        return rotate(split, cosine, sine).reshape(values.shape).astype(BF16)

    queries = turned(qkv[:, :span], sine_table)
    keys = turned(qkv[:, span : 2 * span], sine_table)
    values = qkv[:, 2 * span :].astype(BF16)
    segment = lax.dynamic_slice_in_dim(segment_ids, group * token_count, token_count, 0)
    opens = jnp.concatenate([jnp.ones((1,), jnp.bool_), segment[1:] != segment[:-1]])
    document_start = lax.cummax(jnp.where(opens, position, 0))
    begin = document_start.reshape(BLOCKS, rows)[:, 0] // rows
    slot_pick = picks(rank_first)

    def slot_values(per_token):
        shown = jnp.where(slot_pick, per_token.reshape(BLOCKS, 1, rows), 0)
        return jnp.sum(shown, axis=-1).reshape(-1, 1)

    block_first = jnp.repeat(jnp.arange(BLOCKS, dtype=jnp.int32) * rows, CAP)[:, None]
    filled = slot_values(jnp.ones((token_count,), jnp.int32)) > 0
    low_bound = jnp.where(filled, slot_values(document_start), block_first)
    high_bound = jnp.where(filled, slot_values(position), block_first)
    attention_args = (begin, queries, keys, values, rank_first[:, None, :], low_bound, high_bound)
    attended, lse = attention_forward(*attention_args, head_width)
    gate_first = lax.dynamic_index_in_dim(gates_first, plane, 1, keepdims=False)
    gate_slots_first = slot_values(gate_first)
    branch_slots = scattered(contract_last(attended, out_weight).astype(BF16), CAP, 2)
    branch_first = to_tokens(branch_slots, own_pick_first)
    own_gates_first = own(gates_first)
    residual = tokens.astype(F32) + jnp.sum(own_gates_first.T[:, :, None] * branch_first, axis=0)

    square = grid_sum(jnp.sum(residual * residual, axis=1))
    inverse_second = lax.rsqrt(square / width_all + EPSILON)[:, None]
    normed_second = residual * inverse_second
    hidden_second = (normed_second * mine(gain_second)).astype(BF16)
    slots_second = gathered(to_slots(hidden_second, own_pick_second), 1)
    plane_gates = dot(slots_second, router_second)
    rank_pick = picks(rank_second)

    def slot_values_second(per_token):
        shown = jnp.where(rank_pick, per_token.reshape(BLOCKS, 1, rows), 0)
        return jnp.sum(shown, axis=-1).reshape(-1)

    slot_member = jnp.stack(
        [slot_values_second(member_second[:, e].astype(jnp.int32)) for e in range(PLANES)], axis=1
    )
    filled_second = slot_values_second(jnp.ones((token_count,), jnp.int32))[:, None] > 0
    slot_gates = route_gates(plane_gates, (slot_member > 0) | ~filled_second)
    gate_slots_second = lax.dynamic_index_in_dim(slot_gates, plane, 1, keepdims=True)
    gate_up = dot(slots_second, up_weight)
    gate_pre, up_pre = gate_up[:, :hidden_units], gate_up[:, hidden_units:]
    sigmoid_gate = jax.nn.sigmoid(gate_pre)
    silu_gate = gate_pre * sigmoid_gate
    inner = silu_gate * up_pre
    result_slots = scattered(contract_last(inner.astype(BF16), down_weight).astype(BF16), CAP, 2)
    own_logits = grid_sum(dot(hidden_second, mine(router_second)))
    own_gates_second = route_gates(own_logits, own_member_second)
    branch_second = to_tokens(result_slots, own_pick_second)
    layer_output = residual + jnp.sum(own_gates_second.T[:, :, None] * branch_second, axis=0)
    layer_output = layer_output.astype(BF16)

    grad_inner = gate_slots_second * dot(grad_slots_second, down_weight)
    grad_gate = grad_inner * up_pre * sigmoid_gate * (1.0 + gate_pre * (1.0 - sigmoid_gate))
    grad_gate_up = jnp.concatenate([grad_gate, grad_inner * silu_gate], axis=1).astype(BF16)
    grad_rows = scattered(contract_last(grad_gate_up, up_weight).astype(BF16), CAP, 2)
    grad_up_weight = contract_first(slots_second, grad_gate_up).astype(BF16)
    grad_down = contract_first(grad_slots_second, (gate_slots_second * inner).astype(BF16))
    grad_second = jnp.concatenate([grad_up_weight, grad_down.astype(BF16)], axis=1)
    grad_second = return_gradients(grad_second.reshape(groups, BLOCKS, own_rows, 3 * hidden_units))
    expert_gate_up_grad = grad_second[:, :, : 2 * hidden_units].reshape(
        PLANES, HALVES, own_rows, 2, hidden_units
    )
    expert_gate_up_grad = expert_gate_up_grad.transpose(0, 2, 3, 1, 4).reshape(expert_gate_up.shape)
    expert_down_grad = grad_second[:, :, 2 * hidden_units :].swapaxes(1, 2).reshape(expert_down.shape)

    grad_gates_second = grid_sum(jnp.sum(branch_second * grad_out[None], axis=2).T)
    grad_logits_second = logits_grad(own_gates_second, grad_gates_second)
    grad_hidden_second = jnp.sum(to_tokens(grad_rows, own_pick_second), axis=0)
    grad_hidden_second = grad_hidden_second + exact(
        grad_logits_second, mine(router_second).astype(F32).T
    )
    grad_router_second = exact(hidden_second.astype(F32).T, grad_logits_second)
    grad_gain_second = jnp.sum(grad_hidden_second * normed_second, axis=0)
    grad_normed = grad_hidden_second * mine(gain_second)
    inner_mean = grid_sum(jnp.sum(grad_normed * normed_second, axis=1))[:, None] / width_all
    grad_residual = grad_out + inverse_second * (grad_normed - normed_second * inner_mean)

    grad_slots_first = gathered(to_slots(grad_residual.astype(BF16), own_pick_first), 1)
    grad_attended = gate_slots_first * dot(grad_slots_first, out_weight)
    grad_attended = grad_attended.astype(BF16)
    grad_out_weight = contract_first(
        grad_slots_first, (gate_slots_first * attended.astype(F32)).astype(BF16)
    )
    grad_out_weight = return_gradients(
        grad_out_weight.astype(BF16).reshape(groups, BLOCKS, own_rows, span)
    )
    attention_out_grad = grad_out_weight.swapaxes(1, 2).reshape(attention_out.shape)
    grad_query, grad_keys, grad_values = attention_backward(
        *attention_args, attended, lse, grad_attended, head_width
    )
    grad_query = jnp.einsum(
        "bst,bsf->btf",
        slot_pick.astype(BF16),
        turned_slots(grad_query, high_bound, head_width).reshape(BLOCKS, CAP, span),
        preferred_element_type=F32,
    )
    grad_qkv = jnp.concatenate(
        [
            grad_query.reshape(token_count, span).astype(BF16),
            turned(grad_keys, -sine_table),
            grad_values.astype(BF16),
        ],
        axis=1,
    )
    grad_hidden = contract_last(grad_qkv, qkv_weight).astype(BF16)
    grad_hidden = jnp.sum(scattered(grad_hidden, rows, 3).astype(F32), axis=0)
    grad_qkv_weight = contract_first(hidden_first, grad_qkv).astype(BF16)
    grad_qkv_weight = return_gradients(
        grad_qkv_weight.reshape(groups, BLOCKS, own_rows, 3 * span)
    ).astype(F32)
    attention_query_grad = grad_qkv_weight[..., :span].reshape(PLANES, HALVES, own_rows, span)
    attention_query_grad = attention_query_grad.transpose(0, 2, 1, 3).reshape(attention_query.shape)
    grad_kv_weight = grad_qkv_weight[..., span:].reshape(
        PLANES, HALVES, own_rows, 2, head_pair, head_width
    )
    attention_kv_grad = grad_kv_weight.sum(axis=0).transpose(1, 0, 3, 2, 4)
    attention_kv_grad = attention_kv_grad.reshape(attention_kv.shape)

    own_normed = tokens.astype(F32) * own(inverse_first)
    own_hidden = (own_normed * mine(gain_first)).astype(BF16)
    grad_gates_first = grid_sum(jnp.sum(branch_first * grad_residual[None], axis=2).T)
    grad_logits_first = logits_grad(own_gates_first, grad_gates_first)
    grad_hidden_first = grad_hidden + exact(
        grad_logits_first, mine(router_first).astype(F32).T
    )
    grad_router_first = exact(own_hidden.astype(F32).T, grad_logits_first)
    grad_gain_first = jnp.sum(grad_hidden_first * own_normed, axis=0)
    grad_normed = grad_hidden_first * mine(gain_first)
    inner_mean = grid_sum(jnp.sum(grad_normed * own_normed, axis=1))[:, None] / width_all
    input_grad = grad_residual + own(inverse_first) * (grad_normed - own_normed * inner_mean)

    small_grads = jnp.concatenate(
        [grad_gain_first[None], grad_gain_second[None], grad_router_first.T, grad_router_second.T],
        axis=0,
    )
    small_grads = lax.all_gather(small_grads, "grid", axis=1, tiled=True)
    small_grads = small_grads.reshape(-1, groups * BLOCKS, own_rows).transpose(1, 0, 2)
    small_grads = lax.psum_scatter(
        small_grads, ("t",) + PLACES, scatter_dimension=0, tiled=False
    )
    return (
        layer_output,
        input_grad.astype(BF16),
        small_grads[0],
        attention_kv_grad,
        attention_query_grad,
        attention_out_grad.astype(F32),
        small_grads[2:6].T,
        small_grads[1],
        small_grads[6:10].T,
        expert_gate_up_grad.astype(F32),
        expert_down_grad.astype(F32),
    )


def turned_slots(values, positions, head_width):
    cosine, sine_table = rope_tables(positions[:, 0], head_width)
    split = values.reshape(values.shape[0], -1, head_width)
    turned = rotate(split, cosine[:, None, :], -sine_table[:, None, :])
    return turned.reshape(values.shape).astype(BF16)


def solution(mesh):
    groups = mesh.shape["wide"] // BLOCKS
    shape = (groups, PLANES, HALVES, mesh.shape["grid"])
    inner_mesh = Mesh(mesh.devices.reshape(shape), ("t", "z", "x", "grid"))
    wide = ("t", "z", "x")
    in_specs = (
        P(wide, "grid"),
        P(),
        P(wide, None),
        P(wide, None),
        P(wide),
        P(wide, "grid", None, None),
        P(None, wide, "grid", None),
        P(None, "grid", None, wide),
        P(wide, None),
        P(wide),
        P(wide, None),
        P(None, wide, None, "grid"),
        P(None, "grid", wide),
        P(wide, "grid"),
    )
    out_specs = (
        P(wide, "grid"),
        P(wide, "grid"),
        P(wide),
        P(wide, "grid", None, None),
        P(None, wide, "grid", None),
        P(None, "grid", None, wide),
        P(wide, None),
        P(wide),
        P(wide, None),
        P(None, wide, None, "grid"),
        P(None, "grid", wide),
    )
    return jax.shard_map(
        per_device, mesh=inner_mesh, in_specs=in_specs, out_specs=out_specs, check_vma=False
    )
```

```python
import functools
import math

import jax
import jax.numpy as jnp
import numpy as np
from jax import lax
from jax.experimental import pallas as pl
from jax.experimental.pallas import tpu as pltpu
from jax.sharding import Mesh, PartitionSpec as P

CAP = 320
PLANES = 4
HALVES = 2
BLOCKS = PLANES * HALVES
EPSILON = 1e-05
ROPE_BASE = 10000.0
NEGATIVE = -1e30
BF16 = jnp.bfloat16
F32 = jnp.float32
PLACES = ("z", "x")
MESH = pl.DeviceIdType.MESH
VMEM_BYTES = 56 * 1024 * 1024


def rope_tables(token_count, width):
    half = width // 2
    frequency = np.float32(ROPE_BASE) ** (-np.arange(half, dtype=np.float32) / np.float32(half))
    angles = np.arange(token_count, dtype=np.float32)[:, None] * frequency.astype(np.float32)[None, :]
    cosine, sine = np.cos(angles).astype(np.float32), np.sin(angles).astype(np.float32)
    return np.concatenate([cosine, cosine], axis=1), np.concatenate([-sine, sine], axis=1)


def turned(values, cosine, sine):
    return values * cosine + pltpu.roll(values, values.shape[1] // 2, 1) * sine


def dot(left, right):
    return jnp.dot(left, right, preferred_element_type=F32)


def contract_first(left, right):
    return lax.dot_general(left, right, (((0,), (0,)), ((), ())), preferred_element_type=F32)


def contract_last(left, right):
    return lax.dot_general(left, right, (((1,), (1,)), ((), ())), preferred_element_type=F32)


def exact(left, right):
    return jnp.dot(left, right, precision=lax.Precision.HIGHEST)


def project_kernel(
    tokens_ref, gain_ref, weight_ref, router_ref, cos_ref, sin_ref,
    hidden_ref, q_ref, k_ref, v_ref, logits_ref, inverse_ref, *, head_width
):
    x = tokens_ref[0, 0].astype(F32)
    inverse = lax.rsqrt(jnp.mean(x * x, axis=1, keepdims=True) + EPSILON)
    inverse_ref[...] = inverse
    hidden = (x * inverse * gain_ref[...]).astype(BF16)
    hidden_ref[...] = hidden
    logits_ref[...] = dot(hidden, router_ref[...])
    made = dot(hidden, weight_ref[...])
    span = q_ref.shape[1]
    cosine, sine = cos_ref[...], sin_ref[...]
    for head in range(span // head_width):
        at = slice(head * head_width, (head + 1) * head_width)
        q_ref[:, at] = turned(made[:, at], cosine, sine).astype(BF16)
        k_ref[:, at] = turned(made[:, span:][:, at], cosine, sine).astype(BF16)
    v_ref[...] = made[:, 2 * span :].astype(BF16)


def project(tokens, rows, gain, weight, router, cosine, sine, span, head_width):
    width = tokens.shape[-1]
    token_count = BLOCKS * rows
    whole = lambda b: (0, 0)
    block = lambda b: (b, 0)
    return pl.pallas_call(
        functools.partial(project_kernel, head_width=head_width),
        grid=(BLOCKS,),
        in_specs=[
            pl.BlockSpec((1, 1, rows, width), lambda b: (b // HALVES, b % HALVES, 0, 0)),
            pl.BlockSpec((1, width), whole),
            pl.BlockSpec((width, 3 * span), whole),
            pl.BlockSpec((width, 128), whole),
            pl.BlockSpec((rows, head_width), block),
            pl.BlockSpec((rows, head_width), block),
        ],
        out_specs=[
            pl.BlockSpec((rows, width), block),
            pl.BlockSpec((rows, span), block),
            pl.BlockSpec((rows, span), block),
            pl.BlockSpec((rows, span), block),
            pl.BlockSpec((rows, 128), block),
            pl.BlockSpec((rows, 1), block),
        ],
        out_shape=[
            jax.ShapeDtypeStruct((token_count, width), BF16),
            jax.ShapeDtypeStruct((token_count, span), BF16),
            jax.ShapeDtypeStruct((token_count, span), BF16),
            jax.ShapeDtypeStruct((token_count, span), BF16),
            jax.ShapeDtypeStruct((token_count, 128), F32),
            jax.ShapeDtypeStruct((token_count, 1), F32),
        ],
        compiler_params=pltpu.CompilerParams(vmem_limit_bytes=VMEM_BYTES),
        cost_estimate=pl.CostEstimate(
            flops=20_000_000_000, bytes_accessed=50_000_000, transcendentals=0
        ),
        name="project",
    )(tokens, gain, weight, router, cosine, sine)


def attention_scores(q, k_ref, low_bound, high_bound, tile, tile_rows, scaling):
    rows = pl.ds(pl.multiple_of(tile * tile_rows, tile_rows), tile_rows)
    keys = k_ref[rows, :]
    scores = contract_last(q, keys) * scaling
    column = tile * tile_rows + lax.broadcasted_iota(jnp.int32, scores.shape, 1)
    allowed = (column >= low_bound) & (column <= high_bound)
    return rows, keys, scores, allowed


def attention_forward_kernel(
    begin_ref, q_ref, k_ref, v_ref, rank_ref, low_ref, high_ref, out_ref, lse_ref, *, scaling
):
    block = pl.program_id(1)
    cap, width = out_ref.shape
    tile_rows = q_ref.shape[0]
    pick = (lax.broadcasted_iota(jnp.int32, (cap, tile_rows), 0) == rank_ref[0]).astype(BF16)
    q = dot(pick, q_ref[...]).astype(BF16)
    low_bound, high_bound = low_ref[...], high_ref[...]

    def step(tile, carried):
        largest, total, summed = carried
        rows, _, scores, allowed = attention_scores(
            q, k_ref, low_bound, high_bound, tile, tile_rows, scaling
        )
        scores = jnp.where(allowed, scores, NEGATIVE)
        new_largest = jnp.maximum(largest, jnp.max(scores, axis=1, keepdims=True))
        weights = jnp.where(allowed, jnp.exp(scores - new_largest), 0.0)
        shrink = jnp.exp(largest - new_largest)
        return (
            new_largest,
            total * shrink + jnp.sum(weights, axis=1, keepdims=True),
            summed * shrink + dot(weights.astype(BF16), v_ref[rows, :]),
        )

    largest, total, summed = lax.fori_loop(
        begin_ref[block],
        block + 1,
        step,
        (jnp.full((cap, 1), NEGATIVE, F32), jnp.zeros((cap, 1), F32), jnp.zeros((cap, width), F32)),
    )
    out_ref[...] = (summed / total).astype(BF16)
    lse_ref[0] = largest + jnp.log(total)


def attention_backward_kernel(
    begin_ref, q_ref, k_ref, v_ref, rank_ref, low_ref, high_ref, out_ref, lse_ref, grad_ref,
    cos_ref, sin_ref, dq_ref, dk_ref, dv_ref, dk_sum, dv_sum, *, scaling
):
    block = pl.program_id(1)
    cap, width = out_ref.shape
    tile_rows = q_ref.shape[0]
    pick = (lax.broadcasted_iota(jnp.int32, (cap, tile_rows), 0) == rank_ref[0]).astype(BF16)
    q = dot(pick, q_ref[...]).astype(BF16)
    low_bound, high_bound = low_ref[...], high_ref[...]
    grad = grad_ref[...]
    delta = jnp.sum(grad.astype(F32) * out_ref[...].astype(F32), axis=1, keepdims=True)
    lse = lse_ref[0]

    @pl.when(block == 0)
    def _():
        dk_sum[...] = jnp.zeros_like(dk_sum)
        dv_sum[...] = jnp.zeros_like(dv_sum)

    def step(tile, dq):
        rows, keys, scores, allowed = attention_scores(
            q, k_ref, low_bound, high_bound, tile, tile_rows, scaling
        )
        chances = jnp.where(allowed, jnp.exp(scores - lse), 0.0)
        dv_sum[rows, :] += contract_first(chances.astype(BF16), grad)
        grad_chances = contract_last(grad, v_ref[rows, :])
        grad_scores = (chances * (grad_chances - delta)).astype(BF16)
        dk_sum[rows, :] += contract_first(grad_scores, q) * scaling
        return dq + dot(grad_scores, keys)

    dq = lax.fori_loop(begin_ref[block], block + 1, step, jnp.zeros((cap, width), F32)) * scaling
    high = dq.astype(BF16)
    rest = (dq - high.astype(F32)).astype(BF16)
    dq_tokens = contract_first(pick, high) + contract_first(pick, rest)
    own = pl.ds(pl.multiple_of(block * tile_rows, tile_rows), tile_rows)
    dq_ref[...] = turned(dq_tokens, cos_ref[own, :], -sin_ref[own, :]).astype(BF16)

    @pl.when(block == BLOCKS - 1)
    def _():
        def finish(tile, nothing):
            rows = pl.ds(pl.multiple_of(tile * tile_rows, tile_rows), tile_rows)
            dk_ref[rows, :] = turned(dk_sum[rows, :], cos_ref[rows, :], -sin_ref[rows, :]).astype(BF16)
            dv_ref[rows, :] = dv_sum[rows, :].astype(BF16)
            return nothing

        lax.fori_loop(0, BLOCKS, finish, 0)


def attention_specs(row_count, token_count, width):
    return dict(
        q=pl.BlockSpec((row_count, width), lambda h, b, s: (b, h)),
        k=pl.BlockSpec((token_count, width), lambda h, b, s: (0, h)),
        rank=pl.BlockSpec((1, 1, row_count), lambda h, b, s: (b, 0, 0)),
        bound=pl.BlockSpec((CAP, 1), lambda h, b, s: (b, 0)),
        slots=pl.BlockSpec((CAP, width), lambda h, b, s: (b, h)),
        table=pl.BlockSpec((token_count, width), lambda h, b, s: (0, 0)),
        lse=pl.BlockSpec((1, CAP, 1), lambda h, b, s: (h, b, 0)),
    )


def attention_forward(begin, q, k, v, rank, low_bound, high_bound, width):
    token_count, heads = q.shape[0], q.shape[1] // width
    row_count = token_count // BLOCKS
    s = attention_specs(row_count, token_count, width)
    return pl.pallas_call(
        functools.partial(attention_forward_kernel, scaling=1.0 / math.sqrt(width)),
        grid_spec=pltpu.PrefetchScalarGridSpec(
            num_scalar_prefetch=1,
            grid=(heads, BLOCKS),
            in_specs=[s["q"], s["k"], s["k"], s["rank"], s["bound"], s["bound"]],
            out_specs=[s["slots"], s["lse"]],
        ),
        out_shape=[
            jax.ShapeDtypeStruct((BLOCKS * CAP, heads * width), BF16),
            jax.ShapeDtypeStruct((heads, BLOCKS * CAP, 1), F32),
        ],
        compiler_params=pltpu.CompilerParams(vmem_limit_bytes=VMEM_BYTES),
        cost_estimate=pl.CostEstimate(
            flops=10_000_000_000, bytes_accessed=8_000_000, transcendentals=8_000_000
        ),
        name="attention_forward",
    )(begin, q, k, v, rank, low_bound, high_bound)


def attention_backward(begin, q, k, v, rank, low_bound, high_bound, out, lse, grad, cosine, sine, width):
    token_count, heads = q.shape[0], q.shape[1] // width
    row_count = token_count // BLOCKS
    s = attention_specs(row_count, token_count, width)
    return pl.pallas_call(
        functools.partial(attention_backward_kernel, scaling=1.0 / math.sqrt(width)),
        grid_spec=pltpu.PrefetchScalarGridSpec(
            num_scalar_prefetch=1,
            grid=(heads, BLOCKS),
            in_specs=[
                s["q"], s["k"], s["k"], s["rank"], s["bound"], s["bound"],
                s["slots"], s["lse"], s["slots"], s["table"], s["table"],
            ],
            out_specs=[s["q"], s["k"], s["k"]],
            scratch_shapes=[pltpu.VMEM((token_count, width), F32)] * 2,
        ),
        out_shape=[
            jax.ShapeDtypeStruct((token_count, heads * width), BF16),
            jax.ShapeDtypeStruct((token_count, heads * width), BF16),
            jax.ShapeDtypeStruct((token_count, heads * width), BF16),
        ],
        compiler_params=pltpu.CompilerParams(vmem_limit_bytes=VMEM_BYTES),
        cost_estimate=pl.CostEstimate(
            flops=20_000_000_000, bytes_accessed=16_000_000, transcendentals=8_000_000
        ),
        name="attention_backward",
    )(begin, q, k, v, rank, low_bound, high_bound, out, lse, grad, cosine, sine)


def exchanged(pieces):
    return lax.all_to_all(pieces, PLACES, 0, 0, tiled=True)


def spread_weights(pieces):
    return lax.all_gather(exchanged(pieces), "t", axis=0, tiled=False)


def return_gradients(pieces):
    return exchanged(lax.psum_scatter(pieces, "t", scatter_dimension=0, tiled=False))


def other_core(column):
    return column + 1 - 2 * (column % 2)


def meet(peers):
    barrier = pltpu.get_barrier_semaphore()
    for peer in peers:
        pl.semaphore_signal(barrier, inc=1, device_id=peer, device_id_type=MESH)
    pl.semaphore_wait(barrier, len(peers))


def partners():
    plane, half, column = lax.axis_index("z"), lax.axis_index("x"), lax.axis_index("grid")
    planes = [{"z": (plane + j) % PLANES} for j in range(PLANES)]
    along_x, along_y = {"x": 1 - half}, {"grid": (column + 2) % 4}
    core = {"grid": other_core(column)}
    return plane, half, column, planes, along_x, along_y, core


def gather_kernel(slots_ref, out_ref, send, recv, local, *, same):
    plane, half, column, planes, along_x, along_y, core = partners()
    cap, width = slots_ref.shape[-2:]
    middle = cap // 32 * 16
    meet(planes[1:] + [along_x, along_y, core])

    def piece(source, at_half, at_column, first=0, count=cap):
        columns = pl.ds(pl.multiple_of(at_column * width, width), width)
        return out_ref.at[source, at_half, pl.ds(first, count), columns]

    def source_of(j):
        return (plane - j + PLANES) % PLANES

    def slots_for(j):
        return slots_ref if same else slots_ref.at[(plane + j) % PLANES]

    started = []

    def copy(index, source, target, peer):
        made = pltpu.make_async_remote_copy(
            src_ref=source, dst_ref=target, send_sem=send.at[index], recv_sem=recv.at[index],
            device_id=peer, device_id_type=MESH,
        )
        made.start()
        started.append(made)

    def arrived(index, target, peer):
        pltpu.make_async_remote_copy(
            src_ref=target, dst_ref=target, send_sem=send.at[index], recv_sem=recv.at[index],
            device_id=peer, device_id_type=MESH,
        ).wait_recv()

    y_column, core_column = (column + 2) % 4, other_core(column)
    core_y = (core_column + 2) % 4
    for j in (2, 1, 3):
        copy(j, slots_for(j), piece(plane, half, column), planes[j])
    keep = pltpu.make_async_copy(slots_for(0), piece(plane, half, column), local)
    keep.start()

    def spread(j):
        place = piece(source_of(j), half, column)
        if j:
            arrived(j, place, planes[(PLANES - j) % PLANES])
        source = place if j else slots_for(0)
        copy(4 + j, source, place, along_x)
        copy(8 + j, source, place, along_y)
        copy(12 + j, source, place, core)

    def forward(j):
        source = source_of(j)
        from_x = piece(source, 1 - half, column)
        arrived(4 + j, from_x, along_x)
        part = piece(source, 1 - half, column, 0, middle)
        copy(16 + j, part, part, along_y)
        copy(20 + j, from_x, from_x, core)
        from_y = piece(source, half, y_column)
        arrived(8 + j, from_y, along_y)
        part = piece(source, half, y_column, middle, cap - middle)
        copy(24 + j, part, part, along_x)
        copy(28 + j, from_y, from_y, core)

    def cross(j):
        source = source_of(j)
        arrived(16 + j, piece(source, 1 - half, y_column, 0, middle), along_y)
        arrived(24 + j, piece(source, 1 - half, y_column, middle, cap - middle), along_x)
        place = piece(source, 1 - half, y_column)
        copy(32 + j, place, place, core)

    def from_core(j):
        source = source_of(j)
        arrived(12 + j, piece(source, half, core_column), core)
        arrived(20 + j, piece(source, 1 - half, core_column), core)
        arrived(28 + j, piece(source, half, core_y), core)
        arrived(32 + j, piece(source, 1 - half, core_y), core)

    order = (0, 1, 3, 2)
    for step in range(len(order) + 2):
        if step < len(order):
            spread(order[step])
        if 0 <= step - 1 < len(order):
            forward(order[step - 1])
        if 0 <= step - 2 < len(order):
            cross(order[step - 2])
    for j in order:
        from_core(j)
    for made in started:
        made.wait_send()
    keep.wait()


def gathered(slots, collective_id):
    rows, width = slots.shape[-2:]
    out = pl.pallas_call(
        functools.partial(gather_kernel, same=slots.ndim == 2),
        out_shape=jax.ShapeDtypeStruct((PLANES, HALVES, rows, 4 * width), BF16),
        in_specs=[pl.BlockSpec(memory_space=pl.ANY)],
        out_specs=pl.BlockSpec(memory_space=pl.ANY),
        scratch_shapes=[
            pltpu.SemaphoreType.DMA((36,)),
            pltpu.SemaphoreType.DMA((36,)),
            pltpu.SemaphoreType.DMA,
        ],
        compiler_params=pltpu.CompilerParams(collective_id=collective_id, has_side_effects=True),
        cost_estimate=pl.CostEstimate(flops=0, bytes_accessed=200_000_000, transcendentals=0),
        name="gather_rows",
    )(slots)
    return out


def scatter_kernel(partial_ref, out_ref, own, other, crossing, side, send, recv, load):
    plane, half, column, planes, along_x, along_y, core = partners()
    cap, width = out_ref.shape[-2:]
    middle = cap // 2
    chunk = 32
    meet(planes[1:] + [along_x, along_y, core])
    y_column, core_column = (column + 2) % 4, other_core(column)
    core_y = (core_column + 2) % 4
    halves = (half, 1 - half, half, 1 - half)
    own_columns = (column, column, y_column, y_column)
    core_columns = (core_column, core_column, core_y, core_y)
    started = []

    def copy(index, source, target, peer):
        made = pltpu.make_async_remote_copy(
            src_ref=source, dst_ref=target, send_sem=send.at[index], recv_sem=recv.at[index],
            device_id=peer, device_id_type=MESH,
        )
        made.start()
        started.append(made)

    def arrived(index, target, peer):
        pltpu.make_async_remote_copy(
            src_ref=target, dst_ref=target, send_sem=send.at[index], recv_sem=recv.at[index],
            device_id=peer, device_id_type=MESH,
        ).wait_recv()

    def part(j, q, at_columns):
        columns = pl.ds(pl.multiple_of(at_columns[q] * width, width), width)
        return partial_ref.at[(plane + j) % PLANES, halves[q], :, columns]

    def loading(j, q):
        return pltpu.make_async_copy(part(j, q, own_columns), own.at[j, q], load.at[4 * j + q])

    order = (2, 1, 3, 0)
    for j in order:
        for q in (3, 2, 1, 0):
            copy(4 * j + q, part(j, q, core_columns), other.at[j, q], core)
            loading(j, q).start()

    def add(j, q, first, count, terms):
        def step(i, nothing):
            rows = pl.ds(pl.multiple_of(first + i * chunk, chunk), chunk)
            total = own[j, q, rows, :].astype(F32)
            for ref, index in terms:
                total = total + ref[index + (rows, slice(None))].astype(F32)
            own[j, q, rows, :] = total.astype(BF16)
            return nothing

        lax.fori_loop(0, count // chunk, step, 0)

    def chip_sum(j, q):
        arrived(4 * j + q, other.at[j, q], core)
        loading(j, q).wait()
        add(j, q, 0, cap, [(other, (j, q))])

    def stage_one(j):
        chip_sum(j, 3)
        first, last = pl.ds(0, middle), pl.ds(middle, cap - middle)
        copy(16 + j, own.at[j, 3, first], crossing.at[j, first], along_x)
        copy(20 + j, own.at[j, 3, last], crossing.at[j, last], along_y)
        chip_sum(j, 2)
        chip_sum(j, 1)
        chip_sum(j, 0)

    def stage_two(j):
        arrived(16 + j, crossing.at[j, pl.ds(0, middle)], along_x)
        add(j, 2, 0, middle, [(crossing, (j,))])
        copy(24 + j, own.at[j, 2], side.at[j, 1], along_y)
        arrived(20 + j, crossing.at[j, pl.ds(middle, cap - middle)], along_y)
        add(j, 1, middle, cap - middle, [(crossing, (j,))])
        copy(28 + j, own.at[j, 1], side.at[j, 0], along_x)

    def stage_three(j):
        arrived(24 + j, side.at[j, 1], along_y)
        arrived(28 + j, side.at[j, 0], along_x)
        add(j, 0, 0, cap, [(side, (j, 0)), (side, (j, 1))])
        if j:
            copy(32 + j, own.at[j, 0], out_ref.at[plane], planes[j])

    for step in range(len(order) + 2):
        if step < len(order):
            stage_one(order[step])
        if 0 <= step - 1 < len(order):
            stage_two(order[step - 1])
        if 0 <= step - 2 < len(order):
            stage_three(order[step - 2])
    keep = pltpu.make_async_copy(own.at[0, 0], out_ref.at[plane], load.at[16])
    keep.start()
    for j in range(1, PLANES):
        arrived(32 + j, out_ref.at[(plane - j + PLANES) % PLANES], planes[PLANES - j])
    for made in started:
        made.wait_send()
    keep.wait()


def scattered(partial, rows, collective_id):
    width = partial.shape[1] // 4
    return pl.pallas_call(
        scatter_kernel,
        out_shape=jax.ShapeDtypeStruct((PLANES, rows, width), BF16),
        in_specs=[pl.BlockSpec(memory_space=pl.ANY)],
        out_specs=pl.BlockSpec(memory_space=pl.ANY),
        scratch_shapes=[
            pltpu.VMEM((PLANES, 4, rows, width), BF16),
            pltpu.VMEM((PLANES, 4, rows, width), BF16),
            pltpu.VMEM((PLANES, rows, width), BF16),
            pltpu.VMEM((PLANES, 2, rows, width), BF16),
            pltpu.SemaphoreType.DMA((36,)),
            pltpu.SemaphoreType.DMA((36,)),
            pltpu.SemaphoreType.DMA((17,)),
        ],
        compiler_params=pltpu.CompilerParams(
            collective_id=collective_id, has_side_effects=True, vmem_limit_bytes=VMEM_BYTES
        ),
        cost_estimate=pl.CostEstimate(flops=0, bytes_accessed=200_000_000, transcendentals=0),
        name="scatter_rows",
    )(partial.reshape(PLANES, HALVES, rows, 4 * width))


def grid_sum(values):
    shape = values.shape
    return lax.all_gather(values.reshape(-1, 128), "grid", axis=0).sum(axis=0).reshape(shape)


def ranks(member):
    counted = member.astype(jnp.int32)
    before = jnp.cumsum(counted, axis=-1) - counted
    return jnp.where(member, before, -1)


def picks(rank):
    return jnp.arange(CAP, dtype=jnp.int32)[:, None] == rank[..., None, :]


def routed(routes):
    return routes[:, None, :] == jnp.arange(PLANES, dtype=jnp.int32)[None, :, None]


def route_gates(logits, member):
    shown = jnp.where(member, logits, NEGATIVE)
    weights = jnp.where(member, jnp.exp(shown - jnp.max(shown, axis=1, keepdims=True)), 0.0)
    return weights / jnp.sum(weights, axis=1, keepdims=True)


def logits_grad(gates, grad_gates):
    return gates * (grad_gates - jnp.sum(gates * grad_gates, axis=1, keepdims=True))


def per_device(
    tokens, segment_ids, attention_routes, expert_routes, attention_gain, attention_kv,
    attention_query, attention_out, attention_router, feedforward_gain, feedforward_router,
    expert_gate_up, expert_down, output_grad,
):
    groups = lax.axis_size("t")
    grid_count = lax.axis_size("grid")
    group = lax.axis_index("t")
    plane = lax.axis_index("z")
    place = plane * HALVES + lax.axis_index("x")
    column = lax.axis_index("grid")
    rows, features = tokens.shape
    width_all = features * grid_count
    token_count = BLOCKS * rows
    own_rows = attention_gain.shape[0]
    head_width = attention_kv.shape[3]
    head_pair = attention_kv.shape[1] // HALVES
    span = head_pair * head_width
    hidden_units = expert_gate_up.shape[3] // HALVES

    def mine(array, axis=0):
        return lax.dynamic_slice_in_dim(array, column * features, features, axis)

    def own(array):
        return lax.dynamic_slice_in_dim(array, place * rows, rows, 0)

    query_pieces = attention_query.reshape(PLANES, own_rows, HALVES, span).transpose(0, 2, 1, 3)
    kv_pieces = attention_kv.reshape(own_rows, HALVES, head_pair, 2, head_width)
    kv_pieces = kv_pieces.transpose(1, 0, 3, 2, 4).reshape(1, HALVES, own_rows, 2 * span)
    kv_pieces = jnp.broadcast_to(kv_pieces, (PLANES,) + kv_pieces.shape[1:])
    qkv_pieces = jnp.concatenate([query_pieces, kv_pieces], axis=-1)
    out_pieces = attention_out.reshape(BLOCKS, span, own_rows).swapaxes(1, 2)
    first_pieces = jnp.concatenate([qkv_pieces.reshape(BLOCKS, own_rows, 3 * span), out_pieces], axis=2)
    first_weight = spread_weights(first_pieces).reshape(width_all, 4 * span)
    qkv_weight, out_weight = first_weight[:, : 3 * span], first_weight[:, 3 * span :]
    up_pieces = expert_gate_up.reshape(PLANES, own_rows, 2, HALVES, hidden_units)
    up_pieces = up_pieces.transpose(0, 3, 1, 2, 4).reshape(BLOCKS, own_rows, 2 * hidden_units)
    down_pieces = expert_down.reshape(BLOCKS, hidden_units, own_rows).swapaxes(1, 2)
    second_pieces = jnp.concatenate([up_pieces, down_pieces], axis=2)
    second_weight = spread_weights(second_pieces).reshape(width_all, 3 * hidden_units)
    up_weight, down_weight = second_weight[:, : 2 * hidden_units], second_weight[:, 2 * hidden_units :]

    own_routes = jnp.concatenate([attention_routes, expert_routes], axis=1)
    small = jnp.concatenate(
        [attention_gain[:, None], feedforward_gain[:, None], attention_router, feedforward_router],
        axis=1,
    )
    small = lax.all_gather(small, "t", axis=0).reshape(-1, small.shape[1])
    small = small.T.reshape(small.shape[1], -1)
    spare = jnp.zeros((small.shape[0], features - small.shape[1] % features), BF16)
    small = jnp.concatenate([small, spare], axis=1).reshape(-1, features)
    under = jnp.concatenate([own_routes.T.astype(BF16), small], axis=0)
    under = jnp.pad(under, ((0, -under.shape[0] % 16), (0, 0)))
    everything = gathered(jnp.concatenate([tokens, under], axis=0), 0)
    under = everything[:, :, rows:, :features].reshape(BLOCKS, -1, features)
    all_routes = under[:, :4].swapaxes(1, 2).reshape(token_count, 4).astype(jnp.int32)
    small = under[:, 4 : 4 + 10].reshape(BLOCKS, 10, features)[:, :, : groups * own_rows]
    small = small.reshape(BLOCKS, 10, groups, own_rows).transpose(1, 2, 0, 3).reshape(10, width_all)
    gain_first, gain_second = small[0].astype(F32), small[1].astype(F32)
    router_first, router_second = small[2:6].T, small[6:10].T

    member_first = jnp.any(routed(all_routes[:, :2]), axis=2)
    member_second = jnp.any(routed(all_routes[:, 2:]), axis=2)

    def plane_rank(member):
        shown = lax.dynamic_index_in_dim(member, plane, 1, keepdims=False)
        return ranks(shown.reshape(BLOCKS, rows))

    rank_first, rank_second = plane_rank(member_first), plane_rank(member_second)
    own_member_first, own_member_second = own(member_first), own(member_second)
    own_pick_first = picks(ranks(own_member_first.T)).astype(BF16)
    own_pick_second = picks(ranks(own_member_second.T)).astype(BF16)

    def to_slots(values, pick):
        return jnp.einsum("est,tf->esf", pick, values, preferred_element_type=F32).astype(BF16)

    def to_tokens(slots, pick):
        return jnp.einsum("est,esf->etf", pick, slots, preferred_element_type=F32)

    grad_out = output_grad.astype(F32)
    grad_slots_second = gathered(to_slots(output_grad, own_pick_second), 1).reshape(BLOCKS * CAP, -1)

    cosine, sine = rope_tables(token_count, head_width)
    cosine, sine = jnp.asarray(cosine), jnp.asarray(sine)
    hidden_first, queries, keys, values, logits_first, inverse_first = project(
        everything, rows, gain_first[None], first_weight, jnp.pad(router_first, ((0, 0), (0, 124))),
        cosine, sine, span, head_width,
    )
    gates_first = route_gates(logits_first[:, :PLANES], member_first)
    position = jnp.arange(token_count, dtype=jnp.int32)
    segment = lax.dynamic_slice_in_dim(segment_ids, group * token_count, token_count, 0)
    opens = jnp.concatenate([jnp.ones((1,), jnp.bool_), segment[1:] != segment[:-1]])
    document_start = lax.cummax(jnp.where(opens, position, 0))
    begin = document_start.reshape(BLOCKS, rows)[:, 0] // rows
    slot_pick = picks(rank_first)

    def slot_values(per_token):
        shown = jnp.where(slot_pick, per_token.reshape(BLOCKS, 1, rows), 0)
        return jnp.sum(shown, axis=-1).reshape(-1, 1)

    block_first = jnp.repeat(jnp.arange(BLOCKS, dtype=jnp.int32) * rows, CAP)[:, None]
    filled = slot_values(jnp.ones((token_count,), jnp.int32)) > 0
    low_bound = jnp.where(filled, slot_values(document_start), block_first)
    high_bound = jnp.where(filled, slot_values(position), block_first)
    attention_args = (begin, queries, keys, values, rank_first[:, None, :], low_bound, high_bound)
    attended, lse = attention_forward(*attention_args, head_width)
    gate_first = lax.dynamic_index_in_dim(gates_first, plane, 1, keepdims=False)
    gate_slots_first = slot_values(gate_first)
    branch_slots = scattered(contract_last(attended, out_weight).astype(BF16), CAP, 2)
    branch_first = to_tokens(branch_slots, own_pick_first)
    own_gates_first = own(gates_first)
    residual = tokens.astype(F32) + jnp.sum(own_gates_first.T[:, :, None] * branch_first, axis=0)

    square = grid_sum(jnp.sum(residual * residual, axis=1))
    inverse_second = lax.rsqrt(square / width_all + EPSILON)[:, None]
    normed_second = residual * inverse_second
    hidden_second = (normed_second * mine(gain_second)).astype(BF16)
    slots_second = gathered(to_slots(hidden_second, own_pick_second), 1).reshape(BLOCKS * CAP, -1)
    plane_gates = dot(slots_second, router_second)
    rank_pick = picks(rank_second)

    def slot_values_second(per_token):
        shown = jnp.where(rank_pick, per_token.reshape(BLOCKS, 1, rows), 0)
        return jnp.sum(shown, axis=-1).reshape(-1)

    slot_member = jnp.stack(
        [slot_values_second(member_second[:, e].astype(jnp.int32)) for e in range(PLANES)], axis=1
    )
    filled_second = slot_values_second(jnp.ones((token_count,), jnp.int32))[:, None] > 0
    slot_gates = route_gates(plane_gates, (slot_member > 0) | ~filled_second)
    gate_slots_second = lax.dynamic_index_in_dim(slot_gates, plane, 1, keepdims=True)
    gate_up = dot(slots_second, up_weight)
    gate_pre, up_pre = gate_up[:, :hidden_units], gate_up[:, hidden_units:]
    sigmoid_gate = jax.nn.sigmoid(gate_pre)
    silu_gate = gate_pre * sigmoid_gate
    inner = silu_gate * up_pre
    result_slots = scattered(contract_last(inner.astype(BF16), down_weight).astype(BF16), CAP, 2)
    own_logits = grid_sum(dot(hidden_second, mine(router_second)))
    own_gates_second = route_gates(own_logits, own_member_second)
    branch_second = to_tokens(result_slots, own_pick_second)
    layer_output = residual + jnp.sum(own_gates_second.T[:, :, None] * branch_second, axis=0)
    layer_output = layer_output.astype(BF16)

    grad_inner = gate_slots_second * dot(grad_slots_second, down_weight)
    grad_gate = grad_inner * up_pre * sigmoid_gate * (1.0 + gate_pre * (1.0 - sigmoid_gate))
    grad_gate_up = jnp.concatenate([grad_gate, grad_inner * silu_gate], axis=1).astype(BF16)
    grad_rows = contract_last(grad_gate_up, up_weight).astype(BF16)
    grad_up_weight = contract_first(slots_second, grad_gate_up).astype(BF16)
    grad_down = contract_first(grad_slots_second, (gate_slots_second * inner).astype(BF16))
    grad_second = jnp.concatenate([grad_up_weight, grad_down.astype(BF16)], axis=1)
    grad_rows, grad_second = lax.optimization_barrier((grad_rows, grad_second))
    grad_rows = scattered(grad_rows, CAP, 2)
    grad_second = return_gradients(grad_second.reshape(groups, BLOCKS, own_rows, 3 * hidden_units))
    expert_gate_up_grad = grad_second[:, :, : 2 * hidden_units].reshape(
        PLANES, HALVES, own_rows, 2, hidden_units
    )
    expert_gate_up_grad = expert_gate_up_grad.transpose(0, 2, 3, 1, 4).reshape(expert_gate_up.shape)
    expert_down_grad = grad_second[:, :, 2 * hidden_units :].swapaxes(1, 2).reshape(expert_down.shape)

    grad_gates_second = grid_sum(jnp.sum(branch_second * grad_out[None], axis=2).T)
    grad_logits_second = logits_grad(own_gates_second, grad_gates_second)
    grad_hidden_second = jnp.sum(to_tokens(grad_rows, own_pick_second), axis=0)
    grad_hidden_second = grad_hidden_second + exact(
        grad_logits_second, mine(router_second).astype(F32).T
    )
    grad_router_second = exact(hidden_second.astype(F32).T, grad_logits_second)
    grad_gain_second = jnp.sum(grad_hidden_second * normed_second, axis=0)
    grad_normed = grad_hidden_second * mine(gain_second)
    inner_mean = grid_sum(jnp.sum(grad_normed * normed_second, axis=1))[:, None] / width_all
    grad_residual = grad_out + inverse_second * (grad_normed - normed_second * inner_mean)

    grad_slots_first = gathered(to_slots(grad_residual.astype(BF16), own_pick_first), 1).reshape(BLOCKS * CAP, -1)
    grad_attended = gate_slots_first * dot(grad_slots_first, out_weight)
    grad_attended = grad_attended.astype(BF16)
    grad_out_weight = contract_first(
        grad_slots_first, (gate_slots_first * attended.astype(F32)).astype(BF16)
    )
    grad_qkv = jnp.concatenate(
        attention_backward(
            *attention_args, attended, lse, grad_attended, cosine, sine, head_width
        ),
        axis=1,
    )
    grad_hidden = contract_last(grad_qkv, qkv_weight).astype(BF16)
    grad_first = jnp.concatenate(
        [contract_first(hidden_first, grad_qkv).astype(BF16), grad_out_weight.astype(BF16)], axis=1
    )
    grad_hidden, grad_first = lax.optimization_barrier((grad_hidden, grad_first))
    grad_hidden = jnp.sum(scattered(grad_hidden, rows, 3).astype(F32), axis=0)
    grad_first = return_gradients(grad_first.reshape(groups, BLOCKS, own_rows, 4 * span))
    attention_out_grad = grad_first[..., 3 * span :].swapaxes(1, 2).reshape(attention_out.shape)
    attention_query_grad = grad_first[..., :span].reshape(PLANES, HALVES, own_rows, span)
    attention_query_grad = attention_query_grad.transpose(0, 2, 1, 3).reshape(attention_query.shape)
    grad_kv_weight = grad_first[..., span : 3 * span].astype(F32).reshape(
        PLANES, HALVES, own_rows, 2, head_pair, head_width
    )
    attention_kv_grad = grad_kv_weight.sum(axis=0).transpose(1, 0, 3, 2, 4)
    attention_kv_grad = attention_kv_grad.reshape(attention_kv.shape)

    own_normed = tokens.astype(F32) * own(inverse_first)
    own_hidden = (own_normed * mine(gain_first)).astype(BF16)
    grad_gates_first = grid_sum(jnp.sum(branch_first * grad_residual[None], axis=2).T)
    grad_logits_first = logits_grad(own_gates_first, grad_gates_first)
    grad_hidden_first = grad_hidden + exact(
        grad_logits_first, mine(router_first).astype(F32).T
    )
    grad_router_first = exact(own_hidden.astype(F32).T, grad_logits_first)
    grad_gain_first = jnp.sum(grad_hidden_first * own_normed, axis=0)
    grad_normed = grad_hidden_first * mine(gain_first)
    inner_mean = grid_sum(jnp.sum(grad_normed * own_normed, axis=1))[:, None] / width_all
    input_grad = grad_residual + own(inverse_first) * (grad_normed - own_normed * inner_mean)

    small_grads = jnp.concatenate(
        [grad_gain_first[None], grad_gain_second[None], grad_router_first.T, grad_router_second.T],
        axis=0,
    )
    small_grads = jnp.sum(lax.all_gather(small_grads, ("t",) + PLACES, axis=0), axis=0)
    small_grads = lax.all_gather(small_grads, "grid", axis=1, tiled=True)
    small_grads = lax.dynamic_slice_in_dim(
        small_grads, (group * BLOCKS + place) * own_rows, own_rows, 1
    )
    return (
        layer_output,
        input_grad.astype(BF16),
        small_grads[0],
        attention_kv_grad,
        attention_query_grad.astype(F32),
        attention_out_grad.astype(F32),
        small_grads[2:6].T,
        small_grads[1],
        small_grads[6:10].T,
        expert_gate_up_grad.astype(F32),
        expert_down_grad.astype(F32),
    )


def solution(mesh):
    groups = mesh.shape["wide"] // BLOCKS
    shape = (groups, PLANES, HALVES, mesh.shape["grid"])
    inner_mesh = Mesh(mesh.devices.reshape(shape), ("t", "z", "x", "grid"))
    wide = ("t", "z", "x")
    in_specs = (
        P(wide, "grid"),
        P(),
        P(wide, None),
        P(wide, None),
        P(wide),
        P(wide, "grid", None, None),
        P(None, wide, "grid", None),
        P(None, "grid", None, wide),
        P(wide, None),
        P(wide),
        P(wide, None),
        P(None, wide, None, "grid"),
        P(None, "grid", wide),
        P(wide, "grid"),
    )
    out_specs = (
        P(wide, "grid"),
        P(wide, "grid"),
        P(wide),
        P(wide, "grid", None, None),
        P(None, wide, "grid", None),
        P(None, "grid", None, wide),
        P(wide, None),
        P(wide),
        P(wide, None),
        P(None, wide, None, "grid"),
        P(None, "grid", wide),
    )
    return jax.shard_map(
        per_device, mesh=inner_mesh, in_specs=in_specs, out_specs=out_specs, check_vma=False
    )
```

```python
import functools
import math

import jax
import jax.numpy as jnp
import numpy as np
from jax import lax
from jax.experimental import pallas as pl
from jax.experimental.pallas import tpu as pltpu
from jax.sharding import Mesh, PartitionSpec as P

CAP = 320
PLANES = 4
HALVES = 2
BLOCKS = PLANES * HALVES
EPSILON = 1e-05
ROPE_BASE = 10000.0
NEGATIVE = -1e30
BF16 = jnp.bfloat16
F32 = jnp.float32
PLACES = ("z", "x")
MESH = pl.DeviceIdType.MESH
VMEM_BYTES = 56 * 1024 * 1024


def rope_tables(token_count, width):
    half = width // 2
    frequency = np.float32(ROPE_BASE) ** (-np.arange(half, dtype=np.float32) / np.float32(half))
    angles = np.arange(token_count, dtype=np.float32)[:, None] * frequency.astype(np.float32)[None, :]
    cosine, sine = np.cos(angles).astype(np.float32), np.sin(angles).astype(np.float32)
    return np.concatenate([cosine, cosine], axis=1), np.concatenate([-sine, sine], axis=1)


def turned(values, cosine, sine):
    return values * cosine + pltpu.roll(values, values.shape[1] // 2, 1) * sine


def dot(left, right):
    return jnp.dot(left, right, preferred_element_type=F32)


def contract_first(left, right):
    return lax.dot_general(left, right, (((0,), (0,)), ((), ())), preferred_element_type=F32)


def contract_last(left, right):
    return lax.dot_general(left, right, (((1,), (1,)), ((), ())), preferred_element_type=F32)


def exact(left, right):
    return jnp.dot(left, right, precision=lax.Precision.HIGHEST)


def project_kernel(
    tokens_ref, gain_ref, weight_ref, router_ref, cos_ref, sin_ref,
    hidden_ref, q_ref, k_ref, v_ref, logits_ref, inverse_ref, *, head_width
):
    x = tokens_ref[0, 0].astype(F32)
    inverse = lax.rsqrt(jnp.mean(x * x, axis=1, keepdims=True) + EPSILON)
    inverse_ref[...] = inverse
    hidden = (x * inverse * gain_ref[...]).astype(BF16)
    hidden_ref[...] = hidden
    logits_ref[...] = dot(hidden, router_ref[...])
    made = dot(hidden, weight_ref[...])
    span = q_ref.shape[1]
    cosine, sine = cos_ref[...], sin_ref[...]
    for head in range(span // head_width):
        at = slice(head * head_width, (head + 1) * head_width)
        q_ref[:, at] = turned(made[:, at], cosine, sine).astype(BF16)
        k_ref[:, at] = turned(made[:, span:][:, at], cosine, sine).astype(BF16)
    v_ref[...] = made[:, 2 * span :].astype(BF16)


def project(tokens, rows, gain, weight, router, cosine, sine, span, head_width):
    width = tokens.shape[-1]
    token_count = BLOCKS * rows
    whole = lambda b: (0, 0)
    block = lambda b: (b, 0)
    return pl.pallas_call(
        functools.partial(project_kernel, head_width=head_width),
        grid=(BLOCKS,),
        in_specs=[
            pl.BlockSpec((1, 1, rows, width), lambda b: (b // HALVES, b % HALVES, 0, 0)),
            pl.BlockSpec((1, width), whole),
            pl.BlockSpec((width, 3 * span), whole),
            pl.BlockSpec((width, 128), whole),
            pl.BlockSpec((rows, head_width), block),
            pl.BlockSpec((rows, head_width), block),
        ],
        out_specs=[
            pl.BlockSpec((rows, width), block),
            pl.BlockSpec((rows, span), block),
            pl.BlockSpec((rows, span), block),
            pl.BlockSpec((rows, span), block),
            pl.BlockSpec((rows, 128), block),
            pl.BlockSpec((rows, 1), block),
        ],
        out_shape=[
            jax.ShapeDtypeStruct((token_count, width), BF16),
            jax.ShapeDtypeStruct((token_count, span), BF16),
            jax.ShapeDtypeStruct((token_count, span), BF16),
            jax.ShapeDtypeStruct((token_count, span), BF16),
            jax.ShapeDtypeStruct((token_count, 128), F32),
            jax.ShapeDtypeStruct((token_count, 1), F32),
        ],
        compiler_params=pltpu.CompilerParams(vmem_limit_bytes=VMEM_BYTES),
        name="project",
    )(tokens, gain, weight, router, cosine, sine)


def attention_scores(q, k_ref, low_bound, high_bound, tile, tile_rows, scaling):
    rows = pl.ds(pl.multiple_of(tile * tile_rows, tile_rows), tile_rows)
    keys = k_ref[rows, :]
    scores = contract_last(q, keys) * scaling
    column = tile * tile_rows + lax.broadcasted_iota(jnp.int32, scores.shape, 1)
    allowed = (column >= low_bound) & (column <= high_bound)
    return rows, keys, scores, allowed


def attention_forward_kernel(
    begin_ref, q_ref, k_ref, v_ref, rank_ref, low_ref, high_ref, out_ref, lse_ref, *, scaling
):
    block = pl.program_id(1)
    cap, width = out_ref.shape
    tile_rows = q_ref.shape[0]
    pick = (lax.broadcasted_iota(jnp.int32, (cap, tile_rows), 0) == rank_ref[0]).astype(BF16)
    q = dot(pick, q_ref[...]).astype(BF16)
    low_bound, high_bound = low_ref[...], high_ref[...]

    def step(tile, carried):
        largest, total, summed = carried
        rows, _, scores, allowed = attention_scores(
            q, k_ref, low_bound, high_bound, tile, tile_rows, scaling
        )
        scores = jnp.where(allowed, scores, NEGATIVE)
        new_largest = jnp.maximum(largest, jnp.max(scores, axis=1, keepdims=True))
        weights = jnp.where(allowed, jnp.exp(scores - new_largest), 0.0)
        shrink = jnp.exp(largest - new_largest)
        return (
            new_largest,
            total * shrink + jnp.sum(weights, axis=1, keepdims=True),
            summed * shrink + dot(weights.astype(BF16), v_ref[rows, :]),
        )

    largest, total, summed = lax.fori_loop(
        begin_ref[block],
        block + 1,
        step,
        (jnp.full((cap, 1), NEGATIVE, F32), jnp.zeros((cap, 1), F32), jnp.zeros((cap, width), F32)),
    )
    out_ref[...] = (summed / total).astype(BF16)
    lse_ref[0] = largest + jnp.log(total)


def attention_backward_kernel(
    begin_ref, q_ref, k_ref, v_ref, rank_ref, low_ref, high_ref, out_ref, lse_ref, grad_ref,
    cos_ref, sin_ref, dq_ref, dk_ref, dv_ref, dk_sum, dv_sum, *, scaling
):
    block = pl.program_id(1)
    cap, width = out_ref.shape
    tile_rows = q_ref.shape[0]
    pick = (lax.broadcasted_iota(jnp.int32, (cap, tile_rows), 0) == rank_ref[0]).astype(BF16)
    q = dot(pick, q_ref[...]).astype(BF16)
    low_bound, high_bound = low_ref[...], high_ref[...]
    grad = grad_ref[...]
    delta = jnp.sum(grad.astype(F32) * out_ref[...].astype(F32), axis=1, keepdims=True)
    lse = lse_ref[0]

    @pl.when(block == 0)
    def _():
        dk_sum[...] = jnp.zeros_like(dk_sum)
        dv_sum[...] = jnp.zeros_like(dv_sum)

    def step(tile, dq):
        rows, keys, scores, allowed = attention_scores(
            q, k_ref, low_bound, high_bound, tile, tile_rows, scaling
        )
        chances = jnp.where(allowed, jnp.exp(scores - lse), 0.0)
        dv_sum[rows, :] += contract_first(chances.astype(BF16), grad)
        grad_chances = contract_last(grad, v_ref[rows, :])
        grad_scores = (chances * (grad_chances - delta)).astype(BF16)
        dk_sum[rows, :] += contract_first(grad_scores, q) * scaling
        return dq + dot(grad_scores, keys)

    dq = lax.fori_loop(begin_ref[block], block + 1, step, jnp.zeros((cap, width), F32)) * scaling
    high = dq.astype(BF16)
    rest = (dq - high.astype(F32)).astype(BF16)
    dq_tokens = contract_first(pick, high) + contract_first(pick, rest)
    own = pl.ds(pl.multiple_of(block * tile_rows, tile_rows), tile_rows)
    dq_ref[...] = turned(dq_tokens, cos_ref[own, :], -sin_ref[own, :]).astype(BF16)

    @pl.when(block == BLOCKS - 1)
    def _():
        def finish(tile, nothing):
            rows = pl.ds(pl.multiple_of(tile * tile_rows, tile_rows), tile_rows)
            dk_ref[rows, :] = turned(dk_sum[rows, :], cos_ref[rows, :], -sin_ref[rows, :]).astype(BF16)
            dv_ref[rows, :] = dv_sum[rows, :].astype(BF16)
            return nothing

        lax.fori_loop(0, BLOCKS, finish, 0)


def attention_specs(row_count, token_count, width):
    return dict(
        q=pl.BlockSpec((row_count, width), lambda h, b, s: (b, h)),
        k=pl.BlockSpec((token_count, width), lambda h, b, s: (0, h)),
        rank=pl.BlockSpec((1, 1, row_count), lambda h, b, s: (b, 0, 0)),
        bound=pl.BlockSpec((CAP, 1), lambda h, b, s: (b, 0)),
        slots=pl.BlockSpec((CAP, width), lambda h, b, s: (b, h)),
        table=pl.BlockSpec((token_count, width), lambda h, b, s: (0, 0)),
        lse=pl.BlockSpec((1, CAP, 1), lambda h, b, s: (h, b, 0)),
    )


def attention_forward(begin, q, k, v, rank, low_bound, high_bound, width):
    token_count, heads = q.shape[0], q.shape[1] // width
    row_count = token_count // BLOCKS
    s = attention_specs(row_count, token_count, width)
    return pl.pallas_call(
        functools.partial(attention_forward_kernel, scaling=1.0 / math.sqrt(width)),
        grid_spec=pltpu.PrefetchScalarGridSpec(
            num_scalar_prefetch=1,
            grid=(heads, BLOCKS),
            in_specs=[s["q"], s["k"], s["k"], s["rank"], s["bound"], s["bound"]],
            out_specs=[s["slots"], s["lse"]],
        ),
        out_shape=[
            jax.ShapeDtypeStruct((BLOCKS * CAP, heads * width), BF16),
            jax.ShapeDtypeStruct((heads, BLOCKS * CAP, 1), F32),
        ],
        compiler_params=pltpu.CompilerParams(vmem_limit_bytes=VMEM_BYTES),
        name="attention_forward",
    )(begin, q, k, v, rank, low_bound, high_bound)


def attention_backward(begin, q, k, v, rank, low_bound, high_bound, out, lse, grad, cosine, sine, width):
    token_count, heads = q.shape[0], q.shape[1] // width
    row_count = token_count // BLOCKS
    s = attention_specs(row_count, token_count, width)
    return pl.pallas_call(
        functools.partial(attention_backward_kernel, scaling=1.0 / math.sqrt(width)),
        grid_spec=pltpu.PrefetchScalarGridSpec(
            num_scalar_prefetch=1,
            grid=(heads, BLOCKS),
            in_specs=[
                s["q"], s["k"], s["k"], s["rank"], s["bound"], s["bound"],
                s["slots"], s["lse"], s["slots"], s["table"], s["table"],
            ],
            out_specs=[s["q"], s["k"], s["k"]],
            scratch_shapes=[pltpu.VMEM((token_count, width), F32)] * 2,
        ),
        out_shape=[
            jax.ShapeDtypeStruct((token_count, heads * width), BF16),
            jax.ShapeDtypeStruct((token_count, heads * width), BF16),
            jax.ShapeDtypeStruct((token_count, heads * width), BF16),
        ],
        compiler_params=pltpu.CompilerParams(vmem_limit_bytes=VMEM_BYTES),
        name="attention_backward",
    )(begin, q, k, v, rank, low_bound, high_bound, out, lse, grad, cosine, sine)


def exchanged(pieces):
    return lax.all_to_all(pieces, PLACES, 0, 0, tiled=True)


def spread_weights(pieces):
    return lax.all_gather(exchanged(pieces), "t", axis=0, tiled=False)


def return_gradients(pieces):
    return exchanged(lax.psum_scatter(pieces, "t", scatter_dimension=0, tiled=False))


def other_core(column):
    return column + 1 - 2 * (column % 2)


def meet(peers):
    barrier = pltpu.get_barrier_semaphore()
    for peer in peers:
        pl.semaphore_signal(barrier, inc=1, device_id=peer, device_id_type=MESH)
    pl.semaphore_wait(barrier, len(peers))


def partners():
    plane, half, column = lax.axis_index("z"), lax.axis_index("x"), lax.axis_index("grid")
    planes = [{"z": (plane + j) % PLANES} for j in range(PLANES)]
    along_x, along_y = {"x": 1 - half}, {"grid": (column + 2) % 4}
    core = {"grid": other_core(column)}
    return plane, half, column, planes, along_x, along_y, core


def gather_kernel(slots_ref, out_ref, send, recv, local, *, same):
    plane, half, column, planes, along_x, along_y, core = partners()
    cap, width = slots_ref.shape[-2:]
    middle = cap // 32 * 16
    meet(planes[1:] + [along_x, along_y, core])

    def piece(source, at_half, at_column, first=0, count=cap):
        columns = pl.ds(pl.multiple_of(at_column * width, width), width)
        return out_ref.at[source, at_half, pl.ds(first, count), columns]

    def source_of(j):
        return (plane - j + PLANES) % PLANES

    def slots_for(j):
        return slots_ref if same else slots_ref.at[(plane + j) % PLANES]

    started = []

    def copy(index, source, target, peer):
        made = pltpu.make_async_remote_copy(
            src_ref=source, dst_ref=target, send_sem=send.at[index], recv_sem=recv.at[index],
            device_id=peer, device_id_type=MESH,
        )
        made.start()
        started.append(made)

    def arrived(index, target, peer):
        pltpu.make_async_remote_copy(
            src_ref=target, dst_ref=target, send_sem=send.at[index], recv_sem=recv.at[index],
            device_id=peer, device_id_type=MESH,
        ).wait_recv()

    y_column, core_column = (column + 2) % 4, other_core(column)
    core_y = (core_column + 2) % 4
    for j in (2, 1, 3):
        copy(j, slots_for(j), piece(plane, half, column), planes[j])
    keep = pltpu.make_async_copy(slots_for(0), piece(plane, half, column), local)
    keep.start()

    def spread(j):
        place = piece(source_of(j), half, column)
        if j:
            arrived(j, place, planes[(PLANES - j) % PLANES])
        source = place if j else slots_for(0)
        copy(4 + j, source, place, along_x)
        copy(8 + j, source, place, along_y)
        copy(12 + j, source, place, core)

    def forward(j):
        source = source_of(j)
        from_x = piece(source, 1 - half, column)
        arrived(4 + j, from_x, along_x)
        part = piece(source, 1 - half, column, 0, middle)
        copy(16 + j, part, part, along_y)
        copy(20 + j, from_x, from_x, core)
        from_y = piece(source, half, y_column)
        arrived(8 + j, from_y, along_y)
        part = piece(source, half, y_column, middle, cap - middle)
        copy(24 + j, part, part, along_x)
        copy(28 + j, from_y, from_y, core)

    def cross(j):
        source = source_of(j)
        arrived(16 + j, piece(source, 1 - half, y_column, 0, middle), along_y)
        arrived(24 + j, piece(source, 1 - half, y_column, middle, cap - middle), along_x)
        place = piece(source, 1 - half, y_column)
        copy(32 + j, place, place, core)

    def from_core(j):
        source = source_of(j)
        arrived(12 + j, piece(source, half, core_column), core)
        arrived(20 + j, piece(source, 1 - half, core_column), core)
        arrived(28 + j, piece(source, half, core_y), core)
        arrived(32 + j, piece(source, 1 - half, core_y), core)

    order = (0, 1, 3, 2)
    for step in range(len(order) + 2):
        if step < len(order):
            spread(order[step])
        if 0 <= step - 1 < len(order):
            forward(order[step - 1])
        if 0 <= step - 2 < len(order):
            cross(order[step - 2])
    for j in order:
        from_core(j)
    for made in started:
        made.wait_send()
    keep.wait()


def gathered(slots, collective_id):
    rows, width = slots.shape[-2:]
    out = pl.pallas_call(
        functools.partial(gather_kernel, same=slots.ndim == 2),
        out_shape=jax.ShapeDtypeStruct((PLANES, HALVES, rows, 4 * width), BF16),
        in_specs=[pl.BlockSpec(memory_space=pl.ANY)],
        out_specs=pl.BlockSpec(memory_space=pl.ANY),
        scratch_shapes=[
            pltpu.SemaphoreType.DMA((36,)),
            pltpu.SemaphoreType.DMA((36,)),
            pltpu.SemaphoreType.DMA,
        ],
        compiler_params=pltpu.CompilerParams(collective_id=collective_id, has_side_effects=True),
        name="gather_rows",
    )(slots)
    return out


def scatter_kernel(partial_ref, out_ref, own, other, crossing, side, send, recv, load):
    plane, half, column, planes, along_x, along_y, core = partners()
    cap, width = out_ref.shape[-2:]
    middle = cap // 2
    chunk = 32
    meet(planes[1:] + [along_x, along_y, core])
    y_column, core_column = (column + 2) % 4, other_core(column)
    core_y = (core_column + 2) % 4
    halves = (half, 1 - half, half, 1 - half)
    own_columns = (column, column, y_column, y_column)
    core_columns = (core_column, core_column, core_y, core_y)
    started = []

    def copy(index, source, target, peer):
        made = pltpu.make_async_remote_copy(
            src_ref=source, dst_ref=target, send_sem=send.at[index], recv_sem=recv.at[index],
            device_id=peer, device_id_type=MESH,
        )
        made.start()
        started.append(made)

    def arrived(index, target, peer):
        pltpu.make_async_remote_copy(
            src_ref=target, dst_ref=target, send_sem=send.at[index], recv_sem=recv.at[index],
            device_id=peer, device_id_type=MESH,
        ).wait_recv()

    def part(j, q, at_columns):
        columns = pl.ds(pl.multiple_of(at_columns[q] * width, width), width)
        return partial_ref.at[(plane + j) % PLANES, halves[q], :, columns]

    def loading(j, q):
        return pltpu.make_async_copy(part(j, q, own_columns), own.at[j, q], load.at[4 * j + q])

    order = (2, 1, 3, 0)
    for j in order:
        for q in (3, 2, 1, 0):
            copy(4 * j + q, part(j, q, core_columns), other.at[j, q], core)
            loading(j, q).start()

    def add(j, q, first, count, terms):
        def step(i, nothing):
            rows = pl.ds(pl.multiple_of(first + i * chunk, chunk), chunk)
            total = own[j, q, rows, :].astype(F32)
            for ref, index in terms:
                total = total + ref[index + (rows, slice(None))].astype(F32)
            own[j, q, rows, :] = total.astype(BF16)
            return nothing

        lax.fori_loop(0, count // chunk, step, 0)

    def chip_sum(j, q):
        arrived(4 * j + q, other.at[j, q], core)
        loading(j, q).wait()
        add(j, q, 0, cap, [(other, (j, q))])

    def stage_one(j):
        chip_sum(j, 3)
        first, last = pl.ds(0, middle), pl.ds(middle, cap - middle)
        copy(16 + j, own.at[j, 3, first], crossing.at[j, first], along_x)
        copy(20 + j, own.at[j, 3, last], crossing.at[j, last], along_y)
        chip_sum(j, 2)
        chip_sum(j, 1)
        chip_sum(j, 0)

    def stage_two(j):
        arrived(16 + j, crossing.at[j, pl.ds(0, middle)], along_x)
        add(j, 2, 0, middle, [(crossing, (j,))])
        copy(24 + j, own.at[j, 2], side.at[j, 1], along_y)
        arrived(20 + j, crossing.at[j, pl.ds(middle, cap - middle)], along_y)
        add(j, 1, middle, cap - middle, [(crossing, (j,))])
        copy(28 + j, own.at[j, 1], side.at[j, 0], along_x)

    def stage_three(j):
        arrived(24 + j, side.at[j, 1], along_y)
        arrived(28 + j, side.at[j, 0], along_x)
        add(j, 0, 0, cap, [(side, (j, 0)), (side, (j, 1))])
        if j:
            copy(32 + j, own.at[j, 0], out_ref.at[plane], planes[j])

    for step in range(len(order) + 2):
        if step < len(order):
            stage_one(order[step])
        if 0 <= step - 1 < len(order):
            stage_two(order[step - 1])
        if 0 <= step - 2 < len(order):
            stage_three(order[step - 2])
    keep = pltpu.make_async_copy(own.at[0, 0], out_ref.at[plane], load.at[16])
    keep.start()
    for j in range(1, PLANES):
        arrived(32 + j, out_ref.at[(plane - j + PLANES) % PLANES], planes[PLANES - j])
    for made in started:
        made.wait_send()
    keep.wait()


def scattered(partial, rows, collective_id):
    width = partial.shape[1] // 4
    return pl.pallas_call(
        scatter_kernel,
        out_shape=jax.ShapeDtypeStruct((PLANES, rows, width), BF16),
        in_specs=[pl.BlockSpec(memory_space=pl.ANY)],
        out_specs=pl.BlockSpec(memory_space=pl.ANY),
        scratch_shapes=[
            pltpu.VMEM((PLANES, 4, rows, width), BF16),
            pltpu.VMEM((PLANES, 4, rows, width), BF16),
            pltpu.VMEM((PLANES, rows, width), BF16),
            pltpu.VMEM((PLANES, 2, rows, width), BF16),
            pltpu.SemaphoreType.DMA((36,)),
            pltpu.SemaphoreType.DMA((36,)),
            pltpu.SemaphoreType.DMA((17,)),
        ],
        compiler_params=pltpu.CompilerParams(
            collective_id=collective_id, has_side_effects=True, vmem_limit_bytes=VMEM_BYTES
        ),
        name="scatter_rows",
    )(partial.reshape(PLANES, HALVES, rows, 4 * width))


def grid_sum(values):
    shape = values.shape
    return lax.all_gather(values.reshape(-1, 128), "grid", axis=0).sum(axis=0).reshape(shape)


def ranks(member):
    counted = member.astype(jnp.int32)
    before = jnp.cumsum(counted, axis=-1) - counted
    return jnp.where(member, before, -1)


def picks(rank):
    return jnp.arange(CAP, dtype=jnp.int32)[:, None] == rank[..., None, :]


def routed(routes):
    return routes[:, None, :] == jnp.arange(PLANES, dtype=jnp.int32)[None, :, None]


def route_gates(logits, member):
    shown = jnp.where(member, logits, NEGATIVE)
    weights = jnp.where(member, jnp.exp(shown - jnp.max(shown, axis=1, keepdims=True)), 0.0)
    return weights / jnp.sum(weights, axis=1, keepdims=True)


def logits_grad(gates, grad_gates):
    return gates * (grad_gates - jnp.sum(gates * grad_gates, axis=1, keepdims=True))


def per_device(
    tokens, segment_ids, attention_routes, expert_routes, attention_gain, attention_kv,
    attention_query, attention_out, attention_router, feedforward_gain, feedforward_router,
    expert_gate_up, expert_down, output_grad,
):
    groups = lax.axis_size("t")
    grid_count = lax.axis_size("grid")
    group = lax.axis_index("t")
    plane = lax.axis_index("z")
    place = plane * HALVES + lax.axis_index("x")
    column = lax.axis_index("grid")
    rows, features = tokens.shape
    width_all = features * grid_count
    token_count = BLOCKS * rows
    own_rows = attention_gain.shape[0]
    head_width = attention_kv.shape[3]
    head_pair = attention_kv.shape[1] // HALVES
    span = head_pair * head_width
    hidden_units = expert_gate_up.shape[3] // HALVES

    def mine(array, axis=0):
        return lax.dynamic_slice_in_dim(array, column * features, features, axis)

    def own(array):
        return lax.dynamic_slice_in_dim(array, place * rows, rows, 0)

    query_pieces = attention_query.reshape(PLANES, own_rows, HALVES, span).transpose(0, 2, 1, 3)
    kv_pieces = attention_kv.reshape(own_rows, HALVES, head_pair, 2, head_width)
    kv_pieces = kv_pieces.transpose(1, 0, 3, 2, 4).reshape(1, HALVES, own_rows, 2 * span)
    kv_pieces = jnp.broadcast_to(kv_pieces, (PLANES,) + kv_pieces.shape[1:])
    qkv_pieces = jnp.concatenate([query_pieces, kv_pieces], axis=-1)
    out_pieces = attention_out.reshape(BLOCKS, span, own_rows).swapaxes(1, 2)
    first_pieces = jnp.concatenate([qkv_pieces.reshape(BLOCKS, own_rows, 3 * span), out_pieces], axis=2)
    first_weight = spread_weights(first_pieces).reshape(width_all, 4 * span)
    qkv_weight, out_weight = first_weight[:, : 3 * span], first_weight[:, 3 * span :]
    up_pieces = expert_gate_up.reshape(PLANES, own_rows, 2, HALVES, hidden_units)
    up_pieces = up_pieces.transpose(0, 3, 1, 2, 4).reshape(BLOCKS, own_rows, 2 * hidden_units)
    down_pieces = expert_down.reshape(BLOCKS, hidden_units, own_rows).swapaxes(1, 2)
    second_pieces = jnp.concatenate([up_pieces, down_pieces], axis=2)
    own_routes = jnp.concatenate([attention_routes, expert_routes], axis=1)
    small = jnp.concatenate(
        [attention_gain[:, None], feedforward_gain[:, None], attention_router, feedforward_router],
        axis=1,
    )
    small = lax.all_gather(small, "t", axis=0).reshape(-1, small.shape[1])
    small = small.T.reshape(small.shape[1], -1)
    spare = jnp.zeros((small.shape[0], features - small.shape[1] % features), BF16)
    small = jnp.concatenate([small, spare], axis=1).reshape(-1, features)
    under = jnp.concatenate([own_routes.T.astype(BF16), small], axis=0)
    under = jnp.pad(under, ((0, -under.shape[0] % 16), (0, 0)))
    under, second_pieces = lax.optimization_barrier((under, second_pieces))
    everything = gathered(jnp.concatenate([tokens, under], axis=0), 0)
    second_pieces, everything = lax.optimization_barrier((second_pieces, everything))
    second_weight = spread_weights(second_pieces).reshape(width_all, 3 * hidden_units)
    up_weight, down_weight = second_weight[:, : 2 * hidden_units], second_weight[:, 2 * hidden_units :]
    under = everything[:, :, rows:, :features].reshape(BLOCKS, -1, features)
    all_routes = under[:, :4].swapaxes(1, 2).reshape(token_count, 4).astype(jnp.int32)
    small = under[:, 4 : 4 + 10].reshape(BLOCKS, 10, features)[:, :, : groups * own_rows]
    small = small.reshape(BLOCKS, 10, groups, own_rows).transpose(1, 2, 0, 3).reshape(10, width_all)
    gain_first, gain_second = small[0].astype(F32), small[1].astype(F32)
    router_first, router_second = small[2:6].T, small[6:10].T

    member_first = jnp.any(routed(all_routes[:, :2]), axis=2)
    member_second = jnp.any(routed(all_routes[:, 2:]), axis=2)

    def plane_rank(member):
        shown = lax.dynamic_index_in_dim(member, plane, 1, keepdims=False)
        return ranks(shown.reshape(BLOCKS, rows))

    rank_first, rank_second = plane_rank(member_first), plane_rank(member_second)
    own_member_first, own_member_second = own(member_first), own(member_second)
    own_pick_first = picks(ranks(own_member_first.T)).astype(BF16)
    own_pick_second = picks(ranks(own_member_second.T)).astype(BF16)

    def to_slots(values, pick):
        return jnp.einsum("est,tf->esf", pick, values, preferred_element_type=F32).astype(BF16)

    def to_tokens(slots, pick):
        return jnp.einsum("est,esf->etf", pick, slots, preferred_element_type=F32)

    grad_out = output_grad.astype(F32)
    cosine, sine = rope_tables(token_count, head_width)
    cosine, sine = jnp.asarray(cosine), jnp.asarray(sine)
    hidden_first, queries, keys, values, logits_first, inverse_first = project(
        everything, rows, gain_first[None], first_weight, jnp.pad(router_first, ((0, 0), (0, 124))),
        cosine, sine, span, head_width,
    )
    gates_first = route_gates(logits_first[:, :PLANES], member_first)
    position = jnp.arange(token_count, dtype=jnp.int32)
    segment = lax.dynamic_slice_in_dim(segment_ids, group * token_count, token_count, 0)
    opens = jnp.concatenate([jnp.ones((1,), jnp.bool_), segment[1:] != segment[:-1]])
    document_start = lax.cummax(jnp.where(opens, position, 0))
    begin = document_start.reshape(BLOCKS, rows)[:, 0] // rows
    slot_pick = picks(rank_first)

    def slot_values(per_token):
        shown = jnp.where(slot_pick, per_token.reshape(BLOCKS, 1, rows), 0)
        return jnp.sum(shown, axis=-1).reshape(-1, 1)

    block_first = jnp.repeat(jnp.arange(BLOCKS, dtype=jnp.int32) * rows, CAP)[:, None]
    filled = slot_values(jnp.ones((token_count,), jnp.int32)) > 0
    low_bound = jnp.where(filled, slot_values(document_start), block_first)
    high_bound = jnp.where(filled, slot_values(position), block_first)
    attention_args = (begin, queries, keys, values, rank_first[:, None, :], low_bound, high_bound)
    attended, lse = attention_forward(*attention_args, head_width)
    gate_first = lax.dynamic_index_in_dim(gates_first, plane, 1, keepdims=False)
    gate_slots_first = slot_values(gate_first)
    branch_slots = scattered(contract_last(attended, out_weight).astype(BF16), CAP, 2)
    branch_first = to_tokens(branch_slots, own_pick_first)
    own_gates_first = own(gates_first)
    residual = tokens.astype(F32) + jnp.sum(own_gates_first.T[:, :, None] * branch_first, axis=0)

    square = grid_sum(jnp.sum(residual * residual, axis=1))
    inverse_second = lax.rsqrt(square / width_all + EPSILON)[:, None]
    normed_second = residual * inverse_second
    hidden_second = (normed_second * mine(gain_second)).astype(BF16)
    slots_second = gathered(to_slots(hidden_second, own_pick_second), 1).reshape(BLOCKS * CAP, -1)
    slots_second, grad_slots = lax.optimization_barrier(
        (slots_second, to_slots(output_grad, own_pick_second))
    )
    grad_slots_second = gathered(grad_slots, 1).reshape(BLOCKS * CAP, -1)
    plane_gates = dot(slots_second, router_second)
    rank_pick = picks(rank_second)

    def slot_values_second(per_token):
        shown = jnp.where(rank_pick, per_token.reshape(BLOCKS, 1, rows), 0)
        return jnp.sum(shown, axis=-1).reshape(-1)

    slot_member = jnp.stack(
        [slot_values_second(member_second[:, e].astype(jnp.int32)) for e in range(PLANES)], axis=1
    )
    filled_second = slot_values_second(jnp.ones((token_count,), jnp.int32))[:, None] > 0
    slot_gates = route_gates(plane_gates, (slot_member > 0) | ~filled_second)
    gate_slots_second = lax.dynamic_index_in_dim(slot_gates, plane, 1, keepdims=True)
    gate_up = dot(slots_second, up_weight)
    gate_pre, up_pre = gate_up[:, :hidden_units], gate_up[:, hidden_units:]
    sigmoid_gate = jax.nn.sigmoid(gate_pre)
    silu_gate = gate_pre * sigmoid_gate
    inner = silu_gate * up_pre
    result_slots = scattered(contract_last(inner.astype(BF16), down_weight).astype(BF16), CAP, 2)
    own_logits = grid_sum(dot(hidden_second, mine(router_second)))
    own_gates_second = route_gates(own_logits, own_member_second)
    branch_second = to_tokens(result_slots, own_pick_second)
    layer_output = residual + jnp.sum(own_gates_second.T[:, :, None] * branch_second, axis=0)
    layer_output = layer_output.astype(BF16)

    grad_inner = gate_slots_second * dot(grad_slots_second, down_weight)
    grad_gate = grad_inner * up_pre * sigmoid_gate * (1.0 + gate_pre * (1.0 - sigmoid_gate))
    grad_gate_up = jnp.concatenate([grad_gate, grad_inner * silu_gate], axis=1).astype(BF16)
    grad_rows = contract_last(grad_gate_up, up_weight).astype(BF16)
    grad_up_weight = contract_first(slots_second, grad_gate_up).astype(BF16)
    grad_down = contract_first(grad_slots_second, (gate_slots_second * inner).astype(BF16))
    grad_second = jnp.concatenate([grad_up_weight, grad_down.astype(BF16)], axis=1)
    grad_rows, grad_second = lax.optimization_barrier((grad_rows, grad_second))
    grad_rows = scattered(grad_rows, CAP, 2)
    grad_gates_second = grid_sum(jnp.sum(branch_second * grad_out[None], axis=2).T)
    grad_logits_second = logits_grad(own_gates_second, grad_gates_second)
    grad_hidden_second = jnp.sum(to_tokens(grad_rows, own_pick_second), axis=0)
    grad_hidden_second = grad_hidden_second + exact(
        grad_logits_second, mine(router_second).astype(F32).T
    )
    grad_router_second = exact(hidden_second.astype(F32).T, grad_logits_second)
    grad_gain_second = jnp.sum(grad_hidden_second * normed_second, axis=0)
    grad_normed = grad_hidden_second * mine(gain_second)
    inner_mean = grid_sum(jnp.sum(grad_normed * normed_second, axis=1))[:, None] / width_all
    grad_residual = grad_out + inverse_second * (grad_normed - normed_second * inner_mean)

    grad_slots_first = gathered(to_slots(grad_residual.astype(BF16), own_pick_first), 1).reshape(BLOCKS * CAP, -1)
    grad_second, grad_slots_first = lax.optimization_barrier((grad_second, grad_slots_first))
    grad_second = return_gradients(grad_second.reshape(groups, BLOCKS, own_rows, 3 * hidden_units))
    grad_attended = gate_slots_first * dot(grad_slots_first, out_weight)
    grad_attended = grad_attended.astype(BF16)
    grad_out_weight = contract_first(
        grad_slots_first, (gate_slots_first * attended.astype(F32)).astype(BF16)
    )
    grad_qkv = jnp.concatenate(
        attention_backward(
            *attention_args, attended, lse, grad_attended, cosine, sine, head_width
        ),
        axis=1,
    )
    grad_hidden = contract_last(grad_qkv, qkv_weight).astype(BF16)
    grad_first = jnp.concatenate(
        [contract_first(hidden_first, grad_qkv).astype(BF16), grad_out_weight.astype(BF16)], axis=1
    )
    grad_hidden, grad_first, grad_second = lax.optimization_barrier(
        (grad_hidden, grad_first, grad_second)
    )
    grad_hidden, grad_first = lax.optimization_barrier((scattered(grad_hidden, rows, 3), grad_first))
    grad_hidden = jnp.sum(grad_hidden.astype(F32), axis=0)
    expert_gate_up_grad = grad_second[:, :, : 2 * hidden_units].reshape(
        PLANES, HALVES, own_rows, 2, hidden_units
    )
    expert_gate_up_grad = expert_gate_up_grad.transpose(0, 2, 3, 1, 4).reshape(expert_gate_up.shape)
    expert_down_grad = grad_second[:, :, 2 * hidden_units :].swapaxes(1, 2).reshape(expert_down.shape)
    grad_first = return_gradients(grad_first.reshape(groups, BLOCKS, own_rows, 4 * span))
    attention_out_grad = grad_first[..., 3 * span :].swapaxes(1, 2).reshape(attention_out.shape)
    attention_query_grad = grad_first[..., :span].reshape(PLANES, HALVES, own_rows, span)
    attention_query_grad = attention_query_grad.transpose(0, 2, 1, 3).reshape(attention_query.shape)
    grad_kv_weight = grad_first[..., span : 3 * span].astype(F32).reshape(
        PLANES, HALVES, own_rows, 2, head_pair, head_width
    )
    attention_kv_grad = grad_kv_weight.sum(axis=0).transpose(1, 0, 3, 2, 4)
    attention_kv_grad = attention_kv_grad.reshape(attention_kv.shape)

    own_normed = tokens.astype(F32) * own(inverse_first)
    own_hidden = (own_normed * mine(gain_first)).astype(BF16)
    grad_gates_first = grid_sum(jnp.sum(branch_first * grad_residual[None], axis=2).T)
    grad_logits_first = logits_grad(own_gates_first, grad_gates_first)
    grad_hidden_first = grad_hidden + exact(
        grad_logits_first, mine(router_first).astype(F32).T
    )
    grad_router_first = exact(own_hidden.astype(F32).T, grad_logits_first)
    grad_gain_first = jnp.sum(grad_hidden_first * own_normed, axis=0)
    grad_normed = grad_hidden_first * mine(gain_first)
    inner_mean = grid_sum(jnp.sum(grad_normed * own_normed, axis=1))[:, None] / width_all
    input_grad = grad_residual + own(inverse_first) * (grad_normed - own_normed * inner_mean)

    small_grads = jnp.concatenate(
        [grad_gain_first[None], grad_gain_second[None], grad_router_first.T, grad_router_second.T],
        axis=0,
    )
    small_grads = jnp.sum(lax.all_gather(small_grads, ("t",) + PLACES, axis=0), axis=0)
    small_grads = lax.all_gather(small_grads, "grid", axis=1, tiled=True)
    small_grads = lax.dynamic_slice_in_dim(
        small_grads, (group * BLOCKS + place) * own_rows, own_rows, 1
    )
    return (
        layer_output,
        input_grad.astype(BF16),
        small_grads[0],
        attention_kv_grad,
        attention_query_grad.astype(F32),
        attention_out_grad.astype(F32),
        small_grads[2:6].T,
        small_grads[1],
        small_grads[6:10].T,
        expert_gate_up_grad.astype(F32),
        expert_down_grad.astype(F32),
    )


def solution(mesh):
    groups = mesh.shape["wide"] // BLOCKS
    shape = (groups, PLANES, HALVES, mesh.shape["grid"])
    inner_mesh = Mesh(mesh.devices.reshape(shape), ("t", "z", "x", "grid"))
    wide = ("t", "z", "x")
    in_specs = (
        P(wide, "grid"),
        P(),
        P(wide, None),
        P(wide, None),
        P(wide),
        P(wide, "grid", None, None),
        P(None, wide, "grid", None),
        P(None, "grid", None, wide),
        P(wide, None),
        P(wide),
        P(wide, None),
        P(None, wide, None, "grid"),
        P(None, "grid", wide),
        P(wide, "grid"),
    )
    out_specs = (
        P(wide, "grid"),
        P(wide, "grid"),
        P(wide),
        P(wide, "grid", None, None),
        P(None, wide, "grid", None),
        P(None, "grid", None, wide),
        P(wide, None),
        P(wide),
        P(wide, None),
        P(None, wide, None, "grid"),
        P(None, "grid", wide),
    )
    return jax.shard_map(
        per_device, mesh=inner_mesh, in_specs=in_specs, out_specs=out_specs, check_vma=False
    )
```

```python
import functools
import math

import jax
import jax.numpy as jnp
import numpy as np
from jax import lax
from jax.experimental import pallas as pl
from jax.experimental.pallas import tpu as pltpu
from jax.sharding import Mesh, PartitionSpec as P

CAP = 320
PLANES = 4
HALVES = 2
BLOCKS = PLANES * HALVES
EPSILON = 1e-05
ROPE_BASE = 10000.0
NEGATIVE = -1e30
BF16 = jnp.bfloat16
F32 = jnp.float32
PLACES = ("z", "x")
MESH = pl.DeviceIdType.MESH
VMEM_BYTES = 56 * 1024 * 1024


def rope_tables(token_count, width):
    half = width // 2
    frequency = np.float32(ROPE_BASE) ** (-np.arange(half, dtype=np.float32) / np.float32(half))
    angles = np.arange(token_count, dtype=np.float32)[:, None] * frequency.astype(np.float32)[None, :]
    cosine, sine = np.cos(angles).astype(np.float32), np.sin(angles).astype(np.float32)
    return np.concatenate([cosine, cosine], axis=1), np.concatenate([-sine, sine], axis=1)


def turned(values, cosine, sine):
    return values * cosine + pltpu.roll(values, values.shape[1] // 2, 1) * sine


def dot(left, right):
    return jnp.dot(left, right, preferred_element_type=F32)


def contract_first(left, right):
    return lax.dot_general(left, right, (((0,), (0,)), ((), ())), preferred_element_type=F32)


def contract_last(left, right):
    return lax.dot_general(left, right, (((1,), (1,)), ((), ())), preferred_element_type=F32)


def exact(left, right):
    return jnp.dot(left, right, precision=lax.Precision.HIGHEST)


def project_kernel(
    tokens_ref, small_ref, weight_ref, cos_ref, sin_ref,
    hidden_ref, q_ref, k_ref, v_ref, logits_ref, inverse_ref, *, head_width
):
    x = tokens_ref[0, 0].astype(F32)
    inverse = lax.rsqrt(jnp.mean(x * x, axis=1, keepdims=True) + EPSILON)
    inverse_ref[...] = inverse
    hidden = (x * inverse * small_ref[:1, :].astype(F32)).astype(BF16)
    hidden_ref[...] = hidden
    logits_ref[...] = contract_last(small_ref[...], hidden)
    made = dot(hidden, weight_ref[...])
    span = q_ref.shape[1]
    cosine, sine = cos_ref[...], sin_ref[...]
    for head in range(span // head_width):
        at = slice(head * head_width, (head + 1) * head_width)
        q_ref[:, at] = turned(made[:, at], cosine, sine).astype(BF16)
        k_ref[:, at] = turned(made[:, span:][:, at], cosine, sine).astype(BF16)
    v_ref[...] = made[:, 2 * span :].astype(BF16)


def project(tokens, rows, small, weight, cosine, sine, span, head_width):
    width = tokens.shape[-1]
    token_count = BLOCKS * rows
    whole = lambda b: (0, 0)
    block = lambda b: (b, 0)
    return pl.pallas_call(
        functools.partial(project_kernel, head_width=head_width),
        grid=(BLOCKS,),
        in_specs=[
            pl.BlockSpec((1, 1, rows, width), lambda b: (b // HALVES, b % HALVES, 0, 0)),
            pl.BlockSpec(small.shape, whole),
            pl.BlockSpec((width, 3 * span), whole),
            pl.BlockSpec((rows, head_width), block),
            pl.BlockSpec((rows, head_width), block),
        ],
        out_specs=[
            pl.BlockSpec((rows, width), block),
            pl.BlockSpec((rows, span), block),
            pl.BlockSpec((rows, span), block),
            pl.BlockSpec((rows, span), block),
            pl.BlockSpec((small.shape[0], rows), lambda b: (0, b)),
            pl.BlockSpec((rows, 1), block),
        ],
        out_shape=[
            jax.ShapeDtypeStruct((token_count, width), BF16),
            jax.ShapeDtypeStruct((token_count, span), BF16),
            jax.ShapeDtypeStruct((token_count, span), BF16),
            jax.ShapeDtypeStruct((token_count, span), BF16),
            jax.ShapeDtypeStruct((small.shape[0], token_count), F32),
            jax.ShapeDtypeStruct((token_count, 1), F32),
        ],
        compiler_params=pltpu.CompilerParams(vmem_limit_bytes=VMEM_BYTES),
        name="project",
    )(tokens, small, weight, cosine, sine)


def attention_scores(q, k_ref, low_bound, high_bound, tile, tile_rows, scaling):
    rows = pl.ds(pl.multiple_of(tile * tile_rows, tile_rows), tile_rows)
    keys = k_ref[rows, :]
    scores = contract_last(q, keys) * scaling
    column = tile * tile_rows + lax.broadcasted_iota(jnp.int32, scores.shape, 1)
    allowed = (column >= low_bound) & (column <= high_bound)
    return rows, keys, scores, allowed


def slots_of_block(rank_ref, table_ref, cap):
    rows = table_ref.shape[1]
    pick = (lax.broadcasted_iota(jnp.int32, (cap, rows), 0) == rank_ref[0]).astype(BF16)
    made = contract_last(pick, table_ref[...])
    base = pl.program_id(1) * rows
    filled = made[:, 4:5] > 0.5
    low = (64.0 * made[:, 2:3] + made[:, 3:4]).astype(jnp.int32)
    high = (64.0 * made[:, 0:1] + made[:, 1:2]).astype(jnp.int32)
    gate = made[:, 5:6] + made[:, 6:7] + made[:, 7:8]
    return pick, jnp.where(filled, low, base), jnp.where(filled, high, base), gate


def token_table(position, document_start, gate):
    first = gate.astype(BF16).astype(F32)
    second = (gate - first).astype(BF16).astype(F32)
    rows = [
        position // 64, position % 64, document_start // 64, document_start % 64,
        jnp.ones_like(gate), first, second, gate - first - second,
    ]
    return jnp.pad(jnp.stack([row.astype(BF16) for row in rows]), ((0, 8), (0, 0)))


def attention_forward_kernel(
    begin_ref, q_ref, k_ref, v_ref, rank_ref, table_ref, out_ref, gated_ref, gate_ref, lse_ref, *,
    scaling
):
    block = pl.program_id(1)
    cap, width = out_ref.shape
    tile_rows = q_ref.shape[0]
    pick, low_bound, high_bound, gate = slots_of_block(rank_ref, table_ref, cap)
    q = dot(pick, q_ref[...]).astype(BF16)

    def step(tile, carried):
        largest, total, summed = carried
        rows, _, scores, allowed = attention_scores(
            q, k_ref, low_bound, high_bound, tile, tile_rows, scaling
        )
        scores = jnp.where(allowed, scores, NEGATIVE)
        new_largest = jnp.maximum(largest, jnp.max(scores, axis=1, keepdims=True))
        weights = jnp.where(allowed, jnp.exp(scores - new_largest), 0.0)
        shrink = jnp.exp(largest - new_largest)
        return (
            new_largest,
            total * shrink + jnp.sum(weights, axis=1, keepdims=True),
            summed * shrink + dot(weights.astype(BF16), v_ref[rows, :]),
        )

    largest, total, summed = lax.fori_loop(
        begin_ref[block],
        block + 1,
        step,
        (jnp.full((cap, 1), NEGATIVE, F32), jnp.zeros((cap, 1), F32), jnp.zeros((cap, width), F32)),
    )
    attended = (summed / total).astype(BF16)
    out_ref[...] = attended
    gated_ref[...] = (gate * attended.astype(F32)).astype(BF16)
    gate_ref[...] = gate
    lse_ref[0] = largest + jnp.log(total)


def attention_backward_kernel(
    begin_ref, q_ref, k_ref, v_ref, rank_ref, table_ref, out_ref, lse_ref, grad_ref,
    cos_ref, sin_ref, dq_ref, dk_ref, dv_ref, dk_sum, dv_sum, *, scaling
):
    block = pl.program_id(1)
    cap, width = out_ref.shape
    tile_rows = q_ref.shape[0]
    pick, low_bound, high_bound, _ = slots_of_block(rank_ref, table_ref, cap)
    q = dot(pick, q_ref[...]).astype(BF16)
    grad = grad_ref[...]
    delta = jnp.sum(grad.astype(F32) * out_ref[...].astype(F32), axis=1, keepdims=True)
    lse = lse_ref[0]

    @pl.when(block == 0)
    def _():
        dk_sum[...] = jnp.zeros_like(dk_sum)
        dv_sum[...] = jnp.zeros_like(dv_sum)

    def step(tile, dq):
        rows, keys, scores, allowed = attention_scores(
            q, k_ref, low_bound, high_bound, tile, tile_rows, scaling
        )
        chances = jnp.where(allowed, jnp.exp(scores - lse), 0.0)
        dv_sum[rows, :] += contract_first(chances.astype(BF16), grad)
        grad_chances = contract_last(grad, v_ref[rows, :])
        grad_scores = (chances * (grad_chances - delta)).astype(BF16)
        dk_sum[rows, :] += contract_first(grad_scores, q) * scaling
        return dq + dot(grad_scores, keys)

    dq = lax.fori_loop(begin_ref[block], block + 1, step, jnp.zeros((cap, width), F32)) * scaling
    high = dq.astype(BF16)
    rest = (dq - high.astype(F32)).astype(BF16)
    dq_tokens = contract_first(pick, high) + contract_first(pick, rest)
    own = pl.ds(pl.multiple_of(block * tile_rows, tile_rows), tile_rows)
    dq_ref[...] = turned(dq_tokens, cos_ref[own, :], -sin_ref[own, :]).astype(BF16)

    @pl.when(block == BLOCKS - 1)
    def _():
        def finish(tile, nothing):
            rows = pl.ds(pl.multiple_of(tile * tile_rows, tile_rows), tile_rows)
            dk_ref[rows, :] = turned(dk_sum[rows, :], cos_ref[rows, :], -sin_ref[rows, :]).astype(BF16)
            dv_ref[rows, :] = dv_sum[rows, :].astype(BF16)
            return nothing

        lax.fori_loop(0, BLOCKS, finish, 0)


def attention_specs(row_count, token_count, width):
    return dict(
        q=pl.BlockSpec((row_count, width), lambda h, b, s: (b, h)),
        k=pl.BlockSpec((token_count, width), lambda h, b, s: (0, h)),
        rank=pl.BlockSpec((1, 1, row_count), lambda h, b, s: (b, 0, 0)),
        rows=pl.BlockSpec((16, row_count), lambda h, b, s: (0, b)),
        gate=pl.BlockSpec((CAP, 1), lambda h, b, s: (b, 0)),
        slots=pl.BlockSpec((CAP, width), lambda h, b, s: (b, h)),
        table=pl.BlockSpec((token_count, width), lambda h, b, s: (0, 0)),
        lse=pl.BlockSpec((1, CAP, 1), lambda h, b, s: (h, b, 0)),
    )


def attention_forward(begin, q, k, v, rank, table, width):
    token_count, heads = q.shape[0], q.shape[1] // width
    row_count = token_count // BLOCKS
    s = attention_specs(row_count, token_count, width)
    return pl.pallas_call(
        functools.partial(attention_forward_kernel, scaling=1.0 / math.sqrt(width)),
        grid_spec=pltpu.PrefetchScalarGridSpec(
            num_scalar_prefetch=1,
            grid=(heads, BLOCKS),
            in_specs=[s["q"], s["k"], s["k"], s["rank"], s["rows"]],
            out_specs=[s["slots"], s["slots"], s["gate"], s["lse"]],
        ),
        out_shape=[
            jax.ShapeDtypeStruct((BLOCKS * CAP, heads * width), BF16),
            jax.ShapeDtypeStruct((BLOCKS * CAP, heads * width), BF16),
            jax.ShapeDtypeStruct((BLOCKS * CAP, 1), F32),
            jax.ShapeDtypeStruct((heads, BLOCKS * CAP, 1), F32),
        ],
        compiler_params=pltpu.CompilerParams(vmem_limit_bytes=VMEM_BYTES),
        name="attention_forward",
    )(begin, q, k, v, rank, table)


def attention_backward(begin, q, k, v, rank, table, out, lse, grad, cosine, sine, width):
    token_count, heads = q.shape[0], q.shape[1] // width
    row_count = token_count // BLOCKS
    s = attention_specs(row_count, token_count, width)
    return pl.pallas_call(
        functools.partial(attention_backward_kernel, scaling=1.0 / math.sqrt(width)),
        grid_spec=pltpu.PrefetchScalarGridSpec(
            num_scalar_prefetch=1,
            grid=(heads, BLOCKS),
            in_specs=[
                s["q"], s["k"], s["k"], s["rank"], s["rows"],
                s["slots"], s["lse"], s["slots"], s["table"], s["table"],
            ],
            out_specs=[s["q"], s["k"], s["k"]],
            scratch_shapes=[pltpu.VMEM((token_count, width), F32)] * 2,
        ),
        out_shape=[
            jax.ShapeDtypeStruct((token_count, heads * width), BF16),
            jax.ShapeDtypeStruct((token_count, heads * width), BF16),
            jax.ShapeDtypeStruct((token_count, heads * width), BF16),
        ],
        compiler_params=pltpu.CompilerParams(vmem_limit_bytes=VMEM_BYTES),
        name="attention_backward",
    )(begin, q, k, v, rank, table, out, lse, grad, cosine, sine)


def exchanged(pieces):
    return lax.all_to_all(pieces, PLACES, 0, 0, tiled=True)


def over_groups(landed):
    return lax.all_gather(landed, "t", axis=0, tiled=False)


def group_sums(pieces):
    return lax.psum_scatter(pieces, "t", scatter_dimension=0, tiled=False)


def return_gradients(pieces):
    return exchanged(group_sums(pieces))


def other_core(column):
    return column + 1 - 2 * (column % 2)


def crossed(plane, j):
    return (plane, plane + 1 - 2 * (plane % 2), (plane + 2) % 4, 3 - plane)[j]


def meet(peers):
    barrier = pltpu.get_barrier_semaphore()
    for peer in peers:
        pl.semaphore_signal(barrier, inc=1, device_id=peer, device_id_type=MESH)
    pl.semaphore_wait(barrier, len(peers))


def partners():
    plane, half, column = lax.axis_index("z"), lax.axis_index("x"), lax.axis_index("grid")
    planes = [{"z": crossed(plane, j)} for j in range(PLANES)]
    along_x, along_y = {"x": 1 - half}, {"grid": (column + 2) % 4}
    core = {"grid": other_core(column)}
    return plane, half, column, planes, along_x, along_y, core


class Moves:
    def __init__(self, send, recv):
        self.send, self.recv, self.made = send, recv, {}

    def add(self, index, source, target, peer):
        self.made[index] = (source, target, peer)

    def copy(self, index, source, target, peer):
        return pltpu.make_async_remote_copy(
            src_ref=source, dst_ref=target, send_sem=self.send.at[index],
            recv_sem=self.recv.at[index], device_id=peer, device_id_type=MESH,
        )

    def start(self, index):
        self.copy(index, *self.made[index]).start()

    def arrived(self, index, target, peer):
        self.copy(index, target, target, peer).wait_recv()

    def all_sent(self):
        for index in self.made:
            self.copy(index, *self.made[index]).wait_send()


class Ride:
    def __init__(self, pieces_ref, landed_ref, send, recv, local):
        plane, half = lax.axis_index("z"), lax.axis_index("x")
        self.moves = Moves(send, recv)
        self.landings = {}
        own = plane * HALVES + half
        self.keep = pltpu.make_async_copy(pieces_ref.at[own], landed_ref.at[own], local)
        self.peers = []
        for dz in range(PLANES):
            for dx in range(HALVES):
                index = dz * HALVES + dx
                if index == 0:
                    continue
                at_half = 1 - half if dx else half
                peer = {"z": crossed(plane, dz), "x": at_half}
                other = crossed(plane, dz) * HALVES + at_half
                self.moves.add(index, pieces_ref.at[other], landed_ref.at[own], peer)
                self.landings[index] = (landed_ref.at[other], peer)
                if dz and dx:
                    self.peers.append(peer)

    def begin(self):
        self.keep.start()
        for index in (4, 6, 2):
            self.moves.start(index)

    def go_on(self, number):
        for index in ((5,), (7,), (3,), (1,))[number : number + 1]:
            self.moves.start(index[0])

    def finish(self):
        for index, (landing, peer) in self.landings.items():
            self.moves.arrived(index, landing, peer)
        self.moves.all_sent()
        self.keep.wait()


RIDE_SCRATCH = (
    pltpu.SemaphoreType.DMA((8,)),
    pltpu.SemaphoreType.DMA((8,)),
    pltpu.SemaphoreType.DMA,
)


def run_with_ride(steps, ride):
    steps[0]()
    if ride is not None:
        ride.begin()
    for number, step in enumerate(steps[1:-1]):
        step()
        if ride is not None:
            ride.go_on(number)
    steps[-1]()
    if ride is not None:
        ride.finish()


def gather_steps(slots_ref, out_ref, send, recv, local, same, share=2, more=()):
    plane, half, column, planes, along_x, along_y, core = partners()
    cap, width = slots_ref.shape[-2:]
    middle = cap * share // 64 * 16
    y_column, core_column = (column + 2) % 4, other_core(column)
    core_y = (core_column + 2) % 4
    sources = [crossed(plane, j) for j in range(PLANES)]
    moves = Moves(send, recv)

    def piece(source, at_half, at_column, first=0, count=cap):
        columns = pl.ds(pl.multiple_of(at_column * width, width), width)
        return out_ref.at[source, at_half, pl.ds(first, count), columns]

    def slots_for(j):
        return slots_ref if same else slots_ref.at[sources[j]]

    keep = pltpu.make_async_copy(slots_for(0), piece(plane, half, column), local)
    for j in range(PLANES):
        source = sources[j]
        place = piece(source, half, column)
        if j:
            moves.add(j, slots_for(j), piece(plane, half, column), planes[j])
        here = place if j else slots_for(0)
        moves.add(4 + j, here, place, along_x)
        moves.add(8 + j, here, place, along_y)
        moves.add(12 + j, here, place, core)
        from_x, from_y = piece(source, 1 - half, column), piece(source, half, y_column)
        first = piece(source, 1 - half, column, 0, middle)
        last = piece(source, half, y_column, middle, cap - middle)
        diagonal = piece(source, 1 - half, y_column)
        moves.add(16 + j, first, first, along_y)
        moves.add(20 + j, from_x, from_x, core)
        moves.add(24 + j, last, last, along_x)
        moves.add(28 + j, from_y, from_y, core)
        moves.add(32 + j, diagonal, diagonal, core)

    def begin():
        meet(planes[1:] + [along_x, along_y, core] + list(more))
        for j in (1, 3, 2):
            moves.start(j)
        keep.start()

    def spread(j):
        if j:
            moves.arrived(j, piece(sources[j], half, column), planes[j])
        for index in (4, 8, 12):
            moves.start(index + j)

    def forward(j):
        moves.arrived(4 + j, piece(sources[j], 1 - half, column), along_x)
        moves.start(16 + j)
        moves.start(20 + j)
        moves.arrived(8 + j, piece(sources[j], half, y_column), along_y)
        moves.start(24 + j)
        moves.start(28 + j)

    def cross(j):
        moves.arrived(16 + j, piece(sources[j], 1 - half, y_column, 0, middle), along_y)
        moves.arrived(24 + j, piece(sources[j], 1 - half, y_column, middle, cap - middle), along_x)
        moves.start(32 + j)

    def finish():
        for j in order:
            moves.arrived(12 + j, piece(sources[j], half, core_column), core)
            moves.arrived(20 + j, piece(sources[j], 1 - half, core_column), core)
            moves.arrived(28 + j, piece(sources[j], half, core_y), core)
            moves.arrived(32 + j, piece(sources[j], 1 - half, core_y), core)
        moves.all_sent()
        keep.wait()

    order = (0, 1, 3, 2)

    def step(number):
        if number < len(order):
            spread(order[number])
        if 0 <= number - 1 < len(order):
            forward(order[number - 1])
        if 0 <= number - 2 < len(order):
            cross(order[number - 2])

    return [begin] + [functools.partial(step, number) for number in range(len(order) + 2)] + [finish]


GATHER_SCRATCH = (
    pltpu.SemaphoreType.DMA((36,)),
    pltpu.SemaphoreType.DMA((36,)),
    pltpu.SemaphoreType.DMA,
)


def gather_kernel(*refs, same, share, rides):
    if rides:
        slots_ref, pieces_ref, out_ref, landed_ref = refs[:4]
        ride = Ride(pieces_ref, landed_ref, *refs[7:])
        scratch = refs[4:7]
    else:
        slots_ref, out_ref = refs[:2]
        ride, scratch = None, refs[2:]
    more = ride.peers if rides else ()
    run_with_ride(gather_steps(slots_ref, out_ref, *scratch, same, share, more), ride)


def gathered(slots, collective_id, ride=None, share=2):
    rows, width = slots.shape[-2:]
    rides = () if ride is None else (ride,)
    anywhere = pl.BlockSpec(memory_space=pl.ANY)
    out = pl.pallas_call(
        functools.partial(gather_kernel, same=slots.ndim == 2, share=share, rides=len(rides)),
        out_shape=[jax.ShapeDtypeStruct((PLANES, HALVES, rows, 4 * width), BF16)]
        + [jax.ShapeDtypeStruct(r.shape, BF16) for r in rides],
        in_specs=[anywhere] * (1 + len(rides)),
        out_specs=[anywhere] * (1 + len(rides)),
        scratch_shapes=list(GATHER_SCRATCH) + list(RIDE_SCRATCH) * len(rides),
        compiler_params=pltpu.CompilerParams(collective_id=collective_id, has_side_effects=True),
        name="gather_rows",
    )(slots, *rides)
    return out if rides else out[0]


def scatter_steps(
    partial_ref, out_ref, own, other, crossing, side, send, recv, load, share=2, more=()
):
    plane, half, column, planes, along_x, along_y, core = partners()
    cap, width = out_ref.shape[-2:]
    middle = cap * share // 64 * 16
    chunk = 32 if middle % 32 == 0 and cap % 32 == 0 else 16
    y_column, core_column = (column + 2) % 4, other_core(column)
    core_y = (core_column + 2) % 4
    halves = (half, 1 - half, half, 1 - half)
    own_columns = (column, column, y_column, y_column)
    core_columns = (core_column, core_column, core_y, core_y)
    moves = Moves(send, recv)
    first, last = pl.ds(0, middle), pl.ds(middle, cap - middle)

    def part(j, q, at_columns):
        columns = pl.ds(pl.multiple_of(at_columns[q] * width, width), width)
        return partial_ref.at[crossed(plane, j), halves[q], :, columns]

    def loading(j, q):
        return pltpu.make_async_copy(part(j, q, own_columns), own.at[j, q], load.at[4 * j + q])

    keep = pltpu.make_async_copy(own.at[0, 0], out_ref.at[plane], load.at[16])
    for j in range(PLANES):
        for q in range(4):
            moves.add(4 * j + q, part(j, q, core_columns), other.at[j, q], core)
        moves.add(16 + j, own.at[j, 3, first], crossing.at[j, first], along_x)
        moves.add(20 + j, own.at[j, 3, last], crossing.at[j, last], along_y)
        moves.add(24 + j, own.at[j, 2], side.at[j, 1], along_y)
        moves.add(28 + j, own.at[j, 1], side.at[j, 0], along_x)
        if j:
            moves.add(32 + j, own.at[j, 0], out_ref.at[plane], planes[j])

    def add(j, q, begin_row, count, terms):
        def step(i, nothing):
            rows = pl.ds(pl.multiple_of(begin_row + i * chunk, chunk), chunk)
            total = own[j, q, rows, :].astype(F32)
            for ref, index in terms:
                total = total + ref[index + (rows, slice(None))].astype(F32)
            own[j, q, rows, :] = total.astype(BF16)
            return nothing

        lax.fori_loop(0, count // chunk, step, 0)

    def chip_sum(j, q):
        moves.arrived(4 * j + q, other.at[j, q], core)
        loading(j, q).wait()
        add(j, q, 0, cap, [(other, (j, q))])

    def stage_one(j):
        chip_sum(j, 3)
        moves.start(16 + j)
        moves.start(20 + j)
        chip_sum(j, 2)
        chip_sum(j, 1)
        chip_sum(j, 0)

    def stage_two(j):
        moves.arrived(16 + j, crossing.at[j, first], along_x)
        add(j, 2, 0, middle, [(crossing, (j,))])
        moves.start(24 + j)
        moves.arrived(20 + j, crossing.at[j, last], along_y)
        add(j, 1, middle, cap - middle, [(crossing, (j,))])
        moves.start(28 + j)

    def stage_three(j):
        moves.arrived(24 + j, side.at[j, 1], along_y)
        moves.arrived(28 + j, side.at[j, 0], along_x)
        add(j, 0, 0, cap, [(side, (j, 0)), (side, (j, 1))])
        if j:
            moves.start(32 + j)
        else:
            keep.start()

    order = (2, 3, 1, 0)

    def begin():
        meet(planes[1:] + [along_x, along_y, core] + list(more))
        for j in order:
            for q in (3, 2, 1, 0):
                moves.start(4 * j + q)
                loading(j, q).start()

    def step(number):
        if number < len(order):
            stage_one(order[number])
        if 0 <= number - 1 < len(order):
            stage_two(order[number - 1])
        if 0 <= number - 2 < len(order):
            stage_three(order[number - 2])

    def finish():
        for j in range(1, PLANES):
            moves.arrived(32 + j, out_ref.at[crossed(plane, j)], planes[j])
        moves.all_sent()
        keep.wait()

    return [begin] + [functools.partial(step, number) for number in range(len(order) + 2)] + [finish]


def scatter_scratch(rows, width):
    return [
        pltpu.VMEM((PLANES, 4, rows, width), BF16),
        pltpu.VMEM((PLANES, 4, rows, width), BF16),
        pltpu.VMEM((PLANES, rows, width), BF16),
        pltpu.VMEM((PLANES, 2, rows, width), BF16),
        pltpu.SemaphoreType.DMA((36,)),
        pltpu.SemaphoreType.DMA((36,)),
        pltpu.SemaphoreType.DMA((17,)),
    ]


def scatter_kernel(*refs, share, rides):
    if rides:
        partial_ref, pieces_ref, out_ref, landed_ref = refs[:4]
        ride = Ride(pieces_ref, landed_ref, *refs[11:])
        scratch = refs[4:11]
    else:
        partial_ref, out_ref = refs[:2]
        ride, scratch = None, refs[2:]
    more = ride.peers if rides else ()
    run_with_ride(scatter_steps(partial_ref, out_ref, *scratch, share, more), ride)


def scattered(partial, rows, collective_id, ride=None, share=2):
    width = partial.shape[1] // 4
    rides = () if ride is None else (ride,)
    anywhere = pl.BlockSpec(memory_space=pl.ANY)
    out = pl.pallas_call(
        functools.partial(scatter_kernel, share=share, rides=len(rides)),
        out_shape=[jax.ShapeDtypeStruct((PLANES, rows, width), BF16)]
        + [jax.ShapeDtypeStruct(r.shape, BF16) for r in rides],
        in_specs=[anywhere] * (1 + len(rides)),
        out_specs=[anywhere] * (1 + len(rides)),
        scratch_shapes=scatter_scratch(rows, width) + list(RIDE_SCRATCH) * len(rides),
        compiler_params=pltpu.CompilerParams(
            collective_id=collective_id, has_side_effects=True, vmem_limit_bytes=VMEM_BYTES
        ),
        name="scatter_rows",
    )(partial.reshape(PLANES, HALVES, rows, 4 * width), *rides)
    return out if rides else out[0]


def carry(before, after, last, compute):
    number = pl.program_id(0)

    @pl.when(number == 0)
    def _():
        for step in before:
            step()

    compute()
    for place, step in enumerate(after):
        pl.when(number == place)(step)
    pl.when(number == BLOCKS - 1)(last)


def expert_forward_kernel(
    rows_ref, up_weight_ref, down_weight_ref, small_ref, rank_ref, member_ref, grad_ref,
    gate_ref, up_ref, result_ref, share_ref, grad_rows_ref, *scratch
):
    steps = gather_steps(grad_ref, grad_rows_ref, *scratch, False)
    units = gate_ref.shape[1]

    def compute():
        rows = rows_ref[0]
        made = dot(rows, up_weight_ref[...])
        gate, up = made[:, :units], made[:, units:]
        gate_ref[...] = gate
        up_ref[...] = up
        inner = (gate * jax.nn.sigmoid(gate) * up).astype(BF16)
        result_ref[0] = contract_last(inner, down_weight_ref[...]).astype(BF16)
        cap, count = rows.shape[0], rank_ref.shape[2]
        pick = (lax.broadcasted_iota(jnp.int32, (cap, count), 0) == rank_ref[0]).astype(BF16)
        member = contract_last(pick, member_ref[...]) > 0.5
        logits = jnp.where(member, contract_last(rows, small_ref[...]), NEGATIVE)
        largest = jnp.max(logits, axis=1, keepdims=True)
        weights = jnp.where(member, jnp.exp(logits - largest), 0.0)
        mine = lax.broadcasted_iota(jnp.int32, weights.shape, 1) == 6 + lax.axis_index("z")
        total = jnp.sum(weights, axis=1, keepdims=True)
        own = jnp.sum(jnp.where(mine, weights, 0.0), axis=1, keepdims=True)
        share_ref[...] = own / jnp.where(total > 0.0, total, 1.0)

    carry(steps[:2], steps[2:-1], steps[-1], compute)


def once(shape):
    return pl.BlockSpec(shape, lambda b: (0,) * len(shape), pipeline_mode=pl.Buffered(1))


def expert_forward(rows, up_weight, down_weight, small, rank, member, grad_slots, collective_id):
    _, cap, width = rows.shape
    units = down_weight.shape[1]
    count = BLOCKS * cap
    anywhere = pl.BlockSpec(memory_space=pl.ANY)
    block = lambda b: (b, 0)
    return pl.pallas_call(
        expert_forward_kernel,
        grid=(BLOCKS,),
        in_specs=[
            pl.BlockSpec((1, cap, width), lambda b: (b, 0, 0)),
            once(up_weight.shape),
            once(down_weight.shape),
            once(small.shape),
            pl.BlockSpec((1, 1, rank.shape[2]), lambda b: (b, 0, 0)),
            pl.BlockSpec((16, rank.shape[2]), lambda b: (0, b)),
            anywhere,
        ],
        out_specs=[
            pl.BlockSpec((cap, units), block),
            pl.BlockSpec((cap, units), block),
            pl.BlockSpec((1, cap, width), lambda b: (b, 0, 0)),
            pl.BlockSpec((cap, 1), block),
            anywhere,
        ],
        out_shape=[
            jax.ShapeDtypeStruct((count, units), F32),
            jax.ShapeDtypeStruct((count, units), F32),
            jax.ShapeDtypeStruct((BLOCKS, cap, width), BF16),
            jax.ShapeDtypeStruct((count, 1), F32),
            jax.ShapeDtypeStruct((PLANES, HALVES, cap, width), BF16),
        ],
        scratch_shapes=list(GATHER_SCRATCH),
        compiler_params=pltpu.CompilerParams(
            collective_id=collective_id, has_side_effects=True, vmem_limit_bytes=VMEM_BYTES
        ),
        name="expert_forward",
    )(rows, up_weight, down_weight, small, rank, member, grad_slots)


def expert_backward_kernel(
    gate_ref, up_ref, grad_ref, share_ref, up_weight_ref, down_weight_ref, result_ref,
    grad_rows_ref, grad_gate_up_ref, inner_ref, out_ref, *scratch
):
    steps = scatter_steps(result_ref, out_ref, *scratch)

    def compute():
        share = share_ref[...]
        grad_inner = dot(grad_ref[0], down_weight_ref[...]) * share
        gate, up = gate_ref[...], up_ref[...]
        sigmoid = jax.nn.sigmoid(gate)
        silu = gate * sigmoid
        inner_ref[...] = (share * silu * up).astype(BF16)
        grad_gate = grad_inner * up * sigmoid * (1.0 + gate * (1.0 - sigmoid))
        grad_gate_up = jnp.concatenate([grad_gate, grad_inner * silu], axis=1).astype(BF16)
        grad_gate_up_ref[...] = grad_gate_up
        grad_rows_ref[0] = contract_last(grad_gate_up, up_weight_ref[...]).astype(BF16)

    carry(steps[:1], steps[1:-1], steps[-1], compute)


def expert_backward(
    gate, up, grad_rows, share, up_weight, down_weight, result, collective_id
):
    _, cap, width = grad_rows.shape
    count, units = gate.shape
    anywhere = pl.BlockSpec(memory_space=pl.ANY)
    block = lambda b: (b, 0)
    rows = pl.BlockSpec((1, cap, width), lambda b: (b, 0, 0))
    return pl.pallas_call(
        expert_backward_kernel,
        grid=(BLOCKS,),
        in_specs=[
            pl.BlockSpec((cap, units), block),
            pl.BlockSpec((cap, units), block),
            rows,
            pl.BlockSpec((cap, 1), block),
            once(up_weight.shape),
            once(down_weight.shape),
            anywhere,
        ],
        out_specs=[
            rows,
            pl.BlockSpec((cap, 2 * units), block),
            pl.BlockSpec((cap, units), block),
            anywhere,
        ],
        out_shape=[
            jax.ShapeDtypeStruct((BLOCKS, cap, width), BF16),
            jax.ShapeDtypeStruct((count, 2 * units), BF16),
            jax.ShapeDtypeStruct((count, units), BF16),
            jax.ShapeDtypeStruct((PLANES, cap, width // 4), BF16),
        ],
        scratch_shapes=scatter_scratch(cap, width // 4),
        compiler_params=pltpu.CompilerParams(
            collective_id=collective_id, has_side_effects=True, vmem_limit_bytes=VMEM_BYTES
        ),
        name="expert_backward",
    )(gate, up, grad_rows, share, up_weight, down_weight, result.reshape(PLANES, HALVES, cap, width))


def expert_gradient_kernel(
    rows_ref, grad_ref, grad_gate_up_ref, inner_ref, partial_ref,
    up_grad_ref, down_first_ref, down_last_ref, out_ref, *scratch
):
    steps = scatter_steps(partial_ref, out_ref, *scratch)
    middle = down_first_ref.shape[1]

    def compute():
        up_grad_ref[...] = contract_first(rows_ref[...], grad_gate_up_ref[...]).astype(BF16)
        down_grad = contract_first(grad_ref[...], inner_ref[...]).astype(BF16)
        down_first_ref[0] = down_grad[:middle]
        down_last_ref[0] = down_grad[middle:]

    carry(steps[:1], steps[1:-1], steps[-1], compute)


def expert_gradient(rows, grad_rows, grad_gate_up, inner, partial, collective_id):
    count, width = rows.shape
    units = inner.shape[1]
    cap, tile = count // BLOCKS, width // BLOCKS
    anywhere = pl.BlockSpec(memory_space=pl.ANY)
    columns = pl.BlockSpec((count, tile), lambda b: (0, b))
    return pl.pallas_call(
        expert_gradient_kernel,
        grid=(BLOCKS,),
        in_specs=[columns, columns, once((count, 2 * units)), once((count, units)), anywhere],
        out_specs=[
            pl.BlockSpec((tile, 2 * units), lambda b: (b, 0)),
            pl.BlockSpec((1, tile // 2, units), lambda b: (b, 0, 0)),
            pl.BlockSpec((1, tile // 2, units), lambda b: (b, 0, 0)),
            anywhere,
        ],
        out_shape=[
            jax.ShapeDtypeStruct((width, 2 * units), BF16),
            jax.ShapeDtypeStruct((BLOCKS, tile // 2, units), BF16),
            jax.ShapeDtypeStruct((BLOCKS, tile // 2, units), BF16),
            jax.ShapeDtypeStruct((PLANES, cap, width // 4), BF16),
        ],
        scratch_shapes=scatter_scratch(cap, width // 4),
        compiler_params=pltpu.CompilerParams(
            collective_id=collective_id, has_side_effects=True, vmem_limit_bytes=VMEM_BYTES
        ),
        name="expert_gradient",
    )(rows, grad_rows, grad_gate_up, inner, partial.reshape(PLANES, HALVES, cap, width))


def grid_sum(values):
    shape = values.shape
    return lax.all_gather(values.reshape(-1, 128), "grid", axis=0).sum(axis=0).reshape(shape)


def prefix_ranks(member):
    counted = member.astype(BF16)
    width = member.shape[-1]
    before = jnp.arange(width)[:, None] < jnp.arange(width)[None, :]
    return jnp.where(member, dot(counted, before.astype(BF16)).astype(jnp.int32), -1)


def picks(rank):
    return (jnp.arange(CAP, dtype=jnp.int32)[:, None] == rank[..., None, :]).astype(BF16)


def members(first, second):
    names = jnp.arange(PLANES, dtype=first.dtype).reshape((PLANES,) + (1,) * first.ndim)
    return (first[None] == names) | (second[None] == names)


def route_gates(logits, member):
    shown = jnp.where(member, logits, NEGATIVE)
    weights = jnp.where(member, jnp.exp(shown - jnp.max(shown, axis=0, keepdims=True)), 0.0)
    return weights / jnp.sum(weights, axis=0, keepdims=True)


def logits_grad(gates, grad_gates):
    return gates * (grad_gates - jnp.sum(gates * grad_gates, axis=0, keepdims=True))


def exact_first(left, right):
    return lax.dot_general(
        left, right, (((0,), (0,)), ((), ())), precision=lax.Precision.HIGHEST
    )


def exact_last(left, right):
    return lax.dot_general(
        left, right, (((1,), (1,)), ((), ())), precision=lax.Precision.HIGHEST
    )


def norm_sums(grad_hidden, scaled, router, gates, grad_gates, width):
    parts = jnp.concatenate(
        [
            grad_gates,
            exact_last(router.astype(F32), scaled),
            jnp.sum(grad_hidden * scaled, axis=1)[None],
        ],
        axis=0,
    )
    parts = grid_sum(parts)
    grad_logits = logits_grad(gates, parts[:PLANES])
    inner = parts[2 * PLANES] + jnp.sum(grad_logits * parts[PLANES : 2 * PLANES], axis=0)
    return grad_logits, inner[:, None] / width


def per_device(
    tokens, segment_ids, attention_routes, expert_routes, attention_gain, attention_kv,
    attention_query, attention_out, attention_router, feedforward_gain, feedforward_router,
    expert_gate_up, expert_down, output_grad,
):
    groups = lax.axis_size("t")
    grid_count = lax.axis_size("grid")
    group = lax.axis_index("t")
    plane = lax.axis_index("z")
    place = plane * HALVES + lax.axis_index("x")
    column = lax.axis_index("grid")
    rows, features = tokens.shape
    width_all = features * grid_count
    token_count = BLOCKS * rows
    own_rows = attention_gain.shape[0]
    head_width = attention_kv.shape[3]
    head_pair = attention_kv.shape[1] // HALVES
    span = head_pair * head_width
    hidden_units = expert_gate_up.shape[3] // HALVES

    def mine(array, axis=0):
        return lax.dynamic_slice_in_dim(array, column * features, features, axis)

    def own(array, axis=0):
        return lax.dynamic_slice_in_dim(array, place * rows, rows, axis)

    query_pieces = attention_query.reshape(PLANES, own_rows, HALVES, span).transpose(0, 2, 1, 3)
    kv_pieces = attention_kv.reshape(own_rows, HALVES, head_pair, 2, head_width)
    kv_pieces = kv_pieces.transpose(1, 0, 3, 2, 4).reshape(1, HALVES, own_rows, 2 * span)
    kv_pieces = jnp.broadcast_to(kv_pieces, (PLANES,) + kv_pieces.shape[1:])
    qkv_pieces = jnp.concatenate([query_pieces, kv_pieces], axis=-1)
    out_pieces = attention_out.reshape(BLOCKS, span, own_rows).swapaxes(1, 2)
    first_pieces = jnp.concatenate([qkv_pieces.reshape(BLOCKS, own_rows, 3 * span), out_pieces], axis=2)
    up_pieces = expert_gate_up.reshape(PLANES, own_rows, 2, HALVES, hidden_units)
    up_pieces = up_pieces.transpose(0, 3, 1, 2, 4).reshape(BLOCKS, own_rows, 2 * hidden_units)
    down_pieces = expert_down.reshape(BLOCKS, hidden_units, own_rows).swapaxes(1, 2)
    down_halves = down_pieces[:, : own_rows // 2], down_pieces[:, own_rows // 2 :]

    own_routes = jnp.concatenate([attention_routes, expert_routes], axis=1)
    small = jnp.concatenate(
        [attention_gain[:, None], feedforward_gain[:, None], attention_router, feedforward_router],
        axis=1,
    )
    small = lax.all_gather(small, "t", axis=0).reshape(-1, small.shape[1])
    small = small.T.reshape(small.shape[1], -1)
    spare = jnp.zeros((small.shape[0], features - small.shape[1] % features), BF16)
    small = jnp.concatenate([small, spare], axis=1).reshape(-1, features)
    under = jnp.concatenate([own_routes.T.astype(BF16), small], axis=0)
    under = jnp.pad(under, ((0, -under.shape[0] % 16), (0, 0)))
    everything, first_weight = gathered(
        jnp.concatenate([tokens, under], axis=0), 0, ride=first_pieces, share=3
    )
    first_weight = over_groups(first_weight).reshape(width_all, 4 * span)
    qkv_weight, out_weight = first_weight[:, : 3 * span], first_weight[:, 3 * span :]
    up_pieces, everything = lax.optimization_barrier((up_pieces, everything))
    up_weight = over_groups(exchanged(up_pieces)).reshape(width_all, 2 * hidden_units)
    under = everything[:, :, rows:, :features].reshape(BLOCKS, -1, features).swapaxes(0, 1)
    small = under[4:, :, : groups * own_rows].reshape(-1, BLOCKS, groups, own_rows)
    small = jnp.pad(small.swapaxes(1, 2).reshape(-1, width_all), ((0, 4), (0, 0)))
    gain_first, gain_second = mine(small[0]).astype(F32), mine(small[1]).astype(F32)
    router_first, router_second = mine(small[2:6], 1), mine(small[6:10], 1)

    member_first, member_second = members(under[0], under[1]), members(under[2], under[3])
    own_member_first = lax.dynamic_index_in_dim(member_first, place, 1, keepdims=False)
    own_member_second = lax.dynamic_index_in_dim(member_second, place, 1, keepdims=False)
    rank = prefix_ranks(
        jnp.concatenate(
            [
                lax.dynamic_index_in_dim(member_first, plane, 0, keepdims=False),
                lax.dynamic_index_in_dim(member_second, plane, 0, keepdims=False),
                own_member_first,
                own_member_second,
            ],
            axis=0,
        )
    )
    rank_first, rank_second = rank[:BLOCKS, None], rank[BLOCKS : 2 * BLOCKS, None]
    own_pick_first = picks(rank[2 * BLOCKS : 2 * BLOCKS + PLANES])
    own_pick_second = picks(rank[2 * BLOCKS + PLANES :])
    member_first = member_first.reshape(PLANES, token_count)
    member_second = member_second.reshape(PLANES, token_count)

    def to_slots(values, pick):
        return jnp.einsum("est,tf->esf", pick, values, preferred_element_type=F32).astype(BF16)

    def to_tokens(slots, pick):
        return jnp.einsum("est,esf->etf", pick, slots, preferred_element_type=F32)

    grad_out = output_grad.astype(F32)
    cosine, sine = rope_tables(token_count, head_width)
    cosine, sine = jnp.asarray(cosine), jnp.asarray(sine)
    hidden_first, queries, keys, values, logits_first, inverse_first = project(
        everything, rows, small, first_weight, cosine, sine, span, head_width
    )
    gates_first = route_gates(logits_first[2 : 2 + PLANES], member_first)
    own_gates_first = own(gates_first, 1)
    position = jnp.arange(token_count, dtype=jnp.int32)
    segment = lax.dynamic_slice_in_dim(segment_ids, group * token_count, token_count, 0)
    opens = jnp.concatenate([jnp.ones((1,), jnp.bool_), segment[1:] != segment[:-1]])
    document_start = lax.cummax(jnp.where(opens, position, 0))
    begin = document_start.reshape(BLOCKS, rows)[:, 0] // rows
    table = token_table(
        position, document_start, lax.dynamic_index_in_dim(gates_first, plane, 0, keepdims=False)
    )
    attention_args = (begin, queries, keys, values, rank_first, table)
    attended, gated, gate_slots_first, lse = attention_forward(*attention_args, head_width)
    branch_slots, down_first = scattered(
        contract_last(attended, out_weight).astype(BF16), CAP, 2, ride=down_halves[0], share=1
    )
    branch_first = to_tokens(branch_slots, own_pick_first)
    residual = tokens.astype(F32) + jnp.sum(own_gates_first[:, :, None] * branch_first, axis=0)

    square = grid_sum(jnp.sum(residual * residual, axis=1))
    inverse_second = lax.rsqrt(square / width_all + EPSILON)[:, None]
    normed_second = residual * inverse_second
    hidden_second = (normed_second * gain_second).astype(BF16)
    slots_second, down_last = gathered(
        to_slots(hidden_second, own_pick_second), 1, ride=down_halves[1], share=3
    )
    down_weight = over_groups(jnp.concatenate([down_first, down_last], axis=1))
    down_weight = down_weight.reshape(width_all, hidden_units)
    slots_second = slots_second.reshape(BLOCKS, CAP, width_all)
    gate_pre, up_pre, result, gate_slots_second, grad_slots_second = expert_forward(
        slots_second,
        up_weight,
        down_weight,
        small,
        rank_second,
        jnp.pad(member_second.astype(BF16), ((6, 6), (0, 0))),
        to_slots(output_grad, own_pick_second),
        4,
    )
    grad_slots_second = grad_slots_second.reshape(BLOCKS, CAP, width_all)
    grad_rows, grad_gate_up, inner, result_slots = expert_backward(
        gate_pre, up_pre, grad_slots_second, gate_slots_second, up_weight, down_weight, result, 5
    )
    grad_up, grad_down_first, grad_down_last, grad_rows = expert_gradient(
        slots_second.reshape(-1, width_all), grad_slots_second.reshape(-1, width_all),
        grad_gate_up, inner, grad_rows, 6,
    )
    own_logits = grid_sum(contract_last(router_second, hidden_second))
    own_gates_second = route_gates(own_logits, own_member_second)
    branch_second = to_tokens(result_slots, own_pick_second)
    layer_output = residual + jnp.sum(own_gates_second[:, :, None] * branch_second, axis=0)
    layer_output = layer_output.astype(BF16)

    grad_hidden_second = jnp.sum(to_tokens(grad_rows, own_pick_second), axis=0)
    grad_logits_second, inner_mean = norm_sums(
        grad_hidden_second, normed_second * gain_second, router_second, own_gates_second,
        jnp.sum(branch_second * grad_out[None], axis=2), width_all,
    )
    grad_hidden_second = grad_hidden_second + exact_first(
        grad_logits_second, router_second.astype(F32)
    )
    grad_router_second = exact(grad_logits_second, hidden_second.astype(F32))
    grad_gain_second = jnp.sum(grad_hidden_second * normed_second, axis=0)
    grad_normed = grad_hidden_second * gain_second
    grad_residual = grad_out + inverse_second * (grad_normed - normed_second * inner_mean)

    if groups > 1:
        grad_down = jnp.concatenate([grad_down_first, grad_down_last], axis=1)
        grad_down = group_sums(grad_down.reshape(groups, BLOCKS, own_rows, hidden_units))
        grad_down_first, grad_down_last = jnp.split(grad_down, 2, axis=1)
    grad_slots_first, grad_down_first = gathered(
        to_slots(grad_residual.astype(BF16), own_pick_first), 1, ride=grad_down_first, share=3
    )
    grad_slots_first = grad_slots_first.reshape(BLOCKS * CAP, -1)
    grad_up, grad_slots_first = lax.optimization_barrier((grad_up, grad_slots_first))
    grad_up = return_gradients(grad_up.reshape(groups, BLOCKS, own_rows, 2 * hidden_units))
    grad_attended = gate_slots_first * dot(grad_slots_first, out_weight)
    grad_attended = grad_attended.astype(BF16)
    grad_out_weight = contract_first(
        grad_slots_first, gated
    )
    grad_qkv = jnp.concatenate(
        attention_backward(
            *attention_args, attended, lse, grad_attended, cosine, sine, head_width
        ),
        axis=1,
    )
    grad_hidden = contract_last(grad_qkv, qkv_weight).astype(BF16)
    grad_first = jnp.concatenate(
        [contract_first(hidden_first, grad_qkv).astype(BF16), grad_out_weight.astype(BF16)], axis=1
    )
    grad_hidden, grad_first, grad_up = lax.optimization_barrier((grad_hidden, grad_first, grad_up))
    grad_hidden, grad_down_last = scattered(grad_hidden, rows, 3, ride=grad_down_last, share=1)
    grad_hidden = jnp.sum(grad_hidden.astype(F32), axis=0)
    expert_gate_up_grad = grad_up.reshape(PLANES, HALVES, own_rows, 2, hidden_units)
    expert_gate_up_grad = expert_gate_up_grad.transpose(0, 2, 3, 1, 4).reshape(expert_gate_up.shape)
    expert_down_grad = jnp.concatenate([grad_down_first, grad_down_last], axis=1)
    expert_down_grad = expert_down_grad.swapaxes(1, 2).reshape(expert_down.shape)

    own_normed = tokens.astype(F32) * own(inverse_first)
    own_hidden = (own_normed * gain_first).astype(BF16)
    grad_logits_first, inner_mean = norm_sums(
        grad_hidden, own_normed * gain_first, router_first, own_gates_first,
        jnp.sum(branch_first * grad_residual[None], axis=2), width_all,
    )
    grad_hidden_first = grad_hidden + exact_first(grad_logits_first, router_first.astype(F32))
    grad_router_first = exact(grad_logits_first, own_hidden.astype(F32))
    grad_gain_first = jnp.sum(grad_hidden_first * own_normed, axis=0)
    grad_normed = grad_hidden_first * gain_first
    input_grad = grad_residual + own(inverse_first) * (grad_normed - own_normed * inner_mean)

    small_grads = jnp.concatenate(
        [grad_gain_first[None], grad_gain_second[None], grad_router_first, grad_router_second],
        axis=0,
    )
    small_grads = lax.all_gather(small_grads.astype(BF16), "grid", axis=1, tiled=True)
    small_grads = small_grads.reshape(-1, groups, BLOCKS, own_rows).transpose(1, 2, 0, 3)
    small_grads = jnp.pad(small_grads, ((0, 0), (0, 0), (0, 6), (0, 4 * span - own_rows)))
    grad_first = grad_first.reshape(groups, BLOCKS, own_rows, 4 * span)
    grad_first = return_gradients(jnp.concatenate([grad_first, small_grads], axis=2))
    small_grads = jnp.sum(grad_first[:, own_rows:, :own_rows].astype(F32), axis=0)
    grad_first = grad_first[:, :own_rows]
    attention_out_grad = grad_first[..., 3 * span :].swapaxes(1, 2).reshape(attention_out.shape)
    attention_query_grad = grad_first[..., :span].reshape(PLANES, HALVES, own_rows, span)
    attention_query_grad = attention_query_grad.transpose(0, 2, 1, 3).reshape(attention_query.shape)
    grad_kv_weight = grad_first[..., span : 3 * span].astype(F32).reshape(
        PLANES, HALVES, own_rows, 2, head_pair, head_width
    )
    attention_kv_grad = grad_kv_weight.sum(axis=0).transpose(1, 0, 3, 2, 4)
    attention_kv_grad = attention_kv_grad.reshape(attention_kv.shape)
    return (
        layer_output,
        input_grad.astype(BF16),
        small_grads[0],
        attention_kv_grad,
        attention_query_grad.astype(F32),
        attention_out_grad.astype(F32),
        small_grads[2:6].T,
        small_grads[1],
        small_grads[6:10].T,
        expert_gate_up_grad.astype(F32),
        expert_down_grad.astype(F32),
    )


def solution(mesh):
    groups = mesh.shape["wide"] // BLOCKS
    shape = (groups, PLANES, HALVES, mesh.shape["grid"])
    inner_mesh = Mesh(mesh.devices.reshape(shape), ("t", "z", "x", "grid"))
    wide = ("t", "z", "x")
    in_specs = (
        P(wide, "grid"),
        P(),
        P(wide, None),
        P(wide, None),
        P(wide),
        P(wide, "grid", None, None),
        P(None, wide, "grid", None),
        P(None, "grid", None, wide),
        P(wide, None),
        P(wide),
        P(wide, None),
        P(None, wide, None, "grid"),
        P(None, "grid", wide),
        P(wide, "grid"),
    )
    out_specs = (
        P(wide, "grid"),
        P(wide, "grid"),
        P(wide),
        P(wide, "grid", None, None),
        P(None, wide, "grid", None),
        P(None, "grid", None, wide),
        P(wide, None),
        P(wide),
        P(wide, None),
        P(None, wide, None, "grid"),
        P(None, "grid", wide),
    )
    return jax.shard_map(
        per_device, mesh=inner_mesh, in_specs=in_specs, out_specs=out_specs, check_vma=False
    )
```

```python
import functools
import math

import jax
import jax.numpy as jnp
import numpy as np
from jax import lax
from jax.experimental import pallas as pl
from jax.experimental.layout import Layout, with_layout_constraint
from jax.experimental.pallas import tpu as pltpu
from jax.sharding import Mesh, PartitionSpec as P

CAP = 320
PLANES = 4
HALVES = 2
BLOCKS = PLANES * HALVES
EPSILON = 1e-05
ROPE_BASE = 10000.0
NEGATIVE = -1e30
BF16 = jnp.bfloat16
F32 = jnp.float32
PLACES = ("z", "x")
MESH = pl.DeviceIdType.MESH
VMEM_BYTES = 56 * 1024 * 1024


def rope_tables(token_count, width):
    half = width // 2
    frequency = np.float32(ROPE_BASE) ** (-np.arange(half, dtype=np.float32) / np.float32(half))
    angles = np.arange(token_count, dtype=np.float32)[:, None] * frequency.astype(np.float32)[None, :]
    cosine, sine = np.cos(angles).astype(np.float32), np.sin(angles).astype(np.float32)
    return np.concatenate([cosine, cosine], axis=1), np.concatenate([-sine, sine], axis=1)


def turned(values, cosine, sine):
    return values * cosine + pltpu.roll(values, values.shape[1] // 2, 1) * sine


def dot(left, right):
    return jnp.dot(left, right, preferred_element_type=F32)


def contract_first(left, right):
    return lax.dot_general(left, right, (((0,), (0,)), ((), ())), preferred_element_type=F32)


def contract_last(left, right):
    return lax.dot_general(left, right, (((1,), (1,)), ((), ())), preferred_element_type=F32)


def exact(left, right):
    return jnp.dot(left, right, precision=lax.Precision.HIGHEST)


def project_kernel(
    tokens_ref, small_ref, query_weight_ref, shared_weight_ref, cos_ref, sin_ref,
    hidden_ref, q_ref, k_ref, v_ref, logits_ref, inverse_ref, *, head_width
):
    x = tokens_ref[0, 0].astype(F32)
    inverse = lax.rsqrt(jnp.mean(x * x, axis=1, keepdims=True) + EPSILON)
    inverse_ref[...] = inverse
    hidden = (x * inverse * small_ref[:1, :].astype(F32)).astype(BF16)
    hidden_ref[...] = hidden
    logits_ref[...] = contract_last(small_ref[...], hidden)
    queries = dot(hidden, query_weight_ref[...])
    shared = dot(hidden, shared_weight_ref[...])
    span = q_ref.shape[1]
    cosine, sine = cos_ref[...], sin_ref[...]
    for head in range(span // head_width):
        at = slice(head * head_width, (head + 1) * head_width)
        q_ref[:, at] = turned(queries[:, at], cosine, sine).astype(BF16)
        k_ref[:, at] = turned(shared[:, at], cosine, sine).astype(BF16)
    v_ref[...] = shared[:, span:].astype(BF16)


def project(tokens, rows, small, weight, cosine, sine, span, head_width):
    width = tokens.shape[-1]
    token_count = BLOCKS * rows
    whole = lambda b: (0, 0)
    block = lambda b: (b, 0)
    return pl.pallas_call(
        functools.partial(project_kernel, head_width=head_width),
        grid=(BLOCKS,),
        in_specs=[
            pl.BlockSpec((1, 1, rows, width), lambda b: (b // HALVES, b % HALVES, 0, 0)),
            pl.BlockSpec(small.shape, whole),
            pl.BlockSpec((width, span), lambda b: (0, 1)),
            pl.BlockSpec((width, 2 * span), lambda b: (0, 1)),
            pl.BlockSpec((rows, head_width), block),
            pl.BlockSpec((rows, head_width), block),
        ],
        out_specs=[
            pl.BlockSpec((rows, width), block),
            pl.BlockSpec((rows, span), block),
            pl.BlockSpec((rows, span), block),
            pl.BlockSpec((rows, span), block),
            pl.BlockSpec((small.shape[0], rows), lambda b: (0, b)),
            pl.BlockSpec((rows, 1), block),
        ],
        out_shape=[
            jax.ShapeDtypeStruct((token_count, width), BF16),
            jax.ShapeDtypeStruct((token_count, span), BF16),
            jax.ShapeDtypeStruct((token_count, span), BF16),
            jax.ShapeDtypeStruct((token_count, span), BF16),
            jax.ShapeDtypeStruct((small.shape[0], token_count), F32),
            jax.ShapeDtypeStruct((token_count, 1), F32),
        ],
        compiler_params=pltpu.CompilerParams(vmem_limit_bytes=VMEM_BYTES),
        name="project",
    )(tokens, small, weight, weight, cosine, sine)


def attention_scores(q, k_ref, low_bound, high_bound, tile, tile_rows, scaling):
    rows = pl.ds(pl.multiple_of(tile * tile_rows, tile_rows), tile_rows)
    keys = k_ref[rows, :]
    scores = contract_last(q, keys) * scaling
    column = tile * tile_rows + lax.broadcasted_iota(jnp.int32, scores.shape, 1)
    allowed = (column >= low_bound) & (column <= high_bound)
    return rows, keys, scores, allowed


def slots_of_block(rank_ref, table_ref, cap):
    rows = table_ref.shape[1]
    pick = (lax.broadcasted_iota(jnp.int32, (cap, rows), 0) == rank_ref[0]).astype(BF16)
    made = contract_last(pick, table_ref[...])
    base = pl.program_id(1) * rows
    filled = made[:, 4:5] > 0.5
    low = (64.0 * made[:, 2:3] + made[:, 3:4]).astype(jnp.int32)
    high = (64.0 * made[:, 0:1] + made[:, 1:2]).astype(jnp.int32)
    gate = made[:, 5:6] + made[:, 6:7] + made[:, 7:8]
    return pick, jnp.where(filled, low, base), jnp.where(filled, high, base), gate


def token_table(position, document_start, gate):
    first = gate.astype(BF16).astype(F32)
    second = (gate - first).astype(BF16).astype(F32)
    rows = [
        position // 64, position % 64, document_start // 64, document_start % 64,
        jnp.ones_like(gate), first, second, gate - first - second,
    ]
    return jnp.pad(jnp.stack([row.astype(BF16) for row in rows]), ((0, 8), (0, 0)))


def attention_forward_kernel(
    begin_ref, q_ref, k_ref, v_ref, rank_ref, table_ref, out_ref, gated_ref, gate_ref, lse_ref, *,
    scaling
):
    block = pl.program_id(1)
    cap, width = out_ref.shape
    tile_rows = q_ref.shape[0]
    pick, low_bound, high_bound, gate = slots_of_block(rank_ref, table_ref, cap)
    q = dot(pick, q_ref[...]).astype(BF16)

    def step(tile, carried):
        largest, total, summed = carried
        rows, _, scores, allowed = attention_scores(
            q, k_ref, low_bound, high_bound, tile, tile_rows, scaling
        )
        scores = jnp.where(allowed, scores, NEGATIVE)
        new_largest = jnp.maximum(largest, jnp.max(scores, axis=1, keepdims=True))
        weights = jnp.where(allowed, jnp.exp(scores - new_largest), 0.0)
        shrink = jnp.exp(largest - new_largest)
        return (
            new_largest,
            total * shrink + jnp.sum(weights, axis=1, keepdims=True),
            summed * shrink + dot(weights.astype(BF16), v_ref[rows, :]),
        )

    largest, total, summed = lax.fori_loop(
        begin_ref[block],
        block + 1,
        step,
        (jnp.full((cap, 1), NEGATIVE, F32), jnp.zeros((cap, 1), F32), jnp.zeros((cap, width), F32)),
    )
    attended = (summed / total).astype(BF16)
    out_ref[...] = attended
    gated_ref[...] = (gate * attended.astype(F32)).astype(BF16)
    gate_ref[...] = gate
    lse_ref[0] = largest + jnp.log(total)


def attention_backward_kernel(
    begin_ref, q_ref, k_ref, v_ref, rank_ref, table_ref, out_ref, lse_ref, grad_ref,
    cos_ref, sin_ref, dq_ref, dk_ref, dv_ref, dk_sum, dv_sum, *, scaling
):
    block = pl.program_id(1)
    cap, width = out_ref.shape
    tile_rows = q_ref.shape[0]
    pick, low_bound, high_bound, _ = slots_of_block(rank_ref, table_ref, cap)
    q = dot(pick, q_ref[...]).astype(BF16)
    grad = grad_ref[...]
    delta = jnp.sum(grad.astype(F32) * out_ref[...].astype(F32), axis=1, keepdims=True)
    lse = lse_ref[0]

    @pl.when(block == 0)
    def _():
        dk_sum[...] = jnp.zeros_like(dk_sum)
        dv_sum[...] = jnp.zeros_like(dv_sum)

    def step(tile, dq):
        rows, keys, scores, allowed = attention_scores(
            q, k_ref, low_bound, high_bound, tile, tile_rows, scaling
        )
        chances = jnp.where(allowed, jnp.exp(scores - lse), 0.0)
        dv_sum[rows, :] += contract_first(chances.astype(BF16), grad)
        grad_chances = contract_last(grad, v_ref[rows, :])
        grad_scores = (chances * (grad_chances - delta)).astype(BF16)
        dk_sum[rows, :] += contract_first(grad_scores, q) * scaling
        return dq + dot(grad_scores, keys)

    dq = lax.fori_loop(begin_ref[block], block + 1, step, jnp.zeros((cap, width), F32)) * scaling
    high = dq.astype(BF16)
    rest = (dq - high.astype(F32)).astype(BF16)
    dq_tokens = contract_first(pick, high) + contract_first(pick, rest)
    own = pl.ds(pl.multiple_of(block * tile_rows, tile_rows), tile_rows)
    dq_ref[...] = turned(dq_tokens, cos_ref[own, :], -sin_ref[own, :]).astype(BF16)

    @pl.when(block == BLOCKS - 1)
    def _():
        def finish(tile, nothing):
            rows = pl.ds(pl.multiple_of(tile * tile_rows, tile_rows), tile_rows)
            dk_ref[rows, :] = turned(dk_sum[rows, :], cos_ref[rows, :], -sin_ref[rows, :]).astype(BF16)
            dv_ref[rows, :] = dv_sum[rows, :].astype(BF16)
            return nothing

        lax.fori_loop(0, BLOCKS, finish, 0)


def attention_specs(row_count, token_count, width):
    return dict(
        q=pl.BlockSpec((row_count, width), lambda h, b, s: (b, h)),
        k=pl.BlockSpec((token_count, width), lambda h, b, s: (0, h)),
        rank=pl.BlockSpec((1, 1, row_count), lambda h, b, s: (b, 0, 0)),
        rows=pl.BlockSpec((16, row_count), lambda h, b, s: (0, b)),
        gate=pl.BlockSpec((CAP, 1), lambda h, b, s: (b, 0)),
        slots=pl.BlockSpec((CAP, width), lambda h, b, s: (b, h)),
        table=pl.BlockSpec((token_count, width), lambda h, b, s: (0, 0)),
        lse=pl.BlockSpec((1, CAP, 1), lambda h, b, s: (h, b, 0)),
    )


def attention_forward(begin, q, k, v, rank, table, width):
    token_count, heads = q.shape[0], q.shape[1] // width
    row_count = token_count // BLOCKS
    s = attention_specs(row_count, token_count, width)
    return pl.pallas_call(
        functools.partial(attention_forward_kernel, scaling=1.0 / math.sqrt(width)),
        grid_spec=pltpu.PrefetchScalarGridSpec(
            num_scalar_prefetch=1,
            grid=(heads, BLOCKS),
            in_specs=[s["q"], s["k"], s["k"], s["rank"], s["rows"]],
            out_specs=[s["slots"], s["slots"], s["gate"], s["lse"]],
        ),
        out_shape=[
            jax.ShapeDtypeStruct((BLOCKS * CAP, heads * width), BF16),
            jax.ShapeDtypeStruct((BLOCKS * CAP, heads * width), BF16),
            jax.ShapeDtypeStruct((BLOCKS * CAP, 1), F32),
            jax.ShapeDtypeStruct((heads, BLOCKS * CAP, 1), F32),
        ],
        compiler_params=pltpu.CompilerParams(vmem_limit_bytes=VMEM_BYTES),
        name="attention_forward",
    )(begin, q, k, v, rank, table)


def attention_backward(begin, q, k, v, rank, table, out, lse, grad, cosine, sine, width):
    token_count, heads = q.shape[0], q.shape[1] // width
    row_count = token_count // BLOCKS
    s = attention_specs(row_count, token_count, width)
    return pl.pallas_call(
        functools.partial(attention_backward_kernel, scaling=1.0 / math.sqrt(width)),
        grid_spec=pltpu.PrefetchScalarGridSpec(
            num_scalar_prefetch=1,
            grid=(heads, BLOCKS),
            in_specs=[
                s["q"], s["k"], s["k"], s["rank"], s["rows"],
                s["slots"], s["lse"], s["slots"], s["table"], s["table"],
            ],
            out_specs=[s["q"], s["k"], s["k"]],
            scratch_shapes=[pltpu.VMEM((token_count, width), F32)] * 2,
        ),
        out_shape=[
            jax.ShapeDtypeStruct((token_count, heads * width), BF16),
            jax.ShapeDtypeStruct((token_count, heads * width), BF16),
            jax.ShapeDtypeStruct((token_count, heads * width), BF16),
        ],
        compiler_params=pltpu.CompilerParams(vmem_limit_bytes=VMEM_BYTES),
        name="attention_backward",
    )(begin, q, k, v, rank, table, out, lse, grad, cosine, sine)


def pack_up_kernel(weight_ref, pieces_ref):
    units = pieces_ref.shape[2] // 2
    both = weight_ref[0].astype(F32)
    gate, up = both[:, 0, :], both[:, 1, :]
    for half in range(HALVES):
        at = slice(half * units, (half + 1) * units)
        pieces_ref[half] = jnp.concatenate([gate[:, at], up[:, at]], axis=1).astype(BF16)


def pack_up(weight):
    experts, own_rows, _, units = weight.shape
    tile = own_rows // 2
    return pl.pallas_call(
        pack_up_kernel,
        grid=(experts, 2),
        in_specs=[pl.BlockSpec((1, tile, 2, units), lambda e, r: (e, r, 0, 0))],
        out_specs=pl.BlockSpec((HALVES, tile, units), lambda e, r: (e, r, 0)),
        out_shape=jax.ShapeDtypeStruct((experts * HALVES, own_rows, units), BF16),
        compiler_params=pltpu.CompilerParams(vmem_limit_bytes=VMEM_BYTES),
        name="pack_up",
    )(weight)


def pack_down_kernel(weight_ref, first_ref, last_ref):
    turned_rows = weight_ref[0].astype(F32).T.astype(BF16)
    middle = first_ref.shape[1]
    first_ref[0] = turned_rows[:middle]
    last_ref[0] = turned_rows[middle:]


def pack_down(weight):
    places, units, own_rows = weight.shape
    half = (places, own_rows // 2, units)
    return pl.pallas_call(
        pack_down_kernel,
        grid=(places,),
        in_specs=[pl.BlockSpec((1, units, own_rows), lambda p: (p, 0, 0))],
        out_specs=[pl.BlockSpec((1,) + half[1:], lambda p: (p, 0, 0))] * 2,
        out_shape=[jax.ShapeDtypeStruct(half, BF16)] * 2,
        compiler_params=pltpu.CompilerParams(vmem_limit_bytes=VMEM_BYTES),
        name="pack_down",
    )(weight)


def row_major(array):
    return with_layout_constraint(array, Layout(major_to_minor=tuple(range(array.ndim))))


def exchanged(pieces):
    return row_major(lax.all_to_all(row_major(pieces), PLACES, 0, 0, tiled=True))


def over_groups(landed):
    return lax.all_gather(landed, "t", axis=0, tiled=False)


def group_sums(pieces):
    return lax.psum_scatter(pieces, "t", scatter_dimension=0, tiled=False)


def return_gradients(pieces):
    return exchanged(group_sums(pieces))


def other_core(column):
    return column + 1 - 2 * (column % 2)


def crossed(plane, j):
    return (plane, plane + 1 - 2 * (plane % 2), (plane + 2) % 4, 3 - plane)[j]


def meet(peers):
    barrier = pltpu.get_barrier_semaphore()
    for peer in peers:
        pl.semaphore_signal(barrier, inc=1, device_id=peer, device_id_type=MESH)
    pl.semaphore_wait(barrier, len(peers))


def partners():
    plane, half, column = lax.axis_index("z"), lax.axis_index("x"), lax.axis_index("grid")
    planes = [{"z": crossed(plane, j)} for j in range(PLANES)]
    along_x, along_y = {"x": 1 - half}, {"grid": (column + 2) % 4}
    core = {"grid": other_core(column)}
    return plane, half, column, planes, along_x, along_y, core


class Moves:
    def __init__(self, send, recv):
        self.send, self.recv, self.made = send, recv, {}

    def add(self, index, source, target, peer):
        self.made[index] = (source, target, peer)

    def copy(self, index, source, target, peer):
        return pltpu.make_async_remote_copy(
            src_ref=source, dst_ref=target, send_sem=self.send.at[index],
            recv_sem=self.recv.at[index], device_id=peer, device_id_type=MESH,
        )

    def start(self, index):
        self.copy(index, *self.made[index]).start()

    def arrived(self, index, target, peer):
        self.copy(index, target, target, peer).wait_recv()

    def all_sent(self):
        for index in self.made:
            self.copy(index, *self.made[index]).wait_send()


class Ride:
    def __init__(self, pieces_ref, landed_ref, send, recv, local, columns=None):
        if columns is None:
            columns = pl.ds(0, pieces_ref.shape[2])
        rows = pl.ds(0, pieces_ref.shape[1])
        plane, half = lax.axis_index("z"), lax.axis_index("x")
        self.moves = Moves(send, recv)
        self.landings = {}
        own = plane * HALVES + half
        self.keep = pltpu.make_async_copy(pieces_ref.at[own], landed_ref.at[own], local)
        self.peers = []
        for dz in range(PLANES):
            for dx in range(HALVES):
                index = dz * HALVES + dx
                if index == 0:
                    continue
                at_half = 1 - half if dx else half
                peer = {"z": crossed(plane, dz), "x": at_half}
                other = crossed(plane, dz) * HALVES + at_half
                source = pieces_ref.at[other, rows, columns]
                self.moves.add(index, source, landed_ref.at[own, rows, columns], peer)
                self.landings[index] = (landed_ref.at[other, rows, columns], peer)
                if dz and dx:
                    self.peers.append(peer)

    def begin(self):
        self.keep.start()
        for index in (4, 6, 2):
            self.moves.start(index)

    def go_on(self, number):
        for index in ((5,), (7,), (3,), (1,))[number : number + 1]:
            self.moves.start(index[0])

    def finish(self):
        for index, (landing, peer) in self.landings.items():
            self.moves.arrived(index, landing, peer)
        self.moves.all_sent()
        self.keep.wait()


RIDE_SCRATCH = (
    pltpu.SemaphoreType.DMA((8,)),
    pltpu.SemaphoreType.DMA((8,)),
    pltpu.SemaphoreType.DMA,
)


def run_with_ride(steps, ride):
    steps[0]()
    if ride is not None:
        ride.begin()
    for number, step in enumerate(steps[1:-1]):
        step()
        if ride is not None:
            ride.go_on(number)
    steps[-1]()
    if ride is not None:
        ride.finish()


def gather_parts(slots_ref, out_ref, send, recv, local, same, share=2, more=(), chain=None):
    plane, half, column, planes, along_x, along_y, core = partners()
    cap, width = slots_ref.shape[-2:]
    middle = cap * share // 64 * 16
    y_column, core_column = (column + 2) % 4, other_core(column)
    core_y = (core_column + 2) % 4
    sources = [crossed(plane, j) for j in range(PLANES)]
    moves = Moves(send, recv)

    def piece(source, at_half, at_column, first=0, count=cap):
        columns = pl.ds(pl.multiple_of(at_column * width, width), width)
        return out_ref.at[source, at_half, pl.ds(first, count), columns]

    def slots_for(j):
        return slots_ref if same else slots_ref.at[sources[j]]

    keep = pltpu.make_async_copy(slots_for(0), piece(plane, half, column), local)
    for j in range(PLANES):
        source = sources[j]
        place = piece(source, half, column)
        if j and chain is None:
            moves.add(j, slots_for(j), piece(plane, half, column), planes[j])
        here = place if j else slots_for(0)
        moves.add(4 + j, here, place, along_x)
        moves.add(8 + j, here, place, along_y)
        moves.add(12 + j, here, place, core)
        from_x, from_y = piece(source, 1 - half, column), piece(source, half, y_column)
        first = piece(source, 1 - half, column, 0, middle)
        last = piece(source, half, y_column, middle, cap - middle)
        diagonal = piece(source, 1 - half, y_column)
        moves.add(16 + j, first, first, along_y)
        moves.add(20 + j, from_x, from_x, core)
        moves.add(24 + j, last, last, along_x)
        moves.add(28 + j, from_y, from_y, core)
        moves.add(32 + j, diagonal, diagonal, core)

    def begin():
        meet(planes[1:] + [along_x, along_y, core] + list(more))
        if chain is None:
            for j in (1, 3, 2):
                moves.start(j)
        else:
            chain.begin()
        keep.start()

    def spread(j):
        if j and chain is None:
            moves.arrived(j, piece(sources[j], half, column), planes[j])
        elif j:
            chain.arrived(j)
        for index in (4, 8, 12):
            moves.start(index + j)

    def forward(j):
        moves.arrived(4 + j, piece(sources[j], 1 - half, column), along_x)
        moves.start(16 + j)
        moves.start(20 + j)
        moves.arrived(8 + j, piece(sources[j], half, y_column), along_y)
        moves.start(24 + j)
        moves.start(28 + j)

    def cross(j):
        moves.arrived(16 + j, piece(sources[j], 1 - half, y_column, 0, middle), along_y)
        moves.arrived(24 + j, piece(sources[j], 1 - half, y_column, middle, cap - middle), along_x)
        moves.start(32 + j)

    def finish():
        for j in order:
            moves.arrived(12 + j, piece(sources[j], half, core_column), core)
            moves.arrived(20 + j, piece(sources[j], 1 - half, core_column), core)
            moves.arrived(28 + j, piece(sources[j], half, core_y), core)
            moves.arrived(32 + j, piece(sources[j], 1 - half, core_y), core)
        moves.all_sent()
        keep.wait()

    order = (0, 1, 3, 2)
    return begin, spread, forward, cross, finish, order


def gather_steps(*refs, **settings):
    begin, spread, forward, cross, finish, order = gather_parts(*refs, **settings)

    def step(number):
        if number < len(order):
            spread(order[number])
        if 0 <= number - 1 < len(order):
            forward(order[number - 1])
        if 0 <= number - 2 < len(order):
            cross(order[number - 2])

    return [begin] + [functools.partial(step, number) for number in range(len(order) + 2)] + [finish]


class Chain:
    def __init__(self, view, source, send, recv):
        plane = lax.axis_index("z")
        self.inner = (plane == 1) | (plane == 2)
        near, far = {"z": crossed(plane, 1)}, {"z": crossed(plane, 3)}
        self.views = [view(crossed(plane, j)) for j in range(PLANES)]
        self.send, self.recv = send, recv
        self.near_own = (0, 1, source, self.views[0], near)
        self.far_own = (1, 3, source, self.views[0], far)
        self.on_arrival = {
            1: (2, 2, self.views[1], self.views[1], far),
            3: (3, 2, self.views[3], self.views[3], near),
            2: (4, 3, self.views[2], self.views[2], near),
        }

    def copy(self, at_send, at_recv, source, target, peer):
        return pltpu.make_async_remote_copy(
            src_ref=source, dst_ref=target, send_sem=self.send.at[at_send],
            recv_sem=self.recv.at[at_recv], device_id=peer, device_id_type=MESH,
        )

    def begin(self):
        self.copy(*self.near_own).start()

        @pl.when(self.inner)
        def _():
            self.copy(*self.far_own).start()

    def arrived(self, j):
        place = self.views[j]
        self.copy(0, j, place, place, self.near_own[-1]).wait_recv()

        @pl.when(self.inner)
        def _():
            self.copy(*self.on_arrival[j]).start()

    def finish(self):
        self.copy(*self.near_own).wait_send()

        @pl.when(self.inner)
        def _():
            self.copy(*self.far_own).wait_send()
            for made in self.on_arrival.values():
                self.copy(*made).wait_send()


CHAIN_SCRATCH = (pltpu.SemaphoreType.DMA((5,)), pltpu.SemaphoreType.DMA((4,)))


def opening_kernel(
    tokens_ref, pieces_ref, out_ref, landed_ref, send, recv, local, ride_send, ride_recv,
    ride_local, hop_send, hop_recv, *chain_sems, share
):
    plane, half, column = lax.axis_index("z"), lax.axis_index("x"), lax.axis_index("grid")
    width = tokens_ref.shape[1]
    middle = pieces_ref.shape[2] // 2
    left, right = pl.ds(0, middle), pl.ds(middle, middle)
    rows = pl.ds(0, pieces_ref.shape[1])
    along_x = {"x": 1 - half}

    def tokens_of(source):
        columns = pl.ds(pl.multiple_of(column * width, width), width)
        return out_ref.at[source, half, pl.ds(0, tokens_ref.shape[0]), columns]

    def shared_of(at_half):
        return lambda source: landed_ref.at[source * HALVES + at_half, rows, right]

    own = plane * HALVES + half
    tokens = Chain(tokens_of, tokens_ref, *chain_sems[:2])
    here = Chain(shared_of(half), pieces_ref.at[own, rows, right], *chain_sems[2:4])
    there = Chain(shared_of(1 - half), shared_of(1 - half)(plane), *chain_sems[4:])
    ride = Ride(pieces_ref, landed_ref, ride_send, ride_recv, ride_local, left)
    hop = pltpu.make_async_remote_copy(
        src_ref=pieces_ref.at[plane * HALVES + 1 - half, rows, right],
        dst_ref=landed_ref.at[own, rows, right],
        send_sem=hop_send, recv_sem=hop_recv, device_id=along_x, device_id_type=MESH,
    )
    landing = shared_of(1 - half)(plane)
    hop_here = pltpu.make_async_remote_copy(
        src_ref=landing, dst_ref=landing, send_sem=hop_send, recv_sem=hop_recv,
        device_id=along_x, device_id_type=MESH,
    )
    begin, spread, forward, cross, finish, _ = gather_parts(
        tokens_ref, out_ref, send, recv, local, True, share, ride.peers, tokens
    )
    begin()
    ride.keep.start()
    spread(0)
    hop.start()
    here.begin()
    spread(1)
    forward(0)
    ride.moves.start(2)
    spread(3)
    forward(1)
    cross(0)
    hop_here.wait_recv()
    there.begin()
    here.arrived(1)
    spread(2)
    forward(3)
    cross(1)
    ride.moves.start(6)
    ride.moves.start(4)
    here.arrived(3)
    there.arrived(1)
    forward(2)
    cross(3)
    for index in (3, 7, 5, 1):
        ride.moves.start(index)
    here.arrived(2)
    there.arrived(3)
    cross(2)
    there.arrived(2)
    finish()
    ride.finish()
    hop.wait_send()
    for chain in (tokens, here, there):
        chain.finish()


def opened(tokens, pieces, collective_id, share):
    rows, width = tokens.shape
    anywhere = pl.BlockSpec(memory_space=pl.ANY)
    return pl.pallas_call(
        functools.partial(opening_kernel, share=share),
        out_shape=[
            jax.ShapeDtypeStruct((PLANES, HALVES, rows, 4 * width), BF16),
            jax.ShapeDtypeStruct(pieces.shape, BF16),
        ],
        in_specs=[anywhere] * 2,
        out_specs=[anywhere] * 2,
        scratch_shapes=list(GATHER_SCRATCH) + list(RIDE_SCRATCH)
        + [pltpu.SemaphoreType.DMA, pltpu.SemaphoreType.DMA] + list(CHAIN_SCRATCH) * 3,
        compiler_params=pltpu.CompilerParams(collective_id=collective_id, has_side_effects=True),
        name="open_rows",
    )(tokens, pieces)


GATHER_SCRATCH = (
    pltpu.SemaphoreType.DMA((36,)),
    pltpu.SemaphoreType.DMA((36,)),
    pltpu.SemaphoreType.DMA,
)


def gather_kernel(*refs, same, share, rides):
    if rides:
        slots_ref, pieces_ref, out_ref, landed_ref = refs[:4]
        ride = Ride(pieces_ref, landed_ref, *refs[7:])
        scratch = refs[4:7]
    else:
        slots_ref, out_ref = refs[:2]
        ride, scratch = None, refs[2:]
    more = ride.peers if rides else ()
    run_with_ride(gather_steps(slots_ref, out_ref, *scratch, same, share, more), ride)


def gathered(slots, collective_id, ride=None, share=2):
    rows, width = slots.shape[-2:]
    rides = () if ride is None else (ride,)
    anywhere = pl.BlockSpec(memory_space=pl.ANY)
    out = pl.pallas_call(
        functools.partial(gather_kernel, same=slots.ndim == 2, share=share, rides=len(rides)),
        out_shape=[jax.ShapeDtypeStruct((PLANES, HALVES, rows, 4 * width), BF16)]
        + [jax.ShapeDtypeStruct(r.shape, BF16) for r in rides],
        in_specs=[anywhere] * (1 + len(rides)),
        out_specs=[anywhere] * (1 + len(rides)),
        scratch_shapes=list(GATHER_SCRATCH) + list(RIDE_SCRATCH) * len(rides),
        compiler_params=pltpu.CompilerParams(collective_id=collective_id, has_side_effects=True),
        name="gather_rows",
    )(slots, *rides)
    return out if rides else out[0]


def scatter_steps(
    partial_ref, out_ref, own, other, crossing, side, send, recv, load, share=2, more=()
):
    plane, half, column, planes, along_x, along_y, core = partners()
    cap, width = out_ref.shape[-2:]
    middle = cap * share // 64 * 16
    chunk = 32 if middle % 32 == 0 and cap % 32 == 0 else 16
    y_column, core_column = (column + 2) % 4, other_core(column)
    core_y = (core_column + 2) % 4
    halves = (half, 1 - half, half, 1 - half)
    own_columns = (column, column, y_column, y_column)
    core_columns = (core_column, core_column, core_y, core_y)
    moves = Moves(send, recv)
    first, last = pl.ds(0, middle), pl.ds(middle, cap - middle)

    def part(j, q, at_columns):
        columns = pl.ds(pl.multiple_of(at_columns[q] * width, width), width)
        return partial_ref.at[crossed(plane, j), halves[q], :, columns]

    def loading(j, q):
        return pltpu.make_async_copy(part(j, q, own_columns), own.at[j, q], load.at[4 * j + q])

    keep = pltpu.make_async_copy(own.at[0, 0], out_ref.at[plane], load.at[16])
    for j in range(PLANES):
        for q in range(4):
            moves.add(4 * j + q, part(j, q, core_columns), other.at[j, q], core)
        moves.add(16 + j, own.at[j, 3, first], crossing.at[j, first], along_x)
        moves.add(20 + j, own.at[j, 3, last], crossing.at[j, last], along_y)
        moves.add(24 + j, own.at[j, 2], side.at[j, 1], along_y)
        moves.add(28 + j, own.at[j, 1], side.at[j, 0], along_x)
        if j:
            moves.add(32 + j, own.at[j, 0], out_ref.at[plane], planes[j])

    def add(j, q, begin_row, count, terms):
        def step(i, nothing):
            rows = pl.ds(pl.multiple_of(begin_row + i * chunk, chunk), chunk)
            total = own[j, q, rows, :].astype(F32)
            for ref, index in terms:
                total = total + ref[index + (rows, slice(None))].astype(F32)
            own[j, q, rows, :] = total.astype(BF16)
            return nothing

        lax.fori_loop(0, count // chunk, step, 0)

    def chip_sum(j, q):
        moves.arrived(4 * j + q, other.at[j, q], core)
        loading(j, q).wait()
        add(j, q, 0, cap, [(other, (j, q))])

    def stage_one(j):
        chip_sum(j, 3)
        moves.start(16 + j)
        moves.start(20 + j)
        chip_sum(j, 2)
        chip_sum(j, 1)
        chip_sum(j, 0)

    def stage_two(j):
        moves.arrived(16 + j, crossing.at[j, first], along_x)
        add(j, 2, 0, middle, [(crossing, (j,))])
        moves.start(24 + j)
        moves.arrived(20 + j, crossing.at[j, last], along_y)
        add(j, 1, middle, cap - middle, [(crossing, (j,))])
        moves.start(28 + j)

    def stage_three(j):
        moves.arrived(24 + j, side.at[j, 1], along_y)
        moves.arrived(28 + j, side.at[j, 0], along_x)
        add(j, 0, 0, cap, [(side, (j, 0)), (side, (j, 1))])
        if j:
            moves.start(32 + j)
        else:
            keep.start()

    order = (2, 3, 1, 0)

    def begin():
        meet(planes[1:] + [along_x, along_y, core] + list(more))
        for j in order:
            for q in (3, 2, 1, 0):
                moves.start(4 * j + q)
                loading(j, q).start()

    def step(number):
        if number < len(order):
            stage_one(order[number])
        if 0 <= number - 1 < len(order):
            stage_two(order[number - 1])
        if 0 <= number - 2 < len(order):
            stage_three(order[number - 2])

    def finish():
        for j in range(1, PLANES):
            moves.arrived(32 + j, out_ref.at[crossed(plane, j)], planes[j])
        moves.all_sent()
        keep.wait()

    return [begin] + [functools.partial(step, number) for number in range(len(order) + 2)] + [finish]


def scatter_scratch(rows, width):
    return [
        pltpu.VMEM((PLANES, 4, rows, width), BF16),
        pltpu.VMEM((PLANES, 4, rows, width), BF16),
        pltpu.VMEM((PLANES, rows, width), BF16),
        pltpu.VMEM((PLANES, 2, rows, width), BF16),
        pltpu.SemaphoreType.DMA((36,)),
        pltpu.SemaphoreType.DMA((36,)),
        pltpu.SemaphoreType.DMA((17,)),
    ]


def scatter_kernel(*refs, share, rides):
    if rides:
        partial_ref, pieces_ref, out_ref, landed_ref = refs[:4]
        ride = Ride(pieces_ref, landed_ref, *refs[11:])
        scratch = refs[4:11]
    else:
        partial_ref, out_ref = refs[:2]
        ride, scratch = None, refs[2:]
    more = ride.peers if rides else ()
    run_with_ride(scatter_steps(partial_ref, out_ref, *scratch, share, more), ride)


def scattered(partial, rows, collective_id, ride=None, share=2):
    width = partial.shape[1] // 4
    rides = () if ride is None else (ride,)
    anywhere = pl.BlockSpec(memory_space=pl.ANY)
    out = pl.pallas_call(
        functools.partial(scatter_kernel, share=share, rides=len(rides)),
        out_shape=[jax.ShapeDtypeStruct((PLANES, rows, width), BF16)]
        + [jax.ShapeDtypeStruct(r.shape, BF16) for r in rides],
        in_specs=[anywhere] * (1 + len(rides)),
        out_specs=[anywhere] * (1 + len(rides)),
        scratch_shapes=scatter_scratch(rows, width) + list(RIDE_SCRATCH) * len(rides),
        compiler_params=pltpu.CompilerParams(
            collective_id=collective_id, has_side_effects=True, vmem_limit_bytes=VMEM_BYTES
        ),
        name="scatter_rows",
    )(partial.reshape(PLANES, HALVES, rows, 4 * width), *rides)
    return out if rides else out[0]


def carry(before, after, places, compute):
    number = pl.program_id(0)

    @pl.when(number == 0)
    def _():
        for step in before:
            step()

    compute()
    for at in sorted(set(places)):

        @pl.when(number == at)
        def _(at=at):
            for place, step in zip(places, after):
                if place == at:
                    step()


def expert_forward_kernel(
    rows_ref, up_weight_ref, down_weight_ref, small_ref, rank_ref, member_ref, grad_ref,
    gate_ref, up_ref, result_ref, share_ref, grad_rows_ref, *scratch
):
    steps = gather_steps(grad_ref, grad_rows_ref, *scratch, False)
    units = gate_ref.shape[1]

    def compute():
        rows = rows_ref[0]
        made = dot(rows, up_weight_ref[...])
        gate, up = made[:, :units], made[:, units:]
        gate_ref[...] = gate
        up_ref[...] = up
        inner = (gate * jax.nn.sigmoid(gate) * up).astype(BF16)
        result_ref[0] = contract_last(inner, down_weight_ref[...]).astype(BF16)
        cap, count = rows.shape[0], rank_ref.shape[2]
        pick = (lax.broadcasted_iota(jnp.int32, (cap, count), 0) == rank_ref[0]).astype(BF16)
        member = contract_last(pick, member_ref[...]) > 0.5
        logits = jnp.where(member, contract_last(rows, small_ref[...]), NEGATIVE)
        largest = jnp.max(logits, axis=1, keepdims=True)
        weights = jnp.where(member, jnp.exp(logits - largest), 0.0)
        mine = lax.broadcasted_iota(jnp.int32, weights.shape, 1) == 6 + lax.axis_index("z")
        total = jnp.sum(weights, axis=1, keepdims=True)
        own = jnp.sum(jnp.where(mine, weights, 0.0), axis=1, keepdims=True)
        share_ref[...] = own / jnp.where(total > 0.0, total, 1.0)

    carry(steps[:2], steps[2:], (1, 3, 5, 6, 7, 7), compute)


def once(shape):
    return pl.BlockSpec(shape, lambda b: (0,) * len(shape), pipeline_mode=pl.Buffered(1))


def expert_forward(rows, up_weight, down_weight, small, rank, member, grad_slots, collective_id):
    _, cap, width = rows.shape
    units = down_weight.shape[1]
    count = BLOCKS * cap
    anywhere = pl.BlockSpec(memory_space=pl.ANY)
    block = lambda b: (b, 0)
    return pl.pallas_call(
        expert_forward_kernel,
        grid=(BLOCKS,),
        in_specs=[
            pl.BlockSpec((1, cap, width), lambda b: (b, 0, 0)),
            once(up_weight.shape),
            once(down_weight.shape),
            once(small.shape),
            pl.BlockSpec((1, 1, rank.shape[2]), lambda b: (b, 0, 0)),
            pl.BlockSpec((16, rank.shape[2]), lambda b: (0, b)),
            anywhere,
        ],
        out_specs=[
            pl.BlockSpec((cap, units), block),
            pl.BlockSpec((cap, units), block),
            pl.BlockSpec((1, cap, width), lambda b: (b, 0, 0)),
            pl.BlockSpec((cap, 1), block),
            anywhere,
        ],
        out_shape=[
            jax.ShapeDtypeStruct((count, units), F32),
            jax.ShapeDtypeStruct((count, units), F32),
            jax.ShapeDtypeStruct((BLOCKS, cap, width), BF16),
            jax.ShapeDtypeStruct((count, 1), F32),
            jax.ShapeDtypeStruct((PLANES, HALVES, cap, width), BF16),
        ],
        scratch_shapes=list(GATHER_SCRATCH),
        compiler_params=pltpu.CompilerParams(
            collective_id=collective_id, has_side_effects=True, vmem_limit_bytes=VMEM_BYTES
        ),
        name="expert_forward",
    )(rows, up_weight, down_weight, small, rank, member, grad_slots)


def expert_backward_kernel(
    gate_ref, up_ref, grad_ref, share_ref, up_weight_ref, down_weight_ref, result_ref,
    grad_rows_ref, grad_gate_up_ref, inner_ref, out_ref, *scratch
):
    steps = scatter_steps(result_ref, out_ref, *scratch)

    def compute():
        share = share_ref[...]
        grad_inner = dot(grad_ref[0], down_weight_ref[...]) * share
        gate, up = gate_ref[...], up_ref[...]
        sigmoid = jax.nn.sigmoid(gate)
        silu = gate * sigmoid
        inner_ref[...] = (share * silu * up).astype(BF16)
        grad_gate = grad_inner * up * sigmoid * (1.0 + gate * (1.0 - sigmoid))
        grad_gate_up = jnp.concatenate([grad_gate, grad_inner * silu], axis=1).astype(BF16)
        grad_gate_up_ref[...] = grad_gate_up
        grad_rows_ref[0] = contract_last(grad_gate_up, up_weight_ref[...]).astype(BF16)

    carry(steps[:1], steps[1:], (0, 1, 3, 4, 6, 7, 7), compute)


def expert_backward(
    gate, up, grad_rows, share, up_weight, down_weight, result, collective_id
):
    _, cap, width = grad_rows.shape
    count, units = gate.shape
    anywhere = pl.BlockSpec(memory_space=pl.ANY)
    block = lambda b: (b, 0)
    rows = pl.BlockSpec((1, cap, width), lambda b: (b, 0, 0))
    return pl.pallas_call(
        expert_backward_kernel,
        grid=(BLOCKS,),
        in_specs=[
            pl.BlockSpec((cap, units), block),
            pl.BlockSpec((cap, units), block),
            rows,
            pl.BlockSpec((cap, 1), block),
            once(up_weight.shape),
            once(down_weight.shape),
            anywhere,
        ],
        out_specs=[
            rows,
            pl.BlockSpec((cap, 2 * units), block),
            pl.BlockSpec((cap, units), block),
            anywhere,
        ],
        out_shape=[
            jax.ShapeDtypeStruct((BLOCKS, cap, width), BF16),
            jax.ShapeDtypeStruct((count, 2 * units), BF16),
            jax.ShapeDtypeStruct((count, units), BF16),
            jax.ShapeDtypeStruct((PLANES, cap, width // 4), BF16),
        ],
        scratch_shapes=scatter_scratch(cap, width // 4),
        compiler_params=pltpu.CompilerParams(
            collective_id=collective_id, has_side_effects=True, vmem_limit_bytes=VMEM_BYTES
        ),
        name="expert_backward",
    )(gate, up, grad_rows, share, up_weight, down_weight, result.reshape(PLANES, HALVES, cap, width))


def expert_gradient_kernel(
    rows_ref, grad_ref, grad_gate_up_ref, inner_ref, partial_ref,
    up_grad_ref, down_first_ref, down_last_ref, out_ref, *scratch
):
    steps = scatter_steps(partial_ref, out_ref, *scratch)
    middle = down_first_ref.shape[1]

    def compute():
        up_grad_ref[...] = contract_first(rows_ref[...], grad_gate_up_ref[...]).astype(BF16)
        down_grad = contract_first(grad_ref[...], inner_ref[...]).astype(BF16)
        down_first_ref[0] = down_grad[:middle]
        down_last_ref[0] = down_grad[middle:]

    carry(steps[:1], steps[1:], (0, 2, 4, 5, 6, 7, 7), compute)


def expert_gradient(rows, grad_rows, grad_gate_up, inner, partial, collective_id):
    count, width = rows.shape
    units = inner.shape[1]
    cap, tile = count // BLOCKS, width // BLOCKS
    anywhere = pl.BlockSpec(memory_space=pl.ANY)
    columns = pl.BlockSpec((count, tile), lambda b: (0, b))
    return pl.pallas_call(
        expert_gradient_kernel,
        grid=(BLOCKS,),
        in_specs=[columns, columns, once((count, 2 * units)), once((count, units)), anywhere],
        out_specs=[
            pl.BlockSpec((tile, 2 * units), lambda b: (b, 0)),
            pl.BlockSpec((1, tile // 2, units), lambda b: (b, 0, 0)),
            pl.BlockSpec((1, tile // 2, units), lambda b: (b, 0, 0)),
            anywhere,
        ],
        out_shape=[
            jax.ShapeDtypeStruct((width, 2 * units), BF16),
            jax.ShapeDtypeStruct((BLOCKS, tile // 2, units), BF16),
            jax.ShapeDtypeStruct((BLOCKS, tile // 2, units), BF16),
            jax.ShapeDtypeStruct((PLANES, cap, width // 4), BF16),
        ],
        scratch_shapes=scatter_scratch(cap, width // 4),
        compiler_params=pltpu.CompilerParams(
            collective_id=collective_id, has_side_effects=True, vmem_limit_bytes=VMEM_BYTES
        ),
        name="expert_gradient",
    )(rows, grad_rows, grad_gate_up, inner, partial.reshape(PLANES, HALVES, cap, width))


def grid_sum(values):
    shape = values.shape
    return lax.all_gather(values.reshape(-1, 128), "grid", axis=0).sum(axis=0).reshape(shape)


def closing_kernel(
    hidden_ref, q_ref, k_ref, v_ref, rows_ref, gated_ref, partial_ref, pieces_ref,
    grad_ref, out_ref, landed_ref, *scratch
):
    ride = Ride(pieces_ref, landed_ref, *scratch[7:])
    steps = scatter_steps(partial_ref, out_ref, *scratch[:7], 1, ride.peers)
    span = q_ref.shape[1]

    def compute():
        hidden = hidden_ref[...]
        for place, ref in enumerate((q_ref, k_ref, v_ref)):
            at = slice(place * span, (place + 1) * span)
            grad_ref[:, at] = contract_first(hidden, ref[...]).astype(BF16)
        grad_ref[:, 3 * span :] = contract_first(rows_ref[...], gated_ref[...]).astype(BF16)

    def with_ride(number):
        steps[1 + number]()
        ride.go_on(number)

    after = [functools.partial(with_ride, number) for number in range(6)]
    carry([steps[0], ride.begin], after + [steps[-1], ride.finish], (1, 4, 7, 7, 7, 7, 7, 7), compute)


def closing(hidden, q, k, v, rows, gated, partial, pieces, collective_id):
    count, width = hidden.shape
    slot_count, span = gated.shape
    tile, own_rows = width // BLOCKS, count // BLOCKS
    anywhere = pl.BlockSpec(memory_space=pl.ANY)
    return pl.pallas_call(
        closing_kernel,
        grid=(BLOCKS,),
        in_specs=[
            pl.BlockSpec((count, tile), lambda b: (0, b)),
            once((count, span)),
            once((count, span)),
            once((count, span)),
            pl.BlockSpec((slot_count, tile), lambda b: (0, b)),
            once((slot_count, span)),
            anywhere,
            anywhere,
        ],
        out_specs=[pl.BlockSpec((tile, 4 * span), lambda b: (b, 0)), anywhere, anywhere],
        out_shape=[
            jax.ShapeDtypeStruct((width, 4 * span), BF16),
            jax.ShapeDtypeStruct((PLANES, own_rows, width // 4), BF16),
            jax.ShapeDtypeStruct(pieces.shape, BF16),
        ],
        scratch_shapes=scatter_scratch(own_rows, width // 4) + list(RIDE_SCRATCH),
        compiler_params=pltpu.CompilerParams(
            collective_id=collective_id, has_side_effects=True, vmem_limit_bytes=VMEM_BYTES
        ),
        name="closing",
    )(hidden, q, k, v, rows, gated, partial.reshape(PLANES, HALVES, own_rows, width), pieces)


def finish_kernel(query_ref, all_ref, query_grad_ref, kv_grad_ref, out_grad_ref):
    span = query_ref.shape[2] // 4
    head_width = query_grad_ref.shape[3]
    pair = span // head_width
    own_rows = query_grad_ref.shape[1]
    for half in range(HALVES):
        landed = query_ref[half, :own_rows, :].astype(F32)
        for head in range(pair):
            at = half * pair + head
            query_grad_ref[0, :, at, :] = landed[:, head * head_width : (head + 1) * head_width]
        out_grad_ref[half] = landed[:, 3 * span :].T

    @pl.when(pl.program_id(0) == 0)
    def _():
        for half in range(HALVES):
            total = sum(
                all_ref[z * HALVES + half, :own_rows, span : 3 * span].astype(F32)
                for z in range(PLANES)
            )
            for kind in range(2):
                for head in range(pair):
                    first = kind * span + head * head_width
                    kv_grad_ref[:, half * pair + head, kind, :] = total[:, first : first + head_width]


def finish(landed, own_rows, span, heads, head_width):
    places, height, width = landed.shape
    return pl.pallas_call(
        finish_kernel,
        grid=(PLANES,),
        in_specs=[
            pl.BlockSpec((HALVES, height, width), lambda e: (e, 0, 0)),
            pl.BlockSpec((places, height, width), lambda e: (0, 0, 0)),
        ],
        out_specs=[
            pl.BlockSpec((1, own_rows, heads, head_width), lambda e: (e, 0, 0, 0)),
            pl.BlockSpec((own_rows, heads, 2, head_width), lambda e: (0, 0, 0, 0)),
            pl.BlockSpec((HALVES, span, own_rows), lambda e: (e, 0, 0)),
        ],
        out_shape=[
            jax.ShapeDtypeStruct((PLANES, own_rows, heads, head_width), F32),
            jax.ShapeDtypeStruct((own_rows, heads, 2, head_width), F32),
            jax.ShapeDtypeStruct((places, span, own_rows), F32),
        ],
        compiler_params=pltpu.CompilerParams(vmem_limit_bytes=VMEM_BYTES),
        name="attention_weight_gradients",
    )(landed, landed)


def prefix_ranks(member):
    counted = member.astype(BF16)
    width = member.shape[-1]
    before = jnp.arange(width)[:, None] < jnp.arange(width)[None, :]
    return jnp.where(member, dot(counted, before.astype(BF16)).astype(jnp.int32), -1)


def picks(rank):
    return (jnp.arange(CAP, dtype=jnp.int32)[:, None] == rank[..., None, :]).astype(BF16)


def members(first, second):
    names = jnp.arange(PLANES, dtype=first.dtype).reshape((PLANES,) + (1,) * first.ndim)
    return (first[None] == names) | (second[None] == names)


def route_gates(logits, member):
    shown = jnp.where(member, logits, NEGATIVE)
    weights = jnp.where(member, jnp.exp(shown - jnp.max(shown, axis=0, keepdims=True)), 0.0)
    return weights / jnp.sum(weights, axis=0, keepdims=True)


def logits_grad(gates, grad_gates):
    return gates * (grad_gates - jnp.sum(gates * grad_gates, axis=0, keepdims=True))


def exact_first(left, right):
    return lax.dot_general(
        left, right, (((0,), (0,)), ((), ())), precision=lax.Precision.HIGHEST
    )


def exact_last(left, right):
    return lax.dot_general(
        left, right, (((1,), (1,)), ((), ())), precision=lax.Precision.HIGHEST
    )


def norm_sums(grad_hidden, scaled, router, grad_gates, width, gates=None, hidden=None, member=None):
    parts = [
        grad_gates,
        exact_last(router.astype(F32), scaled),
        jnp.sum(grad_hidden * scaled, axis=1)[None],
    ]
    if gates is None:
        parts.append(contract_last(router, hidden))
    parts = grid_sum(jnp.concatenate(parts, axis=0))
    if gates is None:
        gates = route_gates(parts[2 * PLANES + 1 :], member)
    grad_logits = logits_grad(gates, parts[:PLANES])
    inner = parts[2 * PLANES] + jnp.sum(grad_logits * parts[PLANES : 2 * PLANES], axis=0)
    return grad_logits, inner[:, None] / width, gates


def per_device(
    tokens, segment_ids, attention_routes, expert_routes, attention_gain, attention_kv,
    attention_query, attention_out, attention_router, feedforward_gain, feedforward_router,
    expert_gate_up, expert_down, output_grad,
):
    groups = lax.axis_size("t")
    grid_count = lax.axis_size("grid")
    group = lax.axis_index("t")
    plane = lax.axis_index("z")
    place = plane * HALVES + lax.axis_index("x")
    column = lax.axis_index("grid")
    rows, features = tokens.shape
    width_all = features * grid_count
    token_count = BLOCKS * rows
    own_rows = attention_gain.shape[0]
    head_width = attention_kv.shape[3]
    head_pair = attention_kv.shape[1] // HALVES
    span = head_pair * head_width
    hidden_units = expert_gate_up.shape[3] // HALVES

    def mine(array, axis=0):
        return lax.dynamic_slice_in_dim(array, column * features, features, axis)

    def own(array, axis=0):
        return lax.dynamic_slice_in_dim(array, place * rows, rows, axis)

    query_pieces = attention_query.reshape(PLANES, own_rows, HALVES, span).transpose(0, 2, 1, 3)
    kv_pieces = attention_kv.reshape(own_rows, HALVES, head_pair, 2, head_width)
    kv_pieces = kv_pieces.transpose(1, 0, 3, 2, 4).reshape(1, HALVES, own_rows, 2 * span)
    kv_pieces = jnp.broadcast_to(kv_pieces, (PLANES,) + kv_pieces.shape[1:])
    qkv_pieces = jnp.concatenate([query_pieces, kv_pieces], axis=-1)
    out_pieces = attention_out.reshape(BLOCKS, span, own_rows).swapaxes(1, 2)
    first_pieces = jnp.concatenate([out_pieces, qkv_pieces.reshape(BLOCKS, own_rows, 3 * span)], axis=2)
    up_pieces = pack_up(expert_gate_up)
    down_halves = pack_down(expert_down.reshape(BLOCKS, hidden_units, own_rows))

    own_routes = jnp.concatenate([attention_routes, expert_routes], axis=1)
    small = jnp.concatenate(
        [attention_gain[:, None], feedforward_gain[:, None], attention_router, feedforward_router],
        axis=1,
    )
    small = lax.all_gather(small, "t", axis=0).reshape(-1, small.shape[1])
    small = small.T.reshape(small.shape[1], -1)
    spare = jnp.zeros((small.shape[0], features - small.shape[1] % features), BF16)
    small = jnp.concatenate([small, spare], axis=1).reshape(-1, features)
    under = jnp.concatenate([own_routes.T.astype(BF16), small], axis=0)
    under = jnp.pad(under, ((0, -under.shape[0] % 16), (0, 0)))
    everything, first_weight = opened(
        jnp.concatenate([tokens, under], axis=0), first_pieces, 0, 3
    )
    first_weight = over_groups(first_weight).reshape(width_all, 4 * span)
    out_weight, qkv_weight = first_weight[:, :span], first_weight[:, span:]
    up_pieces, everything = lax.optimization_barrier((up_pieces, everything))
    up_weight = over_groups(exchanged(up_pieces)).reshape(width_all, 2 * hidden_units)
    under = everything[:, :, rows:, :features].reshape(BLOCKS, -1, features).swapaxes(0, 1)
    small = under[4:, :, : groups * own_rows].reshape(-1, BLOCKS, groups, own_rows)
    small = jnp.pad(small.swapaxes(1, 2).reshape(-1, width_all), ((0, 4), (0, 0)))
    gain_first, gain_second = mine(small[0]).astype(F32), mine(small[1]).astype(F32)
    router_first, router_second = mine(small[2:6], 1), mine(small[6:10], 1)

    member_first, member_second = members(under[0], under[1]), members(under[2], under[3])
    own_member_first = lax.dynamic_index_in_dim(member_first, place, 1, keepdims=False)
    own_member_second = lax.dynamic_index_in_dim(member_second, place, 1, keepdims=False)
    rank = prefix_ranks(
        jnp.concatenate(
            [
                lax.dynamic_index_in_dim(member_first, plane, 0, keepdims=False),
                lax.dynamic_index_in_dim(member_second, plane, 0, keepdims=False),
                own_member_first,
                own_member_second,
            ],
            axis=0,
        )
    )
    rank_first, rank_second = rank[:BLOCKS, None], rank[BLOCKS : 2 * BLOCKS, None]
    own_pick_first = picks(rank[2 * BLOCKS : 2 * BLOCKS + PLANES])
    own_pick_second = picks(rank[2 * BLOCKS + PLANES :])
    member_first = member_first.reshape(PLANES, token_count)
    member_second = member_second.reshape(PLANES, token_count)

    def to_slots(values, pick):
        return jnp.einsum("est,tf->esf", pick, values, preferred_element_type=F32).astype(BF16)

    def to_tokens(slots, pick):
        return jnp.einsum("est,esf->etf", pick, slots, preferred_element_type=F32)

    grad_out = output_grad.astype(F32)
    cosine, sine = rope_tables(token_count, head_width)
    cosine, sine = jnp.asarray(cosine), jnp.asarray(sine)
    hidden_first, queries, keys, values, logits_first, inverse_first = project(
        everything, rows, small, first_weight, cosine, sine, span, head_width
    )
    gates_first = route_gates(logits_first[2 : 2 + PLANES], member_first)
    own_gates_first = own(gates_first, 1)
    position = jnp.arange(token_count, dtype=jnp.int32)
    segment = lax.dynamic_slice_in_dim(segment_ids, group * token_count, token_count, 0)
    opens = jnp.concatenate([jnp.ones((1,), jnp.bool_), segment[1:] != segment[:-1]])
    document_start = lax.cummax(jnp.where(opens, position, 0))
    begin = document_start.reshape(BLOCKS, rows)[:, 0] // rows
    table = token_table(
        position, document_start, lax.dynamic_index_in_dim(gates_first, plane, 0, keepdims=False)
    )
    attention_args = (begin, queries, keys, values, rank_first, table)
    attended, gated, gate_slots_first, lse = attention_forward(*attention_args, head_width)
    branch_slots, down_first = scattered(
        contract_last(attended, out_weight).astype(BF16), CAP, 2, ride=down_halves[0], share=1
    )
    branch_first = to_tokens(branch_slots, own_pick_first)
    residual = tokens.astype(F32) + jnp.sum(own_gates_first[:, :, None] * branch_first, axis=0)

    square = grid_sum(jnp.sum(residual * residual, axis=1))
    inverse_second = lax.rsqrt(square / width_all + EPSILON)[:, None]
    normed_second = residual * inverse_second
    hidden_second = (normed_second * gain_second).astype(BF16)
    slots_second, down_last = gathered(
        to_slots(hidden_second, own_pick_second), 1, ride=down_halves[1], share=3
    )
    down_weight = over_groups(jnp.concatenate([down_first, down_last], axis=1))
    down_weight = down_weight.reshape(width_all, hidden_units)
    slots_second = slots_second.reshape(BLOCKS, CAP, width_all)
    gate_pre, up_pre, result, gate_slots_second, grad_slots_second = expert_forward(
        slots_second,
        up_weight,
        down_weight,
        small,
        rank_second,
        jnp.pad(member_second.astype(BF16), ((6, 6), (0, 0))),
        to_slots(output_grad, own_pick_second),
        4,
    )
    grad_slots_second = grad_slots_second.reshape(BLOCKS, CAP, width_all)
    grad_rows, grad_gate_up, inner, result_slots = expert_backward(
        gate_pre, up_pre, grad_slots_second, gate_slots_second, up_weight, down_weight, result, 5
    )
    grad_up, grad_down_first, grad_down_last, grad_rows = expert_gradient(
        slots_second.reshape(-1, width_all), grad_slots_second.reshape(-1, width_all),
        grad_gate_up, inner, grad_rows, 6,
    )
    branch_second = to_tokens(result_slots, own_pick_second)

    grad_hidden_second = jnp.sum(to_tokens(grad_rows, own_pick_second), axis=0)
    grad_logits_second, inner_mean, own_gates_second = norm_sums(
        grad_hidden_second, normed_second * gain_second, router_second,
        jnp.sum(branch_second * grad_out[None], axis=2), width_all,
        hidden=hidden_second, member=own_member_second,
    )
    layer_output = residual + jnp.sum(own_gates_second[:, :, None] * branch_second, axis=0)
    layer_output = layer_output.astype(BF16)
    grad_hidden_second = grad_hidden_second + exact_first(
        grad_logits_second, router_second.astype(F32)
    )
    grad_router_second = exact(grad_logits_second, hidden_second.astype(F32))
    grad_gain_second = jnp.sum(grad_hidden_second * normed_second, axis=0)
    grad_normed = grad_hidden_second * gain_second
    grad_residual = grad_out + inverse_second * (grad_normed - normed_second * inner_mean)

    if groups > 1:
        grad_down = jnp.concatenate([grad_down_first, grad_down_last], axis=1)
        grad_down = group_sums(grad_down.reshape(groups, BLOCKS, own_rows, hidden_units))
        grad_down_first, grad_down_last = jnp.split(grad_down, 2, axis=1)
    grad_slots_first, grad_down_first = gathered(
        to_slots(grad_residual.astype(BF16), own_pick_first), 1, ride=grad_down_first, share=3
    )
    grad_slots_first = grad_slots_first.reshape(BLOCKS * CAP, -1)
    grad_up, grad_slots_first = lax.optimization_barrier((grad_up, grad_slots_first))
    grad_up = return_gradients(grad_up.reshape(groups, BLOCKS, own_rows, 2 * hidden_units))
    grad_attended = gate_slots_first * dot(grad_slots_first, out_weight)
    grad_attended = grad_attended.astype(BF16)
    grad_query, grad_keys, grad_values = attention_backward(
        *attention_args, attended, lse, grad_attended, cosine, sine, head_width
    )
    grad_qkv = jnp.concatenate([grad_query, grad_keys, grad_values], axis=1)
    grad_hidden = contract_last(grad_qkv, qkv_weight).astype(BF16)
    grad_first, grad_hidden, grad_down_last = closing(
        hidden_first, grad_query, grad_keys, grad_values, grad_slots_first, gated,
        grad_hidden, grad_down_last, 3,
    )
    grad_hidden = jnp.sum(grad_hidden.astype(F32), axis=0)
    grad_first, grad_up = lax.optimization_barrier((grad_first, grad_up))
    grad_first = return_gradients(grad_first.reshape(groups, BLOCKS, own_rows, 4 * span))
    expert_gate_up_grad = grad_up.reshape(PLANES, HALVES, own_rows, 2, hidden_units)
    expert_gate_up_grad = expert_gate_up_grad.transpose(0, 2, 3, 1, 4).reshape(expert_gate_up.shape)
    expert_down_grad = jnp.concatenate([grad_down_first, grad_down_last], axis=1)
    expert_down_grad = expert_down_grad.swapaxes(1, 2).reshape(expert_down.shape)

    own_normed = tokens.astype(F32) * own(inverse_first)
    own_hidden = (own_normed * gain_first).astype(BF16)
    grad_logits_first, inner_mean, _ = norm_sums(
        grad_hidden, own_normed * gain_first, router_first,
        jnp.sum(branch_first * grad_residual[None], axis=2), width_all, gates=own_gates_first,
    )
    grad_hidden_first = grad_hidden + exact_first(grad_logits_first, router_first.astype(F32))
    grad_router_first = exact(grad_logits_first, own_hidden.astype(F32))
    grad_gain_first = jnp.sum(grad_hidden_first * own_normed, axis=0)
    grad_normed = grad_hidden_first * gain_first
    input_grad = grad_residual + own(inverse_first) * (grad_normed - own_normed * inner_mean)

    small_grads = jnp.concatenate(
        [grad_gain_first[None], grad_gain_second[None], grad_router_first, grad_router_second],
        axis=0,
    )
    small_grads, grad_first = lax.optimization_barrier((small_grads, grad_first))
    small_grads = jnp.sum(lax.all_gather(small_grads, ("t",) + PLACES, axis=0), axis=0)
    small_grads = lax.all_gather(small_grads, "grid", axis=1, tiled=True)
    small_grads = lax.dynamic_slice_in_dim(
        small_grads, (group * BLOCKS + place) * own_rows, own_rows, 1
    )
    attention_query_grad, attention_kv_grad, attention_out_grad = finish(
        grad_first, own_rows, span, attention_kv.shape[1], head_width
    )
    attention_out_grad = attention_out_grad.reshape(attention_out.shape)
    return (
        layer_output,
        input_grad.astype(BF16),
        small_grads[0],
        attention_kv_grad,
        attention_query_grad.astype(F32),
        attention_out_grad.astype(F32),
        small_grads[2:6].T,
        small_grads[1],
        small_grads[6:10].T,
        expert_gate_up_grad.astype(F32),
        expert_down_grad.astype(F32),
    )


def solution(mesh):
    groups = mesh.shape["wide"] // BLOCKS
    shape = (groups, PLANES, HALVES, mesh.shape["grid"])
    inner_mesh = Mesh(mesh.devices.reshape(shape), ("t", "z", "x", "grid"))
    wide = ("t", "z", "x")
    in_specs = (
        P(wide, "grid"),
        P(),
        P(wide, None),
        P(wide, None),
        P(wide),
        P(wide, "grid", None, None),
        P(None, wide, "grid", None),
        P(None, "grid", None, wide),
        P(wide, None),
        P(wide),
        P(wide, None),
        P(None, wide, None, "grid"),
        P(None, "grid", wide),
        P(wide, "grid"),
    )
    out_specs = (
        P(wide, "grid"),
        P(wide, "grid"),
        P(wide),
        P(wide, "grid", None, None),
        P(None, wide, "grid", None),
        P(None, "grid", None, wide),
        P(wide, None),
        P(wide),
        P(wide, None),
        P(None, wide, None, "grid"),
        P(None, "grid", wide),
    )
    return jax.shard_map(
        per_device, mesh=inner_mesh, in_specs=in_specs, out_specs=out_specs, check_vma=False
    )
```

```python
import functools
import math

import jax
import jax.numpy as jnp
import numpy as np
from jax import lax
from jax.experimental import pallas as pl
from jax.experimental.layout import Layout, with_layout_constraint
from jax.experimental.pallas import tpu as pltpu
from jax.sharding import Mesh, PartitionSpec as P

CAP = 320
PLANES = 4
HALVES = 2
BLOCKS = PLANES * HALVES
EPSILON = 1e-05
ROPE_BASE = 10000.0
NEGATIVE = -1e30
BF16 = jnp.bfloat16
F32 = jnp.float32
PLACES = ("z", "x")
MESH = pl.DeviceIdType.MESH
VMEM_BYTES = 56 * 1024 * 1024


def rope_tables(token_count, width):
    half = width // 2
    frequency = np.float32(ROPE_BASE) ** (-np.arange(half, dtype=np.float32) / np.float32(half))
    angles = np.arange(token_count, dtype=np.float32)[:, None] * frequency.astype(np.float32)[None, :]
    cosine, sine = np.cos(angles).astype(np.float32), np.sin(angles).astype(np.float32)
    return np.concatenate([cosine, cosine], axis=1), np.concatenate([-sine, sine], axis=1)


def turned(values, cosine, sine):
    return values * cosine + pltpu.roll(values, values.shape[1] // 2, 1) * sine


def dot(left, right):
    return jnp.dot(left, right, preferred_element_type=F32)


def contract_first(left, right):
    return lax.dot_general(left, right, (((0,), (0,)), ((), ())), preferred_element_type=F32)


def contract_last(left, right):
    return lax.dot_general(left, right, (((1,), (1,)), ((), ())), preferred_element_type=F32)


def exact(left, right):
    return jnp.dot(left, right, precision=lax.Precision.HIGHEST)


def project_kernel(
    tokens_ref, small_ref, query_weight_ref, shared_weight_ref, cos_ref, sin_ref,
    hidden_ref, q_ref, k_ref, v_ref, logits_ref, inverse_ref, *, head_width
):
    x = tokens_ref[0, 0].astype(F32)
    inverse = lax.rsqrt(jnp.mean(x * x, axis=1, keepdims=True) + EPSILON)
    inverse_ref[...] = inverse
    hidden = (x * inverse * small_ref[:1, :].astype(F32)).astype(BF16)
    hidden_ref[...] = hidden
    logits_ref[...] = contract_last(small_ref[...], hidden)
    queries = dot(hidden, query_weight_ref[...])
    shared = dot(hidden, shared_weight_ref[...])
    span = q_ref.shape[1]
    cosine, sine = cos_ref[...], sin_ref[...]
    for head in range(span // head_width):
        at = slice(head * head_width, (head + 1) * head_width)
        q_ref[:, at] = turned(queries[:, at], cosine, sine).astype(BF16)
        k_ref[:, at] = turned(shared[:, at], cosine, sine).astype(BF16)
    v_ref[...] = shared[:, span:].astype(BF16)


def project(tokens, rows, small, weight, cosine, sine, span, head_width):
    width = tokens.shape[-1]
    token_count = BLOCKS * rows
    whole = lambda b: (0, 0)
    block = lambda b: (b, 0)
    return pl.pallas_call(
        functools.partial(project_kernel, head_width=head_width),
        grid=(BLOCKS,),
        in_specs=[
            pl.BlockSpec((1, 1, rows, width), lambda b: (b // HALVES, b % HALVES, 0, 0)),
            pl.BlockSpec(small.shape, whole),
            pl.BlockSpec((width, span), lambda b: (0, 1)),
            pl.BlockSpec((width, 2 * span), lambda b: (0, 1)),
            pl.BlockSpec((rows, head_width), block),
            pl.BlockSpec((rows, head_width), block),
        ],
        out_specs=[
            pl.BlockSpec((rows, width), block),
            pl.BlockSpec((rows, span), block),
            pl.BlockSpec((rows, span), block),
            pl.BlockSpec((rows, span), block),
            pl.BlockSpec((small.shape[0], rows), lambda b: (0, b)),
            pl.BlockSpec((rows, 1), block),
        ],
        out_shape=[
            jax.ShapeDtypeStruct((token_count, width), BF16),
            jax.ShapeDtypeStruct((token_count, span), BF16),
            jax.ShapeDtypeStruct((token_count, span), BF16),
            jax.ShapeDtypeStruct((token_count, span), BF16),
            jax.ShapeDtypeStruct((small.shape[0], token_count), F32),
            jax.ShapeDtypeStruct((token_count, 1), F32),
        ],
        compiler_params=pltpu.CompilerParams(vmem_limit_bytes=VMEM_BYTES),
        name="project",
    )(tokens, small, weight, weight, cosine, sine)


def attention_scores(q, k_ref, low_bound, high_bound, tile, tile_rows, scaling):
    rows = pl.ds(pl.multiple_of(tile * tile_rows, tile_rows), tile_rows)
    keys = k_ref[rows, :]
    scores = contract_last(q, keys) * scaling
    column = tile * tile_rows + lax.broadcasted_iota(jnp.int32, scores.shape, 1)
    allowed = (column >= low_bound) & (column <= high_bound)
    return rows, keys, scores, allowed


def slots_of_block(rank_ref, table_ref, cap):
    rows = table_ref.shape[1]
    pick = (lax.broadcasted_iota(jnp.int32, (cap, rows), 0) == rank_ref[0]).astype(BF16)
    made = contract_last(pick, table_ref[...])
    base = pl.program_id(1) * rows
    filled = made[:, 4:5] > 0.5
    low = (64.0 * made[:, 2:3] + made[:, 3:4]).astype(jnp.int32)
    high = (64.0 * made[:, 0:1] + made[:, 1:2]).astype(jnp.int32)
    gate = made[:, 5:6] + made[:, 6:7] + made[:, 7:8]
    return pick, jnp.where(filled, low, base), jnp.where(filled, high, base), gate


def token_table(position, document_start, gate):
    first = gate.astype(BF16).astype(F32)
    second = (gate - first).astype(BF16).astype(F32)
    rows = [
        position // 64, position % 64, document_start // 64, document_start % 64,
        jnp.ones_like(gate), first, second, gate - first - second,
    ]
    return jnp.pad(jnp.stack([row.astype(BF16) for row in rows]), ((0, 8), (0, 0)))


def attention_forward_kernel(
    begin_ref, q_ref, k_ref, v_ref, rank_ref, table_ref, out_ref, gated_ref, gate_ref, lse_ref, *,
    scaling
):
    block = pl.program_id(1)
    cap, width = out_ref.shape
    tile_rows = q_ref.shape[0]
    pick, low_bound, high_bound, gate = slots_of_block(rank_ref, table_ref, cap)
    q = dot(pick, q_ref[...]).astype(BF16)

    def step(tile, carried):
        largest, total, summed = carried
        rows, _, scores, allowed = attention_scores(
            q, k_ref, low_bound, high_bound, tile, tile_rows, scaling
        )
        scores = jnp.where(allowed, scores, NEGATIVE)
        new_largest = jnp.maximum(largest, jnp.max(scores, axis=1, keepdims=True))
        weights = jnp.where(allowed, jnp.exp(scores - new_largest), 0.0)
        shrink = jnp.exp(largest - new_largest)
        return (
            new_largest,
            total * shrink + jnp.sum(weights, axis=1, keepdims=True),
            summed * shrink + dot(weights.astype(BF16), v_ref[rows, :]),
        )

    largest, total, summed = lax.fori_loop(
        begin_ref[block],
        block + 1,
        step,
        (jnp.full((cap, 1), NEGATIVE, F32), jnp.zeros((cap, 1), F32), jnp.zeros((cap, width), F32)),
    )
    attended = (summed / total).astype(BF16)
    out_ref[...] = attended
    gated_ref[...] = (gate * attended.astype(F32)).astype(BF16)
    gate_ref[...] = gate
    lse_ref[0] = largest + jnp.log(total)


def attention_backward_kernel(
    begin_ref, q_ref, k_ref, v_ref, rank_ref, table_ref, out_ref, lse_ref, grad_ref,
    cos_ref, sin_ref, dq_ref, dk_ref, dv_ref, dk_sum, dv_sum, *, scaling
):
    block = pl.program_id(1)
    cap, width = out_ref.shape
    tile_rows = q_ref.shape[0]
    pick, low_bound, high_bound, _ = slots_of_block(rank_ref, table_ref, cap)
    q = dot(pick, q_ref[...]).astype(BF16)
    grad = grad_ref[...]
    delta = jnp.sum(grad.astype(F32) * out_ref[...].astype(F32), axis=1, keepdims=True)
    lse = lse_ref[0]

    @pl.when(block == 0)
    def _():
        dk_sum[...] = jnp.zeros_like(dk_sum)
        dv_sum[...] = jnp.zeros_like(dv_sum)

    def step(tile, dq):
        rows, keys, scores, allowed = attention_scores(
            q, k_ref, low_bound, high_bound, tile, tile_rows, scaling
        )
        chances = jnp.where(allowed, jnp.exp(scores - lse), 0.0)
        dv_sum[rows, :] += contract_first(chances.astype(BF16), grad)
        grad_chances = contract_last(grad, v_ref[rows, :])
        grad_scores = (chances * (grad_chances - delta)).astype(BF16)
        dk_sum[rows, :] += contract_first(grad_scores, q) * scaling
        return dq + dot(grad_scores, keys)

    dq = lax.fori_loop(begin_ref[block], block + 1, step, jnp.zeros((cap, width), F32)) * scaling
    high = dq.astype(BF16)
    rest = (dq - high.astype(F32)).astype(BF16)
    dq_tokens = contract_first(pick, high) + contract_first(pick, rest)
    own = pl.ds(pl.multiple_of(block * tile_rows, tile_rows), tile_rows)
    dq_ref[...] = turned(dq_tokens, cos_ref[own, :], -sin_ref[own, :]).astype(BF16)

    @pl.when(block == BLOCKS - 1)
    def _():
        def finish(tile, nothing):
            rows = pl.ds(pl.multiple_of(tile * tile_rows, tile_rows), tile_rows)
            dk_ref[rows, :] = turned(dk_sum[rows, :], cos_ref[rows, :], -sin_ref[rows, :]).astype(BF16)
            dv_ref[rows, :] = dv_sum[rows, :].astype(BF16)
            return nothing

        lax.fori_loop(0, BLOCKS, finish, 0)


def attention_specs(row_count, token_count, width):
    return dict(
        q=pl.BlockSpec((row_count, width), lambda h, b, s: (b, h)),
        k=pl.BlockSpec((token_count, width), lambda h, b, s: (0, h)),
        rank=pl.BlockSpec((1, 1, row_count), lambda h, b, s: (b, 0, 0)),
        rows=pl.BlockSpec((16, row_count), lambda h, b, s: (0, b)),
        gate=pl.BlockSpec((CAP, 1), lambda h, b, s: (b, 0)),
        slots=pl.BlockSpec((CAP, width), lambda h, b, s: (b, h)),
        table=pl.BlockSpec((token_count, width), lambda h, b, s: (0, 0)),
        lse=pl.BlockSpec((1, CAP, 1), lambda h, b, s: (h, b, 0)),
    )


def attention_forward(begin, q, k, v, rank, table, width):
    token_count, heads = q.shape[0], q.shape[1] // width
    row_count = token_count // BLOCKS
    s = attention_specs(row_count, token_count, width)
    return pl.pallas_call(
        functools.partial(attention_forward_kernel, scaling=1.0 / math.sqrt(width)),
        grid_spec=pltpu.PrefetchScalarGridSpec(
            num_scalar_prefetch=1,
            grid=(heads, BLOCKS),
            in_specs=[s["q"], s["k"], s["k"], s["rank"], s["rows"]],
            out_specs=[s["slots"], s["slots"], s["gate"], s["lse"]],
        ),
        out_shape=[
            jax.ShapeDtypeStruct((BLOCKS * CAP, heads * width), BF16),
            jax.ShapeDtypeStruct((BLOCKS * CAP, heads * width), BF16),
            jax.ShapeDtypeStruct((BLOCKS * CAP, 1), F32),
            jax.ShapeDtypeStruct((heads, BLOCKS * CAP, 1), F32),
        ],
        compiler_params=pltpu.CompilerParams(vmem_limit_bytes=VMEM_BYTES),
        name="attention_forward",
    )(begin, q, k, v, rank, table)


def attention_backward(begin, q, k, v, rank, table, out, lse, grad, cosine, sine, width):
    token_count, heads = q.shape[0], q.shape[1] // width
    row_count = token_count // BLOCKS
    s = attention_specs(row_count, token_count, width)
    return pl.pallas_call(
        functools.partial(attention_backward_kernel, scaling=1.0 / math.sqrt(width)),
        grid_spec=pltpu.PrefetchScalarGridSpec(
            num_scalar_prefetch=1,
            grid=(heads, BLOCKS),
            in_specs=[
                s["q"], s["k"], s["k"], s["rank"], s["rows"],
                s["slots"], s["lse"], s["slots"], s["table"], s["table"],
            ],
            out_specs=[s["q"], s["k"], s["k"]],
            scratch_shapes=[pltpu.VMEM((token_count, width), F32)] * 2,
        ),
        out_shape=[
            jax.ShapeDtypeStruct((token_count, heads * width), BF16),
            jax.ShapeDtypeStruct((token_count, heads * width), BF16),
            jax.ShapeDtypeStruct((token_count, heads * width), BF16),
        ],
        compiler_params=pltpu.CompilerParams(vmem_limit_bytes=VMEM_BYTES),
        name="attention_backward",
    )(begin, q, k, v, rank, table, out, lse, grad, cosine, sine)


def pack_up_kernel(weight_ref, pieces_ref):
    units = pieces_ref.shape[2] // 2
    both = weight_ref[0].astype(F32)
    gate, up = both[:, 0, :], both[:, 1, :]
    for half in range(HALVES):
        at = slice(half * units, (half + 1) * units)
        pieces_ref[half] = jnp.concatenate([gate[:, at], up[:, at]], axis=1).astype(BF16)


def pack_down_kernel(weight_ref, first_ref, last_ref):
    turned_rows = weight_ref[0].astype(F32).T.astype(BF16)
    middle = first_ref.shape[1]
    first_ref[0] = turned_rows[:middle]
    last_ref[0] = turned_rows[middle:]


def row_major(array):
    return with_layout_constraint(array, Layout(major_to_minor=tuple(range(array.ndim))))


def exchanged(pieces):
    return row_major(lax.all_to_all(row_major(pieces), PLACES, 0, 0, tiled=True))


def over_groups(landed):
    return lax.all_gather(landed, "t", axis=0, tiled=False)


def group_sums(pieces):
    return lax.psum_scatter(pieces, "t", scatter_dimension=0, tiled=False)


def return_gradients(pieces):
    return exchanged(group_sums(pieces))


def other_core(column):
    return column + 1 - 2 * (column % 2)


def crossed(plane, j):
    return (plane, plane + 1 - 2 * (plane % 2), (plane + 2) % 4, 3 - plane)[j]


def meet(peers):
    barrier = pltpu.get_barrier_semaphore()
    for peer in peers:
        pl.semaphore_signal(barrier, inc=1, device_id=peer, device_id_type=MESH)
    pl.semaphore_wait(barrier, len(peers))


def partners():
    plane, half, column = lax.axis_index("z"), lax.axis_index("x"), lax.axis_index("grid")
    planes = [{"z": crossed(plane, j)} for j in range(PLANES)]
    along_x, along_y = {"x": 1 - half}, {"grid": (column + 2) % 4}
    core = {"grid": other_core(column)}
    return plane, half, column, planes, along_x, along_y, core


class Moves:
    def __init__(self, send, recv):
        self.send, self.recv, self.made = send, recv, {}

    def add(self, index, source, target, peer):
        self.made[index] = (source, target, peer)

    def copy(self, index, source, target, peer):
        return pltpu.make_async_remote_copy(
            src_ref=source, dst_ref=target, send_sem=self.send.at[index],
            recv_sem=self.recv.at[index], device_id=peer, device_id_type=MESH,
        )

    def start(self, index):
        self.copy(index, *self.made[index]).start()

    def arrived(self, index, target, peer):
        self.copy(index, target, target, peer).wait_recv()

    def all_sent(self):
        for index in self.made:
            self.copy(index, *self.made[index]).wait_send()


class Ride:
    def __init__(self, pieces_ref, landed_ref, send, recv, local, columns=None):
        if columns is None:
            columns = pl.ds(0, pieces_ref.shape[2])
        rows = pl.ds(0, pieces_ref.shape[1])
        plane, half = lax.axis_index("z"), lax.axis_index("x")
        self.moves = Moves(send, recv)
        self.landings = {}
        own = plane * HALVES + half
        self.keep = pltpu.make_async_copy(pieces_ref.at[own], landed_ref.at[own], local)
        self.peers = []
        for dz in range(PLANES):
            for dx in range(HALVES):
                index = dz * HALVES + dx
                if index == 0:
                    continue
                at_half = 1 - half if dx else half
                peer = {"z": crossed(plane, dz), "x": at_half}
                other = crossed(plane, dz) * HALVES + at_half
                source = pieces_ref.at[other, rows, columns]
                self.moves.add(index, source, landed_ref.at[own, rows, columns], peer)
                self.landings[index] = (landed_ref.at[other, rows, columns], peer)
                if dz and dx:
                    self.peers.append(peer)

    def begin(self, first=(4, 6, 2)):
        self.keep.start()
        for index in first:
            self.moves.start(index)

    def go_on(self, number, plan=((5,), (7,), (3,), (1,))):
        for index in plan[number] if number < len(plan) else ():
            self.moves.start(index)

    def finish(self):
        for index, (landing, peer) in self.landings.items():
            self.moves.arrived(index, landing, peer)
        self.moves.all_sent()
        self.keep.wait()


RIDE_SCRATCH = (
    pltpu.SemaphoreType.DMA((8,)),
    pltpu.SemaphoreType.DMA((8,)),
    pltpu.SemaphoreType.DMA,
)


def run_with_ride(steps, ride):
    steps[0]()
    if ride is not None:
        ride.begin()
    for number, step in enumerate(steps[1:-1]):
        step()
        if ride is not None:
            ride.go_on(number)
    steps[-1]()
    if ride is not None:
        ride.finish()


def gather_parts(slots_ref, out_ref, send, recv, local, same, share=2, more=(), chain=None):
    plane, half, column, planes, along_x, along_y, core = partners()
    cap, width = slots_ref.shape[-2:]
    middle = cap * share // 64 * 16
    y_column, core_column = (column + 2) % 4, other_core(column)
    core_y = (core_column + 2) % 4
    sources = [crossed(plane, j) for j in range(PLANES)]
    moves = Moves(send, recv)

    def piece(source, at_half, at_column, first=0, count=cap):
        columns = pl.ds(pl.multiple_of(at_column * width, width), width)
        return out_ref.at[source, at_half, pl.ds(first, count), columns]

    def slots_for(j):
        return slots_ref if same else slots_ref.at[sources[j]]

    keep = pltpu.make_async_copy(slots_for(0), piece(plane, half, column), local)
    for j in range(PLANES):
        source = sources[j]
        place = piece(source, half, column)
        if j and chain is None:
            moves.add(j, slots_for(j), piece(plane, half, column), planes[j])
        here = place if j else slots_for(0)
        moves.add(4 + j, here, place, along_x)
        moves.add(8 + j, here, place, along_y)
        moves.add(12 + j, here, place, core)
        from_x, from_y = piece(source, 1 - half, column), piece(source, half, y_column)
        first = piece(source, 1 - half, column, 0, middle)
        last = piece(source, half, y_column, middle, cap - middle)
        diagonal = piece(source, 1 - half, y_column)
        moves.add(16 + j, first, first, along_y)
        moves.add(20 + j, from_x, from_x, core)
        moves.add(24 + j, last, last, along_x)
        moves.add(28 + j, from_y, from_y, core)
        moves.add(32 + j, diagonal, diagonal, core)

    def begin():
        meet(planes[1:] + [along_x, along_y, core] + list(more))
        if chain is None:
            for j in (1, 3, 2):
                moves.start(j)
        else:
            chain.begin()
        keep.start()

    def spread(j):
        if j and chain is None:
            moves.arrived(j, piece(sources[j], half, column), planes[j])
        elif j:
            chain.arrived(j)
        for index in (4, 8, 12):
            moves.start(index + j)

    def forward(j):
        moves.arrived(4 + j, piece(sources[j], 1 - half, column), along_x)
        moves.start(16 + j)
        moves.start(20 + j)
        moves.arrived(8 + j, piece(sources[j], half, y_column), along_y)
        moves.start(24 + j)
        moves.start(28 + j)

    def cross(j):
        moves.arrived(16 + j, piece(sources[j], 1 - half, y_column, 0, middle), along_y)
        moves.arrived(24 + j, piece(sources[j], 1 - half, y_column, middle, cap - middle), along_x)
        moves.start(32 + j)

    def finish():
        for j in order:
            moves.arrived(12 + j, piece(sources[j], half, core_column), core)
            moves.arrived(20 + j, piece(sources[j], 1 - half, core_column), core)
            moves.arrived(28 + j, piece(sources[j], half, core_y), core)
            moves.arrived(32 + j, piece(sources[j], 1 - half, core_y), core)
        moves.all_sent()
        keep.wait()

    order = (0, 1, 3, 2)
    return begin, spread, forward, cross, finish, order


def gather_steps(*refs, **settings):
    begin, spread, forward, cross, finish, order = gather_parts(*refs, **settings)

    def step(number):
        if number < len(order):
            spread(order[number])
        if 0 <= number - 1 < len(order):
            forward(order[number - 1])
        if 0 <= number - 2 < len(order):
            cross(order[number - 2])

    return [begin] + [functools.partial(step, number) for number in range(len(order) + 2)] + [finish]


class Chain:
    def __init__(self, view, source, send, recv):
        plane = lax.axis_index("z")
        self.inner = (plane == 1) | (plane == 2)
        near, far = {"z": crossed(plane, 1)}, {"z": crossed(plane, 3)}
        self.views = [view(crossed(plane, j)) for j in range(PLANES)]
        self.send, self.recv = send, recv
        self.near_own = (0, 1, source, self.views[0], near)
        self.far_own = (1, 3, source, self.views[0], far)
        self.on_arrival = {
            1: (2, 2, self.views[1], self.views[1], far),
            3: (3, 2, self.views[3], self.views[3], near),
            2: (4, 3, self.views[2], self.views[2], near),
        }

    def copy(self, at_send, at_recv, source, target, peer):
        return pltpu.make_async_remote_copy(
            src_ref=source, dst_ref=target, send_sem=self.send.at[at_send],
            recv_sem=self.recv.at[at_recv], device_id=peer, device_id_type=MESH,
        )

    def begin(self):
        self.copy(*self.near_own).start()

        @pl.when(self.inner)
        def _():
            self.copy(*self.far_own).start()

    def arrived(self, j):
        place = self.views[j]
        self.copy(0, j, place, place, self.near_own[-1]).wait_recv()

        @pl.when(self.inner)
        def _():
            self.copy(*self.on_arrival[j]).start()

    def finish(self):
        self.copy(*self.near_own).wait_send()

        @pl.when(self.inner)
        def _():
            self.copy(*self.far_own).wait_send()
            for made in self.on_arrival.values():
                self.copy(*made).wait_send()


CHAIN_SCRATCH = (pltpu.SemaphoreType.DMA((5,)), pltpu.SemaphoreType.DMA((4,)))


def opening_kernel(
    tokens_ref, pieces_ref, up_ref, down_ref, out_ref, landed_ref, up_pieces_ref, first_ref,
    last_ref, send, recv, local, ride_send, ride_recv,
    ride_local, hop_send, hop_recv, *chain_sems, share
):
    plane, half, column = lax.axis_index("z"), lax.axis_index("x"), lax.axis_index("grid")
    width = tokens_ref.shape[1]
    middle = pieces_ref.shape[2] // 2
    left, right = pl.ds(0, middle), pl.ds(middle, middle)
    rows = pl.ds(0, pieces_ref.shape[1])
    along_x = {"x": 1 - half}

    def tokens_of(source):
        columns = pl.ds(pl.multiple_of(column * width, width), width)
        return out_ref.at[source, half, pl.ds(0, tokens_ref.shape[0]), columns]

    def shared_of(at_half):
        return lambda source: landed_ref.at[source * HALVES + at_half, rows, right]

    own = plane * HALVES + half
    tokens = Chain(tokens_of, tokens_ref, *chain_sems[:2])
    here = Chain(shared_of(half), pieces_ref.at[own, rows, right], *chain_sems[2:4])
    there = Chain(shared_of(1 - half), shared_of(1 - half)(plane), *chain_sems[4:])
    ride = Ride(pieces_ref, landed_ref, ride_send, ride_recv, ride_local, left)
    hop = pltpu.make_async_remote_copy(
        src_ref=pieces_ref.at[plane * HALVES + 1 - half, rows, right],
        dst_ref=landed_ref.at[own, rows, right],
        send_sem=hop_send, recv_sem=hop_recv, device_id=along_x, device_id_type=MESH,
    )
    landing = shared_of(1 - half)(plane)
    hop_here = pltpu.make_async_remote_copy(
        src_ref=landing, dst_ref=landing, send_sem=hop_send, recv_sem=hop_recv,
        device_id=along_x, device_id_type=MESH,
    )
    begin, spread, forward, cross, finish, _ = gather_parts(
        tokens_ref, out_ref, send, recv, local, True, share, ride.peers, tokens
    )

    def first():
        begin()
        ride.keep.start()
        spread(0)
        hop.start()
        here.begin()

    def second():
        spread(1)
        forward(0)
        ride.moves.start(2)

    def third():
        spread(3)
        forward(1)
        cross(0)
        hop_here.wait_recv()
        there.begin()
        here.arrived(1)

    def fourth():
        spread(2)
        forward(3)
        cross(1)
        ride.moves.start(6)
        ride.moves.start(4)
        here.arrived(3)
        there.arrived(1)

    def fifth():
        forward(2)
        cross(3)
        for index in (3, 7, 5, 1):
            ride.moves.start(index)
        here.arrived(2)
        there.arrived(3)
        cross(2)
        there.arrived(2)
        finish()
        ride.finish()
        hop.wait_send()
        for chain in (tokens, here, there):
            chain.finish()

    def compute():
        pack_up_kernel(up_ref, up_pieces_ref)
        pack_down_kernel(down_ref, first_ref, last_ref)

    carry([first], [second, third, fourth, fifth], (3, 6, 7, 7), compute)


def opened(tokens, pieces, up, down, collective_id, share):
    rows, width = tokens.shape
    experts, own_rows, _, units = up.shape
    places = experts * HALVES
    tile = own_rows // 2
    down_half = (places, own_rows // 2, units // HALVES)
    anywhere = pl.BlockSpec(memory_space=pl.ANY)
    half = pl.BlockSpec((1,) + down_half[1:], lambda p: (p, 0, 0))
    return pl.pallas_call(
        functools.partial(opening_kernel, share=share),
        grid=(places,),
        in_specs=[
            anywhere,
            anywhere,
            pl.BlockSpec((1, tile, 2, units), lambda p: (p // 2, p % 2, 0, 0)),
            pl.BlockSpec((1,) + down.shape[1:], lambda p: (p, 0, 0)),
        ],
        out_specs=[
            anywhere,
            anywhere,
            pl.BlockSpec((HALVES, tile, units), lambda p: (p // 2, p % 2, 0)),
            half,
            half,
        ],
        out_shape=[
            jax.ShapeDtypeStruct((PLANES, HALVES, rows, 4 * width), BF16),
            jax.ShapeDtypeStruct(pieces.shape, BF16),
            jax.ShapeDtypeStruct((places, own_rows, units), BF16),
            jax.ShapeDtypeStruct(down_half, BF16),
            jax.ShapeDtypeStruct(down_half, BF16),
        ],
        scratch_shapes=list(GATHER_SCRATCH) + list(RIDE_SCRATCH)
        + [pltpu.SemaphoreType.DMA, pltpu.SemaphoreType.DMA] + list(CHAIN_SCRATCH) * 3,
        compiler_params=pltpu.CompilerParams(
            collective_id=collective_id, has_side_effects=True, vmem_limit_bytes=VMEM_BYTES
        ),
        name="open_rows",
    )(tokens, pieces, up, down)


GATHER_SCRATCH = (
    pltpu.SemaphoreType.DMA((36,)),
    pltpu.SemaphoreType.DMA((36,)),
    pltpu.SemaphoreType.DMA,
)


def gather_kernel(*refs, same, share, rides):
    if rides:
        slots_ref, pieces_ref, out_ref, landed_ref = refs[:4]
        ride = Ride(pieces_ref, landed_ref, *refs[7:])
        scratch = refs[4:7]
    else:
        slots_ref, out_ref = refs[:2]
        ride, scratch = None, refs[2:]
    more = ride.peers if rides else ()
    run_with_ride(gather_steps(slots_ref, out_ref, *scratch, same, share, more), ride)


def gathered(slots, collective_id, ride=None, share=2):
    rows, width = slots.shape[-2:]
    rides = () if ride is None else (ride,)
    anywhere = pl.BlockSpec(memory_space=pl.ANY)
    out = pl.pallas_call(
        functools.partial(gather_kernel, same=slots.ndim == 2, share=share, rides=len(rides)),
        out_shape=[jax.ShapeDtypeStruct((PLANES, HALVES, rows, 4 * width), BF16)]
        + [jax.ShapeDtypeStruct(r.shape, BF16) for r in rides],
        in_specs=[anywhere] * (1 + len(rides)),
        out_specs=[anywhere] * (1 + len(rides)),
        scratch_shapes=list(GATHER_SCRATCH) + list(RIDE_SCRATCH) * len(rides),
        compiler_params=pltpu.CompilerParams(collective_id=collective_id, has_side_effects=True),
        name="gather_rows",
    )(slots, *rides)
    return out if rides else out[0]


def scatter_steps(
    partial_ref, out_ref, own, other, crossing, side, send, recv, load, share=2, more=()
):
    plane, half, column, planes, along_x, along_y, core = partners()
    cap, width = out_ref.shape[-2:]
    middle = cap * share // 64 * 16
    chunk = 32 if middle % 32 == 0 and cap % 32 == 0 else 16
    y_column, core_column = (column + 2) % 4, other_core(column)
    core_y = (core_column + 2) % 4
    halves = (half, 1 - half, half, 1 - half)
    own_columns = (column, column, y_column, y_column)
    core_columns = (core_column, core_column, core_y, core_y)
    moves = Moves(send, recv)
    first, last = pl.ds(0, middle), pl.ds(middle, cap - middle)

    def part(j, q, at_columns):
        columns = pl.ds(pl.multiple_of(at_columns[q] * width, width), width)
        return partial_ref.at[crossed(plane, j), halves[q], :, columns]

    def loading(j, q):
        return pltpu.make_async_copy(part(j, q, own_columns), own.at[j, q], load.at[4 * j + q])

    keep = pltpu.make_async_copy(own.at[0, 0], out_ref.at[plane], load.at[16])
    for j in range(PLANES):
        for q in range(4):
            moves.add(4 * j + q, part(j, q, core_columns), other.at[j, q], core)
        moves.add(16 + j, own.at[j, 3, first], crossing.at[j, first], along_x)
        moves.add(20 + j, own.at[j, 3, last], crossing.at[j, last], along_y)
        moves.add(24 + j, own.at[j, 2], side.at[j, 1], along_y)
        moves.add(28 + j, own.at[j, 1], side.at[j, 0], along_x)
        if j:
            moves.add(32 + j, own.at[j, 0], out_ref.at[plane], planes[j])

    def add(j, q, begin_row, count, terms):
        def step(i, nothing):
            rows = pl.ds(pl.multiple_of(begin_row + i * chunk, chunk), chunk)
            total = own[j, q, rows, :].astype(F32)
            for ref, index in terms:
                total = total + ref[index + (rows, slice(None))].astype(F32)
            own[j, q, rows, :] = total.astype(BF16)
            return nothing

        lax.fori_loop(0, count // chunk, step, 0)

    def chip_sum(j, q):
        moves.arrived(4 * j + q, other.at[j, q], core)
        loading(j, q).wait()
        add(j, q, 0, cap, [(other, (j, q))])

    def stage_one(j):
        chip_sum(j, 3)
        moves.start(16 + j)
        moves.start(20 + j)
        chip_sum(j, 2)
        chip_sum(j, 1)
        chip_sum(j, 0)

    def stage_two(j):
        moves.arrived(16 + j, crossing.at[j, first], along_x)
        add(j, 2, 0, middle, [(crossing, (j,))])
        moves.start(24 + j)
        moves.arrived(20 + j, crossing.at[j, last], along_y)
        add(j, 1, middle, cap - middle, [(crossing, (j,))])
        moves.start(28 + j)

    def stage_three(j):
        moves.arrived(24 + j, side.at[j, 1], along_y)
        moves.arrived(28 + j, side.at[j, 0], along_x)
        add(j, 0, 0, cap, [(side, (j, 0)), (side, (j, 1))])
        if j:
            moves.start(32 + j)
        else:
            keep.start()

    order = (2, 3, 1, 0)

    def begin():
        meet(planes[1:] + [along_x, along_y, core] + list(more))
        for j in order:
            for q in (3, 2, 1, 0):
                moves.start(4 * j + q)
                loading(j, q).start()

    def step(number):
        if number < len(order):
            stage_one(order[number])
        if 0 <= number - 1 < len(order):
            stage_two(order[number - 1])
        if 0 <= number - 2 < len(order):
            stage_three(order[number - 2])

    def finish():
        for j in range(1, PLANES):
            moves.arrived(32 + j, out_ref.at[crossed(plane, j)], planes[j])
        moves.all_sent()
        keep.wait()

    return [begin] + [functools.partial(step, number) for number in range(len(order) + 2)] + [finish]


def scatter_scratch(rows, width):
    return [
        pltpu.VMEM((PLANES, 4, rows, width), BF16),
        pltpu.VMEM((PLANES, 4, rows, width), BF16),
        pltpu.VMEM((PLANES, rows, width), BF16),
        pltpu.VMEM((PLANES, 2, rows, width), BF16),
        pltpu.SemaphoreType.DMA((36,)),
        pltpu.SemaphoreType.DMA((36,)),
        pltpu.SemaphoreType.DMA((17,)),
    ]


def scatter_kernel(*refs, share, rides):
    if rides:
        partial_ref, pieces_ref, out_ref, landed_ref = refs[:4]
        ride = Ride(pieces_ref, landed_ref, *refs[11:])
        scratch = refs[4:11]
    else:
        partial_ref, out_ref = refs[:2]
        ride, scratch = None, refs[2:]
    more = ride.peers if rides else ()
    run_with_ride(scatter_steps(partial_ref, out_ref, *scratch, share, more), ride)


def scattered(partial, rows, collective_id, ride=None, share=2):
    width = partial.shape[1] // 4
    rides = () if ride is None else (ride,)
    anywhere = pl.BlockSpec(memory_space=pl.ANY)
    out = pl.pallas_call(
        functools.partial(scatter_kernel, share=share, rides=len(rides)),
        out_shape=[jax.ShapeDtypeStruct((PLANES, rows, width), BF16)]
        + [jax.ShapeDtypeStruct(r.shape, BF16) for r in rides],
        in_specs=[anywhere] * (1 + len(rides)),
        out_specs=[anywhere] * (1 + len(rides)),
        scratch_shapes=scatter_scratch(rows, width) + list(RIDE_SCRATCH) * len(rides),
        compiler_params=pltpu.CompilerParams(
            collective_id=collective_id, has_side_effects=True, vmem_limit_bytes=VMEM_BYTES
        ),
        name="scatter_rows",
    )(partial.reshape(PLANES, HALVES, rows, 4 * width), *rides)
    return out if rides else out[0]


def carry(before, after, places, compute):
    number = pl.program_id(0)

    @pl.when(number == 0)
    def _():
        for step in before:
            step()

    compute()
    for at in sorted(set(places)):

        @pl.when(number == at)
        def _(at=at):
            for place, step in zip(places, after):
                if place == at:
                    step()


def join_halves(first_ref, last_ref, whole_ref):
    count, height, _ = first_ref.shape

    @pl.when(pl.program_id(0) == 0)
    def _():
        for place in range(count):
            whole_ref[2 * place * height : (2 * place + 1) * height, :] = first_ref[place]
            whole_ref[(2 * place + 1) * height : (2 * place + 2) * height, :] = last_ref[place]


def expert_forward_kernel(
    rows_ref, up_weight_ref, first_ref, last_ref, small_ref, rank_ref, member_ref, grad_ref,
    gate_ref, up_ref, result_ref, share_ref, shared_ref, grad_rows_ref, down_weight_ref, *scratch
):
    join_halves(first_ref, last_ref, down_weight_ref)
    steps = gather_steps(grad_ref, grad_rows_ref, *scratch, False)
    units = gate_ref.shape[1]

    def compute():
        rows = rows_ref[0]
        made = dot(rows, up_weight_ref[...])
        gate, up = made[:, :units], made[:, units:]
        gate_ref[...] = gate
        up_ref[...] = up
        inner = gate * jax.nn.sigmoid(gate) * up
        result_ref[0] = contract_last(inner.astype(BF16), down_weight_ref[...]).astype(BF16)
        cap, count = rows.shape[0], rank_ref.shape[2]
        pick = (lax.broadcasted_iota(jnp.int32, (cap, count), 0) == rank_ref[0]).astype(BF16)
        member = contract_last(pick, member_ref[...]) > 0.5
        logits = jnp.where(member, contract_last(rows, small_ref[...]), NEGATIVE)
        largest = jnp.max(logits, axis=1, keepdims=True)
        weights = jnp.where(member, jnp.exp(logits - largest), 0.0)
        mine = lax.broadcasted_iota(jnp.int32, weights.shape, 1) == 6 + lax.axis_index("z")
        total = jnp.sum(weights, axis=1, keepdims=True)
        own = jnp.sum(jnp.where(mine, weights, 0.0), axis=1, keepdims=True)
        share = own / jnp.where(total > 0.0, total, 1.0)
        share_ref[...] = share
        shared_ref[...] = (share * inner).astype(BF16)

    carry(steps[:2], steps[2:], (1, 3, 5, 6, 7, 7), compute)


def once(shape):
    return pl.BlockSpec(shape, lambda b: (0,) * len(shape), pipeline_mode=pl.Buffered(1))


def expert_forward(rows, up_weight, down_halves, small, rank, member, grad_slots, collective_id):
    _, cap, width = rows.shape
    units = down_halves[0].shape[2]
    count = BLOCKS * cap
    anywhere = pl.BlockSpec(memory_space=pl.ANY)
    block = lambda b: (b, 0)
    return pl.pallas_call(
        expert_forward_kernel,
        grid=(BLOCKS,),
        in_specs=[
            pl.BlockSpec((1, cap, width), lambda b: (b, 0, 0)),
            once(up_weight.shape),
            once(down_halves[0].shape),
            once(down_halves[1].shape),
            once(small.shape),
            pl.BlockSpec((1, 1, rank.shape[2]), lambda b: (b, 0, 0)),
            pl.BlockSpec((16, rank.shape[2]), lambda b: (0, b)),
            anywhere,
        ],
        out_specs=[
            pl.BlockSpec((cap, units), block),
            pl.BlockSpec((cap, units), block),
            pl.BlockSpec((1, cap, width), lambda b: (b, 0, 0)),
            pl.BlockSpec((cap, 1), block),
            pl.BlockSpec((cap, units), block),
            anywhere,
        ],
        out_shape=[
            jax.ShapeDtypeStruct((count, units), F32),
            jax.ShapeDtypeStruct((count, units), F32),
            jax.ShapeDtypeStruct((BLOCKS, cap, width), BF16),
            jax.ShapeDtypeStruct((count, 1), F32),
            jax.ShapeDtypeStruct((count, units), BF16),
            jax.ShapeDtypeStruct((PLANES, HALVES, cap, width), BF16),
        ],
        scratch_shapes=[pltpu.VMEM((width, units), BF16)] + list(GATHER_SCRATCH),
        compiler_params=pltpu.CompilerParams(
            collective_id=collective_id, has_side_effects=True, vmem_limit_bytes=VMEM_BYTES
        ),
        name="expert_forward",
    )(rows, up_weight, *down_halves, small, rank, member, grad_slots)


def expert_backward_kernel(
    gate_ref, up_ref, grad_ref, share_ref, up_weight_ref, first_ref, last_ref, columns_ref, inner_ref,
    result_ref, grad_rows_ref, grad_gate_up_ref, down_first_ref, down_last_ref, out_ref,
    down_weight_ref, *scratch
):
    join_halves(first_ref, last_ref, down_weight_ref)
    steps = scatter_steps(result_ref, out_ref, *scratch)
    middle = down_first_ref.shape[1]

    def compute():
        grad_inner = dot(grad_ref[0], down_weight_ref[...]) * share_ref[...]
        gate, up = gate_ref[...], up_ref[...]
        sigmoid = jax.nn.sigmoid(gate)
        grad_gate = grad_inner * up * sigmoid * (1.0 + gate * (1.0 - sigmoid))
        grad_up = grad_inner * gate * sigmoid
        grad_gate_up = jnp.concatenate([grad_gate, grad_up], axis=1).astype(BF16)
        grad_gate_up_ref[...] = grad_gate_up
        grad_rows_ref[0] = contract_last(grad_gate_up, up_weight_ref[...]).astype(BF16)
        down_grad = contract_first(columns_ref[...], inner_ref[...]).astype(BF16)
        down_first_ref[0] = down_grad[:middle]
        down_last_ref[0] = down_grad[middle:]

    carry(steps[:1], steps[1:], (0, 1, 2, 4, 5, 7, 7), compute)


def expert_backward(
    gate, up, grad_rows, share, up_weight, down_halves, inner, result, collective_id
):
    _, cap, width = grad_rows.shape
    count, units = gate.shape
    tile = width // BLOCKS
    anywhere = pl.BlockSpec(memory_space=pl.ANY)
    block = lambda b: (b, 0)
    rows = pl.BlockSpec((1, cap, width), lambda b: (b, 0, 0))
    half = pl.BlockSpec((1, tile // 2, units), lambda b: (b, 0, 0))
    return pl.pallas_call(
        expert_backward_kernel,
        grid=(BLOCKS,),
        in_specs=[
            pl.BlockSpec((cap, units), block),
            pl.BlockSpec((cap, units), block),
            rows,
            pl.BlockSpec((cap, 1), block),
            once(up_weight.shape),
            once(down_halves[0].shape),
            once(down_halves[1].shape),
            pl.BlockSpec((count, tile), lambda b: (0, b)),
            once(inner.shape),
            anywhere,
        ],
        out_specs=[rows, pl.BlockSpec((cap, 2 * units), block), half, half, anywhere],
        out_shape=[
            jax.ShapeDtypeStruct((BLOCKS, cap, width), BF16),
            jax.ShapeDtypeStruct((count, 2 * units), BF16),
            jax.ShapeDtypeStruct((BLOCKS, tile // 2, units), BF16),
            jax.ShapeDtypeStruct((BLOCKS, tile // 2, units), BF16),
            jax.ShapeDtypeStruct((PLANES, cap, width // 4), BF16),
        ],
        scratch_shapes=[pltpu.VMEM((width, units), BF16)] + scatter_scratch(cap, width // 4),
        compiler_params=pltpu.CompilerParams(
            collective_id=collective_id, has_side_effects=True, vmem_limit_bytes=VMEM_BYTES
        ),
        name="expert_backward",
    )(
        gate, up, grad_rows, share, up_weight, *down_halves, grad_rows.reshape(count, width), inner,
        result.reshape(PLANES, HALVES, cap, width),
    )


def expert_gradient_kernel(
    rows_ref, grad_gate_up_ref, partial_ref, pieces_ref, up_grad_ref, out_ref, landed_ref, *scratch
):
    ride = Ride(pieces_ref, landed_ref, *scratch[7:])
    steps = scatter_steps(partial_ref, out_ref, *scratch[:7], 1, ride.peers)

    def compute():
        up_grad_ref[...] = contract_first(rows_ref[...], grad_gate_up_ref[...]).astype(BF16)

    def with_ride(number):
        steps[1 + number]()
        ride.go_on(number)

    after = [functools.partial(with_ride, number) for number in range(6)]
    carry([steps[0], ride.begin], after + [steps[-1], ride.finish], (0, 2, 4, 6, 7, 7, 7, 7), compute)


def expert_gradient(rows, grad_gate_up, partial, pieces, collective_id):
    count, width = rows.shape
    units = grad_gate_up.shape[1]
    cap, tile = count // BLOCKS, width // BLOCKS
    anywhere = pl.BlockSpec(memory_space=pl.ANY)
    return pl.pallas_call(
        expert_gradient_kernel,
        grid=(BLOCKS,),
        in_specs=[
            pl.BlockSpec((count, tile), lambda b: (0, b)),
            once((count, units)),
            anywhere,
            anywhere,
        ],
        out_specs=[pl.BlockSpec((tile, units), lambda b: (b, 0)), anywhere, anywhere],
        out_shape=[
            jax.ShapeDtypeStruct((width, units), BF16),
            jax.ShapeDtypeStruct((PLANES, cap, width // 4), BF16),
            jax.ShapeDtypeStruct(pieces.shape, BF16),
        ],
        scratch_shapes=scatter_scratch(cap, width // 4) + list(RIDE_SCRATCH),
        compiler_params=pltpu.CompilerParams(
            collective_id=collective_id, has_side_effects=True, vmem_limit_bytes=VMEM_BYTES
        ),
        name="expert_gradient",
    )(rows, grad_gate_up, partial.reshape(PLANES, HALVES, cap, width), pieces)


def closing_kernel(
    hidden_ref, q_ref, k_ref, v_ref, rows_ref, gated_ref, partial_ref, grad_ref, out_ref, *scratch
):
    steps = scatter_steps(partial_ref, out_ref, *scratch)
    span = q_ref.shape[1]

    def compute():
        hidden = hidden_ref[...]
        for place, ref in enumerate((q_ref, k_ref, v_ref)):
            at = slice(place * span, (place + 1) * span)
            grad_ref[:, at] = contract_first(hidden, ref[...]).astype(BF16)
        grad_ref[:, 3 * span :] = contract_first(rows_ref[...], gated_ref[...]).astype(BF16)

    carry(steps[:1], steps[1:], (1, 4, 7, 7, 7, 7, 7), compute)


def closing(hidden, q, k, v, rows, gated, partial, collective_id):
    count, width = hidden.shape
    slot_count, span = gated.shape
    tile, own_rows = width // BLOCKS, count // BLOCKS
    anywhere = pl.BlockSpec(memory_space=pl.ANY)
    return pl.pallas_call(
        closing_kernel,
        grid=(BLOCKS,),
        in_specs=[
            pl.BlockSpec((count, tile), lambda b: (0, b)),
            once((count, span)),
            once((count, span)),
            once((count, span)),
            pl.BlockSpec((slot_count, tile), lambda b: (0, b)),
            once((slot_count, span)),
            anywhere,
        ],
        out_specs=[pl.BlockSpec((tile, 4 * span), lambda b: (b, 0)), anywhere],
        out_shape=[
            jax.ShapeDtypeStruct((width, 4 * span), BF16),
            jax.ShapeDtypeStruct((PLANES, own_rows, width // 4), BF16),
        ],
        scratch_shapes=scatter_scratch(own_rows, width // 4),
        compiler_params=pltpu.CompilerParams(
            collective_id=collective_id, has_side_effects=True, vmem_limit_bytes=VMEM_BYTES
        ),
        name="closing",
    )(hidden, q, k, v, rows, gated, partial.reshape(PLANES, HALVES, own_rows, width))


def finish_kernel(
    query_ref, all_ref, small_ref, query_grad_ref, kv_grad_ref, out_grad_ref, gains_ref,
    router_first_ref, router_second_ref, landed_ref, *scratch
):
    ride = Ride(small_ref, landed_ref, *scratch)

    @pl.when(pl.program_id(0) == 0)
    def _():
        meet([peer for _, _, peer in ride.moves.made.values()])
        ride.begin(tuple(ride.moves.made))

    span = query_ref.shape[2] // 4
    head_width = query_grad_ref.shape[3]
    pair = span // head_width
    own_rows = query_grad_ref.shape[1]
    for half in range(HALVES):
        landed = query_ref[half, :own_rows, :].astype(F32)
        for head in range(pair):
            at = half * pair + head
            query_grad_ref[0, :, at, :] = landed[:, head * head_width : (head + 1) * head_width]
        out_grad_ref[half] = landed[:, 3 * span :].T

    @pl.when(pl.program_id(0) == 0)
    def _():
        for half in range(HALVES):
            total = sum(
                all_ref[z * HALVES + half, :own_rows, span : 3 * span].astype(F32)
                for z in range(PLANES)
            )
            for kind in range(2):
                for head in range(pair):
                    first = kind * span + head * head_width
                    kv_grad_ref[:, half * pair + head, kind, :] = total[:, first : first + head_width]

    @pl.when(pl.program_id(0) == PLANES - 1)
    def _():
        ride.finish()
        total = sum(landed_ref[place] for place in range(BLOCKS))
        gains_ref[...] = total[:8]
        spare = jnp.zeros((128 - total.shape[0], total.shape[1]), F32)
        columns = jnp.concatenate([total, spare], axis=0).T
        router_first_ref[...] = columns[:own_rows, 2 : 2 + PLANES]
        router_second_ref[...] = columns[:own_rows, 2 + PLANES : 2 + 2 * PLANES]


def finish(landed, small, own_rows, span, heads, head_width, collective_id):
    places, height, width = landed.shape
    return pl.pallas_call(
        finish_kernel,
        grid=(PLANES,),
        in_specs=[
            pl.BlockSpec((HALVES, height, width), lambda e: (e, 0, 0)),
            once((places, height, width)),
            once(small.shape),
        ],
        out_specs=[
            pl.BlockSpec((1, own_rows, heads, head_width), lambda e: (e, 0, 0, 0)),
            pl.BlockSpec((own_rows, heads, 2, head_width), lambda e: (0, 0, 0, 0)),
            pl.BlockSpec((HALVES, span, own_rows), lambda e: (e, 0, 0)),
            pl.BlockSpec((8, small.shape[2]), lambda e: (0, 0)),
            pl.BlockSpec((own_rows, PLANES), lambda e: (0, 0)),
            pl.BlockSpec((own_rows, PLANES), lambda e: (0, 0)),
        ],
        out_shape=[
            jax.ShapeDtypeStruct((PLANES, own_rows, heads, head_width), F32),
            jax.ShapeDtypeStruct((own_rows, heads, 2, head_width), F32),
            jax.ShapeDtypeStruct((places, span, own_rows), F32),
            jax.ShapeDtypeStruct((8, small.shape[2]), F32),
            jax.ShapeDtypeStruct((own_rows, PLANES), F32),
            jax.ShapeDtypeStruct((own_rows, PLANES), F32),
        ],
        scratch_shapes=[pltpu.VMEM(small.shape, F32)] + list(RIDE_SCRATCH),
        compiler_params=pltpu.CompilerParams(
            collective_id=collective_id, has_side_effects=True, vmem_limit_bytes=VMEM_BYTES
        ),
        name="attention_weight_gradients",
    )(landed, landed, small)


def grid_sum(values):
    shape = values.shape
    return lax.all_gather(values.reshape(-1, 128), "grid", axis=0).sum(axis=0).reshape(shape)


def prefix_ranks(member):
    counted = member.astype(BF16)
    width = member.shape[-1]
    before = jnp.arange(width)[:, None] < jnp.arange(width)[None, :]
    return jnp.where(member, dot(counted, before.astype(BF16)).astype(jnp.int32), -1)


def picks(rank):
    return (jnp.arange(CAP, dtype=jnp.int32)[:, None] == rank[..., None, :]).astype(BF16)


def members(first, second):
    names = jnp.arange(PLANES, dtype=first.dtype).reshape((PLANES,) + (1,) * first.ndim)
    return (first[None] == names) | (second[None] == names)


def route_gates(logits, member):
    shown = jnp.where(member, logits, NEGATIVE)
    weights = jnp.where(member, jnp.exp(shown - jnp.max(shown, axis=0, keepdims=True)), 0.0)
    return weights / jnp.sum(weights, axis=0, keepdims=True)


def logits_grad(gates, grad_gates):
    return gates * (grad_gates - jnp.sum(gates * grad_gates, axis=0, keepdims=True))


def exact_first(left, right):
    return lax.dot_general(
        left, right, (((0,), (0,)), ((), ())), precision=lax.Precision.HIGHEST
    )


def exact_last(left, right):
    return lax.dot_general(
        left, right, (((1,), (1,)), ((), ())), precision=lax.Precision.HIGHEST
    )


def norm_sums(grad_hidden, scaled, router, grad_gates, width, gates=None, hidden=None, member=None):
    parts = [
        grad_gates,
        exact_last(router.astype(F32), scaled),
        jnp.sum(grad_hidden * scaled, axis=1)[None],
    ]
    if gates is None:
        parts.append(contract_last(router, hidden))
    parts = grid_sum(jnp.concatenate(parts, axis=0))
    if gates is None:
        gates = route_gates(parts[2 * PLANES + 1 :], member)
    grad_logits = logits_grad(gates, parts[:PLANES])
    inner = parts[2 * PLANES] + jnp.sum(grad_logits * parts[PLANES : 2 * PLANES], axis=0)
    return grad_logits, inner[:, None] / width, gates


def per_device(
    tokens, segment_ids, attention_routes, expert_routes, attention_gain, attention_kv,
    attention_query, attention_out, attention_router, feedforward_gain, feedforward_router,
    expert_gate_up, expert_down, output_grad,
):
    groups = lax.axis_size("t")
    grid_count = lax.axis_size("grid")
    group = lax.axis_index("t")
    plane = lax.axis_index("z")
    place = plane * HALVES + lax.axis_index("x")
    column = lax.axis_index("grid")
    rows, features = tokens.shape
    width_all = features * grid_count
    token_count = BLOCKS * rows
    own_rows = attention_gain.shape[0]
    head_width = attention_kv.shape[3]
    head_pair = attention_kv.shape[1] // HALVES
    span = head_pair * head_width
    hidden_units = expert_gate_up.shape[3] // HALVES

    def mine(array, axis=0):
        return lax.dynamic_slice_in_dim(array, column * features, features, axis)

    def own(array, axis=0):
        return lax.dynamic_slice_in_dim(array, place * rows, rows, axis)

    query_pieces = attention_query.reshape(PLANES, own_rows, HALVES, span).transpose(0, 2, 1, 3)
    kv_pieces = attention_kv.reshape(own_rows, HALVES, head_pair, 2, head_width)
    kv_pieces = kv_pieces.transpose(1, 0, 3, 2, 4).reshape(1, HALVES, own_rows, 2 * span)
    kv_pieces = jnp.broadcast_to(kv_pieces, (PLANES,) + kv_pieces.shape[1:])
    qkv_pieces = jnp.concatenate([query_pieces, kv_pieces], axis=-1)
    out_pieces = attention_out.reshape(BLOCKS, span, own_rows).swapaxes(1, 2)
    first_pieces = jnp.concatenate([out_pieces, qkv_pieces.reshape(BLOCKS, own_rows, 3 * span)], axis=2)
    own_routes = jnp.concatenate([attention_routes, expert_routes], axis=1)
    small = jnp.concatenate(
        [attention_gain[:, None], feedforward_gain[:, None], attention_router, feedforward_router],
        axis=1,
    )
    small = lax.all_gather(small, "t", axis=0).reshape(-1, small.shape[1])
    small = small.T.reshape(small.shape[1], -1)
    spare = jnp.zeros((small.shape[0], features - small.shape[1] % features), BF16)
    small = jnp.concatenate([small, spare], axis=1).reshape(-1, features)
    under = jnp.concatenate([own_routes.T.astype(BF16), small], axis=0)
    under = jnp.pad(under, ((0, -under.shape[0] % 16), (0, 0)))
    everything, first_weight, up_pieces, *down_halves = opened(
        jnp.concatenate([tokens, under], axis=0), first_pieces, expert_gate_up,
        expert_down.reshape(BLOCKS, hidden_units, own_rows), 0, 3,
    )
    first_weight = over_groups(first_weight).reshape(width_all, 4 * span)
    out_weight, qkv_weight = first_weight[:, :span], first_weight[:, span:]
    up_weight = over_groups(exchanged(up_pieces)).reshape(width_all, 2 * hidden_units)
    under = everything[:, :, rows:, :features].reshape(BLOCKS, -1, features).swapaxes(0, 1)
    small = under[4:, :, : groups * own_rows].reshape(-1, BLOCKS, groups, own_rows)
    small = jnp.pad(small.swapaxes(1, 2).reshape(-1, width_all), ((0, 4), (0, 0)))
    gain_first, gain_second = mine(small[0]).astype(F32), mine(small[1]).astype(F32)
    router_first, router_second = mine(small[2:6], 1), mine(small[6:10], 1)

    member_first, member_second = members(under[0], under[1]), members(under[2], under[3])
    own_member_first = lax.dynamic_index_in_dim(member_first, place, 1, keepdims=False)
    own_member_second = lax.dynamic_index_in_dim(member_second, place, 1, keepdims=False)
    rank = prefix_ranks(
        jnp.concatenate(
            [
                lax.dynamic_index_in_dim(member_first, plane, 0, keepdims=False),
                lax.dynamic_index_in_dim(member_second, plane, 0, keepdims=False),
                own_member_first,
                own_member_second,
            ],
            axis=0,
        )
    )
    rank_first, rank_second = rank[:BLOCKS, None], rank[BLOCKS : 2 * BLOCKS, None]
    own_pick_first = picks(rank[2 * BLOCKS : 2 * BLOCKS + PLANES])
    own_pick_second = picks(rank[2 * BLOCKS + PLANES :])
    member_first = member_first.reshape(PLANES, token_count)
    member_second = member_second.reshape(PLANES, token_count)

    def to_slots(values, pick):
        return jnp.einsum("est,tf->esf", pick, values, preferred_element_type=F32).astype(BF16)

    def to_tokens(slots, pick):
        return jnp.einsum("est,esf->etf", pick, slots, preferred_element_type=F32)

    grad_out = output_grad.astype(F32)
    cosine, sine = rope_tables(token_count, head_width)
    cosine, sine = jnp.asarray(cosine), jnp.asarray(sine)
    hidden_first, queries, keys, values, logits_first, inverse_first = project(
        everything, rows, small, first_weight, cosine, sine, span, head_width
    )
    gates_first = route_gates(logits_first[2 : 2 + PLANES], member_first)
    own_gates_first = own(gates_first, 1)
    position = jnp.arange(token_count, dtype=jnp.int32)
    segment = lax.dynamic_slice_in_dim(segment_ids, group * token_count, token_count, 0)
    opens = jnp.concatenate([jnp.ones((1,), jnp.bool_), segment[1:] != segment[:-1]])
    document_start = lax.cummax(jnp.where(opens, position, 0))
    begin = document_start.reshape(BLOCKS, rows)[:, 0] // rows
    table = token_table(
        position, document_start, lax.dynamic_index_in_dim(gates_first, plane, 0, keepdims=False)
    )
    attention_args = (begin, queries, keys, values, rank_first, table)
    attended, gated, gate_slots_first, lse = attention_forward(*attention_args, head_width)
    branch, grad_out_slots = lax.optimization_barrier(
        (contract_last(attended, out_weight).astype(BF16), to_slots(output_grad, own_pick_second))
    )
    branch_slots, down_first = scattered(
        branch, CAP, 2, ride=down_halves[0], share=1
    )
    branch_first = to_tokens(branch_slots, own_pick_first)
    residual = tokens.astype(F32) + jnp.sum(own_gates_first[:, :, None] * branch_first, axis=0)

    square = grid_sum(jnp.sum(residual * residual, axis=1))
    inverse_second = lax.rsqrt(square / width_all + EPSILON)[:, None]
    normed_second = residual * inverse_second
    hidden_second = (normed_second * gain_second).astype(BF16)
    slots_second, down_last = gathered(
        to_slots(hidden_second, own_pick_second), 1, ride=down_halves[1], share=3
    )
    down_weight = [
        over_groups(half).reshape((groups * BLOCKS,) + half.shape[1:]) for half in (down_first, down_last)
    ]
    slots_second = slots_second.reshape(BLOCKS, CAP, width_all)
    gate_pre, up_pre, result, gate_slots_second, inner, grad_slots_second = expert_forward(
        slots_second,
        up_weight,
        down_weight,
        small,
        rank_second,
        jnp.pad(member_second.astype(BF16), ((6, 6), (0, 0))),
        grad_out_slots,
        4,
    )
    grad_slots_second = grad_slots_second.reshape(BLOCKS, CAP, width_all)
    grad_rows, grad_gate_up, grad_down_first, grad_down_last, result_slots = expert_backward(
        gate_pre, up_pre, grad_slots_second, gate_slots_second, up_weight, down_weight, inner, result, 5
    )
    if groups > 1:
        grad_down = jnp.concatenate([grad_down_first, grad_down_last], axis=1)
        grad_down = group_sums(grad_down.reshape(groups, BLOCKS, own_rows, hidden_units))
        grad_down_first, grad_down_last = jnp.split(grad_down, 2, axis=1)
    grad_up, grad_rows, grad_down_first = expert_gradient(
        slots_second.reshape(-1, width_all), grad_gate_up, grad_rows, grad_down_first, 6
    )
    grad_rows, grad_down_last = lax.optimization_barrier((grad_rows, grad_down_last))
    branch_second = to_tokens(result_slots, own_pick_second)

    grad_hidden_second = jnp.sum(to_tokens(grad_rows, own_pick_second), axis=0)
    grad_logits_second, inner_mean, own_gates_second = norm_sums(
        grad_hidden_second, normed_second * gain_second, router_second,
        jnp.sum(branch_second * grad_out[None], axis=2), width_all,
        hidden=hidden_second, member=own_member_second,
    )
    grad_hidden_second = grad_hidden_second + exact_first(
        grad_logits_second, router_second.astype(F32)
    )
    grad_normed = grad_hidden_second * gain_second
    grad_residual = grad_out + inverse_second * (grad_normed - normed_second * inner_mean)

    grad_down_last = exchanged(grad_down_last)
    grad_slots_first = gathered(to_slots(grad_residual.astype(BF16), own_pick_first), 8)
    (
        grad_slots_first, grad_down_last, residual, own_gates_second, branch_second, hidden_second,
        grad_logits_second, grad_hidden_second, normed_second,
    ) = lax.optimization_barrier(
        (
            grad_slots_first, grad_down_last, residual, own_gates_second, branch_second, hidden_second,
            grad_logits_second, grad_hidden_second, normed_second,
        )
    )
    layer_output = residual + jnp.sum(own_gates_second[:, :, None] * branch_second, axis=0)
    layer_output = layer_output.astype(BF16)
    grad_router_second = exact(grad_logits_second, hidden_second.astype(F32))
    grad_gain_second = jnp.sum(grad_hidden_second * normed_second, axis=0)
    grad_slots_first = grad_slots_first.reshape(BLOCKS * CAP, -1)
    grad_up, grad_slots_first = lax.optimization_barrier((grad_up, grad_slots_first))
    grad_up = return_gradients(grad_up.reshape(groups, BLOCKS, own_rows, 2 * hidden_units))
    grad_attended = gate_slots_first * dot(grad_slots_first, out_weight)
    grad_attended = grad_attended.astype(BF16)
    grad_query, grad_keys, grad_values = attention_backward(
        *attention_args, attended, lse, grad_attended, cosine, sine, head_width
    )
    grad_qkv = jnp.concatenate([grad_query, grad_keys, grad_values], axis=1)
    grad_hidden = contract_last(grad_qkv, qkv_weight).astype(BF16)
    grad_first, grad_hidden = closing(
        hidden_first, grad_query, grad_keys, grad_values, grad_slots_first, gated, grad_hidden, 3
    )
    grad_hidden = jnp.sum(grad_hidden.astype(F32), axis=0)
    grad_first, grad_up = lax.optimization_barrier((grad_first, grad_up))
    grad_first = return_gradients(grad_first.reshape(groups, BLOCKS, own_rows, 4 * span))
    expert_gate_up_grad = grad_up.reshape(PLANES, HALVES, own_rows, 2, hidden_units)
    expert_gate_up_grad = expert_gate_up_grad.transpose(0, 2, 3, 1, 4).reshape(expert_gate_up.shape)
    expert_down_grad = jnp.concatenate([grad_down_first, grad_down_last], axis=1)
    expert_down_grad = expert_down_grad.swapaxes(1, 2).reshape(expert_down.shape)

    own_normed = tokens.astype(F32) * own(inverse_first)
    own_hidden = (own_normed * gain_first).astype(BF16)
    grad_logits_first, inner_mean, _ = norm_sums(
        grad_hidden, own_normed * gain_first, router_first,
        jnp.sum(branch_first * grad_residual[None], axis=2), width_all, gates=own_gates_first,
    )
    grad_hidden_first = grad_hidden + exact_first(grad_logits_first, router_first.astype(F32))
    grad_router_first = exact(grad_logits_first, own_hidden.astype(F32))
    grad_gain_first = jnp.sum(grad_hidden_first * own_normed, axis=0)
    grad_normed = grad_hidden_first * gain_first
    input_grad = grad_residual + own(inverse_first) * (grad_normed - own_normed * inner_mean)

    small_grads = jnp.concatenate(
        [grad_gain_first[None], grad_gain_second[None], grad_router_first, grad_router_second],
        axis=0,
    )
    small_grads = lax.all_gather(small_grads, "grid", axis=1, tiled=True)
    if groups > 1:
        small_grads = lax.psum(small_grads, "t")
    small_grads = small_grads.reshape(-1, groups, BLOCKS, own_rows)
    small_grads = lax.dynamic_index_in_dim(small_grads, group, 1, keepdims=False).swapaxes(0, 1)
    small_grads = jnp.pad(small_grads, ((0, 0), (0, 6), (0, -own_rows % 128)))
    (
        attention_query_grad, attention_kv_grad, attention_out_grad, gain_grads,
        attention_router_grad, feedforward_router_grad,
    ) = finish(grad_first, small_grads, own_rows, span, attention_kv.shape[1], head_width, 7)
    attention_out_grad = attention_out_grad.reshape(attention_out.shape)
    return (
        layer_output,
        input_grad.astype(BF16),
        gain_grads[0, :own_rows],
        attention_kv_grad,
        attention_query_grad.astype(F32),
        attention_out_grad.astype(F32),
        attention_router_grad,
        gain_grads[1, :own_rows],
        feedforward_router_grad,
        expert_gate_up_grad.astype(F32),
        expert_down_grad.astype(F32),
    )


def solution(mesh):
    groups = mesh.shape["wide"] // BLOCKS
    shape = (groups, PLANES, HALVES, mesh.shape["grid"])
    inner_mesh = Mesh(mesh.devices.reshape(shape), ("t", "z", "x", "grid"))
    wide = ("t", "z", "x")
    in_specs = (
        P(wide, "grid"),
        P(),
        P(wide, None),
        P(wide, None),
        P(wide),
        P(wide, "grid", None, None),
        P(None, wide, "grid", None),
        P(None, "grid", None, wide),
        P(wide, None),
        P(wide),
        P(wide, None),
        P(None, wide, None, "grid"),
        P(None, "grid", wide),
        P(wide, "grid"),
    )
    out_specs = (
        P(wide, "grid"),
        P(wide, "grid"),
        P(wide),
        P(wide, "grid", None, None),
        P(None, wide, "grid", None),
        P(None, "grid", None, wide),
        P(wide, None),
        P(wide),
        P(wide, None),
        P(None, wide, None, "grid"),
        P(None, "grid", wide),
    )
    return jax.shard_map(
        per_device, mesh=inner_mesh, in_specs=in_specs, out_specs=out_specs, check_vma=False
    )
```

```python
import functools
import math

import jax
import jax.numpy as jnp
import numpy as np
from jax import lax
from jax.experimental import pallas as pl
from jax.experimental.layout import Layout, with_layout_constraint
from jax.experimental.pallas import tpu as pltpu
from jax.sharding import Mesh, PartitionSpec as P

CAP = 320
PLANES = 4
HALVES = 2
BLOCKS = PLANES * HALVES
EPSILON = 1e-05
ROPE_BASE = 10000.0
NEGATIVE = -1e30
BF16 = jnp.bfloat16
F32 = jnp.float32
PLACES = ("z", "x")
MESH = pl.DeviceIdType.MESH
VMEM_BYTES = 56 * 1024 * 1024


def rope_tables(token_count, width):
    half = width // 2
    frequency = np.float32(ROPE_BASE) ** (-np.arange(half, dtype=np.float32) / np.float32(half))
    angles = np.arange(token_count, dtype=np.float32)[:, None] * frequency.astype(np.float32)[None, :]
    cosine, sine = np.cos(angles).astype(np.float32), np.sin(angles).astype(np.float32)
    return np.concatenate([cosine, cosine], axis=1), np.concatenate([-sine, sine], axis=1)


def turned(values, cosine, sine):
    return values * cosine + pltpu.roll(values, values.shape[1] // 2, 1) * sine


def dot(left, right):
    return jnp.dot(left, right, preferred_element_type=F32)


def contract_first(left, right):
    return lax.dot_general(left, right, (((0,), (0,)), ((), ())), preferred_element_type=F32)


def contract_last(left, right):
    return lax.dot_general(left, right, (((1,), (1,)), ((), ())), preferred_element_type=F32)


def exact(left, right):
    return jnp.dot(left, right, precision=lax.Precision.HIGHEST)


def project_kernel(
    tokens_ref, small_ref, query_weight_ref, shared_weight_ref, cos_ref, sin_ref,
    hidden_ref, q_ref, k_ref, v_ref, logits_ref, inverse_ref, *, head_width
):
    x = tokens_ref[0, 0].astype(F32)
    inverse = lax.rsqrt(jnp.mean(x * x, axis=1, keepdims=True) + EPSILON)
    inverse_ref[...] = inverse
    hidden = (x * inverse * small_ref[:1, :].astype(F32)).astype(BF16)
    hidden_ref[...] = hidden
    logits_ref[...] = contract_last(small_ref[...], hidden)
    queries = dot(hidden, query_weight_ref[...])
    shared = dot(hidden, shared_weight_ref[...])
    span = q_ref.shape[1]
    cosine, sine = cos_ref[...], sin_ref[...]
    for head in range(span // head_width):
        at = slice(head * head_width, (head + 1) * head_width)
        q_ref[:, at] = turned(queries[:, at], cosine, sine).astype(BF16)
        k_ref[:, at] = turned(shared[:, at], cosine, sine).astype(BF16)
    v_ref[...] = shared[:, span:].astype(BF16)


def project(tokens, rows, small, weight, cosine, sine, span, head_width):
    width = tokens.shape[-1]
    token_count = BLOCKS * rows
    whole = lambda b: (0, 0)
    block = lambda b: (b, 0)
    return pl.pallas_call(
        functools.partial(project_kernel, head_width=head_width),
        grid=(BLOCKS,),
        in_specs=[
            pl.BlockSpec((1, 1, rows, width), lambda b: (b // HALVES, b % HALVES, 0, 0)),
            pl.BlockSpec(small.shape, whole),
            pl.BlockSpec((width, span), lambda b: (0, 1)),
            pl.BlockSpec((width, 2 * span), lambda b: (0, 1)),
            pl.BlockSpec((rows, head_width), block),
            pl.BlockSpec((rows, head_width), block),
        ],
        out_specs=[
            pl.BlockSpec((rows, width), block),
            pl.BlockSpec((rows, span), block),
            pl.BlockSpec((rows, span), block),
            pl.BlockSpec((rows, span), block),
            pl.BlockSpec((small.shape[0], rows), lambda b: (0, b)),
            pl.BlockSpec((rows, 1), block),
        ],
        out_shape=[
            jax.ShapeDtypeStruct((token_count, width), BF16),
            jax.ShapeDtypeStruct((token_count, span), BF16),
            jax.ShapeDtypeStruct((token_count, span), BF16),
            jax.ShapeDtypeStruct((token_count, span), BF16),
            jax.ShapeDtypeStruct((small.shape[0], token_count), F32),
            jax.ShapeDtypeStruct((token_count, 1), F32),
        ],
        compiler_params=pltpu.CompilerParams(vmem_limit_bytes=VMEM_BYTES),
        name="project",
    )(tokens, small, weight, weight, cosine, sine)


def attention_scores(q, k_ref, low_bound, high_bound, tile, tile_rows, scaling):
    rows = pl.ds(pl.multiple_of(tile * tile_rows, tile_rows), tile_rows)
    keys = k_ref[rows, :]
    scores = contract_last(q, keys) * scaling
    column = tile * tile_rows + lax.broadcasted_iota(jnp.int32, scores.shape, 1)
    allowed = (column >= low_bound) & (column <= high_bound)
    return rows, keys, scores, allowed


def slots_of_block(rank_ref, table_ref, cap):
    rows = table_ref.shape[1]
    pick = (lax.broadcasted_iota(jnp.int32, (cap, rows), 0) == rank_ref[0]).astype(BF16)
    made = contract_last(pick, table_ref[...])
    base = pl.program_id(1) * rows
    filled = made[:, 4:5] > 0.5
    low = (64.0 * made[:, 2:3] + made[:, 3:4]).astype(jnp.int32)
    high = (64.0 * made[:, 0:1] + made[:, 1:2]).astype(jnp.int32)
    gate = made[:, 5:6] + made[:, 6:7] + made[:, 7:8]
    return pick, jnp.where(filled, low, base), jnp.where(filled, high, base), gate


def token_table(position, document_start, gate):
    first = gate.astype(BF16).astype(F32)
    second = (gate - first).astype(BF16).astype(F32)
    rows = [
        position // 64, position % 64, document_start // 64, document_start % 64,
        jnp.ones_like(gate), first, second, gate - first - second,
    ]
    return jnp.pad(jnp.stack([row.astype(BF16) for row in rows]), ((0, 8), (0, 0)))


def attention_forward_kernel(
    begin_ref, q_ref, k_ref, v_ref, rank_ref, table_ref, out_ref, gated_ref, gate_ref, lse_ref, *,
    scaling
):
    block = pl.program_id(1)
    cap, width = out_ref.shape
    tile_rows = q_ref.shape[0]
    pick, low_bound, high_bound, gate = slots_of_block(rank_ref, table_ref, cap)
    q = dot(pick, q_ref[...]).astype(BF16)

    def step(tile, carried):
        largest, total, summed = carried
        rows, _, scores, allowed = attention_scores(
            q, k_ref, low_bound, high_bound, tile, tile_rows, scaling
        )
        scores = jnp.where(allowed, scores, NEGATIVE)
        new_largest = jnp.maximum(largest, jnp.max(scores, axis=1, keepdims=True))
        weights = jnp.where(allowed, jnp.exp(scores - new_largest), 0.0)
        shrink = jnp.exp(largest - new_largest)
        return (
            new_largest,
            total * shrink + jnp.sum(weights, axis=1, keepdims=True),
            summed * shrink + dot(weights.astype(BF16), v_ref[rows, :]),
        )

    largest, total, summed = lax.fori_loop(
        begin_ref[block],
        block + 1,
        step,
        (jnp.full((cap, 1), NEGATIVE, F32), jnp.zeros((cap, 1), F32), jnp.zeros((cap, width), F32)),
    )
    attended = (summed / total).astype(BF16)
    out_ref[...] = attended
    gated_ref[...] = (gate * attended.astype(F32)).astype(BF16)
    gate_ref[...] = gate
    lse_ref[0] = largest + jnp.log(total)


def attention_backward_kernel(
    begin_ref, q_ref, k_ref, v_ref, rank_ref, table_ref, out_ref, lse_ref, grad_ref,
    cos_ref, sin_ref, dq_ref, dk_ref, dv_ref, dk_sum, dv_sum, *, scaling
):
    block = pl.program_id(1)
    cap, width = out_ref.shape
    tile_rows = q_ref.shape[0]
    pick, low_bound, high_bound, _ = slots_of_block(rank_ref, table_ref, cap)
    q = dot(pick, q_ref[...]).astype(BF16)
    grad = grad_ref[...]
    delta = jnp.sum(grad.astype(F32) * out_ref[...].astype(F32), axis=1, keepdims=True)
    lse = lse_ref[0]

    @pl.when(block == 0)
    def _():
        dk_sum[...] = jnp.zeros_like(dk_sum)
        dv_sum[...] = jnp.zeros_like(dv_sum)

    def step(tile, dq):
        rows, keys, scores, allowed = attention_scores(
            q, k_ref, low_bound, high_bound, tile, tile_rows, scaling
        )
        chances = jnp.where(allowed, jnp.exp(scores - lse), 0.0)
        dv_sum[rows, :] += contract_first(chances.astype(BF16), grad)
        grad_chances = contract_last(grad, v_ref[rows, :])
        grad_scores = (chances * (grad_chances - delta)).astype(BF16)
        dk_sum[rows, :] += contract_first(grad_scores, q) * scaling
        return dq + dot(grad_scores, keys)

    dq = lax.fori_loop(begin_ref[block], block + 1, step, jnp.zeros((cap, width), F32)) * scaling
    high = dq.astype(BF16)
    rest = (dq - high.astype(F32)).astype(BF16)
    dq_tokens = contract_first(pick, high) + contract_first(pick, rest)
    own = pl.ds(pl.multiple_of(block * tile_rows, tile_rows), tile_rows)
    dq_ref[...] = turned(dq_tokens, cos_ref[own, :], -sin_ref[own, :]).astype(BF16)

    @pl.when(block == BLOCKS - 1)
    def _():
        def finish(tile, nothing):
            rows = pl.ds(pl.multiple_of(tile * tile_rows, tile_rows), tile_rows)
            dk_ref[rows, :] = turned(dk_sum[rows, :], cos_ref[rows, :], -sin_ref[rows, :]).astype(BF16)
            dv_ref[rows, :] = dv_sum[rows, :].astype(BF16)
            return nothing

        lax.fori_loop(0, BLOCKS, finish, 0)


def attention_specs(row_count, token_count, width):
    return dict(
        q=pl.BlockSpec((row_count, width), lambda h, b, s: (b, h)),
        k=pl.BlockSpec((token_count, width), lambda h, b, s: (0, h)),
        rank=pl.BlockSpec((1, 1, row_count), lambda h, b, s: (b, 0, 0)),
        rows=pl.BlockSpec((16, row_count), lambda h, b, s: (0, b)),
        gate=pl.BlockSpec((CAP, 1), lambda h, b, s: (b, 0)),
        slots=pl.BlockSpec((CAP, width), lambda h, b, s: (b, h)),
        table=pl.BlockSpec((token_count, width), lambda h, b, s: (0, 0)),
        lse=pl.BlockSpec((1, CAP, 1), lambda h, b, s: (h, b, 0)),
    )


def attention_forward(begin, q, k, v, rank, table, width):
    token_count, heads = q.shape[0], q.shape[1] // width
    row_count = token_count // BLOCKS
    s = attention_specs(row_count, token_count, width)
    return pl.pallas_call(
        functools.partial(attention_forward_kernel, scaling=1.0 / math.sqrt(width)),
        grid_spec=pltpu.PrefetchScalarGridSpec(
            num_scalar_prefetch=1,
            grid=(heads, BLOCKS),
            in_specs=[s["q"], s["k"], s["k"], s["rank"], s["rows"]],
            out_specs=[s["slots"], s["slots"], s["gate"], s["lse"]],
        ),
        out_shape=[
            jax.ShapeDtypeStruct((BLOCKS * CAP, heads * width), BF16),
            jax.ShapeDtypeStruct((BLOCKS * CAP, heads * width), BF16),
            jax.ShapeDtypeStruct((BLOCKS * CAP, 1), F32),
            jax.ShapeDtypeStruct((heads, BLOCKS * CAP, 1), F32),
        ],
        compiler_params=pltpu.CompilerParams(vmem_limit_bytes=VMEM_BYTES),
        name="attention_forward",
    )(begin, q, k, v, rank, table)


def attention_backward(begin, q, k, v, rank, table, out, lse, grad, cosine, sine, width):
    token_count, heads = q.shape[0], q.shape[1] // width
    row_count = token_count // BLOCKS
    s = attention_specs(row_count, token_count, width)
    return pl.pallas_call(
        functools.partial(attention_backward_kernel, scaling=1.0 / math.sqrt(width)),
        grid_spec=pltpu.PrefetchScalarGridSpec(
            num_scalar_prefetch=1,
            grid=(heads, BLOCKS),
            in_specs=[
                s["q"], s["k"], s["k"], s["rank"], s["rows"],
                s["slots"], s["lse"], s["slots"], s["table"], s["table"],
            ],
            out_specs=[s["q"], s["k"], s["k"]],
            scratch_shapes=[pltpu.VMEM((token_count, width), F32)] * 2,
        ),
        out_shape=[
            jax.ShapeDtypeStruct((token_count, heads * width), BF16),
            jax.ShapeDtypeStruct((token_count, heads * width), BF16),
            jax.ShapeDtypeStruct((token_count, heads * width), BF16),
        ],
        compiler_params=pltpu.CompilerParams(vmem_limit_bytes=VMEM_BYTES),
        name="attention_backward",
    )(begin, q, k, v, rank, table, out, lse, grad, cosine, sine)


def pack_up_kernel(weight_ref, pieces_ref):
    units = pieces_ref.shape[2] // 2
    both = weight_ref[0].astype(F32)
    gate, up = both[:, 0, :], both[:, 1, :]
    for half in range(HALVES):
        at = slice(half * units, (half + 1) * units)
        pieces_ref[half] = jnp.concatenate([gate[:, at], up[:, at]], axis=1).astype(BF16)


def pack_down_kernel(weight_ref, first_ref, last_ref):
    turned_rows = weight_ref[0].astype(F32).T.astype(BF16)
    middle = first_ref.shape[1]
    first_ref[0] = turned_rows[:middle]
    last_ref[0] = turned_rows[middle:]


def row_major(array):
    return with_layout_constraint(array, Layout(major_to_minor=tuple(range(array.ndim))))


def exchanged(pieces):
    return row_major(lax.all_to_all(row_major(pieces), PLACES, 0, 0, tiled=True))


def over_groups(landed):
    return lax.all_gather(landed, "t", axis=0, tiled=False)


def group_sums(pieces):
    return lax.psum_scatter(pieces, "t", scatter_dimension=0, tiled=False)


def return_gradients(pieces):
    return exchanged(group_sums(pieces))


def other_core(column):
    return column + 1 - 2 * (column % 2)


def crossed(plane, j):
    return (plane, plane + 1 - 2 * (plane % 2), (plane + 2) % 4, 3 - plane)[j]


def meet(peers):
    barrier = pltpu.get_barrier_semaphore()
    for peer in peers:
        pl.semaphore_signal(barrier, inc=1, device_id=peer, device_id_type=MESH)
    pl.semaphore_wait(barrier, len(peers))


def partners():
    plane, half, column = lax.axis_index("z"), lax.axis_index("x"), lax.axis_index("grid")
    planes = [{"z": crossed(plane, j)} for j in range(PLANES)]
    along_x, along_y = {"x": 1 - half}, {"grid": (column + 2) % 4}
    core = {"grid": other_core(column)}
    return plane, half, column, planes, along_x, along_y, core


class Moves:
    def __init__(self, send, recv):
        self.send, self.recv, self.made = send, recv, {}

    def add(self, index, source, target, peer):
        self.made[index] = (source, target, peer)

    def copy(self, index, source, target, peer):
        return pltpu.make_async_remote_copy(
            src_ref=source, dst_ref=target, send_sem=self.send.at[index],
            recv_sem=self.recv.at[index], device_id=peer, device_id_type=MESH,
        )

    def start(self, index):
        self.copy(index, *self.made[index]).start()

    def arrived(self, index, target, peer):
        self.copy(index, target, target, peer).wait_recv()

    def all_sent(self):
        for index in self.made:
            self.copy(index, *self.made[index]).wait_send()


class Ride:
    def __init__(self, pieces_ref, landed_ref, send, recv, local, columns=None):
        if columns is None:
            columns = pl.ds(0, pieces_ref.shape[2])
        rows = pl.ds(0, pieces_ref.shape[1])
        plane, half = lax.axis_index("z"), lax.axis_index("x")
        self.moves = Moves(send, recv)
        self.landings = {}
        own = plane * HALVES + half
        self.keep = pltpu.make_async_copy(pieces_ref.at[own], landed_ref.at[own], local)
        self.peers = []
        for dz in range(PLANES):
            for dx in range(HALVES):
                index = dz * HALVES + dx
                if index == 0:
                    continue
                at_half = 1 - half if dx else half
                peer = {"z": crossed(plane, dz), "x": at_half}
                other = crossed(plane, dz) * HALVES + at_half
                source = pieces_ref.at[other, rows, columns]
                self.moves.add(index, source, landed_ref.at[own, rows, columns], peer)
                self.landings[index] = (landed_ref.at[other, rows, columns], peer)
                if dz and dx:
                    self.peers.append(peer)

    def begin(self, first=(4, 6, 2)):
        self.keep.start()
        for index in first:
            self.moves.start(index)

    def go_on(self, number, plan=((5,), (7,), (3,), (1,))):
        for index in plan[number] if number < len(plan) else ():
            self.moves.start(index)

    def finish(self):
        for index, (landing, peer) in self.landings.items():
            self.moves.arrived(index, landing, peer)
        self.moves.all_sent()
        self.keep.wait()


RIDE_SCRATCH = (
    pltpu.SemaphoreType.DMA((8,)),
    pltpu.SemaphoreType.DMA((8,)),
    pltpu.SemaphoreType.DMA,
)


def run_with_ride(steps, ride):
    steps[0]()
    if ride is not None:
        ride.begin()
    for number, step in enumerate(steps[1:-1]):
        step()
        if ride is not None:
            ride.go_on(number)
    steps[-1]()
    if ride is not None:
        ride.finish()


def gather_parts(slots_ref, out_ref, send, recv, local, same, share=2, more=(), chain=None):
    plane, half, column, planes, along_x, along_y, core = partners()
    cap, width = slots_ref.shape[-2:]
    middle = cap * share // 64 * 16
    y_column, core_column = (column + 2) % 4, other_core(column)
    core_y = (core_column + 2) % 4
    sources = [crossed(plane, j) for j in range(PLANES)]
    moves = Moves(send, recv)

    def piece(source, at_half, at_column, first=0, count=cap):
        columns = pl.ds(pl.multiple_of(at_column * width, width), width)
        return out_ref.at[source, at_half, pl.ds(first, count), columns]

    def slots_for(j):
        return slots_ref if same else slots_ref.at[sources[j]]

    keep = pltpu.make_async_copy(slots_for(0), piece(plane, half, column), local)
    for j in range(PLANES):
        source = sources[j]
        place = piece(source, half, column)
        if j and chain is None:
            moves.add(j, slots_for(j), piece(plane, half, column), planes[j])
        here = place if j else slots_for(0)
        moves.add(4 + j, here, place, along_x)
        moves.add(8 + j, here, place, along_y)
        moves.add(12 + j, here, place, core)
        from_x, from_y = piece(source, 1 - half, column), piece(source, half, y_column)
        first = piece(source, 1 - half, column, 0, middle)
        last = piece(source, half, y_column, middle, cap - middle)
        diagonal = piece(source, 1 - half, y_column)
        moves.add(16 + j, first, first, along_y)
        moves.add(20 + j, from_x, from_x, core)
        moves.add(24 + j, last, last, along_x)
        moves.add(28 + j, from_y, from_y, core)
        moves.add(32 + j, diagonal, diagonal, core)

    def begin():
        meet(planes[1:] + [along_x, along_y, core] + list(more))
        if chain is None:
            for j in (1, 3, 2):
                moves.start(j)
        else:
            chain.begin()
        keep.start()

    def spread(j):
        if j and chain is None:
            moves.arrived(j, piece(sources[j], half, column), planes[j])
        elif j:
            chain.arrived(j)
        for index in (4, 8, 12):
            moves.start(index + j)

    def forward(j):
        moves.arrived(4 + j, piece(sources[j], 1 - half, column), along_x)
        moves.start(16 + j)
        moves.start(20 + j)
        moves.arrived(8 + j, piece(sources[j], half, y_column), along_y)
        moves.start(24 + j)
        moves.start(28 + j)

    def cross(j):
        moves.arrived(16 + j, piece(sources[j], 1 - half, y_column, 0, middle), along_y)
        moves.arrived(24 + j, piece(sources[j], 1 - half, y_column, middle, cap - middle), along_x)
        moves.start(32 + j)

    def finish():
        for j in order:
            moves.arrived(12 + j, piece(sources[j], half, core_column), core)
            moves.arrived(20 + j, piece(sources[j], 1 - half, core_column), core)
            moves.arrived(28 + j, piece(sources[j], half, core_y), core)
            moves.arrived(32 + j, piece(sources[j], 1 - half, core_y), core)
        moves.all_sent()
        keep.wait()

    order = (0, 1, 3, 2)
    return begin, spread, forward, cross, finish, order


def gather_steps(*refs, **settings):
    begin, spread, forward, cross, finish, order = gather_parts(*refs, **settings)

    def step(number):
        if number < len(order):
            spread(order[number])
        if 0 <= number - 1 < len(order):
            forward(order[number - 1])
        if 0 <= number - 2 < len(order):
            cross(order[number - 2])

    return [begin] + [functools.partial(step, number) for number in range(len(order) + 2)] + [finish]


class Chain:
    def __init__(self, view, source, send, recv):
        plane = lax.axis_index("z")
        self.inner = (plane == 1) | (plane == 2)
        near, far = {"z": crossed(plane, 1)}, {"z": crossed(plane, 3)}
        self.views = [view(crossed(plane, j)) for j in range(PLANES)]
        self.send, self.recv = send, recv
        self.near_own = (0, 1, source, self.views[0], near)
        self.far_own = (1, 3, source, self.views[0], far)
        self.on_arrival = {
            1: (2, 2, self.views[1], self.views[1], far),
            3: (3, 2, self.views[3], self.views[3], near),
            2: (4, 3, self.views[2], self.views[2], near),
        }

    def copy(self, at_send, at_recv, source, target, peer):
        return pltpu.make_async_remote_copy(
            src_ref=source, dst_ref=target, send_sem=self.send.at[at_send],
            recv_sem=self.recv.at[at_recv], device_id=peer, device_id_type=MESH,
        )

    def begin(self):
        self.copy(*self.near_own).start()

        @pl.when(self.inner)
        def _():
            self.copy(*self.far_own).start()

    def arrived(self, j):
        place = self.views[j]
        self.copy(0, j, place, place, self.near_own[-1]).wait_recv()

        @pl.when(self.inner)
        def _():
            self.copy(*self.on_arrival[j]).start()

    def finish(self):
        self.copy(*self.near_own).wait_send()

        @pl.when(self.inner)
        def _():
            self.copy(*self.far_own).wait_send()
            for made in self.on_arrival.values():
                self.copy(*made).wait_send()


CHAIN_SCRATCH = (pltpu.SemaphoreType.DMA((5,)), pltpu.SemaphoreType.DMA((4,)))


def opening_kernel(
    tokens_ref, pieces_ref, up_ref, down_ref, out_ref, landed_ref, up_pieces_ref, first_ref,
    last_ref, send, recv, local, ride_send, ride_recv,
    ride_local, hop_send, hop_recv, *chain_sems, share
):
    plane, half, column = lax.axis_index("z"), lax.axis_index("x"), lax.axis_index("grid")
    width = tokens_ref.shape[1]
    middle = pieces_ref.shape[2] // 2
    left, right = pl.ds(0, middle), pl.ds(middle, middle)
    rows = pl.ds(0, pieces_ref.shape[1])
    along_x = {"x": 1 - half}

    def tokens_of(source):
        columns = pl.ds(pl.multiple_of(column * width, width), width)
        return out_ref.at[source, half, pl.ds(0, tokens_ref.shape[0]), columns]

    def shared_of(at_half):
        return lambda source: landed_ref.at[source * HALVES + at_half, rows, right]

    own = plane * HALVES + half
    tokens = Chain(tokens_of, tokens_ref, *chain_sems[:2])
    here = Chain(shared_of(half), pieces_ref.at[own, rows, right], *chain_sems[2:4])
    there = Chain(shared_of(1 - half), shared_of(1 - half)(plane), *chain_sems[4:])
    ride = Ride(pieces_ref, landed_ref, ride_send, ride_recv, ride_local, left)
    hop = pltpu.make_async_remote_copy(
        src_ref=pieces_ref.at[plane * HALVES + 1 - half, rows, right],
        dst_ref=landed_ref.at[own, rows, right],
        send_sem=hop_send, recv_sem=hop_recv, device_id=along_x, device_id_type=MESH,
    )
    landing = shared_of(1 - half)(plane)
    hop_here = pltpu.make_async_remote_copy(
        src_ref=landing, dst_ref=landing, send_sem=hop_send, recv_sem=hop_recv,
        device_id=along_x, device_id_type=MESH,
    )
    begin, spread, forward, cross, finish, _ = gather_parts(
        tokens_ref, out_ref, send, recv, local, True, share, ride.peers, tokens
    )

    def first():
        begin()
        ride.keep.start()
        spread(0)
        hop.start()
        here.begin()

    def second():
        spread(1)
        forward(0)
        ride.moves.start(2)

    def third():
        spread(3)
        forward(1)
        cross(0)
        hop_here.wait_recv()
        there.begin()
        here.arrived(1)

    def fourth():
        spread(2)
        forward(3)
        cross(1)
        ride.moves.start(6)
        ride.moves.start(4)
        here.arrived(3)
        there.arrived(1)

    def fifth():
        forward(2)
        cross(3)
        for index in (3, 7, 5, 1):
            ride.moves.start(index)
        here.arrived(2)
        there.arrived(3)
        cross(2)
        there.arrived(2)
        finish()
        ride.finish()
        hop.wait_send()
        for chain in (tokens, here, there):
            chain.finish()

    def compute():
        pack_up_kernel(up_ref, up_pieces_ref)
        pack_down_kernel(down_ref, first_ref, last_ref)

    carry([first], [second, third, fourth, fifth], (3, 6, 7, 7), compute)


def opened(tokens, pieces, up, down, collective_id, share):
    rows, width = tokens.shape
    experts, own_rows, _, units = up.shape
    places = experts * HALVES
    tile = own_rows // 2
    down_half = (places, own_rows // 2, units // HALVES)
    anywhere = pl.BlockSpec(memory_space=pl.ANY)
    half = pl.BlockSpec((1,) + down_half[1:], lambda p: (p, 0, 0))
    return pl.pallas_call(
        functools.partial(opening_kernel, share=share),
        grid=(places,),
        in_specs=[
            anywhere,
            anywhere,
            pl.BlockSpec((1, tile, 2, units), lambda p: (p // 2, p % 2, 0, 0)),
            pl.BlockSpec((1,) + down.shape[1:], lambda p: (p, 0, 0)),
        ],
        out_specs=[
            anywhere,
            anywhere,
            pl.BlockSpec((HALVES, tile, units), lambda p: (p // 2, p % 2, 0)),
            half,
            half,
        ],
        out_shape=[
            jax.ShapeDtypeStruct((PLANES, HALVES, rows, 4 * width), BF16),
            jax.ShapeDtypeStruct(pieces.shape, BF16),
            jax.ShapeDtypeStruct((places, own_rows, units), BF16),
            jax.ShapeDtypeStruct(down_half, BF16),
            jax.ShapeDtypeStruct(down_half, BF16),
        ],
        scratch_shapes=list(GATHER_SCRATCH) + list(RIDE_SCRATCH)
        + [pltpu.SemaphoreType.DMA, pltpu.SemaphoreType.DMA] + list(CHAIN_SCRATCH) * 3,
        compiler_params=pltpu.CompilerParams(
            collective_id=collective_id, has_side_effects=True, vmem_limit_bytes=VMEM_BYTES
        ),
        name="open_rows",
    )(tokens, pieces, up, down)


GATHER_SCRATCH = (
    pltpu.SemaphoreType.DMA((36,)),
    pltpu.SemaphoreType.DMA((36,)),
    pltpu.SemaphoreType.DMA,
)


def gather_kernel(*refs, same, share, rides):
    if rides:
        slots_ref, pieces_ref, out_ref, landed_ref = refs[:4]
        ride = Ride(pieces_ref, landed_ref, *refs[7:])
        scratch = refs[4:7]
    else:
        slots_ref, out_ref = refs[:2]
        ride, scratch = None, refs[2:]
    more = ride.peers if rides else ()
    run_with_ride(gather_steps(slots_ref, out_ref, *scratch, same, share, more), ride)


def gathered(slots, collective_id, ride=None, share=2):
    rows, width = slots.shape[-2:]
    rides = () if ride is None else (ride,)
    anywhere = pl.BlockSpec(memory_space=pl.ANY)
    out = pl.pallas_call(
        functools.partial(gather_kernel, same=slots.ndim == 2, share=share, rides=len(rides)),
        out_shape=[jax.ShapeDtypeStruct((PLANES, HALVES, rows, 4 * width), BF16)]
        + [jax.ShapeDtypeStruct(r.shape, BF16) for r in rides],
        in_specs=[anywhere] * (1 + len(rides)),
        out_specs=[anywhere] * (1 + len(rides)),
        scratch_shapes=list(GATHER_SCRATCH) + list(RIDE_SCRATCH) * len(rides),
        compiler_params=pltpu.CompilerParams(collective_id=collective_id, has_side_effects=True),
        name="gather_rows",
    )(slots, *rides)
    return out if rides else out[0]


def scatter_steps(
    partial_ref, out_ref, own, other, crossing, side, send, recv, load, share=2, more=()
):
    plane, half, column, planes, along_x, along_y, core = partners()
    cap, width = out_ref.shape[-2:]
    middle = cap * share // 64 * 16
    chunk = 32 if middle % 32 == 0 and cap % 32 == 0 else 16
    y_column, core_column = (column + 2) % 4, other_core(column)
    core_y = (core_column + 2) % 4
    halves = (half, 1 - half, half, 1 - half)
    own_columns = (column, column, y_column, y_column)
    core_columns = (core_column, core_column, core_y, core_y)
    moves = Moves(send, recv)
    first, last = pl.ds(0, middle), pl.ds(middle, cap - middle)

    def part(j, q, at_columns):
        columns = pl.ds(pl.multiple_of(at_columns[q] * width, width), width)
        return partial_ref.at[crossed(plane, j), halves[q], :, columns]

    def loading(j, q):
        return pltpu.make_async_copy(part(j, q, own_columns), own.at[j, q], load.at[4 * j + q])

    keep = pltpu.make_async_copy(own.at[0, 0], out_ref.at[plane], load.at[16])
    for j in range(PLANES):
        for q in range(4):
            moves.add(4 * j + q, part(j, q, core_columns), other.at[j, q], core)
        moves.add(16 + j, own.at[j, 3, first], crossing.at[j, first], along_x)
        moves.add(20 + j, own.at[j, 3, last], crossing.at[j, last], along_y)
        moves.add(24 + j, own.at[j, 2], side.at[j, 1], along_y)
        moves.add(28 + j, own.at[j, 1], side.at[j, 0], along_x)
        if j:
            moves.add(32 + j, own.at[j, 0], out_ref.at[plane], planes[j])

    def add(j, q, begin_row, count, terms):
        def step(i, nothing):
            rows = pl.ds(pl.multiple_of(begin_row + i * chunk, chunk), chunk)
            total = own[j, q, rows, :].astype(F32)
            for ref, index in terms:
                total = total + ref[index + (rows, slice(None))].astype(F32)
            own[j, q, rows, :] = total.astype(BF16)
            return nothing

        lax.fori_loop(0, count // chunk, step, 0)

    def chip_sum(j, q):
        moves.arrived(4 * j + q, other.at[j, q], core)
        loading(j, q).wait()
        add(j, q, 0, cap, [(other, (j, q))])

    def stage_one(j):
        chip_sum(j, 3)
        moves.start(16 + j)
        moves.start(20 + j)
        chip_sum(j, 2)
        chip_sum(j, 1)
        chip_sum(j, 0)

    def stage_two(j):
        moves.arrived(16 + j, crossing.at[j, first], along_x)
        add(j, 2, 0, middle, [(crossing, (j,))])
        moves.start(24 + j)
        moves.arrived(20 + j, crossing.at[j, last], along_y)
        add(j, 1, middle, cap - middle, [(crossing, (j,))])
        moves.start(28 + j)

    def stage_three(j):
        moves.arrived(24 + j, side.at[j, 1], along_y)
        moves.arrived(28 + j, side.at[j, 0], along_x)
        add(j, 0, 0, cap, [(side, (j, 0)), (side, (j, 1))])
        if j:
            moves.start(32 + j)
        else:
            keep.start()

    order = (2, 3, 1, 0)

    def begin():
        meet(planes[1:] + [along_x, along_y, core] + list(more))
        for j in order:
            for q in (3, 2, 1, 0):
                moves.start(4 * j + q)
                loading(j, q).start()

    def step(number):
        if number < len(order):
            stage_one(order[number])
        if 0 <= number - 1 < len(order):
            stage_two(order[number - 1])
        if 0 <= number - 2 < len(order):
            stage_three(order[number - 2])

    def finish():
        for j in range(1, PLANES):
            moves.arrived(32 + j, out_ref.at[crossed(plane, j)], planes[j])
        moves.all_sent()
        keep.wait()

    return [begin] + [functools.partial(step, number) for number in range(len(order) + 2)] + [finish]


def scatter_scratch(rows, width):
    return [
        pltpu.VMEM((PLANES, 4, rows, width), BF16),
        pltpu.VMEM((PLANES, 4, rows, width), BF16),
        pltpu.VMEM((PLANES, rows, width), BF16),
        pltpu.VMEM((PLANES, 2, rows, width), BF16),
        pltpu.SemaphoreType.DMA((36,)),
        pltpu.SemaphoreType.DMA((36,)),
        pltpu.SemaphoreType.DMA((17,)),
    ]


def scatter_kernel(*refs, share, rides):
    if rides:
        partial_ref, pieces_ref, out_ref, landed_ref = refs[:4]
        ride = Ride(pieces_ref, landed_ref, *refs[11:])
        scratch = refs[4:11]
    else:
        partial_ref, out_ref = refs[:2]
        ride, scratch = None, refs[2:]
    more = ride.peers if rides else ()
    run_with_ride(scatter_steps(partial_ref, out_ref, *scratch, share, more), ride)


def scattered(partial, rows, collective_id, ride=None, share=2):
    width = partial.shape[1] // 4
    rides = () if ride is None else (ride,)
    anywhere = pl.BlockSpec(memory_space=pl.ANY)
    out = pl.pallas_call(
        functools.partial(scatter_kernel, share=share, rides=len(rides)),
        out_shape=[jax.ShapeDtypeStruct((PLANES, rows, width), BF16)]
        + [jax.ShapeDtypeStruct(r.shape, BF16) for r in rides],
        in_specs=[anywhere] * (1 + len(rides)),
        out_specs=[anywhere] * (1 + len(rides)),
        scratch_shapes=scatter_scratch(rows, width) + list(RIDE_SCRATCH) * len(rides),
        compiler_params=pltpu.CompilerParams(
            collective_id=collective_id, has_side_effects=True, vmem_limit_bytes=VMEM_BYTES
        ),
        name="scatter_rows",
    )(partial.reshape(PLANES, HALVES, rows, 4 * width), *rides)
    return out if rides else out[0]


def carry(before, after, places, compute):
    number = pl.program_id(0)

    @pl.when(number == 0)
    def _():
        for step in before:
            step()

    compute()
    for at in sorted(set(places)):

        @pl.when(number == at)
        def _(at=at):
            for place, step in zip(places, after):
                if place == at:
                    step()


def join_halves(first_ref, last_ref, whole_ref):
    count, height, _ = first_ref.shape

    @pl.when(pl.program_id(0) == 0)
    def _():
        for place in range(count):
            whole_ref[2 * place * height : (2 * place + 1) * height, :] = first_ref[place]
            whole_ref[(2 * place + 1) * height : (2 * place + 2) * height, :] = last_ref[place]


def expert_forward_kernel(
    rows_ref, up_weight_ref, first_ref, last_ref, small_ref, rank_ref, member_ref, grad_ref,
    slope_ref, silu_ref, result_ref, share_ref, shared_ref, grad_rows_ref, down_weight_ref, *scratch
):
    join_halves(first_ref, last_ref, down_weight_ref)
    steps = gather_steps(grad_ref, grad_rows_ref, *scratch, False)
    units = slope_ref.shape[1]

    def compute():
        rows = rows_ref[0]
        made = dot(rows, up_weight_ref[...])
        gate, up = made[:, :units], made[:, units:]
        sigmoid = jax.nn.sigmoid(gate)
        silu = gate * sigmoid
        slope_ref[...] = up * sigmoid * (1.0 + gate * (1.0 - sigmoid))
        silu_ref[...] = silu
        inner = silu * up
        result_ref[0] = contract_last(inner.astype(BF16), down_weight_ref[...]).astype(BF16)
        cap, count = rows.shape[0], rank_ref.shape[2]
        pick = (lax.broadcasted_iota(jnp.int32, (cap, count), 0) == rank_ref[0]).astype(BF16)
        member = contract_last(pick, member_ref[...]) > 0.5
        logits = jnp.where(member, contract_last(rows, small_ref[...]), NEGATIVE)
        largest = jnp.max(logits, axis=1, keepdims=True)
        weights = jnp.where(member, jnp.exp(logits - largest), 0.0)
        mine = lax.broadcasted_iota(jnp.int32, weights.shape, 1) == 6 + lax.axis_index("z")
        total = jnp.sum(weights, axis=1, keepdims=True)
        own = jnp.sum(jnp.where(mine, weights, 0.0), axis=1, keepdims=True)
        share = own / jnp.where(total > 0.0, total, 1.0)
        share_ref[...] = share
        shared_ref[...] = (share * inner).astype(BF16)

    carry(steps[:2], steps[2:], (1, 3, 5, 6, 7, 7), compute)


def once(shape):
    return pl.BlockSpec(shape, lambda b: (0,) * len(shape), pipeline_mode=pl.Buffered(1))


def expert_forward(rows, up_weight, down_halves, small, rank, member, grad_slots, collective_id):
    _, cap, width = rows.shape
    units = down_halves[0].shape[2]
    count = BLOCKS * cap
    anywhere = pl.BlockSpec(memory_space=pl.ANY)
    block = lambda b: (b, 0)
    return pl.pallas_call(
        expert_forward_kernel,
        grid=(BLOCKS,),
        in_specs=[
            pl.BlockSpec((1, cap, width), lambda b: (b, 0, 0)),
            once(up_weight.shape),
            once(down_halves[0].shape),
            once(down_halves[1].shape),
            once(small.shape),
            pl.BlockSpec((1, 1, rank.shape[2]), lambda b: (b, 0, 0)),
            pl.BlockSpec((16, rank.shape[2]), lambda b: (0, b)),
            anywhere,
        ],
        out_specs=[
            pl.BlockSpec((cap, units), block),
            pl.BlockSpec((cap, units), block),
            pl.BlockSpec((1, cap, width), lambda b: (b, 0, 0)),
            pl.BlockSpec((cap, 1), block),
            pl.BlockSpec((cap, units), block),
            anywhere,
        ],
        out_shape=[
            jax.ShapeDtypeStruct((count, units), F32),
            jax.ShapeDtypeStruct((count, units), F32),
            jax.ShapeDtypeStruct((BLOCKS, cap, width), BF16),
            jax.ShapeDtypeStruct((count, 1), F32),
            jax.ShapeDtypeStruct((count, units), BF16),
            jax.ShapeDtypeStruct((PLANES, HALVES, cap, width), BF16),
        ],
        scratch_shapes=[pltpu.VMEM((width, units), BF16)] + list(GATHER_SCRATCH),
        compiler_params=pltpu.CompilerParams(
            collective_id=collective_id, has_side_effects=True, vmem_limit_bytes=VMEM_BYTES
        ),
        name="expert_forward",
    )(rows, up_weight, *down_halves, small, rank, member, grad_slots)


def expert_backward_kernel(
    slope_ref, silu_ref, grad_ref, share_ref, up_weight_ref, first_ref, last_ref, columns_ref,
    inner_ref, result_ref, *refs, rides
):
    count = 6 if rides else 5
    grad_rows_ref, grad_gate_up_ref, down_first_ref, down_last_ref, out_ref = refs[:5]
    down_weight_ref, kept_ref, scratch = refs[count], refs[count + 1], refs[count + 2 :]
    ride = Ride(kept_ref, refs[5], *scratch[7:]) if rides else None
    steps = scatter_steps(result_ref, out_ref, *scratch[:7], 1, ride.peers if rides else ())
    middle = down_first_ref.shape[1]
    number = pl.program_id(0)
    join_halves(first_ref, last_ref, down_weight_ref)

    def down_gradient():
        down_grad = contract_first(columns_ref[...], inner_ref[...]).astype(BF16)
        kept_ref[number] = down_grad[:middle]
        down_first_ref[0] = down_grad[:middle]
        down_last_ref[0] = down_grad[middle:]

    def rows_gradient():
        grad_inner = dot(grad_ref[0], down_weight_ref[...]) * share_ref[...]
        grad_gate_up = jnp.concatenate(
            [grad_inner * slope_ref[...], grad_inner * silu_ref[...]], axis=1
        ).astype(BF16)
        grad_gate_up_ref[...] = grad_gate_up
        grad_rows_ref[0] = contract_last(grad_gate_up, up_weight_ref[...]).astype(BF16)

    def compute():
        pl.when(number < BLOCKS)(down_gradient)
        pl.when(number >= BLOCKS)(rows_gradient)

    after, places = list(steps[1:]), [3, 7, 9, 11, 13, 15, 15]
    if rides:
        after += [ride.begin] + [functools.partial(ride.go_on, i) for i in range(4)] + [ride.finish]
        places += [7, 8, 9, 10, 12, 15]
    carry(steps[:1], after, places, compute)


def expert_backward(
    slope, silu, grad_rows, share, up_weight, down_halves, inner, result, rides, collective_id
):
    _, cap, width = grad_rows.shape
    count, units = slope.shape
    tile = width // BLOCKS
    anywhere = pl.BlockSpec(memory_space=pl.ANY)
    at_row = lambda b: jnp.maximum(b - BLOCKS, 0)
    at_tile = lambda b: jnp.minimum(b, BLOCKS - 1)
    block = lambda b: (at_row(b), 0)
    rows = pl.BlockSpec((1, cap, width), lambda b: (at_row(b), 0, 0))
    half = pl.BlockSpec((1, tile // 2, units), lambda b: (at_tile(b), 0, 0))
    half_shape = jax.ShapeDtypeStruct((BLOCKS, tile // 2, units), BF16)
    return pl.pallas_call(
        functools.partial(expert_backward_kernel, rides=rides),
        grid=(2 * BLOCKS,),
        in_specs=[
            pl.BlockSpec((cap, units), block),
            pl.BlockSpec((cap, units), block),
            rows,
            pl.BlockSpec((cap, 1), block),
            once(up_weight.shape),
            once(down_halves[0].shape),
            once(down_halves[1].shape),
            pl.BlockSpec((count, tile), lambda b: (0, at_tile(b))),
            once(inner.shape),
            anywhere,
        ],
        out_specs=[rows, pl.BlockSpec((cap, 2 * units), block), half, half, anywhere]
        + [anywhere] * rides,
        out_shape=[
            jax.ShapeDtypeStruct((BLOCKS, cap, width), BF16),
            jax.ShapeDtypeStruct((count, 2 * units), BF16),
            half_shape,
            half_shape,
            jax.ShapeDtypeStruct((PLANES, cap, width // 4), BF16),
        ]
        + [half_shape] * rides,
        scratch_shapes=[
            pltpu.VMEM((width, units), BF16),
            pltpu.VMEM((BLOCKS, tile // 2, units), BF16),
        ]
        + scatter_scratch(cap, width // 4)
        + list(RIDE_SCRATCH) * rides,
        compiler_params=pltpu.CompilerParams(
            collective_id=collective_id, has_side_effects=True, vmem_limit_bytes=VMEM_BYTES
        ),
        name="expert_backward",
    )(
        slope, silu, grad_rows, share, up_weight, *down_halves, grad_rows.reshape(count, width), inner,
        result.reshape(PLANES, HALVES, cap, width),
    )


def expert_gradient_kernel(
    rows_ref, grad_gate_up_ref, partial_ref, pieces_ref, up_grad_ref, out_ref, landed_ref, *scratch
):
    ride = Ride(pieces_ref, landed_ref, *scratch[7:])
    steps = scatter_steps(partial_ref, out_ref, *scratch[:7], 1, ride.peers)

    def compute():
        up_grad_ref[...] = contract_first(rows_ref[...], grad_gate_up_ref[...]).astype(BF16)

    def with_ride(number):
        steps[1 + number]()
        ride.go_on(number)

    after = [functools.partial(with_ride, number) for number in range(6)]
    carry([steps[0], ride.begin], after + [steps[-1], ride.finish], (0, 2, 4, 6, 7, 7, 7, 7), compute)


def expert_gradient(rows, grad_gate_up, partial, pieces, collective_id):
    count, width = rows.shape
    units = grad_gate_up.shape[1]
    cap, tile = count // BLOCKS, width // BLOCKS
    anywhere = pl.BlockSpec(memory_space=pl.ANY)
    return pl.pallas_call(
        expert_gradient_kernel,
        grid=(BLOCKS,),
        in_specs=[
            pl.BlockSpec((count, tile), lambda b: (0, b)),
            once((count, units)),
            anywhere,
            anywhere,
        ],
        out_specs=[pl.BlockSpec((tile, units), lambda b: (b, 0)), anywhere, anywhere],
        out_shape=[
            jax.ShapeDtypeStruct((width, units), BF16),
            jax.ShapeDtypeStruct((PLANES, cap, width // 4), BF16),
            jax.ShapeDtypeStruct(pieces.shape, BF16),
        ],
        scratch_shapes=scatter_scratch(cap, width // 4) + list(RIDE_SCRATCH),
        compiler_params=pltpu.CompilerParams(
            collective_id=collective_id, has_side_effects=True, vmem_limit_bytes=VMEM_BYTES
        ),
        name="expert_gradient",
    )(rows, grad_gate_up, partial.reshape(PLANES, HALVES, cap, width), pieces)


def closing_kernel(
    hidden_ref, q_ref, k_ref, v_ref, rows_ref, gated_ref, partial_ref, grad_ref, out_ref, *scratch
):
    steps = scatter_steps(partial_ref, out_ref, *scratch)
    span = q_ref.shape[1]

    def compute():
        hidden = hidden_ref[...]
        for place, ref in enumerate((q_ref, k_ref, v_ref)):
            at = slice(place * span, (place + 1) * span)
            grad_ref[:, at] = contract_first(hidden, ref[...]).astype(BF16)
        grad_ref[:, 3 * span :] = contract_first(rows_ref[...], gated_ref[...]).astype(BF16)

    carry(steps[:1], steps[1:], (1, 4, 7, 7, 7, 7, 7), compute)


def closing(hidden, q, k, v, rows, gated, partial, collective_id):
    count, width = hidden.shape
    slot_count, span = gated.shape
    tile, own_rows = width // BLOCKS, count // BLOCKS
    anywhere = pl.BlockSpec(memory_space=pl.ANY)
    return pl.pallas_call(
        closing_kernel,
        grid=(BLOCKS,),
        in_specs=[
            pl.BlockSpec((count, tile), lambda b: (0, b)),
            once((count, span)),
            once((count, span)),
            once((count, span)),
            pl.BlockSpec((slot_count, tile), lambda b: (0, b)),
            once((slot_count, span)),
            anywhere,
        ],
        out_specs=[pl.BlockSpec((tile, 4 * span), lambda b: (b, 0)), anywhere],
        out_shape=[
            jax.ShapeDtypeStruct((width, 4 * span), BF16),
            jax.ShapeDtypeStruct((PLANES, own_rows, width // 4), BF16),
        ],
        scratch_shapes=scatter_scratch(own_rows, width // 4),
        compiler_params=pltpu.CompilerParams(
            collective_id=collective_id, has_side_effects=True, vmem_limit_bytes=VMEM_BYTES
        ),
        name="closing",
    )(hidden, q, k, v, rows, gated, partial.reshape(PLANES, HALVES, own_rows, width))


def finish_kernel(
    query_ref, all_ref, small_ref, query_grad_ref, kv_grad_ref, out_grad_ref, gain_first_ref,
    gain_second_ref, router_first_ref, router_second_ref
):
    span = query_ref.shape[2] // 4
    head_width = query_grad_ref.shape[3]
    pair = span // head_width
    own_rows = query_grad_ref.shape[1]
    for half in range(HALVES):
        landed = query_ref[half, :own_rows, :].astype(F32)
        for head in range(pair):
            at = half * pair + head
            query_grad_ref[0, :, at, :] = landed[:, head * head_width : (head + 1) * head_width]
        out_grad_ref[half] = landed[:, 3 * span :].T

    @pl.when(pl.program_id(0) == 0)
    def _():
        for half in range(HALVES):
            total = sum(
                all_ref[z * HALVES + half, :own_rows, span : 3 * span].astype(F32)
                for z in range(PLANES)
            )
            for kind in range(2):
                for head in range(pair):
                    first = kind * span + head * head_width
                    kv_grad_ref[:, half * pair + head, kind, :] = total[:, first : first + head_width]

        total = sum(small_ref[place] for place in range(BLOCKS))
        gain_first_ref[...] = total[0:1]
        gain_second_ref[...] = total[1:2]
        router_first_ref[...] = total[2 : 2 + PLANES]
        router_second_ref[...] = total[2 + PLANES : 2 + 2 * PLANES]


def swap_kernel(pieces_ref, landed_ref, *scratch):
    ride = Ride(pieces_ref, landed_ref, *scratch)
    meet([peer for _, _, peer in ride.moves.made.values()])
    ride.begin(tuple(ride.moves.made))
    ride.finish()


def swapped(pieces, collective_id):
    whole = pl.BlockSpec(memory_space=pltpu.VMEM)
    return pl.pallas_call(
        swap_kernel,
        out_shape=jax.ShapeDtypeStruct(pieces.shape, pieces.dtype),
        in_specs=[whole],
        out_specs=whole,
        scratch_shapes=list(RIDE_SCRATCH),
        compiler_params=pltpu.CompilerParams(collective_id=collective_id, has_side_effects=True),
        name="swap_small",
    )(pieces)


def finish(landed, small, own_rows, span, heads, head_width):
    places, height, width = landed.shape
    return pl.pallas_call(
        finish_kernel,
        grid=(PLANES,),
        in_specs=[
            pl.BlockSpec((HALVES, height, width), lambda e: (e, 0, 0)),
            once((places, height, width)),
            once(small.shape),
        ],
        out_specs=[
            pl.BlockSpec((1, own_rows, heads, head_width), lambda e: (e, 0, 0, 0)),
            pl.BlockSpec((own_rows, heads, 2, head_width), lambda e: (0, 0, 0, 0)),
            pl.BlockSpec((HALVES, span, own_rows), lambda e: (e, 0, 0)),
            pl.BlockSpec((1, small.shape[2]), lambda e: (0, 0)),
            pl.BlockSpec((1, small.shape[2]), lambda e: (0, 0)),
            pl.BlockSpec((PLANES, small.shape[2]), lambda e: (0, 0)),
            pl.BlockSpec((PLANES, small.shape[2]), lambda e: (0, 0)),
        ],
        out_shape=[
            jax.ShapeDtypeStruct((PLANES, own_rows, heads, head_width), F32),
            jax.ShapeDtypeStruct((own_rows, heads, 2, head_width), F32),
            jax.ShapeDtypeStruct((places, span, own_rows), F32),
            jax.ShapeDtypeStruct((1, small.shape[2]), F32),
            jax.ShapeDtypeStruct((1, small.shape[2]), F32),
            jax.ShapeDtypeStruct((PLANES, small.shape[2]), F32),
            jax.ShapeDtypeStruct((PLANES, small.shape[2]), F32),
        ],
        compiler_params=pltpu.CompilerParams(vmem_limit_bytes=VMEM_BYTES),
        name="attention_weight_gradients",
    )(landed, landed, small)


def grid_sum(values):
    shape = values.shape
    return lax.all_gather(values.reshape(-1, 128), "grid", axis=0).sum(axis=0).reshape(shape)


def prefix_ranks(member):
    counted = member.astype(BF16)
    width = member.shape[-1]
    before = jnp.arange(width)[:, None] < jnp.arange(width)[None, :]
    return jnp.where(member, dot(counted, before.astype(BF16)).astype(jnp.int32), -1)


def picks(rank):
    return (jnp.arange(CAP, dtype=jnp.int32)[:, None] == rank[..., None, :]).astype(BF16)


def members(first, second):
    names = jnp.arange(PLANES, dtype=first.dtype).reshape((PLANES,) + (1,) * first.ndim)
    return (first[None] == names) | (second[None] == names)


def route_gates(logits, member):
    shown = jnp.where(member, logits, NEGATIVE)
    weights = jnp.where(member, jnp.exp(shown - jnp.max(shown, axis=0, keepdims=True)), 0.0)
    return weights / jnp.sum(weights, axis=0, keepdims=True)


def logits_grad(gates, grad_gates):
    return gates * (grad_gates - jnp.sum(gates * grad_gates, axis=0, keepdims=True))


def exact_first(left, right):
    return lax.dot_general(
        left, right, (((0,), (0,)), ((), ())), precision=lax.Precision.HIGHEST
    )


def exact_last(left, right):
    return lax.dot_general(
        left, right, (((1,), (1,)), ((), ())), precision=lax.Precision.HIGHEST
    )


def norm_sums(grad_hidden, scaled, router, grad_gates, width, gates=None, hidden=None, member=None):
    parts = [
        grad_gates,
        exact_last(router.astype(F32), scaled),
        jnp.sum(grad_hidden * scaled, axis=1)[None],
    ]
    if gates is None:
        parts.append(contract_last(router, hidden))
    parts = grid_sum(jnp.concatenate(parts, axis=0))
    if gates is None:
        gates = route_gates(parts[2 * PLANES + 1 :], member)
    grad_logits = logits_grad(gates, parts[:PLANES])
    inner = parts[2 * PLANES] + jnp.sum(grad_logits * parts[PLANES : 2 * PLANES], axis=0)
    return grad_logits, inner[:, None] / width, gates


def per_device(
    tokens, segment_ids, attention_routes, expert_routes, attention_gain, attention_kv,
    attention_query, attention_out, attention_router, feedforward_gain, feedforward_router,
    expert_gate_up, expert_down, output_grad,
):
    groups = lax.axis_size("t")
    grid_count = lax.axis_size("grid")
    group = lax.axis_index("t")
    plane = lax.axis_index("z")
    place = plane * HALVES + lax.axis_index("x")
    column = lax.axis_index("grid")
    rows, features = tokens.shape
    width_all = features * grid_count
    token_count = BLOCKS * rows
    own_rows = attention_gain.shape[0]
    head_width = attention_kv.shape[3]
    head_pair = attention_kv.shape[1] // HALVES
    span = head_pair * head_width
    hidden_units = expert_gate_up.shape[3] // HALVES

    def mine(array, axis=0):
        return lax.dynamic_slice_in_dim(array, column * features, features, axis)

    def own(array, axis=0):
        return lax.dynamic_slice_in_dim(array, place * rows, rows, axis)

    query_pieces = attention_query.reshape(PLANES, own_rows, HALVES, span).transpose(0, 2, 1, 3)
    kv_pieces = attention_kv.reshape(own_rows, HALVES, head_pair, 2, head_width)
    kv_pieces = kv_pieces.transpose(1, 0, 3, 2, 4).reshape(1, HALVES, own_rows, 2 * span)
    kv_pieces = jnp.broadcast_to(kv_pieces, (PLANES,) + kv_pieces.shape[1:])
    qkv_pieces = jnp.concatenate([query_pieces, kv_pieces], axis=-1)
    out_pieces = attention_out.reshape(BLOCKS, span, own_rows).swapaxes(1, 2)
    first_pieces = jnp.concatenate([out_pieces, qkv_pieces.reshape(BLOCKS, own_rows, 3 * span)], axis=2)
    own_routes = jnp.concatenate([attention_routes, expert_routes], axis=1)
    small = jnp.concatenate(
        [attention_gain[:, None], feedforward_gain[:, None], attention_router, feedforward_router],
        axis=1,
    )
    small = lax.all_gather(small, "t", axis=0).reshape(-1, small.shape[1])
    small = small.T.reshape(small.shape[1], -1)
    spare = jnp.zeros((small.shape[0], features - small.shape[1] % features), BF16)
    small = jnp.concatenate([small, spare], axis=1).reshape(-1, features)
    under = jnp.concatenate([own_routes.T.astype(BF16), small], axis=0)
    under = jnp.pad(under, ((0, -under.shape[0] % 16), (0, 0)))
    everything, first_weight, up_pieces, *down_halves = opened(
        jnp.concatenate([tokens, under], axis=0), first_pieces, expert_gate_up,
        expert_down.reshape(BLOCKS, hidden_units, own_rows), 0, 3,
    )
    first_weight = over_groups(first_weight).reshape(width_all, 4 * span)
    out_weight, qkv_weight = first_weight[:, :span], first_weight[:, span:]
    up_weight = over_groups(exchanged(up_pieces)).reshape(width_all, 2 * hidden_units)
    under = everything[:, :, rows:, :features].reshape(BLOCKS, -1, features).swapaxes(0, 1)
    small = under[4:, :, : groups * own_rows].reshape(-1, BLOCKS, groups, own_rows)
    small = jnp.pad(small.swapaxes(1, 2).reshape(-1, width_all), ((0, 4), (0, 0)))
    gain_first, gain_second = mine(small[0]).astype(F32), mine(small[1]).astype(F32)
    router_first, router_second = mine(small[2:6], 1), mine(small[6:10], 1)

    member_first, member_second = members(under[0], under[1]), members(under[2], under[3])
    own_member_first = lax.dynamic_index_in_dim(member_first, place, 1, keepdims=False)
    own_member_second = lax.dynamic_index_in_dim(member_second, place, 1, keepdims=False)
    rank = prefix_ranks(
        jnp.concatenate(
            [
                lax.dynamic_index_in_dim(member_first, plane, 0, keepdims=False),
                lax.dynamic_index_in_dim(member_second, plane, 0, keepdims=False),
                own_member_first,
                own_member_second,
            ],
            axis=0,
        )
    )
    rank_first, rank_second = rank[:BLOCKS, None], rank[BLOCKS : 2 * BLOCKS, None]
    own_pick_first = picks(rank[2 * BLOCKS : 2 * BLOCKS + PLANES])
    own_pick_second = picks(rank[2 * BLOCKS + PLANES :])
    member_first = member_first.reshape(PLANES, token_count)
    member_second = member_second.reshape(PLANES, token_count)

    def to_slots(values, pick):
        return jnp.einsum("est,tf->esf", pick, values, preferred_element_type=F32).astype(BF16)

    def to_tokens(slots, pick):
        return jnp.einsum("est,esf->etf", pick, slots, preferred_element_type=F32)

    grad_out = output_grad.astype(F32)
    cosine, sine = rope_tables(token_count, head_width)
    cosine, sine = jnp.asarray(cosine), jnp.asarray(sine)
    hidden_first, queries, keys, values, logits_first, inverse_first = project(
        everything, rows, small, first_weight, cosine, sine, span, head_width
    )
    gates_first = route_gates(logits_first[2 : 2 + PLANES], member_first)
    own_gates_first = own(gates_first, 1)
    position = jnp.arange(token_count, dtype=jnp.int32)
    segment = lax.dynamic_slice_in_dim(segment_ids, group * token_count, token_count, 0)
    opens = jnp.concatenate([jnp.ones((1,), jnp.bool_), segment[1:] != segment[:-1]])
    document_start = lax.cummax(jnp.where(opens, position, 0))
    begin = document_start.reshape(BLOCKS, rows)[:, 0] // rows
    table = token_table(
        position, document_start, lax.dynamic_index_in_dim(gates_first, plane, 0, keepdims=False)
    )
    attention_args = (begin, queries, keys, values, rank_first, table)
    attended, gated, gate_slots_first, lse = attention_forward(*attention_args, head_width)
    branch, grad_out_slots = lax.optimization_barrier(
        (contract_last(attended, out_weight).astype(BF16), to_slots(output_grad, own_pick_second))
    )
    branch_slots, down_first = scattered(
        branch, CAP, 2, ride=down_halves[0], share=1
    )
    branch_first = to_tokens(branch_slots, own_pick_first)
    residual = tokens.astype(F32) + jnp.sum(own_gates_first[:, :, None] * branch_first, axis=0)

    square = grid_sum(jnp.sum(residual * residual, axis=1))
    inverse_second = lax.rsqrt(square / width_all + EPSILON)[:, None]
    normed_second = residual * inverse_second
    hidden_second = (normed_second * gain_second).astype(BF16)
    slots_second, down_last = gathered(
        to_slots(hidden_second, own_pick_second), 1, ride=down_halves[1], share=3
    )
    down_weight = [
        over_groups(half).reshape((groups * BLOCKS,) + half.shape[1:]) for half in (down_first, down_last)
    ]
    slots_second = slots_second.reshape(BLOCKS, CAP, width_all)
    gate_pre, up_pre, result, gate_slots_second, inner, grad_slots_second = expert_forward(
        slots_second,
        up_weight,
        down_weight,
        small,
        rank_second,
        jnp.pad(member_second.astype(BF16), ((6, 6), (0, 0))),
        grad_out_slots,
        4,
    )
    grad_slots_second = grad_slots_second.reshape(BLOCKS, CAP, width_all)
    grad_rows, grad_gate_up, grad_down_first, grad_down_last, result_slots, *landed = expert_backward(
        gate_pre, up_pre, grad_slots_second, gate_slots_second, up_weight, down_weight, inner, result,
        int(groups == 1), 5,
    )
    if groups > 1:
        grad_down = jnp.concatenate([grad_down_first, grad_down_last], axis=1)
        grad_down = group_sums(grad_down.reshape(groups, BLOCKS, own_rows, hidden_units))
        grad_down_first, grad_down_last = jnp.split(grad_down, 2, axis=1)
        landed = [exchanged(grad_down_first)]
    grad_down_first = landed[0]
    grad_up, grad_rows, grad_down_last = expert_gradient(
        slots_second.reshape(-1, width_all), grad_gate_up, grad_rows, grad_down_last, 6
    )
    branch_second = to_tokens(result_slots, own_pick_second)

    grad_hidden_second = jnp.sum(to_tokens(grad_rows, own_pick_second), axis=0)
    grad_logits_second, inner_mean, own_gates_second = norm_sums(
        grad_hidden_second, normed_second * gain_second, router_second,
        jnp.sum(branch_second * grad_out[None], axis=2), width_all,
        hidden=hidden_second, member=own_member_second,
    )
    grad_hidden_second = grad_hidden_second + exact_first(
        grad_logits_second, router_second.astype(F32)
    )
    grad_normed = grad_hidden_second * gain_second
    grad_residual = grad_out + inverse_second * (grad_normed - normed_second * inner_mean)

    grad_slots_first = gathered(to_slots(grad_residual.astype(BF16), own_pick_first), 8)
    (
        grad_slots_first, residual, own_gates_second, branch_second, hidden_second,
        grad_logits_second, grad_hidden_second, normed_second,
    ) = lax.optimization_barrier(
        (
            grad_slots_first, residual, own_gates_second, branch_second, hidden_second,
            grad_logits_second, grad_hidden_second, normed_second,
        )
    )
    layer_output = residual + jnp.sum(own_gates_second[:, :, None] * branch_second, axis=0)
    layer_output = layer_output.astype(BF16)
    grad_router_second = exact(grad_logits_second, hidden_second.astype(F32))
    grad_gain_second = jnp.sum(grad_hidden_second * normed_second, axis=0)
    grad_slots_first = grad_slots_first.reshape(BLOCKS * CAP, -1)
    grad_up, grad_slots_first = lax.optimization_barrier((grad_up, grad_slots_first))
    grad_up = return_gradients(grad_up.reshape(groups, BLOCKS, own_rows, 2 * hidden_units))
    grad_attended = gate_slots_first * dot(grad_slots_first, out_weight)
    grad_attended = grad_attended.astype(BF16)
    grad_query, grad_keys, grad_values = attention_backward(
        *attention_args, attended, lse, grad_attended, cosine, sine, head_width
    )
    grad_qkv = jnp.concatenate([grad_query, grad_keys, grad_values], axis=1)
    grad_hidden = contract_last(grad_qkv, qkv_weight).astype(BF16)
    grad_first, grad_hidden = closing(
        hidden_first, grad_query, grad_keys, grad_values, grad_slots_first, gated, grad_hidden, 3
    )
    grad_hidden = jnp.sum(grad_hidden.astype(F32), axis=0)
    grad_first, grad_up = lax.optimization_barrier((grad_first, grad_up))
    grad_first = return_gradients(grad_first.reshape(groups, BLOCKS, own_rows, 4 * span))
    expert_gate_up_grad = grad_up.reshape(PLANES, HALVES, own_rows, 2, hidden_units)
    expert_gate_up_grad = expert_gate_up_grad.transpose(0, 2, 3, 1, 4).reshape(expert_gate_up.shape)
    expert_down_grad = jnp.concatenate([grad_down_first, grad_down_last], axis=1)
    expert_down_grad = expert_down_grad.swapaxes(1, 2).reshape(expert_down.shape)

    own_normed = tokens.astype(F32) * own(inverse_first)
    own_hidden = (own_normed * gain_first).astype(BF16)
    grad_logits_first, inner_mean, _ = norm_sums(
        grad_hidden, own_normed * gain_first, router_first,
        jnp.sum(branch_first * grad_residual[None], axis=2), width_all, gates=own_gates_first,
    )
    grad_hidden_first = grad_hidden + exact_first(grad_logits_first, router_first.astype(F32))
    grad_router_first = exact(grad_logits_first, own_hidden.astype(F32))
    grad_gain_first = jnp.sum(grad_hidden_first * own_normed, axis=0)
    grad_normed = grad_hidden_first * gain_first
    input_grad = grad_residual + own(inverse_first) * (grad_normed - own_normed * inner_mean)

    small_grads = jnp.concatenate(
        [grad_gain_first[None], grad_gain_second[None], grad_router_first, grad_router_second],
        axis=0,
    )
    small_grads = lax.all_gather(small_grads, "grid", axis=1, tiled=True)
    if groups > 1:
        small_grads = lax.psum(small_grads, "t")
    small_grads = small_grads.reshape(-1, groups, BLOCKS, own_rows)
    small_grads = lax.dynamic_index_in_dim(small_grads, group, 1, keepdims=False).swapaxes(0, 1)
    small_grads = jnp.pad(small_grads, ((0, 0), (0, 6), (0, -own_rows % 128)))
    small_grads, grad_first = lax.optimization_barrier((small_grads, grad_first))
    (
        attention_query_grad, attention_kv_grad, attention_out_grad, gain_grad_first,
        gain_grad_second, router_grad_first, router_grad_second,
    ) = finish(
        grad_first, swapped(small_grads, 7), own_rows, span, attention_kv.shape[1], head_width
    )
    attention_out_grad = attention_out_grad.reshape(attention_out.shape)
    return (
        layer_output,
        input_grad.astype(BF16),
        gain_grad_first[0, :own_rows],
        attention_kv_grad,
        attention_query_grad.astype(F32),
        attention_out_grad.astype(F32),
        router_grad_first[:, :own_rows].T,
        gain_grad_second[0, :own_rows],
        router_grad_second[:, :own_rows].T,
        expert_gate_up_grad.astype(F32),
        expert_down_grad.astype(F32),
    )


def solution(mesh):
    groups = mesh.shape["wide"] // BLOCKS
    shape = (groups, PLANES, HALVES, mesh.shape["grid"])
    inner_mesh = Mesh(mesh.devices.reshape(shape), ("t", "z", "x", "grid"))
    wide = ("t", "z", "x")
    in_specs = (
        P(wide, "grid"),
        P(),
        P(wide, None),
        P(wide, None),
        P(wide),
        P(wide, "grid", None, None),
        P(None, wide, "grid", None),
        P(None, "grid", None, wide),
        P(wide, None),
        P(wide),
        P(wide, None),
        P(None, wide, None, "grid"),
        P(None, "grid", wide),
        P(wide, "grid"),
    )
    out_specs = (
        P(wide, "grid"),
        P(wide, "grid"),
        P(wide),
        P(wide, "grid", None, None),
        P(None, wide, "grid", None),
        P(None, "grid", None, wide),
        P(wide, None),
        P(wide),
        P(wide, None),
        P(None, wide, None, "grid"),
        P(None, "grid", wide),
    )
    return jax.shard_map(
        per_device, mesh=inner_mesh, in_specs=in_specs, out_specs=out_specs, check_vma=False
    )
```

```python
import functools
import math

import jax
import jax.numpy as jnp
import numpy as np
from jax import lax
from jax.experimental import pallas as pl
from jax.experimental.layout import Layout, with_layout_constraint
from jax.experimental.pallas import tpu as pltpu
from jax.sharding import Mesh, PartitionSpec as P

CAP = 320
PLANES = 4
HALVES = 2
BLOCKS = PLANES * HALVES
EPSILON = 1e-05
ROPE_BASE = 10000.0
NEGATIVE = -1e30
BF16 = jnp.bfloat16
F32 = jnp.float32
PLACES = ("z", "x")
MESH = pl.DeviceIdType.MESH
VMEM_BYTES = 56 * 1024 * 1024
EARLY = 128


def rope_tables(token_count, width):
    half = width // 2
    frequency = np.float32(ROPE_BASE) ** (-np.arange(half, dtype=np.float32) / np.float32(half))
    angles = np.arange(token_count, dtype=np.float32)[:, None] * frequency.astype(np.float32)[None, :]
    cosine, sine = np.cos(angles).astype(np.float32), np.sin(angles).astype(np.float32)
    return np.concatenate([cosine, cosine], axis=1), np.concatenate([-sine, sine], axis=1)


def turned(values, cosine, sine):
    return values * cosine + pltpu.roll(values, values.shape[1] // 2, 1) * sine


def dot(left, right):
    return jnp.dot(left, right, preferred_element_type=F32)


def contract_first(left, right):
    return lax.dot_general(left, right, (((0,), (0,)), ((), ())), preferred_element_type=F32)


def contract_last(left, right):
    return lax.dot_general(left, right, (((1,), (1,)), ((), ())), preferred_element_type=F32)


def exact(left, right):
    return jnp.dot(left, right, precision=lax.Precision.HIGHEST)


def project_kernel(
    tokens_ref, small_ref, query_weight_ref, shared_weight_ref, cos_ref, sin_ref,
    hidden_ref, q_ref, k_ref, v_ref, logits_ref, inverse_ref, *, head_width
):
    x = tokens_ref[0, 0].astype(F32)
    inverse = lax.rsqrt(jnp.mean(x * x, axis=1, keepdims=True) + EPSILON)
    inverse_ref[...] = inverse
    hidden = (x * inverse * small_ref[:1, :].astype(F32)).astype(BF16)
    hidden_ref[...] = hidden
    logits_ref[...] = contract_last(small_ref[...], hidden)
    queries = dot(hidden, query_weight_ref[...])
    shared = dot(hidden, shared_weight_ref[...])
    span = q_ref.shape[1]
    cosine, sine = cos_ref[...], sin_ref[...]
    for head in range(span // head_width):
        at = slice(head * head_width, (head + 1) * head_width)
        q_ref[:, at] = turned(queries[:, at], cosine, sine).astype(BF16)
        k_ref[:, at] = turned(shared[:, at], cosine, sine).astype(BF16)
    v_ref[...] = shared[:, span:].astype(BF16)


def project(tokens, rows, small, weight, cosine, sine, span, head_width):
    width = tokens.shape[-1]
    token_count = BLOCKS * rows
    whole = lambda b: (0, 0)
    block = lambda b: (b, 0)
    return pl.pallas_call(
        functools.partial(project_kernel, head_width=head_width),
        grid=(BLOCKS,),
        in_specs=[
            pl.BlockSpec((1, 1, rows, width), lambda b: (b // HALVES, b % HALVES, 0, 0)),
            pl.BlockSpec(small.shape, whole),
            pl.BlockSpec((width, span), lambda b: (0, 1)),
            pl.BlockSpec((width, 2 * span), lambda b: (0, 1)),
            pl.BlockSpec((rows, head_width), block),
            pl.BlockSpec((rows, head_width), block),
        ],
        out_specs=[
            pl.BlockSpec((rows, width), block),
            pl.BlockSpec((rows, span), block),
            pl.BlockSpec((rows, span), block),
            pl.BlockSpec((rows, span), block),
            pl.BlockSpec((small.shape[0], rows), lambda b: (0, b)),
            pl.BlockSpec((rows, 1), block),
        ],
        out_shape=[
            jax.ShapeDtypeStruct((token_count, width), BF16),
            jax.ShapeDtypeStruct((token_count, span), BF16),
            jax.ShapeDtypeStruct((token_count, span), BF16),
            jax.ShapeDtypeStruct((token_count, span), BF16),
            jax.ShapeDtypeStruct((small.shape[0], token_count), F32),
            jax.ShapeDtypeStruct((token_count, 1), F32),
        ],
        compiler_params=pltpu.CompilerParams(vmem_limit_bytes=VMEM_BYTES),
        name="project",
    )(tokens, small, weight, weight, cosine, sine)


def attention_scores(q, k_ref, low_bound, high_bound, tile, tile_rows, scaling):
    rows = pl.ds(pl.multiple_of(tile * tile_rows, tile_rows), tile_rows)
    keys = k_ref[rows, :]
    scores = contract_last(q, keys) * scaling
    column = tile * tile_rows + lax.broadcasted_iota(jnp.int32, scores.shape, 1)
    allowed = (column >= low_bound) & (column <= high_bound)
    return rows, keys, scores, allowed


def slots_of_block(rank_ref, table_ref, cap, block):
    rows = table_ref.shape[1]
    pick = (lax.broadcasted_iota(jnp.int32, (cap, rows), 0) == rank_ref[0]).astype(BF16)
    made = contract_last(pick, table_ref[...])
    base = block * rows
    filled = made[:, 4:5] > 0.5
    low = (64.0 * made[:, 2:3] + made[:, 3:4]).astype(jnp.int32)
    high = (64.0 * made[:, 0:1] + made[:, 1:2]).astype(jnp.int32)
    gate = made[:, 5:6] + made[:, 6:7] + made[:, 7:8]
    return pick, jnp.where(filled, low, base), jnp.where(filled, high, base), gate


def rows_of_block(rank_ref, table_ref, cap, block):
    rows = table_ref.shape[1]
    pick = (lax.broadcasted_iota(jnp.int32, (cap, rows), 0) == rank_ref[0]).astype(BF16)
    made = contract_last(table_ref[...], pick)
    filled = made[4:5] > 0.5
    low = (64.0 * made[2:3] + made[3:4]).astype(jnp.int32)
    high = (64.0 * made[0:1] + made[1:2]).astype(jnp.int32)
    return pick, jnp.where(filled, low, block * rows), jnp.where(filled, high, block * rows)


def token_table(position, document_start, gate):
    first = gate.astype(BF16).astype(F32)
    second = (gate - first).astype(BF16).astype(F32)
    rows = [
        position // 64, position % 64, document_start // 64, document_start % 64,
        jnp.ones_like(gate), first, second, gate - first - second,
    ]
    return jnp.pad(jnp.stack([row.astype(BF16) for row in rows]), ((0, 8), (0, 0)))


def attention_forward_kernel(
    begin_ref, q_ref, k_ref, v_ref, rank_ref, table_ref, out_ref, gated_ref, gate_ref, lse_ref, *,
    scaling
):
    block = pl.program_id(1)
    cap, width = out_ref.shape
    tile_rows = q_ref.shape[0]
    pick, low_bound, high_bound, gate = slots_of_block(rank_ref, table_ref, cap, block)
    q = dot(pick, q_ref[...]).astype(BF16)

    def step(tile, carried):
        largest, total, summed = carried
        rows, _, scores, allowed = attention_scores(
            q, k_ref, low_bound, high_bound, tile, tile_rows, scaling
        )
        scores = jnp.where(allowed, scores, NEGATIVE)
        new_largest = jnp.maximum(largest, jnp.max(scores, axis=1, keepdims=True))
        weights = jnp.where(allowed, jnp.exp(scores - new_largest), 0.0)
        shrink = jnp.exp(largest - new_largest)
        return (
            new_largest,
            total * shrink + jnp.sum(weights, axis=1, keepdims=True),
            summed * shrink + dot(weights.astype(BF16), v_ref[rows, :]),
        )

    largest, total, summed = lax.fori_loop(
        begin_ref[block],
        block + 1,
        step,
        (jnp.full((cap, 1), NEGATIVE, F32), jnp.zeros((cap, 1), F32), jnp.zeros((cap, width), F32)),
    )
    attended = (summed / total).astype(BF16)
    out_ref[...] = attended
    gated_ref[...] = (gate * attended.astype(F32)).astype(BF16)
    gate_ref[...] = gate
    lse_ref[0] = largest + jnp.log(total)


def attention_backward_kernel(
    begin_ref, q_ref, k_ref, v_ref, rank_ref, table_ref, out_ref, lse_ref, grad_ref,
    cos_ref, sin_ref, dq_ref, dk_ref, dv_ref, dk_sum, dv_sum, *, scaling, width
):
    block = pl.program_id(0)
    cap = out_ref.shape[0]
    tile_rows = q_ref.shape[0]
    heads = [slice(h * width, (h + 1) * width) for h in range(out_ref.shape[1] // width)]
    pick, low_bound, high_bound = rows_of_block(rank_ref, table_ref, cap, block)
    queries = dot(pick, q_ref[...]).astype(BF16)
    grads = grad_ref[...]
    product = grads.astype(F32) * out_ref[...].astype(F32)
    ones = jnp.ones((8, width), F32)
    deltas = [exact_last(ones, product[:, at])[:1] for at in heads]

    @pl.when(block == 0)
    def _():
        dk_sum[...] = jnp.zeros_like(dk_sum)
        dv_sum[...] = jnp.zeros_like(dv_sum)

    def step(tile, dq):
        rows = pl.ds(pl.multiple_of(tile * tile_rows, tile_rows), tile_rows)
        position = tile * tile_rows + lax.broadcasted_iota(jnp.int32, (tile_rows, cap), 0)
        allowed = (position >= low_bound) & (position <= high_bound)
        made = []
        for h, at in enumerate(heads):
            q, grad, keys = queries[:, at], grads[:, at], k_ref[rows, at]
            scores = contract_last(keys, q) * scaling
            chances = jnp.where(allowed, jnp.exp(scores - lse_ref[h, 0]), 0.0)
            dv_sum[rows, at] += dot(chances.astype(BF16), grad)
            grad_chances = contract_last(v_ref[rows, at], grad)
            grad_scores = (chances * (grad_chances - deltas[h])).astype(BF16)
            dk_sum[rows, at] += dot(grad_scores, q) * scaling
            made.append(dq[h] + contract_first(grad_scores, keys))
        return tuple(made)

    zero = jnp.zeros((cap, width), F32)
    dq = lax.fori_loop(begin_ref[block], block + 1, step, (zero,) * len(heads))
    own = pl.ds(pl.multiple_of(block * tile_rows, tile_rows), tile_rows)
    for h, at in enumerate(heads):
        scaled = dq[h] * scaling
        high = scaled.astype(BF16)
        rest = (scaled - high.astype(F32)).astype(BF16)
        dq_tokens = contract_first(pick, high) + contract_first(pick, rest)
        dq_ref[:, at] = turned(dq_tokens, cos_ref[own, :], -sin_ref[own, :]).astype(BF16)

    @pl.when(block == BLOCKS - 1)
    def _():
        def finish_tile(tile, nothing):
            rows = pl.ds(pl.multiple_of(tile * tile_rows, tile_rows), tile_rows)
            for at in heads:
                dk_ref[rows, at] = turned(
                    dk_sum[rows, at], cos_ref[rows, :], -sin_ref[rows, :]
                ).astype(BF16)
            dv_ref[rows, :] = dv_sum[rows, :].astype(BF16)
            return nothing

        lax.fori_loop(0, BLOCKS, finish_tile, 0)


def attention_specs(row_count, token_count, width):
    return dict(
        q=pl.BlockSpec((row_count, width), lambda h, b, s: (b, h)),
        k=pl.BlockSpec((token_count, width), lambda h, b, s: (0, h)),
        rank=pl.BlockSpec((1, 1, row_count), lambda h, b, s: (b, 0, 0)),
        rows=pl.BlockSpec((16, row_count), lambda h, b, s: (0, b)),
        gate=pl.BlockSpec((CAP, 1), lambda h, b, s: (b, 0)),
        slots=pl.BlockSpec((CAP, width), lambda h, b, s: (b, h)),
        lse=pl.BlockSpec((1, CAP, 1), lambda h, b, s: (h, b, 0)),
    )


def attention_forward(begin, q, k, v, rank, table, width):
    token_count, heads = q.shape[0], q.shape[1] // width
    row_count = token_count // BLOCKS
    s = attention_specs(row_count, token_count, width)
    return pl.pallas_call(
        functools.partial(attention_forward_kernel, scaling=1.0 / math.sqrt(width)),
        grid_spec=pltpu.PrefetchScalarGridSpec(
            num_scalar_prefetch=1,
            grid=(heads, BLOCKS),
            in_specs=[s["q"], s["k"], s["k"], s["rank"], s["rows"]],
            out_specs=[s["slots"], s["slots"], s["gate"], s["lse"]],
        ),
        out_shape=[
            jax.ShapeDtypeStruct((BLOCKS * CAP, heads * width), BF16),
            jax.ShapeDtypeStruct((BLOCKS * CAP, heads * width), BF16),
            jax.ShapeDtypeStruct((BLOCKS * CAP, 1), F32),
            jax.ShapeDtypeStruct((heads, BLOCKS * CAP, 1), F32),
        ],
        compiler_params=pltpu.CompilerParams(vmem_limit_bytes=VMEM_BYTES),
        name="attention_forward",
    )(begin, q, k, v, rank, table)


def attention_backward(begin, q, k, v, rank, table, out, lse, grad, cosine, sine, width):
    token_count, span = q.shape
    row_count = token_count // BLOCKS
    block = lambda b, s: (b, 0)
    whole = lambda b, s: (0, 0)
    tokens = pl.BlockSpec((row_count, span), block)
    keys = pl.BlockSpec((token_count, span), whole)
    slots = pl.BlockSpec((CAP, span), block)
    angles = pl.BlockSpec((token_count, width), whole)
    rows = [
        pl.BlockSpec((1, 1, row_count), lambda b, s: (b, 0, 0)),
        pl.BlockSpec((16, row_count), lambda b, s: (0, b)),
    ]
    sums = pl.BlockSpec((span // width, 1, 1, CAP), lambda b, s: (0, b, 0, 0))
    return pl.pallas_call(
        functools.partial(
            attention_backward_kernel, scaling=1.0 / math.sqrt(width), width=width
        ),
        grid_spec=pltpu.PrefetchScalarGridSpec(
            num_scalar_prefetch=1,
            grid=(BLOCKS,),
            in_specs=[tokens, keys, keys] + rows + [slots, sums, slots, angles, angles],
            out_specs=[tokens, keys, keys],
            scratch_shapes=[pltpu.VMEM((token_count, span), F32)] * 2,
        ),
        out_shape=[jax.ShapeDtypeStruct((token_count, span), BF16)] * 3,
        compiler_params=pltpu.CompilerParams(vmem_limit_bytes=VMEM_BYTES),
        name="attention_backward",
    )(begin, q, k, v, rank, table, out, lse.reshape(-1, BLOCKS, 1, CAP), grad, cosine, sine)


def pack_up_kernel(weight_ref, pieces_ref):
    units = pieces_ref.shape[2] // 2
    both = weight_ref[0].astype(F32)
    gate, up = both[:, 0, :], both[:, 1, :]
    for half in range(HALVES):
        at = slice(half * units, (half + 1) * units)
        pieces_ref[half] = jnp.concatenate([gate[:, at], up[:, at]], axis=1).astype(BF16)


def pack_down_kernel(weight_ref, first_ref, last_ref):
    turned_rows = weight_ref[0].astype(F32).T.astype(BF16)
    middle = first_ref.shape[1]
    first_ref[0] = turned_rows[:middle]
    last_ref[0] = turned_rows[middle:]


def row_major(array):
    return with_layout_constraint(array, Layout(major_to_minor=tuple(range(array.ndim))))


def exchanged(pieces):
    return row_major(lax.all_to_all(row_major(pieces), PLACES, 0, 0, tiled=True))


def over_groups(landed):
    return lax.all_gather(landed, "t", axis=0, tiled=False)


def group_sums(pieces):
    return lax.psum_scatter(pieces, "t", scatter_dimension=0, tiled=False)


def return_gradients(pieces):
    return exchanged(group_sums(pieces))


def other_core(column):
    return column + 1 - 2 * (column % 2)


def crossed(plane, j):
    return (plane, plane + 1 - 2 * (plane % 2), (plane + 2) % 4, 3 - plane)[j]


def meet(peers):
    barrier = pltpu.get_barrier_semaphore()
    for peer in peers:
        pl.semaphore_signal(barrier, inc=1, device_id=peer, device_id_type=MESH)
    pl.semaphore_wait(barrier, len(peers))


def partners():
    plane, half, column = lax.axis_index("z"), lax.axis_index("x"), lax.axis_index("grid")
    planes = [{"z": crossed(plane, j)} for j in range(PLANES)]
    along_x, along_y = {"x": 1 - half}, {"grid": (column + 2) % 4}
    core = {"grid": other_core(column)}
    return plane, half, column, planes, along_x, along_y, core


class Moves:
    def __init__(self, send, recv):
        self.send, self.recv, self.made = send, recv, {}

    def add(self, index, source, target, peer):
        self.made[index] = (source, target, peer)

    def copy(self, index, source, target, peer):
        return pltpu.make_async_remote_copy(
            src_ref=source, dst_ref=target, send_sem=self.send.at[index],
            recv_sem=self.recv.at[index], device_id=peer, device_id_type=MESH,
        )

    def start(self, index):
        self.copy(index, *self.made[index]).start()

    def arrived(self, index, target, peer):
        self.copy(index, target, target, peer).wait_recv()

    def all_sent(self):
        for index in self.made:
            self.copy(index, *self.made[index]).wait_send()


class Ride:
    def __init__(self, pieces_ref, landed_ref, send, recv, local, columns=None):
        if columns is None:
            columns = pl.ds(0, pieces_ref.shape[2])
        rows = pl.ds(0, pieces_ref.shape[1])
        plane, half = lax.axis_index("z"), lax.axis_index("x")
        self.moves = Moves(send, recv)
        self.landings = {}
        own = plane * HALVES + half
        self.keep = pltpu.make_async_copy(pieces_ref.at[own], landed_ref.at[own], local)
        self.peers = []
        for dz in range(PLANES):
            for dx in range(HALVES):
                index = dz * HALVES + dx
                if index == 0:
                    continue
                at_half = 1 - half if dx else half
                peer = {"z": crossed(plane, dz), "x": at_half}
                other = crossed(plane, dz) * HALVES + at_half
                source = pieces_ref.at[other, rows, columns]
                self.moves.add(index, source, landed_ref.at[own, rows, columns], peer)
                self.landings[index] = (landed_ref.at[other, rows, columns], peer)
                if dz and dx:
                    self.peers.append(peer)

    def begin(self, first=(4, 6, 2)):
        self.keep.start()
        for index in first:
            self.moves.start(index)

    def go_on(self, number, plan=((5,), (7,), (3,), (1,))):
        for index in plan[number] if number < len(plan) else ():
            self.moves.start(index)

    def finish(self):
        for index, (landing, peer) in self.landings.items():
            self.moves.arrived(index, landing, peer)
        self.moves.all_sent()
        self.keep.wait()


RIDE_SCRATCH = (
    pltpu.SemaphoreType.DMA((8,)),
    pltpu.SemaphoreType.DMA((8,)),
    pltpu.SemaphoreType.DMA,
)


def run_with_ride(steps, ride):
    steps[0]()
    if ride is not None:
        ride.begin()
    for number, step in enumerate(steps[1:-1]):
        step()
        if ride is not None:
            ride.go_on(number)
    steps[-1]()
    if ride is not None:
        ride.finish()


def gather_parts(slots_ref, out_ref, send, recv, local, same, share=2, more=(), chain=None):
    plane, half, column, planes, along_x, along_y, core = partners()
    cap, width = slots_ref.shape[-2:]
    middle = cap * share // 64 * 16
    y_column, core_column = (column + 2) % 4, other_core(column)
    core_y = (core_column + 2) % 4
    sources = [crossed(plane, j) for j in range(PLANES)]
    moves = Moves(send, recv)

    def piece(source, at_half, at_column, first=0, count=cap):
        columns = pl.ds(pl.multiple_of(at_column * width, width), width)
        return out_ref.at[source, at_half, pl.ds(first, count), columns]

    def slots_for(j):
        return slots_ref if same else slots_ref.at[sources[j]]

    keep = pltpu.make_async_copy(slots_for(0), piece(plane, half, column), local)
    for j in range(PLANES):
        source = sources[j]
        place = piece(source, half, column)
        if j and chain is None:
            moves.add(j, slots_for(j), piece(plane, half, column), planes[j])
        here = place if j else slots_for(0)
        moves.add(4 + j, here, place, along_x)
        moves.add(8 + j, here, place, along_y)
        moves.add(12 + j, here, place, core)
        from_x, from_y = piece(source, 1 - half, column), piece(source, half, y_column)
        first = piece(source, 1 - half, column, 0, middle)
        last = piece(source, half, y_column, middle, cap - middle)
        diagonal = piece(source, 1 - half, y_column)
        moves.add(16 + j, first, first, along_y)
        moves.add(20 + j, from_x, from_x, core)
        moves.add(24 + j, last, last, along_x)
        moves.add(28 + j, from_y, from_y, core)
        moves.add(32 + j, diagonal, diagonal, core)

    def begin():
        meet(planes[1:] + [along_x, along_y, core] + list(more))
        if chain is None:
            for j in (1, 3, 2):
                moves.start(j)
        else:
            chain.begin()
        keep.start()

    def spread(j):
        if j and chain is None:
            moves.arrived(j, piece(sources[j], half, column), planes[j])
        elif j:
            chain.arrived(j)
        for index in (4, 8, 12):
            moves.start(index + j)

    def forward(j):
        moves.arrived(4 + j, piece(sources[j], 1 - half, column), along_x)
        moves.start(16 + j)
        moves.start(20 + j)
        moves.arrived(8 + j, piece(sources[j], half, y_column), along_y)
        moves.start(24 + j)
        moves.start(28 + j)

    def cross(j):
        moves.arrived(16 + j, piece(sources[j], 1 - half, y_column, 0, middle), along_y)
        moves.arrived(24 + j, piece(sources[j], 1 - half, y_column, middle, cap - middle), along_x)
        moves.start(32 + j)

    def finish():
        for j in order:
            moves.arrived(12 + j, piece(sources[j], half, core_column), core)
            moves.arrived(20 + j, piece(sources[j], 1 - half, core_column), core)
            moves.arrived(28 + j, piece(sources[j], half, core_y), core)
            moves.arrived(32 + j, piece(sources[j], 1 - half, core_y), core)
        moves.all_sent()
        keep.wait()

    order = (0, 1, 3, 2)
    return begin, spread, forward, cross, finish, order


def gather_steps(*refs, **settings):
    begin, spread, forward, cross, finish, order = gather_parts(*refs, **settings)

    def step(number):
        if number < len(order):
            spread(order[number])
        if 0 <= number - 1 < len(order):
            forward(order[number - 1])
        if 0 <= number - 2 < len(order):
            cross(order[number - 2])

    return [begin] + [functools.partial(step, number) for number in range(len(order) + 2)] + [finish]


class Chain:
    def __init__(self, view, source, send, recv):
        plane = lax.axis_index("z")
        self.inner = (plane == 1) | (plane == 2)
        near, far = {"z": crossed(plane, 1)}, {"z": crossed(plane, 3)}
        self.views = [view(crossed(plane, j)) for j in range(PLANES)]
        self.send, self.recv = send, recv
        self.near_own = (0, 1, source, self.views[0], near)
        self.far_own = (1, 3, source, self.views[0], far)
        self.on_arrival = {
            1: (2, 2, self.views[1], self.views[1], far),
            3: (3, 2, self.views[3], self.views[3], near),
            2: (4, 3, self.views[2], self.views[2], near),
        }

    def copy(self, at_send, at_recv, source, target, peer):
        return pltpu.make_async_remote_copy(
            src_ref=source, dst_ref=target, send_sem=self.send.at[at_send],
            recv_sem=self.recv.at[at_recv], device_id=peer, device_id_type=MESH,
        )

    def begin(self):
        self.copy(*self.near_own).start()

        @pl.when(self.inner)
        def _():
            self.copy(*self.far_own).start()

    def arrived(self, j):
        place = self.views[j]
        self.copy(0, j, place, place, self.near_own[-1]).wait_recv()

        @pl.when(self.inner)
        def _():
            self.copy(*self.on_arrival[j]).start()

    def finish(self):
        self.copy(*self.near_own).wait_send()

        @pl.when(self.inner)
        def _():
            self.copy(*self.far_own).wait_send()
            for made in self.on_arrival.values():
                self.copy(*made).wait_send()


CHAIN_SCRATCH = (pltpu.SemaphoreType.DMA((5,)), pltpu.SemaphoreType.DMA((4,)))


def opening_kernel(
    tokens_ref, pieces_ref, up_ref, down_ref, out_ref, landed_ref, up_pieces_ref, first_ref,
    last_ref, send, recv, local, ride_send, ride_recv,
    ride_local, hop_send, hop_recv, *chain_sems, share
):
    plane, half, column = lax.axis_index("z"), lax.axis_index("x"), lax.axis_index("grid")
    width = tokens_ref.shape[1]
    middle = pieces_ref.shape[2] // 2
    left, right = pl.ds(0, middle), pl.ds(middle, middle)
    rows = pl.ds(0, pieces_ref.shape[1])
    along_x = {"x": 1 - half}

    def tokens_of(source):
        columns = pl.ds(pl.multiple_of(column * width, width), width)
        return out_ref.at[source, half, pl.ds(0, tokens_ref.shape[0]), columns]

    def shared_of(at_half):
        return lambda source: landed_ref.at[source * HALVES + at_half, rows, right]

    own = plane * HALVES + half
    tokens = Chain(tokens_of, tokens_ref, *chain_sems[:2])
    here = Chain(shared_of(half), pieces_ref.at[own, rows, right], *chain_sems[2:4])
    there = Chain(shared_of(1 - half), shared_of(1 - half)(plane), *chain_sems[4:])
    ride = Ride(pieces_ref, landed_ref, ride_send, ride_recv, ride_local, left)
    hop = pltpu.make_async_remote_copy(
        src_ref=pieces_ref.at[plane * HALVES + 1 - half, rows, right],
        dst_ref=landed_ref.at[own, rows, right],
        send_sem=hop_send, recv_sem=hop_recv, device_id=along_x, device_id_type=MESH,
    )
    landing = shared_of(1 - half)(plane)
    hop_here = pltpu.make_async_remote_copy(
        src_ref=landing, dst_ref=landing, send_sem=hop_send, recv_sem=hop_recv,
        device_id=along_x, device_id_type=MESH,
    )
    begin, spread, forward, cross, finish, _ = gather_parts(
        tokens_ref, out_ref, send, recv, local, True, share, ride.peers, tokens
    )

    def first():
        begin()
        ride.keep.start()
        spread(0)
        hop.start()
        here.begin()

    def second():
        spread(1)
        forward(0)
        ride.moves.start(2)

    def third():
        spread(3)
        forward(1)
        cross(0)
        hop_here.wait_recv()
        there.begin()
        here.arrived(1)

    def fourth():
        spread(2)
        forward(3)
        cross(1)
        ride.moves.start(6)
        ride.moves.start(4)
        here.arrived(3)
        there.arrived(1)

    def fifth():
        forward(2)
        cross(3)
        for index in (3, 7, 5, 1):
            ride.moves.start(index)
        here.arrived(2)
        there.arrived(3)
        cross(2)
        there.arrived(2)
        finish()
        ride.finish()
        hop.wait_send()
        for chain in (tokens, here, there):
            chain.finish()

    def compute():
        pack_up_kernel(up_ref, up_pieces_ref)
        pack_down_kernel(down_ref, first_ref, last_ref)

    carry([first], [second, third, fourth, fifth], (3, 6, 7, 7), compute)


def opened(tokens, pieces, up, down, collective_id, share):
    rows, width = tokens.shape
    experts, own_rows, _, units = up.shape
    places = experts * HALVES
    tile = own_rows // 2
    down_half = (places, own_rows // 2, units // HALVES)
    anywhere = pl.BlockSpec(memory_space=pl.ANY)
    half = pl.BlockSpec((1,) + down_half[1:], lambda p: (p, 0, 0))
    return pl.pallas_call(
        functools.partial(opening_kernel, share=share),
        grid=(places,),
        in_specs=[
            anywhere,
            anywhere,
            pl.BlockSpec((1, tile, 2, units), lambda p: (p // 2, p % 2, 0, 0)),
            pl.BlockSpec((1,) + down.shape[1:], lambda p: (p, 0, 0)),
        ],
        out_specs=[
            anywhere,
            anywhere,
            pl.BlockSpec((HALVES, tile, units), lambda p: (p // 2, p % 2, 0)),
            half,
            half,
        ],
        out_shape=[
            jax.ShapeDtypeStruct((PLANES, HALVES, rows, 4 * width), BF16),
            jax.ShapeDtypeStruct(pieces.shape, BF16),
            jax.ShapeDtypeStruct((places, own_rows, units), BF16),
            jax.ShapeDtypeStruct(down_half, BF16),
            jax.ShapeDtypeStruct(down_half, BF16),
        ],
        scratch_shapes=list(GATHER_SCRATCH) + list(RIDE_SCRATCH)
        + [pltpu.SemaphoreType.DMA, pltpu.SemaphoreType.DMA] + list(CHAIN_SCRATCH) * 3,
        compiler_params=pltpu.CompilerParams(
            collective_id=collective_id, has_side_effects=True, vmem_limit_bytes=VMEM_BYTES
        ),
        name="open_rows",
    )(tokens, pieces, up, down)


GATHER_SCRATCH = (
    pltpu.SemaphoreType.DMA((36,)),
    pltpu.SemaphoreType.DMA((36,)),
    pltpu.SemaphoreType.DMA,
)


def gather_kernel(*refs, same, share, rides):
    if rides:
        slots_ref, pieces_ref, out_ref, landed_ref = refs[:4]
        ride = Ride(pieces_ref, landed_ref, *refs[7:])
        scratch = refs[4:7]
    else:
        slots_ref, out_ref = refs[:2]
        ride, scratch = None, refs[2:]
    more = ride.peers if rides else ()
    run_with_ride(gather_steps(slots_ref, out_ref, *scratch, same, share, more), ride)


def gathered(slots, collective_id, ride=None, share=2):
    rows, width = slots.shape[-2:]
    rides = () if ride is None else (ride,)
    anywhere = pl.BlockSpec(memory_space=pl.ANY)
    out = pl.pallas_call(
        functools.partial(gather_kernel, same=slots.ndim == 2, share=share, rides=len(rides)),
        out_shape=[jax.ShapeDtypeStruct((PLANES, HALVES, rows, 4 * width), BF16)]
        + [jax.ShapeDtypeStruct(r.shape, BF16) for r in rides],
        in_specs=[anywhere] * (1 + len(rides)),
        out_specs=[anywhere] * (1 + len(rides)),
        scratch_shapes=list(GATHER_SCRATCH) + list(RIDE_SCRATCH) * len(rides),
        compiler_params=pltpu.CompilerParams(collective_id=collective_id, has_side_effects=True),
        name="gather_rows",
    )(slots, *rides)
    return out if rides else out[0]


def scatter_steps(
    partial_ref, out_ref, own, other, crossing, side, send, recv, load, share=2, more=()
):
    plane, half, column, planes, along_x, along_y, core = partners()
    cap, width = out_ref.shape[-2:]
    middle = cap * share // 64 * 16
    chunk = 32 if middle % 32 == 0 and cap % 32 == 0 else 16
    y_column, core_column = (column + 2) % 4, other_core(column)
    core_y = (core_column + 2) % 4
    halves = (half, 1 - half, half, 1 - half)
    own_columns = (column, column, y_column, y_column)
    core_columns = (core_column, core_column, core_y, core_y)
    moves = Moves(send, recv)
    first, last = pl.ds(0, middle), pl.ds(middle, cap - middle)

    def part(j, q, at_columns):
        columns = pl.ds(pl.multiple_of(at_columns[q] * width, width), width)
        return partial_ref.at[crossed(plane, j), halves[q], :, columns]

    def loading(j, q):
        return pltpu.make_async_copy(part(j, q, own_columns), own.at[j, q], load.at[4 * j + q])

    keep = pltpu.make_async_copy(own.at[0, 0], out_ref.at[plane], load.at[16])
    for j in range(PLANES):
        for q in range(4):
            moves.add(4 * j + q, part(j, q, core_columns), other.at[j, q], core)
        moves.add(16 + j, own.at[j, 3, first], crossing.at[j, first], along_x)
        moves.add(20 + j, own.at[j, 3, last], crossing.at[j, last], along_y)
        moves.add(24 + j, own.at[j, 2], side.at[j, 1], along_y)
        moves.add(28 + j, own.at[j, 1], side.at[j, 0], along_x)
        if j:
            moves.add(32 + j, own.at[j, 0], out_ref.at[plane], planes[j])

    def add(j, q, begin_row, count, terms):
        def step(i, nothing):
            rows = pl.ds(pl.multiple_of(begin_row + i * chunk, chunk), chunk)
            total = own[j, q, rows, :].astype(F32)
            for ref, index in terms:
                total = total + ref[index + (rows, slice(None))].astype(F32)
            own[j, q, rows, :] = total.astype(BF16)
            return nothing

        lax.fori_loop(0, count // chunk, step, 0)

    def chip_sum(j, q):
        moves.arrived(4 * j + q, other.at[j, q], core)
        loading(j, q).wait()
        add(j, q, 0, cap, [(other, (j, q))])

    def stage_one(j):
        chip_sum(j, 3)
        moves.start(16 + j)
        moves.start(20 + j)
        chip_sum(j, 2)
        chip_sum(j, 1)
        chip_sum(j, 0)

    def stage_two(j):
        moves.arrived(16 + j, crossing.at[j, first], along_x)
        add(j, 2, 0, middle, [(crossing, (j,))])
        moves.start(24 + j)
        moves.arrived(20 + j, crossing.at[j, last], along_y)
        add(j, 1, middle, cap - middle, [(crossing, (j,))])
        moves.start(28 + j)

    def stage_three(j):
        moves.arrived(24 + j, side.at[j, 1], along_y)
        moves.arrived(28 + j, side.at[j, 0], along_x)
        add(j, 0, 0, cap, [(side, (j, 0)), (side, (j, 1))])
        if j:
            moves.start(32 + j)
        else:
            keep.start()

    order = (2, 3, 1, 0)

    def begin():
        meet(planes[1:] + [along_x, along_y, core] + list(more))
        for j in order:
            for q in (3, 2, 1, 0):
                moves.start(4 * j + q)
                loading(j, q).start()

    def step(number):
        if number < len(order):
            stage_one(order[number])
        if 0 <= number - 1 < len(order):
            stage_two(order[number - 1])
        if 0 <= number - 2 < len(order):
            stage_three(order[number - 2])

    def finish():
        for j in range(1, PLANES):
            moves.arrived(32 + j, out_ref.at[crossed(plane, j)], planes[j])
        moves.all_sent()
        keep.wait()

    return [begin] + [functools.partial(step, number) for number in range(len(order) + 2)] + [finish]


def scatter_scratch(rows, width):
    return [
        pltpu.VMEM((PLANES, 4, rows, width), BF16),
        pltpu.VMEM((PLANES, 4, rows, width), BF16),
        pltpu.VMEM((PLANES, rows, width), BF16),
        pltpu.VMEM((PLANES, 2, rows, width), BF16),
        pltpu.SemaphoreType.DMA((36,)),
        pltpu.SemaphoreType.DMA((36,)),
        pltpu.SemaphoreType.DMA((17,)),
    ]


def scatter_kernel(*refs, share, rides):
    if rides:
        partial_ref, pieces_ref, out_ref, landed_ref = refs[:4]
        ride = Ride(pieces_ref, landed_ref, *refs[11:])
        scratch = refs[4:11]
    else:
        partial_ref, out_ref = refs[:2]
        ride, scratch = None, refs[2:]
    more = ride.peers if rides else ()
    run_with_ride(scatter_steps(partial_ref, out_ref, *scratch, share, more), ride)


def scattered(partial, rows, collective_id, ride=None, share=2):
    width = partial.shape[1] // 4
    rides = () if ride is None else (ride,)
    anywhere = pl.BlockSpec(memory_space=pl.ANY)
    out = pl.pallas_call(
        functools.partial(scatter_kernel, share=share, rides=len(rides)),
        out_shape=[jax.ShapeDtypeStruct((PLANES, rows, width), BF16)]
        + [jax.ShapeDtypeStruct(r.shape, BF16) for r in rides],
        in_specs=[anywhere] * (1 + len(rides)),
        out_specs=[anywhere] * (1 + len(rides)),
        scratch_shapes=scatter_scratch(rows, width) + list(RIDE_SCRATCH) * len(rides),
        compiler_params=pltpu.CompilerParams(
            collective_id=collective_id, has_side_effects=True, vmem_limit_bytes=VMEM_BYTES
        ),
        name="scatter_rows",
    )(partial.reshape(PLANES, HALVES, rows, 4 * width), *rides)
    return out if rides else out[0]


def carry(before, after, places, compute):
    number = pl.program_id(0)

    @pl.when(number == 0)
    def _():
        for step in before:
            step()

    compute()
    for at in sorted(set(places)):

        @pl.when(number == at)
        def _(at=at):
            for place, step in zip(places, after):
                if place == at:
                    step()


def join_halves(first_ref, last_ref, whole_ref):
    count, height, _ = first_ref.shape

    @pl.when(pl.program_id(0) == 0)
    def _():
        for place in range(count):
            whole_ref[2 * place * height : (2 * place + 1) * height, :] = first_ref[place]
            whole_ref[(2 * place + 1) * height : (2 * place + 2) * height, :] = last_ref[place]


def expert_forward_kernel(
    rows_ref, up_weight_ref, first_ref, last_ref, small_ref, rank_ref, member_ref, grad_ref,
    slope_ref, silu_ref, result_ref, share_ref, shared_ref, grad_rows_ref, down_weight_ref, *scratch
):
    join_halves(first_ref, last_ref, down_weight_ref)
    steps = gather_steps(grad_ref, grad_rows_ref, *scratch, False)
    units = slope_ref.shape[1]

    def compute():
        rows = rows_ref[0]
        made = dot(rows, up_weight_ref[...])
        gate, up = made[:, :units], made[:, units:]
        sigmoid = jax.nn.sigmoid(gate)
        silu = gate * sigmoid
        slope_ref[...] = up * sigmoid * (1.0 + gate * (1.0 - sigmoid))
        silu_ref[...] = silu
        inner = silu * up
        result_ref[0] = contract_last(inner.astype(BF16), down_weight_ref[...]).astype(BF16)
        cap, count = rows.shape[0], rank_ref.shape[2]
        pick = (lax.broadcasted_iota(jnp.int32, (cap, count), 0) == rank_ref[0]).astype(BF16)
        member = contract_last(pick, member_ref[...]) > 0.5
        logits = jnp.where(member, contract_last(rows, small_ref[...]), NEGATIVE)
        largest = jnp.max(logits, axis=1, keepdims=True)
        weights = jnp.where(member, jnp.exp(logits - largest), 0.0)
        mine = lax.broadcasted_iota(jnp.int32, weights.shape, 1) == 6 + lax.axis_index("z")
        total = jnp.sum(weights, axis=1, keepdims=True)
        own = jnp.sum(jnp.where(mine, weights, 0.0), axis=1, keepdims=True)
        share = own / jnp.where(total > 0.0, total, 1.0)
        share_ref[...] = share
        shared_ref[...] = (share * inner).astype(BF16)

    carry(steps[:2], steps[2:], (1, 3, 5, 6, 7, 7), compute)


def once(shape):
    return pl.BlockSpec(shape, lambda b: (0,) * len(shape), pipeline_mode=pl.Buffered(1))


def expert_forward(rows, up_weight, down_halves, small, rank, member, grad_slots, collective_id):
    _, cap, width = rows.shape
    units = down_halves[0].shape[2]
    count = BLOCKS * cap
    anywhere = pl.BlockSpec(memory_space=pl.ANY)
    block = lambda b: (b, 0)
    return pl.pallas_call(
        expert_forward_kernel,
        grid=(BLOCKS,),
        in_specs=[
            pl.BlockSpec((1, cap, width), lambda b: (b, 0, 0)),
            once(up_weight.shape),
            once(down_halves[0].shape),
            once(down_halves[1].shape),
            once(small.shape),
            pl.BlockSpec((1, 1, rank.shape[2]), lambda b: (b, 0, 0)),
            pl.BlockSpec((16, rank.shape[2]), lambda b: (0, b)),
            anywhere,
        ],
        out_specs=[
            pl.BlockSpec((cap, units), block),
            pl.BlockSpec((cap, units), block),
            pl.BlockSpec((1, cap, width), lambda b: (b, 0, 0)),
            pl.BlockSpec((cap, 1), block),
            pl.BlockSpec((cap, units), block),
            anywhere,
        ],
        out_shape=[
            jax.ShapeDtypeStruct((count, units), F32),
            jax.ShapeDtypeStruct((count, units), F32),
            jax.ShapeDtypeStruct((BLOCKS, cap, width), BF16),
            jax.ShapeDtypeStruct((count, 1), F32),
            jax.ShapeDtypeStruct((count, units), BF16),
            jax.ShapeDtypeStruct((PLANES, HALVES, cap, width), BF16),
        ],
        scratch_shapes=[pltpu.VMEM((width, units), BF16)] + list(GATHER_SCRATCH),
        compiler_params=pltpu.CompilerParams(
            collective_id=collective_id, has_side_effects=True, vmem_limit_bytes=VMEM_BYTES
        ),
        name="expert_forward",
    )(rows, up_weight, *down_halves, small, rank, member, grad_slots)


def expert_backward_kernel(
    slope_ref, silu_ref, grad_ref, share_ref, up_weight_ref, first_ref, last_ref, columns_ref,
    inner_ref, result_ref, *refs, rides
):
    count = 6 if rides else 5
    grad_rows_ref, grad_gate_up_ref, down_first_ref, down_last_ref, out_ref = refs[:5]
    down_weight_ref, kept_ref, scratch = refs[count], refs[count + 1], refs[count + 2 :]
    ride = Ride(kept_ref, refs[5], *scratch[7:]) if rides else None
    steps = scatter_steps(result_ref, out_ref, *scratch[:7], 1, ride.peers if rides else ())
    middle = down_first_ref.shape[1]
    number = pl.program_id(0)
    join_halves(first_ref, last_ref, down_weight_ref)

    def down_gradient():
        down_grad = contract_first(columns_ref[...], inner_ref[...]).astype(BF16)
        kept_ref[number] = down_grad[:middle]
        down_first_ref[0] = down_grad[:middle]
        down_last_ref[0] = down_grad[middle:]

    def rows_gradient():
        grad_inner = dot(grad_ref[0], down_weight_ref[...]) * share_ref[...]
        grad_gate_up = jnp.concatenate(
            [grad_inner * slope_ref[...], grad_inner * silu_ref[...]], axis=1
        ).astype(BF16)
        grad_gate_up_ref[...] = grad_gate_up
        grad_rows_ref[0] = contract_last(grad_gate_up, up_weight_ref[...]).astype(BF16)

    def compute():
        pl.when(number < BLOCKS)(down_gradient)
        pl.when(number >= BLOCKS)(rows_gradient)

    after, places = list(steps[1:]), [3, 7, 9, 11, 13, 15, 15]
    if rides:
        after += [ride.begin] + [functools.partial(ride.go_on, i) for i in range(4)] + [ride.finish]
        places += [7, 8, 9, 10, 12, 15]
    carry(steps[:1], after, places, compute)


def expert_backward(
    slope, silu, grad_rows, share, up_weight, down_halves, inner, result, rides, collective_id
):
    _, cap, width = grad_rows.shape
    count, units = slope.shape
    tile = width // BLOCKS
    anywhere = pl.BlockSpec(memory_space=pl.ANY)
    at_row = lambda b: jnp.maximum(b - BLOCKS, 0)
    at_tile = lambda b: jnp.minimum(b, BLOCKS - 1)
    block = lambda b: (at_row(b), 0)
    rows = pl.BlockSpec((1, cap, width), lambda b: (at_row(b), 0, 0))
    half = pl.BlockSpec((1, tile // 2, units), lambda b: (at_tile(b), 0, 0))
    half_shape = jax.ShapeDtypeStruct((BLOCKS, tile // 2, units), BF16)
    return pl.pallas_call(
        functools.partial(expert_backward_kernel, rides=rides),
        grid=(2 * BLOCKS,),
        in_specs=[
            pl.BlockSpec((cap, units), block),
            pl.BlockSpec((cap, units), block),
            rows,
            pl.BlockSpec((cap, 1), block),
            once(up_weight.shape),
            once(down_halves[0].shape),
            once(down_halves[1].shape),
            pl.BlockSpec((count, tile), lambda b: (0, at_tile(b))),
            once(inner.shape),
            anywhere,
        ],
        out_specs=[rows, pl.BlockSpec((cap, 2 * units), block), half, half, anywhere]
        + [anywhere] * rides,
        out_shape=[
            jax.ShapeDtypeStruct((BLOCKS, cap, width), BF16),
            jax.ShapeDtypeStruct((count, 2 * units), BF16),
            half_shape,
            half_shape,
            jax.ShapeDtypeStruct((PLANES, cap, width // 4), BF16),
        ]
        + [half_shape] * rides,
        scratch_shapes=[
            pltpu.VMEM((width, units), BF16),
            pltpu.VMEM((BLOCKS, tile // 2, units), BF16),
        ]
        + scatter_scratch(cap, width // 4)
        + list(RIDE_SCRATCH) * rides,
        compiler_params=pltpu.CompilerParams(
            collective_id=collective_id, has_side_effects=True, vmem_limit_bytes=VMEM_BYTES
        ),
        name="expert_backward",
    )(
        slope, silu, grad_rows, share, up_weight, *down_halves, grad_rows.reshape(count, width), inner,
        result.reshape(PLANES, HALVES, cap, width),
    )


def expert_gradient_kernel(
    rows_ref, grad_gate_up_ref, partial_ref, pieces_ref, up_first_ref, up_last_ref, out_ref,
    landed_ref, *scratch
):
    ride = Ride(pieces_ref, landed_ref, *scratch[7:])
    steps = scatter_steps(partial_ref, out_ref, *scratch[:7], 1, ride.peers)

    def compute():
        up_grad = contract_first(rows_ref[...], grad_gate_up_ref[...]).astype(BF16)
        up_first_ref[...] = up_grad[:, :EARLY]
        up_last_ref[...] = up_grad[:, EARLY:]

    def with_ride(number):
        steps[1 + number]()
        ride.go_on(number)

    after = [functools.partial(with_ride, number) for number in range(6)]
    carry([steps[0], ride.begin], after + [steps[-1], ride.finish], (0, 2, 4, 6, 7, 7, 7, 7), compute)


def expert_gradient(rows, grad_gate_up, partial, pieces, collective_id):
    count, width = rows.shape
    units = grad_gate_up.shape[1]
    cap, tile = count // BLOCKS, width // BLOCKS
    anywhere = pl.BlockSpec(memory_space=pl.ANY)
    return pl.pallas_call(
        expert_gradient_kernel,
        grid=(BLOCKS,),
        in_specs=[
            pl.BlockSpec((count, tile), lambda b: (0, b)),
            once((count, units)),
            anywhere,
            anywhere,
        ],
        out_specs=[
            pl.BlockSpec((tile, EARLY), lambda b: (b, 0)),
            pl.BlockSpec((tile, units - EARLY), lambda b: (b, 0)),
            anywhere,
            anywhere,
        ],
        out_shape=[
            jax.ShapeDtypeStruct((width, EARLY), BF16),
            jax.ShapeDtypeStruct((width, units - EARLY), BF16),
            jax.ShapeDtypeStruct((PLANES, cap, width // 4), BF16),
            jax.ShapeDtypeStruct(pieces.shape, BF16),
        ],
        scratch_shapes=scatter_scratch(cap, width // 4) + list(RIDE_SCRATCH),
        compiler_params=pltpu.CompilerParams(
            collective_id=collective_id, has_side_effects=True, vmem_limit_bytes=VMEM_BYTES
        ),
        name="expert_gradient",
    )(rows, grad_gate_up, partial.reshape(PLANES, HALVES, cap, width), pieces)


def closing_kernel(
    hidden_ref, q_ref, k_ref, v_ref, rows_ref, gated_ref, partial_ref, grad_ref, out_ref, *scratch
):
    steps = scatter_steps(partial_ref, out_ref, *scratch)
    span = q_ref.shape[1]

    def compute():
        hidden = hidden_ref[...]
        for place, ref in enumerate((q_ref, k_ref, v_ref)):
            at = slice(place * span, (place + 1) * span)
            grad_ref[:, at] = contract_first(hidden, ref[...]).astype(BF16)
        grad_ref[:, 3 * span :] = contract_first(rows_ref[...], gated_ref[...]).astype(BF16)

    carry(steps[:1], steps[1:], (1, 3, 6, 7, 7, 7, 7), compute)


def closing(hidden, q, k, v, rows, gated, partial, collective_id):
    count, width = hidden.shape
    slot_count, span = gated.shape
    tile, own_rows = width // BLOCKS, count // BLOCKS
    anywhere = pl.BlockSpec(memory_space=pl.ANY)
    return pl.pallas_call(
        closing_kernel,
        grid=(BLOCKS,),
        in_specs=[
            pl.BlockSpec((count, tile), lambda b: (0, b)),
            once((count, span)),
            once((count, span)),
            once((count, span)),
            pl.BlockSpec((slot_count, tile), lambda b: (0, b)),
            once((slot_count, span)),
            anywhere,
        ],
        out_specs=[pl.BlockSpec((tile, 4 * span), lambda b: (b, 0)), anywhere],
        out_shape=[
            jax.ShapeDtypeStruct((width, 4 * span), BF16),
            jax.ShapeDtypeStruct((PLANES, own_rows, width // 4), BF16),
        ],
        scratch_shapes=scatter_scratch(own_rows, width // 4),
        compiler_params=pltpu.CompilerParams(
            collective_id=collective_id, has_side_effects=True, vmem_limit_bytes=VMEM_BYTES
        ),
        name="closing",
    )(hidden, q, k, v, rows, gated, partial.reshape(PLANES, HALVES, own_rows, width))


def finish_kernel(
    query_ref, all_ref, small_ref, query_grad_ref, kv_grad_ref, out_grad_ref, gain_first_ref,
    gain_second_ref, router_first_ref, router_second_ref
):
    span = query_ref.shape[2] // 4
    head_width = query_grad_ref.shape[3]
    pair = span // head_width
    own_rows = query_grad_ref.shape[1]
    for half in range(HALVES):
        landed = query_ref[half, :own_rows, :].astype(F32)
        for head in range(pair):
            at = half * pair + head
            query_grad_ref[0, :, at, :] = landed[:, head * head_width : (head + 1) * head_width]
        out_grad_ref[half] = landed[:, 3 * span :].T

    @pl.when(pl.program_id(0) == 0)
    def _():
        for half in range(HALVES):
            total = sum(
                all_ref[z * HALVES + half, :own_rows, span : 3 * span].astype(F32)
                for z in range(PLANES)
            )
            for kind in range(2):
                for head in range(pair):
                    first = kind * span + head * head_width
                    kv_grad_ref[:, half * pair + head, kind, :] = total[:, first : first + head_width]

        total = sum(small_ref[place] for place in range(BLOCKS))
        gain_first_ref[...] = total[0:1]
        gain_second_ref[...] = total[1:2]
        router_first_ref[...] = total[2 : 2 + PLANES]
        router_second_ref[...] = total[2 + PLANES : 2 + 2 * PLANES]


def unpack_up_kernel(first_ref, last_ref, grad_ref):
    units = grad_ref.shape[3] // HALVES
    halves = [
        jnp.concatenate([first_ref[half], last_ref[half]], axis=1).astype(F32) for half in range(HALVES)
    ]
    for kind in range(2):
        at = slice(kind * units, (kind + 1) * units)
        grad_ref[0, :, kind, :] = jnp.concatenate([half[:, at] for half in halves], axis=1)


def unpack_up(first, last):
    places, own_rows, early = first.shape
    units = early + last.shape[2]
    tile = own_rows // 2
    return pl.pallas_call(
        unpack_up_kernel,
        grid=(places // HALVES, 2),
        in_specs=[
            pl.BlockSpec((HALVES, tile, early), lambda e, r: (e, r, 0)),
            pl.BlockSpec((HALVES, tile, units - early), lambda e, r: (e, r, 0)),
        ],
        out_specs=pl.BlockSpec((1, tile, 2, units), lambda e, r: (e, r, 0, 0)),
        out_shape=jax.ShapeDtypeStruct((places // HALVES, own_rows, 2, units), F32),
        compiler_params=pltpu.CompilerParams(vmem_limit_bytes=VMEM_BYTES),
        name="unpack_up",
    )(first, last)


def swap_kernel(pieces_ref, landed_ref, *scratch):
    ride = Ride(pieces_ref, landed_ref, *scratch)
    meet([peer for _, _, peer in ride.moves.made.values()])
    ride.begin(tuple(ride.moves.made))
    ride.finish()


def swapped(pieces, collective_id):
    whole = pl.BlockSpec(memory_space=pltpu.VMEM)
    return pl.pallas_call(
        swap_kernel,
        out_shape=jax.ShapeDtypeStruct(pieces.shape, pieces.dtype),
        in_specs=[whole],
        out_specs=whole,
        scratch_shapes=list(RIDE_SCRATCH),
        compiler_params=pltpu.CompilerParams(collective_id=collective_id, has_side_effects=True),
        name="swap_small",
    )(pieces)


def finish(landed, small, own_rows, span, heads, head_width):
    places, height, width = landed.shape
    return pl.pallas_call(
        finish_kernel,
        grid=(PLANES,),
        in_specs=[
            pl.BlockSpec((HALVES, height, width), lambda e: (e, 0, 0)),
            once((places, height, width)),
            once(small.shape),
        ],
        out_specs=[
            pl.BlockSpec((1, own_rows, heads, head_width), lambda e: (e, 0, 0, 0)),
            pl.BlockSpec((own_rows, heads, 2, head_width), lambda e: (0, 0, 0, 0)),
            pl.BlockSpec((HALVES, span, own_rows), lambda e: (e, 0, 0)),
            pl.BlockSpec((1, small.shape[2]), lambda e: (0, 0)),
            pl.BlockSpec((1, small.shape[2]), lambda e: (0, 0)),
            pl.BlockSpec((PLANES, small.shape[2]), lambda e: (0, 0)),
            pl.BlockSpec((PLANES, small.shape[2]), lambda e: (0, 0)),
        ],
        out_shape=[
            jax.ShapeDtypeStruct((PLANES, own_rows, heads, head_width), F32),
            jax.ShapeDtypeStruct((own_rows, heads, 2, head_width), F32),
            jax.ShapeDtypeStruct((places, span, own_rows), F32),
            jax.ShapeDtypeStruct((1, small.shape[2]), F32),
            jax.ShapeDtypeStruct((1, small.shape[2]), F32),
            jax.ShapeDtypeStruct((PLANES, small.shape[2]), F32),
            jax.ShapeDtypeStruct((PLANES, small.shape[2]), F32),
        ],
        compiler_params=pltpu.CompilerParams(vmem_limit_bytes=VMEM_BYTES),
        name="attention_weight_gradients",
    )(landed, landed, small)


def grid_sum(values):
    shape = values.shape
    return lax.all_gather(values.reshape(-1, 128), "grid", axis=0).sum(axis=0).reshape(shape)


def prefix_ranks(member):
    counted = member.astype(BF16)
    width = member.shape[-1]
    before = jnp.arange(width)[:, None] < jnp.arange(width)[None, :]
    return jnp.where(member, dot(counted, before.astype(BF16)).astype(jnp.int32), -1)


def picks(rank):
    return (jnp.arange(CAP, dtype=jnp.int32)[:, None] == rank[..., None, :]).astype(BF16)


def members(first, second):
    names = jnp.arange(PLANES, dtype=first.dtype).reshape((PLANES,) + (1,) * first.ndim)
    return (first[None] == names) | (second[None] == names)


def route_gates(logits, member):
    shown = jnp.where(member, logits, NEGATIVE)
    weights = jnp.where(member, jnp.exp(shown - jnp.max(shown, axis=0, keepdims=True)), 0.0)
    return weights / jnp.sum(weights, axis=0, keepdims=True)


def logits_grad(gates, grad_gates):
    return gates * (grad_gates - jnp.sum(gates * grad_gates, axis=0, keepdims=True))


def exact_first(left, right):
    return lax.dot_general(
        left, right, (((0,), (0,)), ((), ())), precision=lax.Precision.HIGHEST
    )


def exact_last(left, right):
    return lax.dot_general(
        left, right, (((1,), (1,)), ((), ())), precision=lax.Precision.HIGHEST
    )


def norm_sums(grad_hidden, scaled, router, grad_gates, width, gates=None, hidden=None, member=None):
    parts = [
        grad_gates,
        exact_last(router.astype(F32), scaled),
        jnp.sum(grad_hidden * scaled, axis=1)[None],
    ]
    if gates is None:
        parts.append(contract_last(router, hidden))
    parts = grid_sum(jnp.concatenate(parts, axis=0))
    if gates is None:
        gates = route_gates(parts[2 * PLANES + 1 :], member)
    grad_logits = logits_grad(gates, parts[:PLANES])
    inner = parts[2 * PLANES] + jnp.sum(grad_logits * parts[PLANES : 2 * PLANES], axis=0)
    return grad_logits, inner[:, None] / width, gates


def per_device(
    tokens, segment_ids, attention_routes, expert_routes, attention_gain, attention_kv,
    attention_query, attention_out, attention_router, feedforward_gain, feedforward_router,
    expert_gate_up, expert_down, output_grad,
):
    groups = lax.axis_size("t")
    grid_count = lax.axis_size("grid")
    group = lax.axis_index("t")
    plane = lax.axis_index("z")
    place = plane * HALVES + lax.axis_index("x")
    column = lax.axis_index("grid")
    rows, features = tokens.shape
    width_all = features * grid_count
    token_count = BLOCKS * rows
    own_rows = attention_gain.shape[0]
    head_width = attention_kv.shape[3]
    head_pair = attention_kv.shape[1] // HALVES
    span = head_pair * head_width
    hidden_units = expert_gate_up.shape[3] // HALVES

    def mine(array, axis=0):
        return lax.dynamic_slice_in_dim(array, column * features, features, axis)

    def own(array, axis=0):
        return lax.dynamic_slice_in_dim(array, place * rows, rows, axis)

    query_pieces = attention_query.reshape(PLANES, own_rows, HALVES, span).transpose(0, 2, 1, 3)
    kv_pieces = attention_kv.reshape(own_rows, HALVES, head_pair, 2, head_width)
    kv_pieces = kv_pieces.transpose(1, 0, 3, 2, 4).reshape(1, HALVES, own_rows, 2 * span)
    kv_pieces = jnp.broadcast_to(kv_pieces, (PLANES,) + kv_pieces.shape[1:])
    qkv_pieces = jnp.concatenate([query_pieces, kv_pieces], axis=-1)
    out_pieces = attention_out.reshape(BLOCKS, span, own_rows).swapaxes(1, 2)
    first_pieces = jnp.concatenate([out_pieces, qkv_pieces.reshape(BLOCKS, own_rows, 3 * span)], axis=2)
    own_routes = jnp.concatenate([attention_routes, expert_routes], axis=1)
    small = jnp.concatenate(
        [attention_gain[:, None], feedforward_gain[:, None], attention_router, feedforward_router],
        axis=1,
    )
    small = lax.all_gather(small, "t", axis=0).reshape(-1, small.shape[1])
    small = small.T.reshape(small.shape[1], -1)
    spare = jnp.zeros((small.shape[0], features - small.shape[1] % features), BF16)
    small = jnp.concatenate([small, spare], axis=1).reshape(-1, features)
    under = jnp.concatenate([own_routes.T.astype(BF16), small], axis=0)
    under = jnp.pad(under, ((0, -under.shape[0] % 16), (0, 0)))
    everything, first_weight, up_pieces, *down_halves = opened(
        jnp.concatenate([tokens, under], axis=0), first_pieces, expert_gate_up,
        expert_down.reshape(BLOCKS, hidden_units, own_rows), 0, 3,
    )
    first_weight = over_groups(first_weight).reshape(width_all, 4 * span)
    out_weight, qkv_weight = first_weight[:, :span], first_weight[:, span:]
    up_weight = over_groups(exchanged(up_pieces)).reshape(width_all, 2 * hidden_units)
    under = everything[:, :, rows:, :features].reshape(BLOCKS, -1, features).swapaxes(0, 1)
    small = under[4:, :, : groups * own_rows].reshape(-1, BLOCKS, groups, own_rows)
    small = jnp.pad(small.swapaxes(1, 2).reshape(-1, width_all), ((0, 4), (0, 0)))
    gain_first, gain_second = mine(small[0]).astype(F32), mine(small[1]).astype(F32)
    router_first, router_second = mine(small[2:6], 1), mine(small[6:10], 1)

    member_first, member_second = members(under[0], under[1]), members(under[2], under[3])
    own_member_first = lax.dynamic_index_in_dim(member_first, place, 1, keepdims=False)
    own_member_second = lax.dynamic_index_in_dim(member_second, place, 1, keepdims=False)
    rank = prefix_ranks(
        jnp.concatenate(
            [
                lax.dynamic_index_in_dim(member_first, plane, 0, keepdims=False),
                lax.dynamic_index_in_dim(member_second, plane, 0, keepdims=False),
                own_member_first,
                own_member_second,
            ],
            axis=0,
        )
    )
    rank_first, rank_second = rank[:BLOCKS, None], rank[BLOCKS : 2 * BLOCKS, None]
    own_pick_first = picks(rank[2 * BLOCKS : 2 * BLOCKS + PLANES])
    own_pick_second = picks(rank[2 * BLOCKS + PLANES :])
    member_first = member_first.reshape(PLANES, token_count)
    member_second = member_second.reshape(PLANES, token_count)

    def to_slots(values, pick):
        return jnp.einsum("est,tf->esf", pick, values, preferred_element_type=F32).astype(BF16)

    def to_tokens(slots, pick):
        return jnp.einsum("est,esf->etf", pick, slots, preferred_element_type=F32)

    grad_out = output_grad.astype(F32)
    cosine, sine = rope_tables(token_count, head_width)
    cosine, sine = jnp.asarray(cosine), jnp.asarray(sine)
    hidden_first, queries, keys, values, logits_first, inverse_first = project(
        everything, rows, small, first_weight, cosine, sine, span, head_width
    )
    gates_first = route_gates(logits_first[2 : 2 + PLANES], member_first)
    own_gates_first = own(gates_first, 1)
    position = jnp.arange(token_count, dtype=jnp.int32)
    segment = lax.dynamic_slice_in_dim(segment_ids, group * token_count, token_count, 0)
    opens = jnp.concatenate([jnp.ones((1,), jnp.bool_), segment[1:] != segment[:-1]])
    document_start = lax.cummax(jnp.where(opens, position, 0))
    begin = document_start.reshape(BLOCKS, rows)[:, 0] // rows
    table = token_table(
        position, document_start, lax.dynamic_index_in_dim(gates_first, plane, 0, keepdims=False)
    )
    attention_args = (begin, queries, keys, values, rank_first, table)
    attended, gated, gate_slots_first, lse = attention_forward(*attention_args, head_width)
    branch, grad_out_slots = lax.optimization_barrier(
        (contract_last(attended, out_weight).astype(BF16), to_slots(output_grad, own_pick_second))
    )
    branch_slots, down_first = scattered(
        branch, CAP, 2, ride=down_halves[0], share=1
    )
    branch_first = to_tokens(branch_slots, own_pick_first)
    residual = tokens.astype(F32) + jnp.sum(own_gates_first[:, :, None] * branch_first, axis=0)

    square = grid_sum(jnp.sum(residual * residual, axis=1))
    inverse_second = lax.rsqrt(square / width_all + EPSILON)[:, None]
    normed_second = residual * inverse_second
    hidden_second = (normed_second * gain_second).astype(BF16)
    slots_second, down_last = gathered(
        to_slots(hidden_second, own_pick_second), 1, ride=down_halves[1], share=3
    )
    down_weight = [
        over_groups(half).reshape((groups * BLOCKS,) + half.shape[1:]) for half in (down_first, down_last)
    ]
    slots_second = slots_second.reshape(BLOCKS, CAP, width_all)
    gate_pre, up_pre, result, gate_slots_second, inner, grad_slots_second = expert_forward(
        slots_second,
        up_weight,
        down_weight,
        small,
        rank_second,
        jnp.pad(member_second.astype(BF16), ((6, 6), (0, 0))),
        grad_out_slots,
        4,
    )
    grad_slots_second = grad_slots_second.reshape(BLOCKS, CAP, width_all)
    grad_rows, grad_gate_up, grad_down_first, grad_down_last, result_slots, *landed = expert_backward(
        gate_pre, up_pre, grad_slots_second, gate_slots_second, up_weight, down_weight, inner, result,
        int(groups == 1), 5,
    )
    if groups > 1:
        grad_down = jnp.concatenate([grad_down_first, grad_down_last], axis=1)
        grad_down = group_sums(grad_down.reshape(groups, BLOCKS, own_rows, hidden_units))
        grad_down_first, grad_down_last = jnp.split(grad_down, 2, axis=1)
        landed = [exchanged(grad_down_first)]
    grad_down_first = landed[0]
    grad_up_first, grad_up, grad_rows, grad_down_last = expert_gradient(
        slots_second.reshape(-1, width_all), grad_gate_up, grad_rows, grad_down_last, 6
    )
    branch_second = to_tokens(result_slots, own_pick_second)

    grad_hidden_second = jnp.sum(to_tokens(grad_rows, own_pick_second), axis=0)
    grad_logits_second, inner_mean, own_gates_second = norm_sums(
        grad_hidden_second, normed_second * gain_second, router_second,
        jnp.sum(branch_second * grad_out[None], axis=2), width_all,
        hidden=hidden_second, member=own_member_second,
    )
    grad_hidden_second = grad_hidden_second + exact_first(
        grad_logits_second, router_second.astype(F32)
    )
    grad_normed = grad_hidden_second * gain_second
    grad_residual = grad_out + inverse_second * (grad_normed - normed_second * inner_mean)

    grad_up_first = return_gradients(grad_up_first.reshape(groups, BLOCKS, own_rows, EARLY))
    grad_slots_first = gathered(to_slots(grad_residual.astype(BF16), own_pick_first), 8)
    (
        grad_slots_first, grad_up_first, residual, own_gates_second, branch_second, hidden_second,
        grad_logits_second, grad_hidden_second, normed_second,
    ) = lax.optimization_barrier(
        (
            grad_slots_first, grad_up_first, residual, own_gates_second, branch_second, hidden_second,
            grad_logits_second, grad_hidden_second, normed_second,
        )
    )
    layer_output = residual + jnp.sum(own_gates_second[:, :, None] * branch_second, axis=0)
    layer_output = layer_output.astype(BF16)
    grad_router_second = exact(grad_logits_second, hidden_second.astype(F32))
    grad_gain_second = jnp.sum(grad_hidden_second * normed_second, axis=0)
    grad_slots_first = grad_slots_first.reshape(BLOCKS * CAP, -1)
    grad_up, grad_slots_first = lax.optimization_barrier((grad_up, grad_slots_first))
    grad_up = return_gradients(grad_up.reshape(groups, BLOCKS, own_rows, 2 * hidden_units - EARLY))
    grad_attended = gate_slots_first * dot(grad_slots_first, out_weight)
    grad_attended = grad_attended.astype(BF16)
    grad_query, grad_keys, grad_values = attention_backward(
        *attention_args, attended, lse, grad_attended, cosine, sine, head_width
    )
    grad_qkv = jnp.concatenate([grad_query, grad_keys, grad_values], axis=1)
    grad_hidden = contract_last(grad_qkv, qkv_weight).astype(BF16)
    grad_first, grad_hidden = closing(
        hidden_first, grad_query, grad_keys, grad_values, grad_slots_first, gated, grad_hidden, 3
    )
    grad_hidden = jnp.sum(grad_hidden.astype(F32), axis=0)
    grad_first, grad_up = lax.optimization_barrier((grad_first, grad_up))
    grad_first = return_gradients(grad_first.reshape(groups, BLOCKS, own_rows, 4 * span))
    expert_gate_up_grad = unpack_up(grad_up_first, grad_up)
    expert_down_grad = jnp.concatenate([grad_down_first, grad_down_last], axis=1)
    expert_down_grad = expert_down_grad.swapaxes(1, 2).reshape(expert_down.shape)

    own_normed = tokens.astype(F32) * own(inverse_first)
    own_hidden = (own_normed * gain_first).astype(BF16)
    grad_logits_first, inner_mean, _ = norm_sums(
        grad_hidden, own_normed * gain_first, router_first,
        jnp.sum(branch_first * grad_residual[None], axis=2), width_all, gates=own_gates_first,
    )
    grad_hidden_first = grad_hidden + exact_first(grad_logits_first, router_first.astype(F32))
    grad_router_first = exact(grad_logits_first, own_hidden.astype(F32))
    grad_gain_first = jnp.sum(grad_hidden_first * own_normed, axis=0)
    grad_normed = grad_hidden_first * gain_first
    input_grad = grad_residual + own(inverse_first) * (grad_normed - own_normed * inner_mean)

    small_grads = jnp.concatenate(
        [grad_gain_first[None], grad_gain_second[None], grad_router_first, grad_router_second],
        axis=0,
    )
    small_grads = lax.all_gather(small_grads, "grid", axis=1, tiled=True)
    if groups > 1:
        small_grads = lax.psum(small_grads, "t")
    small_grads = small_grads.reshape(-1, groups, BLOCKS, own_rows)
    small_grads = lax.dynamic_index_in_dim(small_grads, group, 1, keepdims=False).swapaxes(0, 1)
    small_grads = jnp.pad(small_grads, ((0, 0), (0, 6), (0, -own_rows % 128)))
    small_grads, grad_first = lax.optimization_barrier((small_grads, grad_first))
    (
        attention_query_grad, attention_kv_grad, attention_out_grad, gain_grad_first,
        gain_grad_second, router_grad_first, router_grad_second,
    ) = finish(
        grad_first, swapped(small_grads, 7), own_rows, span, attention_kv.shape[1], head_width
    )
    attention_out_grad = attention_out_grad.reshape(attention_out.shape)
    return (
        layer_output,
        input_grad.astype(BF16),
        gain_grad_first[0, :own_rows],
        attention_kv_grad,
        attention_query_grad.astype(F32),
        attention_out_grad.astype(F32),
        router_grad_first[:, :own_rows].T,
        gain_grad_second[0, :own_rows],
        router_grad_second[:, :own_rows].T,
        expert_gate_up_grad,
        expert_down_grad.astype(F32),
    )


def solution(mesh):
    groups = mesh.shape["wide"] // BLOCKS
    shape = (groups, PLANES, HALVES, mesh.shape["grid"])
    inner_mesh = Mesh(mesh.devices.reshape(shape), ("t", "z", "x", "grid"))
    wide = ("t", "z", "x")
    in_specs = (
        P(wide, "grid"),
        P(),
        P(wide, None),
        P(wide, None),
        P(wide),
        P(wide, "grid", None, None),
        P(None, wide, "grid", None),
        P(None, "grid", None, wide),
        P(wide, None),
        P(wide),
        P(wide, None),
        P(None, wide, None, "grid"),
        P(None, "grid", wide),
        P(wide, "grid"),
    )
    out_specs = (
        P(wide, "grid"),
        P(wide, "grid"),
        P(wide),
        P(wide, "grid", None, None),
        P(None, wide, "grid", None),
        P(None, "grid", None, wide),
        P(wide, None),
        P(wide),
        P(wide, None),
        P(None, wide, None, "grid"),
        P(None, "grid", wide),
    )
    return jax.shard_map(
        per_device, mesh=inner_mesh, in_specs=in_specs, out_specs=out_specs, check_vma=False
    )
```

```python
import functools
import math

import jax
import jax.numpy as jnp
import numpy as np
from jax import lax
from jax.experimental import pallas as pl
from jax.experimental.layout import Layout, with_layout_constraint
from jax.experimental.pallas import tpu as pltpu
from jax.sharding import Mesh, PartitionSpec as P

CAP = 320
PLANES = 4
HALVES = 2
BLOCKS = PLANES * HALVES
EPSILON = 1e-05
ROPE_BASE = 10000.0
NEGATIVE = -1e30
BF16 = jnp.bfloat16
F32 = jnp.float32
PLACES = ("z", "x")
MESH = pl.DeviceIdType.MESH
VMEM_BYTES = 56 * 1024 * 1024
EARLY = 128


def rope_tables(token_count, width):
    half = width // 2
    frequency = np.float32(ROPE_BASE) ** (-np.arange(half, dtype=np.float32) / np.float32(half))
    angles = np.arange(token_count, dtype=np.float32)[:, None] * frequency.astype(np.float32)[None, :]
    cosine, sine = np.cos(angles).astype(np.float32), np.sin(angles).astype(np.float32)
    return np.concatenate([cosine, cosine], axis=1), np.concatenate([-sine, sine], axis=1)


def turned(values, cosine, sine):
    return values * cosine + pltpu.roll(values, values.shape[1] // 2, 1) * sine


def dot(left, right):
    return jnp.dot(left, right, preferred_element_type=F32)


def contract_first(left, right):
    return lax.dot_general(left, right, (((0,), (0,)), ((), ())), preferred_element_type=F32)


def contract_last(left, right):
    return lax.dot_general(left, right, (((1,), (1,)), ((), ())), preferred_element_type=F32)


def exact(left, right):
    return jnp.dot(left, right, precision=lax.Precision.HIGHEST)


def project_kernel(
    tokens_ref, small_ref, query_weight_ref, shared_weight_ref, cos_ref, sin_ref,
    hidden_ref, q_ref, k_ref, v_ref, logits_ref, inverse_ref, *, head_width
):
    x = tokens_ref[0, 0].astype(F32)
    inverse = lax.rsqrt(jnp.mean(x * x, axis=1, keepdims=True) + EPSILON)
    inverse_ref[...] = inverse
    hidden = (x * inverse * small_ref[:1, :].astype(F32)).astype(BF16)
    hidden_ref[...] = hidden
    logits_ref[...] = contract_last(small_ref[...], hidden)
    queries = dot(hidden, query_weight_ref[...])
    shared = dot(hidden, shared_weight_ref[...])
    span = q_ref.shape[1]
    cosine, sine = cos_ref[...], sin_ref[...]
    for head in range(span // head_width):
        at = slice(head * head_width, (head + 1) * head_width)
        q_ref[:, at] = turned(queries[:, at], cosine, sine).astype(BF16)
        k_ref[:, at] = turned(shared[:, at], cosine, sine).astype(BF16)
    v_ref[...] = shared[:, span:].astype(BF16)


def project(tokens, rows, small, weight, cosine, sine, span, head_width):
    width = tokens.shape[-1]
    token_count = BLOCKS * rows
    whole = lambda b: (0, 0)
    block = lambda b: (b, 0)
    return pl.pallas_call(
        functools.partial(project_kernel, head_width=head_width),
        grid=(BLOCKS,),
        in_specs=[
            pl.BlockSpec((1, 1, rows, width), lambda b: (b // HALVES, b % HALVES, 0, 0)),
            pl.BlockSpec(small.shape, whole),
            pl.BlockSpec((width, span), lambda b: (0, 1)),
            pl.BlockSpec((width, 2 * span), lambda b: (0, 1)),
            pl.BlockSpec((rows, head_width), block),
            pl.BlockSpec((rows, head_width), block),
        ],
        out_specs=[
            pl.BlockSpec((rows, width), block),
            pl.BlockSpec((rows, span), block),
            pl.BlockSpec((rows, span), block),
            pl.BlockSpec((rows, span), block),
            pl.BlockSpec((small.shape[0], rows), lambda b: (0, b)),
            pl.BlockSpec((rows, 1), block),
        ],
        out_shape=[
            jax.ShapeDtypeStruct((token_count, width), BF16),
            jax.ShapeDtypeStruct((token_count, span), BF16),
            jax.ShapeDtypeStruct((token_count, span), BF16),
            jax.ShapeDtypeStruct((token_count, span), BF16),
            jax.ShapeDtypeStruct((small.shape[0], token_count), F32),
            jax.ShapeDtypeStruct((token_count, 1), F32),
        ],
        compiler_params=pltpu.CompilerParams(vmem_limit_bytes=VMEM_BYTES),
        name="project",
    )(tokens, small, weight, weight, cosine, sine)


def attention_scores(q, k_ref, low_bound, high_bound, tile, tile_rows, scaling):
    rows = pl.ds(pl.multiple_of(tile * tile_rows, tile_rows), tile_rows)
    keys = k_ref[rows, :]
    scores = contract_last(q, keys) * scaling
    column = tile * tile_rows + lax.broadcasted_iota(jnp.int32, scores.shape, 1)
    allowed = (column >= low_bound) & (column <= high_bound)
    return rows, keys, scores, allowed


def slots_of_block(rank_ref, table_ref, cap, block):
    rows = table_ref.shape[1]
    pick = (lax.broadcasted_iota(jnp.int32, (cap, rows), 0) == rank_ref[0]).astype(BF16)
    made = contract_last(pick, table_ref[...])
    base = block * rows
    filled = made[:, 4:5] > 0.5
    low = (64.0 * made[:, 2:3] + made[:, 3:4]).astype(jnp.int32)
    high = (64.0 * made[:, 0:1] + made[:, 1:2]).astype(jnp.int32)
    gate = made[:, 5:6] + made[:, 6:7] + made[:, 7:8]
    return pick, jnp.where(filled, low, base), jnp.where(filled, high, base), gate


def rows_of_block(rank_ref, table_ref, cap, block):
    rows = table_ref.shape[1]
    pick = (lax.broadcasted_iota(jnp.int32, (cap, rows), 0) == rank_ref[0]).astype(BF16)
    made = contract_last(table_ref[...], pick)
    filled = made[4:5] > 0.5
    low = (64.0 * made[2:3] + made[3:4]).astype(jnp.int32)
    high = (64.0 * made[0:1] + made[1:2]).astype(jnp.int32)
    return pick, jnp.where(filled, low, block * rows), jnp.where(filled, high, block * rows)


def token_table(position, document_start, gate):
    first = gate.astype(BF16).astype(F32)
    second = (gate - first).astype(BF16).astype(F32)
    rows = [
        position // 64, position % 64, document_start // 64, document_start % 64,
        jnp.ones_like(gate), first, second, gate - first - second,
    ]
    return jnp.pad(jnp.stack([row.astype(BF16) for row in rows]), ((0, 8), (0, 0)))


def attention_forward_kernel(
    begin_ref, q_ref, k_ref, v_ref, rank_ref, table_ref, out_ref, gated_ref, gate_ref, lse_ref, *,
    scaling
):
    block = pl.program_id(1)
    cap, width = out_ref.shape
    tile_rows = q_ref.shape[0]
    pick, low_bound, high_bound, gate = slots_of_block(rank_ref, table_ref, cap, block)
    q = dot(pick, q_ref[...]).astype(BF16)

    def step(tile, carried):
        largest, total, summed = carried
        rows, _, scores, allowed = attention_scores(
            q, k_ref, low_bound, high_bound, tile, tile_rows, scaling
        )
        scores = jnp.where(allowed, scores, NEGATIVE)
        new_largest = jnp.maximum(largest, jnp.max(scores, axis=1, keepdims=True))
        weights = jnp.where(allowed, jnp.exp(scores - new_largest), 0.0)
        shrink = jnp.exp(largest - new_largest)
        return (
            new_largest,
            total * shrink + jnp.sum(weights, axis=1, keepdims=True),
            summed * shrink + dot(weights.astype(BF16), v_ref[rows, :]),
        )

    largest, total, summed = lax.fori_loop(
        begin_ref[block],
        block + 1,
        step,
        (jnp.full((cap, 1), NEGATIVE, F32), jnp.zeros((cap, 1), F32), jnp.zeros((cap, width), F32)),
    )
    attended = (summed / total).astype(BF16)
    out_ref[...] = attended
    gated_ref[...] = (gate * attended.astype(F32)).astype(BF16)
    gate_ref[...] = gate
    lse_ref[0] = largest + jnp.log(total)


def attention_backward_kernel(
    begin_ref, q_ref, k_ref, v_ref, rank_ref, table_ref, out_ref, lse_ref, grad_ref,
    cos_ref, sin_ref, dq_ref, dk_ref, dv_ref, dk_sum, dv_sum, *, scaling, width
):
    block = pl.program_id(0)
    cap = out_ref.shape[0]
    tile_rows = q_ref.shape[0]
    heads = [slice(h * width, (h + 1) * width) for h in range(out_ref.shape[1] // width)]
    pick, low_bound, high_bound = rows_of_block(rank_ref, table_ref, cap, block)
    queries = dot(pick, q_ref[...]).astype(BF16)
    grads = grad_ref[...]
    product = grads.astype(F32) * out_ref[...].astype(F32)
    ones = jnp.ones((8, width), F32)
    deltas = [exact_last(ones, product[:, at])[:1] for at in heads]

    @pl.when(block == 0)
    def _():
        dk_sum[...] = jnp.zeros_like(dk_sum)
        dv_sum[...] = jnp.zeros_like(dv_sum)

    def step(tile, dq):
        rows = pl.ds(pl.multiple_of(tile * tile_rows, tile_rows), tile_rows)
        position = tile * tile_rows + lax.broadcasted_iota(jnp.int32, (tile_rows, cap), 0)
        allowed = (position >= low_bound) & (position <= high_bound)
        made = []
        for h, at in enumerate(heads):
            q, grad, keys = queries[:, at], grads[:, at], k_ref[rows, at]
            scores = contract_last(keys, q) * scaling
            chances = jnp.where(allowed, jnp.exp(scores - lse_ref[h, 0]), 0.0)
            dv_sum[rows, at] += dot(chances.astype(BF16), grad)
            grad_chances = contract_last(v_ref[rows, at], grad)
            grad_scores = (chances * (grad_chances - deltas[h])).astype(BF16)
            dk_sum[rows, at] += dot(grad_scores, q) * scaling
            made.append(dq[h] + contract_first(grad_scores, keys))
        return tuple(made)

    zero = jnp.zeros((cap, width), F32)
    dq = lax.fori_loop(begin_ref[block], block + 1, step, (zero,) * len(heads))
    own = pl.ds(pl.multiple_of(block * tile_rows, tile_rows), tile_rows)
    for h, at in enumerate(heads):
        scaled = dq[h] * scaling
        high = scaled.astype(BF16)
        rest = (scaled - high.astype(F32)).astype(BF16)
        dq_tokens = contract_first(pick, high) + contract_first(pick, rest)
        dq_ref[:, at] = turned(dq_tokens, cos_ref[own, :], -sin_ref[own, :]).astype(BF16)

    @pl.when(block == BLOCKS - 1)
    def _():
        def finish_tile(tile, nothing):
            rows = pl.ds(pl.multiple_of(tile * tile_rows, tile_rows), tile_rows)
            for at in heads:
                dk_ref[rows, at] = turned(
                    dk_sum[rows, at], cos_ref[rows, :], -sin_ref[rows, :]
                ).astype(BF16)
            dv_ref[rows, :] = dv_sum[rows, :].astype(BF16)
            return nothing

        lax.fori_loop(0, BLOCKS, finish_tile, 0)


def attention_specs(row_count, token_count, width):
    return dict(
        q=pl.BlockSpec((row_count, width), lambda h, b, s: (b, h)),
        k=pl.BlockSpec((token_count, width), lambda h, b, s: (0, h)),
        rank=pl.BlockSpec((1, 1, row_count), lambda h, b, s: (b, 0, 0)),
        rows=pl.BlockSpec((16, row_count), lambda h, b, s: (0, b)),
        gate=pl.BlockSpec((CAP, 1), lambda h, b, s: (b, 0)),
        slots=pl.BlockSpec((CAP, width), lambda h, b, s: (b, h)),
        lse=pl.BlockSpec((1, CAP, 1), lambda h, b, s: (h, b, 0)),
    )


def attention_forward(begin, q, k, v, rank, table, width):
    token_count, heads = q.shape[0], q.shape[1] // width
    row_count = token_count // BLOCKS
    s = attention_specs(row_count, token_count, width)
    return pl.pallas_call(
        functools.partial(attention_forward_kernel, scaling=1.0 / math.sqrt(width)),
        grid_spec=pltpu.PrefetchScalarGridSpec(
            num_scalar_prefetch=1,
            grid=(heads, BLOCKS),
            in_specs=[s["q"], s["k"], s["k"], s["rank"], s["rows"]],
            out_specs=[s["slots"], s["slots"], s["gate"], s["lse"]],
        ),
        out_shape=[
            jax.ShapeDtypeStruct((BLOCKS * CAP, heads * width), BF16),
            jax.ShapeDtypeStruct((BLOCKS * CAP, heads * width), BF16),
            jax.ShapeDtypeStruct((BLOCKS * CAP, 1), F32),
            jax.ShapeDtypeStruct((heads, BLOCKS * CAP, 1), F32),
        ],
        compiler_params=pltpu.CompilerParams(vmem_limit_bytes=VMEM_BYTES),
        name="attention_forward",
    )(begin, q, k, v, rank, table)


def attention_backward(begin, q, k, v, rank, table, out, lse, grad, cosine, sine, width):
    token_count, span = q.shape
    row_count = token_count // BLOCKS
    block = lambda b, s: (b, 0)
    whole = lambda b, s: (0, 0)
    tokens = pl.BlockSpec((row_count, span), block)
    keys = pl.BlockSpec((token_count, span), whole)
    slots = pl.BlockSpec((CAP, span), block)
    angles = pl.BlockSpec((token_count, width), whole)
    rows = [
        pl.BlockSpec((1, 1, row_count), lambda b, s: (b, 0, 0)),
        pl.BlockSpec((16, row_count), lambda b, s: (0, b)),
    ]
    sums = pl.BlockSpec((span // width, 1, 1, CAP), lambda b, s: (0, b, 0, 0))
    return pl.pallas_call(
        functools.partial(
            attention_backward_kernel, scaling=1.0 / math.sqrt(width), width=width
        ),
        grid_spec=pltpu.PrefetchScalarGridSpec(
            num_scalar_prefetch=1,
            grid=(BLOCKS,),
            in_specs=[tokens, keys, keys] + rows + [slots, sums, slots, angles, angles],
            out_specs=[tokens, keys, keys],
            scratch_shapes=[pltpu.VMEM((token_count, span), F32)] * 2,
        ),
        out_shape=[jax.ShapeDtypeStruct((token_count, span), BF16)] * 3,
        compiler_params=pltpu.CompilerParams(vmem_limit_bytes=VMEM_BYTES),
        name="attention_backward",
    )(begin, q, k, v, rank, table, out, lse, grad, cosine, sine)


def pack_up_kernel(weight_ref, pieces_ref):
    units = pieces_ref.shape[2] // 2
    both = weight_ref[0].astype(F32)
    gate, up = both[:, 0, :], both[:, 1, :]
    for half in range(HALVES):
        at = slice(half * units, (half + 1) * units)
        pieces_ref[half] = jnp.concatenate([gate[:, at], up[:, at]], axis=1).astype(BF16)


def pack_down_kernel(weight_ref, first_ref, last_ref):
    turned_rows = weight_ref[0].astype(F32).T.astype(BF16)
    middle = first_ref.shape[1]
    first_ref[0] = turned_rows[:middle]
    last_ref[0] = turned_rows[middle:]


def row_major(array):
    return with_layout_constraint(array, Layout(major_to_minor=tuple(range(array.ndim))))


def exchanged(pieces):
    return row_major(lax.all_to_all(row_major(pieces), PLACES, 0, 0, tiled=True))


def over_groups(landed):
    return lax.all_gather(landed, "t", axis=0, tiled=False)


def group_sums(pieces):
    return lax.psum_scatter(pieces, "t", scatter_dimension=0, tiled=False)


def return_gradients(pieces):
    return exchanged(group_sums(pieces))


def other_core(column):
    return column + 1 - 2 * (column % 2)


def crossed(plane, j):
    return (plane, plane + 1 - 2 * (plane % 2), (plane + 2) % 4, 3 - plane)[j]


def meet(peers):
    barrier = pltpu.get_barrier_semaphore()
    for peer in peers:
        pl.semaphore_signal(barrier, inc=1, device_id=peer, device_id_type=MESH)
    pl.semaphore_wait(barrier, len(peers))


def partners():
    plane, half, column = lax.axis_index("z"), lax.axis_index("x"), lax.axis_index("grid")
    planes = [{"z": crossed(plane, j)} for j in range(PLANES)]
    along_x, along_y = {"x": 1 - half}, {"grid": (column + 2) % 4}
    core = {"grid": other_core(column)}
    return plane, half, column, planes, along_x, along_y, core


class Moves:
    def __init__(self, send, recv):
        self.send, self.recv, self.made = send, recv, {}

    def add(self, index, source, target, peer):
        self.made[index] = (source, target, peer)

    def copy(self, index, source, target, peer):
        return pltpu.make_async_remote_copy(
            src_ref=source, dst_ref=target, send_sem=self.send.at[index],
            recv_sem=self.recv.at[index], device_id=peer, device_id_type=MESH,
        )

    def start(self, index):
        self.copy(index, *self.made[index]).start()

    def arrived(self, index, target, peer):
        self.copy(index, target, target, peer).wait_recv()

    def all_sent(self):
        for index in self.made:
            self.copy(index, *self.made[index]).wait_send()


class Ride:
    def __init__(self, pieces_ref, landed_ref, send, recv, local, columns=None):
        if columns is None:
            columns = pl.ds(0, pieces_ref.shape[2])
        rows = pl.ds(0, pieces_ref.shape[1])
        plane, half = lax.axis_index("z"), lax.axis_index("x")
        self.moves = Moves(send, recv)
        self.landings = {}
        own = plane * HALVES + half
        self.keep = pltpu.make_async_copy(pieces_ref.at[own], landed_ref.at[own], local)
        self.peers = []
        for dz in range(PLANES):
            for dx in range(HALVES):
                index = dz * HALVES + dx
                if index == 0:
                    continue
                at_half = 1 - half if dx else half
                peer = {"z": crossed(plane, dz), "x": at_half}
                other = crossed(plane, dz) * HALVES + at_half
                source = pieces_ref.at[other, rows, columns]
                self.moves.add(index, source, landed_ref.at[own, rows, columns], peer)
                self.landings[index] = (landed_ref.at[other, rows, columns], peer)
                if dz and dx:
                    self.peers.append(peer)

    def begin(self, first=(4, 6, 2)):
        self.keep.start()
        for index in first:
            self.moves.start(index)

    def go_on(self, number, plan=((5,), (7,), (3,), (1,))):
        for index in plan[number] if number < len(plan) else ():
            self.moves.start(index)

    def finish(self):
        for index, (landing, peer) in self.landings.items():
            self.moves.arrived(index, landing, peer)
        self.moves.all_sent()
        self.keep.wait()


RIDE_SCRATCH = (
    pltpu.SemaphoreType.DMA((8,)),
    pltpu.SemaphoreType.DMA((8,)),
    pltpu.SemaphoreType.DMA,
)


def run_with_ride(steps, ride):
    steps[0]()
    if ride is not None:
        ride.begin()
    for number, step in enumerate(steps[1:-1]):
        step()
        if ride is not None:
            ride.go_on(number)
    steps[-1]()
    if ride is not None:
        ride.finish()


def gather_parts(slots_ref, out_ref, send, recv, local, same, share=2, more=(), chain=None):
    plane, half, column, planes, along_x, along_y, core = partners()
    cap, width = slots_ref.shape[-2:]
    middle = cap * share // 64 * 16
    y_column, core_column = (column + 2) % 4, other_core(column)
    core_y = (core_column + 2) % 4
    sources = [crossed(plane, j) for j in range(PLANES)]
    moves = Moves(send, recv)

    def piece(source, at_half, at_column, first=0, count=cap):
        columns = pl.ds(pl.multiple_of(at_column * width, width), width)
        return out_ref.at[source, at_half, pl.ds(first, count), columns]

    def slots_for(j):
        return slots_ref if same else slots_ref.at[sources[j]]

    keep = pltpu.make_async_copy(slots_for(0), piece(plane, half, column), local)
    for j in range(PLANES):
        source = sources[j]
        place = piece(source, half, column)
        if j and chain is None:
            moves.add(j, slots_for(j), piece(plane, half, column), planes[j])
        here = place if j else slots_for(0)
        moves.add(4 + j, here, place, along_x)
        moves.add(8 + j, here, place, along_y)
        moves.add(12 + j, here, place, core)
        from_x, from_y = piece(source, 1 - half, column), piece(source, half, y_column)
        first = piece(source, 1 - half, column, 0, middle)
        last = piece(source, half, y_column, middle, cap - middle)
        diagonal = piece(source, 1 - half, y_column)
        moves.add(16 + j, first, first, along_y)
        moves.add(20 + j, from_x, from_x, core)
        moves.add(24 + j, last, last, along_x)
        moves.add(28 + j, from_y, from_y, core)
        moves.add(32 + j, diagonal, diagonal, core)

    def begin():
        meet(planes[1:] + [along_x, along_y, core] + list(more))
        if chain is None:
            for j in (1, 3, 2):
                moves.start(j)
        else:
            chain.begin()
        keep.start()

    def spread(j):
        if j and chain is None:
            moves.arrived(j, piece(sources[j], half, column), planes[j])
        elif j:
            chain.arrived(j)
        for index in (4, 8, 12):
            moves.start(index + j)

    def forward(j):
        moves.arrived(4 + j, piece(sources[j], 1 - half, column), along_x)
        moves.start(16 + j)
        moves.start(20 + j)
        moves.arrived(8 + j, piece(sources[j], half, y_column), along_y)
        moves.start(24 + j)
        moves.start(28 + j)

    def cross(j):
        moves.arrived(16 + j, piece(sources[j], 1 - half, y_column, 0, middle), along_y)
        moves.arrived(24 + j, piece(sources[j], 1 - half, y_column, middle, cap - middle), along_x)
        moves.start(32 + j)

    def finish():
        for j in order:
            moves.arrived(12 + j, piece(sources[j], half, core_column), core)
            moves.arrived(20 + j, piece(sources[j], 1 - half, core_column), core)
            moves.arrived(28 + j, piece(sources[j], half, core_y), core)
            moves.arrived(32 + j, piece(sources[j], 1 - half, core_y), core)
        moves.all_sent()
        keep.wait()

    order = (0, 1, 3, 2)
    return begin, spread, forward, cross, finish, order


def gather_steps(*refs, **settings):
    begin, spread, forward, cross, finish, order = gather_parts(*refs, **settings)

    def step(number):
        if number < len(order):
            spread(order[number])
        if 0 <= number - 1 < len(order):
            forward(order[number - 1])
        if 0 <= number - 2 < len(order):
            cross(order[number - 2])

    return [begin] + [functools.partial(step, number) for number in range(len(order) + 2)] + [finish]


class Chain:
    def __init__(self, view, source, send, recv):
        plane = lax.axis_index("z")
        self.inner = (plane == 1) | (plane == 2)
        near, far = {"z": crossed(plane, 1)}, {"z": crossed(plane, 3)}
        self.views = [view(crossed(plane, j)) for j in range(PLANES)]
        self.send, self.recv = send, recv
        self.near_own = (0, 1, source, self.views[0], near)
        self.far_own = (1, 3, source, self.views[0], far)
        self.on_arrival = {
            1: (2, 2, self.views[1], self.views[1], far),
            3: (3, 2, self.views[3], self.views[3], near),
            2: (4, 3, self.views[2], self.views[2], near),
        }

    def copy(self, at_send, at_recv, source, target, peer):
        return pltpu.make_async_remote_copy(
            src_ref=source, dst_ref=target, send_sem=self.send.at[at_send],
            recv_sem=self.recv.at[at_recv], device_id=peer, device_id_type=MESH,
        )

    def begin(self):
        self.copy(*self.near_own).start()

        @pl.when(self.inner)
        def _():
            self.copy(*self.far_own).start()

    def arrived(self, j):
        place = self.views[j]
        self.copy(0, j, place, place, self.near_own[-1]).wait_recv()

        @pl.when(self.inner)
        def _():
            self.copy(*self.on_arrival[j]).start()

    def finish(self):
        self.copy(*self.near_own).wait_send()

        @pl.when(self.inner)
        def _():
            self.copy(*self.far_own).wait_send()
            for made in self.on_arrival.values():
                self.copy(*made).wait_send()


CHAIN_SCRATCH = (pltpu.SemaphoreType.DMA((5,)), pltpu.SemaphoreType.DMA((4,)))


def opening_kernel(
    tokens_ref, pieces_ref, up_ref, down_ref, out_ref, landed_ref, up_pieces_ref, first_ref,
    last_ref, send, recv, local, ride_send, ride_recv,
    ride_local, hop_send, hop_recv, *chain_sems, share
):
    plane, half, column = lax.axis_index("z"), lax.axis_index("x"), lax.axis_index("grid")
    width = tokens_ref.shape[1]
    middle = pieces_ref.shape[2] // 2
    left, right = pl.ds(0, middle), pl.ds(middle, middle)
    rows = pl.ds(0, pieces_ref.shape[1])
    along_x = {"x": 1 - half}

    def tokens_of(source):
        columns = pl.ds(pl.multiple_of(column * width, width), width)
        return out_ref.at[source, half, pl.ds(0, tokens_ref.shape[0]), columns]

    def shared_of(at_half):
        return lambda source: landed_ref.at[source * HALVES + at_half, rows, right]

    own = plane * HALVES + half
    tokens = Chain(tokens_of, tokens_ref, *chain_sems[:2])
    here = Chain(shared_of(half), pieces_ref.at[own, rows, right], *chain_sems[2:4])
    there = Chain(shared_of(1 - half), shared_of(1 - half)(plane), *chain_sems[4:])
    ride = Ride(pieces_ref, landed_ref, ride_send, ride_recv, ride_local, left)
    hop = pltpu.make_async_remote_copy(
        src_ref=pieces_ref.at[plane * HALVES + 1 - half, rows, right],
        dst_ref=landed_ref.at[own, rows, right],
        send_sem=hop_send, recv_sem=hop_recv, device_id=along_x, device_id_type=MESH,
    )
    landing = shared_of(1 - half)(plane)
    hop_here = pltpu.make_async_remote_copy(
        src_ref=landing, dst_ref=landing, send_sem=hop_send, recv_sem=hop_recv,
        device_id=along_x, device_id_type=MESH,
    )
    begin, spread, forward, cross, finish, _ = gather_parts(
        tokens_ref, out_ref, send, recv, local, True, share, ride.peers, tokens
    )

    def first():
        begin()
        ride.keep.start()
        spread(0)
        hop.start()
        here.begin()

    def second():
        spread(1)
        forward(0)
        ride.moves.start(2)

    def third():
        spread(3)
        forward(1)
        cross(0)
        hop_here.wait_recv()
        there.begin()
        here.arrived(1)

    def fourth():
        spread(2)
        forward(3)
        cross(1)
        ride.moves.start(6)
        ride.moves.start(4)
        here.arrived(3)
        there.arrived(1)

    def fifth():
        forward(2)
        cross(3)
        for index in (3, 7, 5, 1):
            ride.moves.start(index)
        here.arrived(2)
        there.arrived(3)
        cross(2)
        there.arrived(2)
        finish()
        ride.finish()
        hop.wait_send()
        for chain in (tokens, here, there):
            chain.finish()

    def compute():
        pack_up_kernel(up_ref, up_pieces_ref)
        pack_down_kernel(down_ref, first_ref, last_ref)

    carry([first], [second, third, fourth, fifth], (3, 6, 7, 7), compute)


def opened(tokens, pieces, up, down, collective_id, share):
    rows, width = tokens.shape
    experts, own_rows, _, units = up.shape
    places = experts * HALVES
    tile = own_rows // 2
    down_half = (places, own_rows // 2, units // HALVES)
    anywhere = pl.BlockSpec(memory_space=pl.ANY)
    half = pl.BlockSpec((1,) + down_half[1:], lambda p: (p, 0, 0))
    return pl.pallas_call(
        functools.partial(opening_kernel, share=share),
        grid=(places,),
        in_specs=[
            anywhere,
            anywhere,
            pl.BlockSpec((1, tile, 2, units), lambda p: (p // 2, p % 2, 0, 0)),
            pl.BlockSpec((1,) + down.shape[1:], lambda p: (p, 0, 0)),
        ],
        out_specs=[
            anywhere,
            anywhere,
            pl.BlockSpec((HALVES, tile, units), lambda p: (p // 2, p % 2, 0)),
            half,
            half,
        ],
        out_shape=[
            jax.ShapeDtypeStruct((PLANES, HALVES, rows, 4 * width), BF16),
            jax.ShapeDtypeStruct(pieces.shape, BF16),
            jax.ShapeDtypeStruct((places, own_rows, units), BF16),
            jax.ShapeDtypeStruct(down_half, BF16),
            jax.ShapeDtypeStruct(down_half, BF16),
        ],
        scratch_shapes=list(GATHER_SCRATCH) + list(RIDE_SCRATCH)
        + [pltpu.SemaphoreType.DMA, pltpu.SemaphoreType.DMA] + list(CHAIN_SCRATCH) * 3,
        compiler_params=pltpu.CompilerParams(
            collective_id=collective_id, has_side_effects=True, vmem_limit_bytes=VMEM_BYTES
        ),
        name="open_rows",
    )(tokens, pieces, up, down)


GATHER_SCRATCH = (
    pltpu.SemaphoreType.DMA((36,)),
    pltpu.SemaphoreType.DMA((36,)),
    pltpu.SemaphoreType.DMA,
)


def gather_kernel(*refs, same, share, rides):
    if rides:
        slots_ref, pieces_ref, out_ref, landed_ref = refs[:4]
        ride = Ride(pieces_ref, landed_ref, *refs[7:])
        scratch = refs[4:7]
    else:
        slots_ref, out_ref = refs[:2]
        ride, scratch = None, refs[2:]
    more = ride.peers if rides else ()
    run_with_ride(gather_steps(slots_ref, out_ref, *scratch, same, share, more), ride)


def gathered(slots, collective_id, ride=None, share=2):
    rows, width = slots.shape[-2:]
    rides = () if ride is None else (ride,)
    anywhere = pl.BlockSpec(memory_space=pl.ANY)
    out = pl.pallas_call(
        functools.partial(gather_kernel, same=slots.ndim == 2, share=share, rides=len(rides)),
        out_shape=[jax.ShapeDtypeStruct((PLANES, HALVES, rows, 4 * width), BF16)]
        + [jax.ShapeDtypeStruct(r.shape, BF16) for r in rides],
        in_specs=[anywhere] * (1 + len(rides)),
        out_specs=[anywhere] * (1 + len(rides)),
        scratch_shapes=list(GATHER_SCRATCH) + list(RIDE_SCRATCH) * len(rides),
        compiler_params=pltpu.CompilerParams(collective_id=collective_id, has_side_effects=True),
        name="gather_rows",
    )(slots, *rides)
    return out if rides else out[0]


def scatter_steps(
    partial_ref, out_ref, own, other, crossing, side, send, recv, load, share=2, more=()
):
    plane, half, column, planes, along_x, along_y, core = partners()
    cap, width = out_ref.shape[-2:]
    middle = cap * share // 64 * 16
    chunk = 32 if middle % 32 == 0 and cap % 32 == 0 else 16
    y_column, core_column = (column + 2) % 4, other_core(column)
    core_y = (core_column + 2) % 4
    halves = (half, 1 - half, half, 1 - half)
    own_columns = (column, column, y_column, y_column)
    core_columns = (core_column, core_column, core_y, core_y)
    moves = Moves(send, recv)
    first, last = pl.ds(0, middle), pl.ds(middle, cap - middle)

    def part(j, q, at_columns):
        columns = pl.ds(pl.multiple_of(at_columns[q] * width, width), width)
        return partial_ref.at[crossed(plane, j), halves[q], :, columns]

    def loading(j, q):
        return pltpu.make_async_copy(part(j, q, own_columns), own.at[j, q], load.at[4 * j + q])

    keep = pltpu.make_async_copy(own.at[0, 0], out_ref.at[plane], load.at[16])
    for j in range(PLANES):
        for q in range(4):
            moves.add(4 * j + q, part(j, q, core_columns), other.at[j, q], core)
        moves.add(16 + j, own.at[j, 3, first], crossing.at[j, first], along_x)
        moves.add(20 + j, own.at[j, 3, last], crossing.at[j, last], along_y)
        moves.add(24 + j, own.at[j, 2], side.at[j, 1], along_y)
        moves.add(28 + j, own.at[j, 1], side.at[j, 0], along_x)
        if j:
            moves.add(32 + j, own.at[j, 0], out_ref.at[plane], planes[j])

    def add(j, q, begin_row, count, terms):
        def step(i, nothing):
            rows = pl.ds(pl.multiple_of(begin_row + i * chunk, chunk), chunk)
            total = own[j, q, rows, :].astype(F32)
            for ref, index in terms:
                total = total + ref[index + (rows, slice(None))].astype(F32)
            own[j, q, rows, :] = total.astype(BF16)
            return nothing

        lax.fori_loop(0, count // chunk, step, 0)

    def chip_sum(j, q):
        moves.arrived(4 * j + q, other.at[j, q], core)
        loading(j, q).wait()
        add(j, q, 0, cap, [(other, (j, q))])

    def stage_one(j):
        chip_sum(j, 3)
        moves.start(16 + j)
        moves.start(20 + j)
        chip_sum(j, 2)
        chip_sum(j, 1)
        chip_sum(j, 0)

    def stage_two(j):
        moves.arrived(16 + j, crossing.at[j, first], along_x)
        add(j, 2, 0, middle, [(crossing, (j,))])
        moves.start(24 + j)
        moves.arrived(20 + j, crossing.at[j, last], along_y)
        add(j, 1, middle, cap - middle, [(crossing, (j,))])
        moves.start(28 + j)

    def stage_three(j):
        moves.arrived(24 + j, side.at[j, 1], along_y)
        moves.arrived(28 + j, side.at[j, 0], along_x)
        add(j, 0, 0, cap, [(side, (j, 0)), (side, (j, 1))])
        if j:
            moves.start(32 + j)
        else:
            keep.start()

    order = (2, 3, 1, 0)

    def begin():
        meet(planes[1:] + [along_x, along_y, core] + list(more))
        for j in order:
            for q in (3, 2, 1, 0):
                moves.start(4 * j + q)
                loading(j, q).start()

    def step(number):
        if number < len(order):
            stage_one(order[number])
        if 0 <= number - 1 < len(order):
            stage_two(order[number - 1])
        if 0 <= number - 2 < len(order):
            stage_three(order[number - 2])

    def finish():
        for j in range(1, PLANES):
            moves.arrived(32 + j, out_ref.at[crossed(plane, j)], planes[j])
        moves.all_sent()
        keep.wait()

    return [begin] + [functools.partial(step, number) for number in range(len(order) + 2)] + [finish]


def scatter_scratch(rows, width):
    return [
        pltpu.VMEM((PLANES, 4, rows, width), BF16),
        pltpu.VMEM((PLANES, 4, rows, width), BF16),
        pltpu.VMEM((PLANES, rows, width), BF16),
        pltpu.VMEM((PLANES, 2, rows, width), BF16),
        pltpu.SemaphoreType.DMA((36,)),
        pltpu.SemaphoreType.DMA((36,)),
        pltpu.SemaphoreType.DMA((17,)),
    ]


def scatter_kernel(*refs, share, rides):
    if rides:
        partial_ref, pieces_ref, out_ref, landed_ref = refs[:4]
        ride = Ride(pieces_ref, landed_ref, *refs[11:])
        scratch = refs[4:11]
    else:
        partial_ref, out_ref = refs[:2]
        ride, scratch = None, refs[2:]
    more = ride.peers if rides else ()
    run_with_ride(scatter_steps(partial_ref, out_ref, *scratch, share, more), ride)


def scattered(partial, rows, collective_id, ride=None, share=2):
    width = partial.shape[1] // 4
    rides = () if ride is None else (ride,)
    anywhere = pl.BlockSpec(memory_space=pl.ANY)
    out = pl.pallas_call(
        functools.partial(scatter_kernel, share=share, rides=len(rides)),
        out_shape=[jax.ShapeDtypeStruct((PLANES, rows, width), BF16)]
        + [jax.ShapeDtypeStruct(r.shape, BF16) for r in rides],
        in_specs=[anywhere] * (1 + len(rides)),
        out_specs=[anywhere] * (1 + len(rides)),
        scratch_shapes=scatter_scratch(rows, width) + list(RIDE_SCRATCH) * len(rides),
        compiler_params=pltpu.CompilerParams(
            collective_id=collective_id, has_side_effects=True, vmem_limit_bytes=VMEM_BYTES
        ),
        name="scatter_rows",
    )(partial.reshape(PLANES, HALVES, rows, 4 * width), *rides)
    return out if rides else out[0]


def carry(before, after, places, compute):
    number = pl.program_id(0)

    @pl.when(number == 0)
    def _():
        for step in before:
            step()

    compute()
    for at in sorted(set(places)):

        @pl.when(number == at)
        def _(at=at):
            for place, step in zip(places, after):
                if place == at:
                    step()


def join_halves(first_ref, last_ref, whole_ref):
    count, height, _ = first_ref.shape

    @pl.when(pl.program_id(0) == 0)
    def _():
        for place in range(count):
            whole_ref[2 * place * height : (2 * place + 1) * height, :] = first_ref[place]
            whole_ref[(2 * place + 1) * height : (2 * place + 2) * height, :] = last_ref[place]


def expert_forward_kernel(
    rows_ref, up_weight_ref, first_ref, last_ref, small_ref, rank_ref, member_ref, grad_ref,
    slope_ref, silu_ref, result_ref, share_ref, shared_ref, grad_rows_ref, down_weight_ref, *scratch
):
    join_halves(first_ref, last_ref, down_weight_ref)
    steps = gather_steps(grad_ref, grad_rows_ref, *scratch, False)
    units = slope_ref.shape[1]

    def compute():
        rows = rows_ref[0]
        made = dot(rows, up_weight_ref[...])
        gate, up = made[:, :units], made[:, units:]
        sigmoid = jax.nn.sigmoid(gate)
        silu = gate * sigmoid
        slope_ref[...] = up * sigmoid * (1.0 + gate * (1.0 - sigmoid))
        silu_ref[...] = silu
        inner = silu * up
        result_ref[0] = contract_last(inner.astype(BF16), down_weight_ref[...]).astype(BF16)
        cap, count = rows.shape[0], rank_ref.shape[2]
        pick = (lax.broadcasted_iota(jnp.int32, (cap, count), 0) == rank_ref[0]).astype(BF16)
        member = contract_last(pick, member_ref[...]) > 0.5
        logits = jnp.where(member, contract_last(rows, small_ref[...]), NEGATIVE)
        largest = jnp.max(logits, axis=1, keepdims=True)
        weights = jnp.where(member, jnp.exp(logits - largest), 0.0)
        mine = lax.broadcasted_iota(jnp.int32, weights.shape, 1) == 6 + lax.axis_index("z")
        total = jnp.sum(weights, axis=1, keepdims=True)
        own = jnp.sum(jnp.where(mine, weights, 0.0), axis=1, keepdims=True)
        share = own / jnp.where(total > 0.0, total, 1.0)
        share_ref[...] = share
        shared_ref[...] = (share * inner).astype(BF16)

    carry(steps[:2], steps[2:], (1, 3, 5, 6, 7, 7), compute)


def once(shape):
    return pl.BlockSpec(shape, lambda b: (0,) * len(shape), pipeline_mode=pl.Buffered(1))


def expert_forward(rows, up_weight, down_halves, small, rank, member, grad_slots, collective_id):
    _, cap, width = rows.shape
    units = down_halves[0].shape[2]
    count = BLOCKS * cap
    anywhere = pl.BlockSpec(memory_space=pl.ANY)
    block = lambda b: (b, 0)
    return pl.pallas_call(
        expert_forward_kernel,
        grid=(BLOCKS,),
        in_specs=[
            pl.BlockSpec((1, cap, width), lambda b: (b, 0, 0)),
            once(up_weight.shape),
            once(down_halves[0].shape),
            once(down_halves[1].shape),
            once(small.shape),
            pl.BlockSpec((1, 1, rank.shape[2]), lambda b: (b, 0, 0)),
            pl.BlockSpec((16, rank.shape[2]), lambda b: (0, b)),
            anywhere,
        ],
        out_specs=[
            pl.BlockSpec((cap, units), block),
            pl.BlockSpec((cap, units), block),
            pl.BlockSpec((1, cap, width), lambda b: (b, 0, 0)),
            pl.BlockSpec((cap, 1), block),
            pl.BlockSpec((cap, units), block),
            anywhere,
        ],
        out_shape=[
            jax.ShapeDtypeStruct((count, units), F32),
            jax.ShapeDtypeStruct((count, units), F32),
            jax.ShapeDtypeStruct((BLOCKS, cap, width), BF16),
            jax.ShapeDtypeStruct((count, 1), F32),
            jax.ShapeDtypeStruct((count, units), BF16),
            jax.ShapeDtypeStruct((PLANES, HALVES, cap, width), BF16),
        ],
        scratch_shapes=[pltpu.VMEM((width, units), BF16)] + list(GATHER_SCRATCH),
        compiler_params=pltpu.CompilerParams(
            collective_id=collective_id, has_side_effects=True, vmem_limit_bytes=VMEM_BYTES
        ),
        name="expert_forward",
    )(rows, up_weight, *down_halves, small, rank, member, grad_slots)


def expert_backward_kernel(
    slope_ref, silu_ref, grad_ref, share_ref, up_weight_ref, first_ref, last_ref, columns_ref,
    inner_ref, result_ref, *refs, rides
):
    count = 6 if rides else 5
    grad_rows_ref, grad_gate_up_ref, down_first_ref, down_last_ref, out_ref = refs[:5]
    down_weight_ref, kept_ref, scratch = refs[count], refs[count + 1], refs[count + 2 :]
    ride = Ride(kept_ref, refs[5], *scratch[7:]) if rides else None
    steps = scatter_steps(result_ref, out_ref, *scratch[:7], 1, ride.peers if rides else ())
    middle = down_first_ref.shape[1]
    number = pl.program_id(0)
    join_halves(first_ref, last_ref, down_weight_ref)

    def down_gradient():
        down_grad = contract_first(columns_ref[...], inner_ref[...]).astype(BF16)
        kept_ref[number] = down_grad[:middle]
        down_first_ref[0] = down_grad[:middle]
        down_last_ref[0] = down_grad[middle:]

    def rows_gradient():
        grad_inner = dot(grad_ref[0], down_weight_ref[...]) * share_ref[...]
        grad_gate_up = jnp.concatenate(
            [grad_inner * slope_ref[...], grad_inner * silu_ref[...]], axis=1
        ).astype(BF16)
        grad_gate_up_ref[...] = grad_gate_up
        grad_rows_ref[0] = contract_last(grad_gate_up, up_weight_ref[...]).astype(BF16)

    def compute():
        pl.when(number < BLOCKS)(down_gradient)
        pl.when(number >= BLOCKS)(rows_gradient)

    after, places = list(steps[1:]), [3, 7, 9, 11, 13, 15, 15]
    if rides:
        after += [ride.begin] + [functools.partial(ride.go_on, i) for i in range(4)] + [ride.finish]
        places += [7, 8, 9, 10, 12, 15]
    carry(steps[:1], after, places, compute)


def expert_backward(
    slope, silu, grad_rows, share, up_weight, down_halves, inner, result, rides, collective_id
):
    _, cap, width = grad_rows.shape
    count, units = slope.shape
    tile = width // BLOCKS
    anywhere = pl.BlockSpec(memory_space=pl.ANY)
    at_row = lambda b: jnp.maximum(b - BLOCKS, 0)
    at_tile = lambda b: jnp.minimum(b, BLOCKS - 1)
    block = lambda b: (at_row(b), 0)
    rows = pl.BlockSpec((1, cap, width), lambda b: (at_row(b), 0, 0))
    half = pl.BlockSpec((1, tile // 2, units), lambda b: (at_tile(b), 0, 0))
    half_shape = jax.ShapeDtypeStruct((BLOCKS, tile // 2, units), BF16)
    return pl.pallas_call(
        functools.partial(expert_backward_kernel, rides=rides),
        grid=(2 * BLOCKS,),
        in_specs=[
            pl.BlockSpec((cap, units), block),
            pl.BlockSpec((cap, units), block),
            rows,
            pl.BlockSpec((cap, 1), block),
            once(up_weight.shape),
            once(down_halves[0].shape),
            once(down_halves[1].shape),
            pl.BlockSpec((count, tile), lambda b: (0, at_tile(b))),
            once(inner.shape),
            anywhere,
        ],
        out_specs=[rows, pl.BlockSpec((cap, 2 * units), block), half, half, anywhere]
        + [anywhere] * rides,
        out_shape=[
            jax.ShapeDtypeStruct((BLOCKS, cap, width), BF16),
            jax.ShapeDtypeStruct((count, 2 * units), BF16),
            half_shape,
            half_shape,
            jax.ShapeDtypeStruct((PLANES, cap, width // 4), BF16),
        ]
        + [half_shape] * rides,
        scratch_shapes=[
            pltpu.VMEM((width, units), BF16),
            pltpu.VMEM((BLOCKS, tile // 2, units), BF16),
        ]
        + scatter_scratch(cap, width // 4)
        + list(RIDE_SCRATCH) * rides,
        compiler_params=pltpu.CompilerParams(
            collective_id=collective_id, has_side_effects=True, vmem_limit_bytes=VMEM_BYTES
        ),
        name="expert_backward",
    )(
        slope, silu, grad_rows, share, up_weight, *down_halves, grad_rows.reshape(count, width), inner,
        result.reshape(PLANES, HALVES, cap, width),
    )


def expert_gradient_kernel(
    rows_ref, grad_gate_up_ref, partial_ref, pieces_ref, up_first_ref, up_last_ref, out_ref,
    landed_ref, *scratch
):
    ride = Ride(pieces_ref, landed_ref, *scratch[7:])
    steps = scatter_steps(partial_ref, out_ref, *scratch[:7], 1, ride.peers)

    def compute():
        up_grad = contract_first(rows_ref[...], grad_gate_up_ref[...]).astype(BF16)
        up_first_ref[...] = up_grad[:, :EARLY]
        up_last_ref[...] = up_grad[:, EARLY:]

    def with_ride(number):
        steps[1 + number]()
        ride.go_on(number)

    after = [functools.partial(with_ride, number) for number in range(6)]
    carry([steps[0], ride.begin], after + [steps[-1], ride.finish], (0, 1, 3, 5, 6, 7, 7, 7), compute)


def expert_gradient(rows, grad_gate_up, partial, pieces, collective_id):
    count, width = rows.shape
    units = grad_gate_up.shape[1]
    cap, tile = count // BLOCKS, width // BLOCKS
    anywhere = pl.BlockSpec(memory_space=pl.ANY)
    return pl.pallas_call(
        expert_gradient_kernel,
        grid=(BLOCKS,),
        in_specs=[
            pl.BlockSpec((count, tile), lambda b: (0, b)),
            once((count, units)),
            anywhere,
            anywhere,
        ],
        out_specs=[
            pl.BlockSpec((tile, EARLY), lambda b: (b, 0)),
            pl.BlockSpec((tile, units - EARLY), lambda b: (b, 0)),
            anywhere,
            anywhere,
        ],
        out_shape=[
            jax.ShapeDtypeStruct((width, EARLY), BF16),
            jax.ShapeDtypeStruct((width, units - EARLY), BF16),
            jax.ShapeDtypeStruct((PLANES, cap, width // 4), BF16),
            jax.ShapeDtypeStruct(pieces.shape, BF16),
        ],
        scratch_shapes=scatter_scratch(cap, width // 4) + list(RIDE_SCRATCH),
        compiler_params=pltpu.CompilerParams(
            collective_id=collective_id, has_side_effects=True, vmem_limit_bytes=VMEM_BYTES
        ),
        name="expert_gradient",
    )(rows, grad_gate_up, partial.reshape(PLANES, HALVES, cap, width), pieces)


def closing_kernel(
    hidden_ref, q_ref, k_ref, v_ref, rows_ref, gated_ref, partial_ref, grad_ref, out_ref, *scratch
):
    steps = scatter_steps(partial_ref, out_ref, *scratch)
    span = q_ref.shape[1]

    def compute():
        hidden = hidden_ref[...]
        for place, ref in enumerate((q_ref, k_ref, v_ref)):
            at = slice(place * span, (place + 1) * span)
            grad_ref[:, at] = contract_first(hidden, ref[...]).astype(BF16)
        grad_ref[:, 3 * span :] = contract_first(rows_ref[...], gated_ref[...]).astype(BF16)

    carry(steps[:1], steps[1:], (1, 3, 6, 7, 7, 7, 7), compute)


def closing(hidden, q, k, v, rows, gated, partial, collective_id):
    count, width = hidden.shape
    slot_count, span = gated.shape
    tile, own_rows = width // BLOCKS, count // BLOCKS
    anywhere = pl.BlockSpec(memory_space=pl.ANY)
    return pl.pallas_call(
        closing_kernel,
        grid=(BLOCKS,),
        in_specs=[
            pl.BlockSpec((count, tile), lambda b: (0, b)),
            once((count, span)),
            once((count, span)),
            once((count, span)),
            pl.BlockSpec((slot_count, tile), lambda b: (0, b)),
            once((slot_count, span)),
            anywhere,
        ],
        out_specs=[pl.BlockSpec((tile, 4 * span), lambda b: (b, 0)), anywhere],
        out_shape=[
            jax.ShapeDtypeStruct((width, 4 * span), BF16),
            jax.ShapeDtypeStruct((PLANES, own_rows, width // 4), BF16),
        ],
        scratch_shapes=scatter_scratch(own_rows, width // 4),
        compiler_params=pltpu.CompilerParams(
            collective_id=collective_id, has_side_effects=True, vmem_limit_bytes=VMEM_BYTES
        ),
        name="closing",
    )(hidden, q, k, v, rows, gated, partial.reshape(PLANES, HALVES, own_rows, width))


def finish_kernel(
    query_ref, all_ref, small_ref, query_grad_ref, kv_grad_ref, out_grad_ref, gain_first_ref,
    gain_second_ref, router_first_ref, router_second_ref
):
    span = query_ref.shape[2] // 4
    head_width = query_grad_ref.shape[3]
    pair = span // head_width
    own_rows = query_grad_ref.shape[1]
    for half in range(HALVES):
        landed = query_ref[half, :own_rows, :].astype(F32)
        for head in range(pair):
            at = half * pair + head
            query_grad_ref[0, :, at, :] = landed[:, head * head_width : (head + 1) * head_width]
        out_grad_ref[half] = landed[:, 3 * span :].T

    @pl.when(pl.program_id(0) == 0)
    def _():
        for half in range(HALVES):
            total = sum(
                all_ref[z * HALVES + half, :own_rows, span : 3 * span].astype(F32)
                for z in range(PLANES)
            )
            for kind in range(2):
                for head in range(pair):
                    first = kind * span + head * head_width
                    kv_grad_ref[:, half * pair + head, kind, :] = total[:, first : first + head_width]

        total = sum(small_ref[place] for place in range(BLOCKS))
        gain_first_ref[...] = total[0:1]
        gain_second_ref[...] = total[1:2]
        router_first_ref[...] = total[2 : 2 + PLANES]
        router_second_ref[...] = total[2 + PLANES : 2 + 2 * PLANES]


def unpack_up_kernel(first_ref, last_ref, grad_ref):
    units = grad_ref.shape[3] // HALVES
    halves = [
        jnp.concatenate([first_ref[half], last_ref[half]], axis=1).astype(F32) for half in range(HALVES)
    ]
    for kind in range(2):
        at = slice(kind * units, (kind + 1) * units)
        grad_ref[0, :, kind, :] = jnp.concatenate([half[:, at] for half in halves], axis=1)


def unpack_up(first, last):
    places, own_rows, early = first.shape
    units = early + last.shape[2]
    tile = own_rows // 2
    return pl.pallas_call(
        unpack_up_kernel,
        grid=(places // HALVES, 2),
        in_specs=[
            pl.BlockSpec((HALVES, tile, early), lambda e, r: (e, r, 0)),
            pl.BlockSpec((HALVES, tile, units - early), lambda e, r: (e, r, 0)),
        ],
        out_specs=pl.BlockSpec((1, tile, 2, units), lambda e, r: (e, r, 0, 0)),
        out_shape=jax.ShapeDtypeStruct((places // HALVES, own_rows, 2, units), F32),
        compiler_params=pltpu.CompilerParams(vmem_limit_bytes=VMEM_BYTES),
        name="unpack_up",
    )(first, last)


def swap_kernel(pieces_ref, landed_ref, *scratch):
    ride = Ride(pieces_ref, landed_ref, *scratch)
    meet([peer for _, _, peer in ride.moves.made.values()])
    ride.begin(tuple(ride.moves.made))
    ride.finish()


def swapped(pieces, collective_id):
    whole = pl.BlockSpec(memory_space=pltpu.VMEM)
    return pl.pallas_call(
        swap_kernel,
        out_shape=jax.ShapeDtypeStruct(pieces.shape, pieces.dtype),
        in_specs=[whole],
        out_specs=whole,
        scratch_shapes=list(RIDE_SCRATCH),
        compiler_params=pltpu.CompilerParams(collective_id=collective_id, has_side_effects=True),
        name="swap_small",
    )(pieces)


def finish(landed, small, own_rows, span, heads, head_width):
    places, height, width = landed.shape
    return pl.pallas_call(
        finish_kernel,
        grid=(PLANES,),
        in_specs=[
            pl.BlockSpec((HALVES, height, width), lambda e: (e, 0, 0)),
            once((places, height, width)),
            once(small.shape),
        ],
        out_specs=[
            pl.BlockSpec((1, own_rows, heads, head_width), lambda e: (e, 0, 0, 0)),
            pl.BlockSpec((own_rows, heads, 2, head_width), lambda e: (0, 0, 0, 0)),
            pl.BlockSpec((HALVES, span, own_rows), lambda e: (e, 0, 0)),
            pl.BlockSpec((1, small.shape[2]), lambda e: (0, 0)),
            pl.BlockSpec((1, small.shape[2]), lambda e: (0, 0)),
            pl.BlockSpec((PLANES, small.shape[2]), lambda e: (0, 0)),
            pl.BlockSpec((PLANES, small.shape[2]), lambda e: (0, 0)),
        ],
        out_shape=[
            jax.ShapeDtypeStruct((PLANES, own_rows, heads, head_width), F32),
            jax.ShapeDtypeStruct((own_rows, heads, 2, head_width), F32),
            jax.ShapeDtypeStruct((places, span, own_rows), F32),
            jax.ShapeDtypeStruct((1, small.shape[2]), F32),
            jax.ShapeDtypeStruct((1, small.shape[2]), F32),
            jax.ShapeDtypeStruct((PLANES, small.shape[2]), F32),
            jax.ShapeDtypeStruct((PLANES, small.shape[2]), F32),
        ],
        compiler_params=pltpu.CompilerParams(vmem_limit_bytes=VMEM_BYTES),
        name="attention_weight_gradients",
    )(landed, landed, small)


def grid_sum(values):
    shape = values.shape
    return lax.all_gather(values.reshape(-1, 128), "grid", axis=0).sum(axis=0).reshape(shape)


def prefix_ranks(member):
    counted = member.astype(BF16)
    width = member.shape[-1]
    before = jnp.arange(width)[:, None] < jnp.arange(width)[None, :]
    return jnp.where(member, dot(counted, before.astype(BF16)).astype(jnp.int32), -1)


def picks(rank):
    return (jnp.arange(CAP, dtype=jnp.int32)[:, None] == rank[..., None, :]).astype(BF16)


def members(first, second):
    names = jnp.arange(PLANES, dtype=first.dtype).reshape((PLANES,) + (1,) * first.ndim)
    return (first[None] == names) | (second[None] == names)


def route_gates(logits, member):
    shown = jnp.where(member, logits, NEGATIVE)
    weights = jnp.where(member, jnp.exp(shown - jnp.max(shown, axis=0, keepdims=True)), 0.0)
    return weights / jnp.sum(weights, axis=0, keepdims=True)


def logits_grad(gates, grad_gates):
    return gates * (grad_gates - jnp.sum(gates * grad_gates, axis=0, keepdims=True))


def exact_first(left, right):
    return lax.dot_general(
        left, right, (((0,), (0,)), ((), ())), precision=lax.Precision.HIGHEST
    )


def exact_last(left, right):
    return lax.dot_general(
        left, right, (((1,), (1,)), ((), ())), precision=lax.Precision.HIGHEST
    )


def norm_sums(grad_hidden, scaled, router, grad_gates, width, gates=None, hidden=None, member=None):
    parts = [
        grad_gates,
        exact_last(router.astype(F32), scaled),
        jnp.sum(grad_hidden * scaled, axis=1)[None],
    ]
    if gates is None:
        parts.append(contract_last(router, hidden))
    parts = grid_sum(jnp.concatenate(parts, axis=0))
    if gates is None:
        gates = route_gates(parts[2 * PLANES + 1 :], member)
    grad_logits = logits_grad(gates, parts[:PLANES])
    inner = parts[2 * PLANES] + jnp.sum(grad_logits * parts[PLANES : 2 * PLANES], axis=0)
    return grad_logits, inner[:, None] / width, gates


def per_device(
    tokens, segment_ids, attention_routes, expert_routes, attention_gain, attention_kv,
    attention_query, attention_out, attention_router, feedforward_gain, feedforward_router,
    expert_gate_up, expert_down, output_grad,
):
    groups = lax.axis_size("t")
    grid_count = lax.axis_size("grid")
    group = lax.axis_index("t")
    plane = lax.axis_index("z")
    place = plane * HALVES + lax.axis_index("x")
    column = lax.axis_index("grid")
    rows, features = tokens.shape
    width_all = features * grid_count
    token_count = BLOCKS * rows
    own_rows = attention_gain.shape[0]
    head_width = attention_kv.shape[3]
    head_pair = attention_kv.shape[1] // HALVES
    span = head_pair * head_width
    hidden_units = expert_gate_up.shape[3] // HALVES

    def mine(array, axis=0):
        return lax.dynamic_slice_in_dim(array, column * features, features, axis)

    def own(array, axis=0):
        return lax.dynamic_slice_in_dim(array, place * rows, rows, axis)

    query_pieces = attention_query.reshape(PLANES, own_rows, HALVES, span).transpose(0, 2, 1, 3)
    kv_pieces = attention_kv.reshape(own_rows, HALVES, head_pair, 2, head_width)
    kv_pieces = kv_pieces.transpose(1, 0, 3, 2, 4).reshape(1, HALVES, own_rows, 2 * span)
    kv_pieces = jnp.broadcast_to(kv_pieces, (PLANES,) + kv_pieces.shape[1:])
    qkv_pieces = jnp.concatenate([query_pieces, kv_pieces], axis=-1)
    out_pieces = attention_out.reshape(BLOCKS, span, own_rows).swapaxes(1, 2)
    first_pieces = jnp.concatenate([out_pieces, qkv_pieces.reshape(BLOCKS, own_rows, 3 * span)], axis=2)
    own_routes = jnp.concatenate([attention_routes, expert_routes], axis=1)
    small = jnp.concatenate(
        [attention_gain[:, None], feedforward_gain[:, None], attention_router, feedforward_router],
        axis=1,
    )
    small = lax.all_gather(small, "t", axis=0).reshape(-1, small.shape[1])
    small = small.T.reshape(small.shape[1], -1)
    spare = jnp.zeros((small.shape[0], features - small.shape[1] % features), BF16)
    small = jnp.concatenate([small, spare], axis=1).reshape(-1, features)
    under = jnp.concatenate([own_routes.T.astype(BF16), small], axis=0)
    under = jnp.pad(under, ((0, -under.shape[0] % 16), (0, 0)))
    everything, first_weight, up_pieces, *down_halves = opened(
        jnp.concatenate([tokens, under], axis=0), first_pieces, expert_gate_up,
        expert_down.reshape(BLOCKS, hidden_units, own_rows), 0, 3,
    )
    first_weight = over_groups(first_weight).reshape(width_all, 4 * span)
    out_weight, qkv_weight = first_weight[:, :span], first_weight[:, span:]
    up_weight = over_groups(exchanged(up_pieces)).reshape(width_all, 2 * hidden_units)
    under = everything[:, :, rows:, :features].reshape(BLOCKS, -1, features).swapaxes(0, 1)
    small = under[4:, :, : groups * own_rows].reshape(-1, BLOCKS, groups, own_rows)
    small = jnp.pad(small.swapaxes(1, 2).reshape(-1, width_all), ((0, 4), (0, 0)))
    gain_first, gain_second = mine(small[0]).astype(F32), mine(small[1]).astype(F32)
    router_first, router_second = mine(small[2:6], 1), mine(small[6:10], 1)

    member_first, member_second = members(under[0], under[1]), members(under[2], under[3])
    own_member_first = lax.dynamic_index_in_dim(member_first, place, 1, keepdims=False)
    own_member_second = lax.dynamic_index_in_dim(member_second, place, 1, keepdims=False)
    rank = prefix_ranks(
        jnp.concatenate(
            [
                lax.dynamic_index_in_dim(member_first, plane, 0, keepdims=False),
                lax.dynamic_index_in_dim(member_second, plane, 0, keepdims=False),
                own_member_first,
                own_member_second,
            ],
            axis=0,
        )
    )
    rank_first, rank_second = rank[:BLOCKS, None], rank[BLOCKS : 2 * BLOCKS, None]
    own_pick_first = picks(rank[2 * BLOCKS : 2 * BLOCKS + PLANES])
    own_pick_second = picks(rank[2 * BLOCKS + PLANES :])
    member_first = member_first.reshape(PLANES, token_count)
    member_second = member_second.reshape(PLANES, token_count)

    def to_slots(values, pick):
        return jnp.einsum("est,tf->esf", pick, values, preferred_element_type=F32).astype(BF16)

    def to_tokens(slots, pick):
        return jnp.einsum("est,esf->etf", pick, slots, preferred_element_type=F32)

    grad_out = output_grad.astype(F32)
    cosine, sine = rope_tables(token_count, head_width)
    cosine, sine = jnp.asarray(cosine), jnp.asarray(sine)
    hidden_first, queries, keys, values, logits_first, inverse_first = project(
        everything, rows, small, first_weight, cosine, sine, span, head_width
    )
    gates_first = route_gates(logits_first[2 : 2 + PLANES], member_first)
    own_gates_first = own(gates_first, 1)
    position = jnp.arange(token_count, dtype=jnp.int32)
    segment = lax.dynamic_slice_in_dim(segment_ids, group * token_count, token_count, 0)
    opens = jnp.concatenate([jnp.ones((1,), jnp.bool_), segment[1:] != segment[:-1]])
    document_start = lax.cummax(jnp.where(opens, position, 0))
    begin = document_start.reshape(BLOCKS, rows)[:, 0] // rows
    table = token_table(
        position, document_start, lax.dynamic_index_in_dim(gates_first, plane, 0, keepdims=False)
    )
    attention_args = (begin, queries, keys, values, rank_first, table)
    attended, gated, gate_slots_first, lse = attention_forward(*attention_args, head_width)
    branch, grad_out_slots, lse = lax.optimization_barrier(
        (
            contract_last(attended, out_weight).astype(BF16),
            to_slots(output_grad, own_pick_second),
            lse.reshape(-1, BLOCKS, 1, CAP),
        )
    )
    branch_slots, down_first = scattered(
        branch, CAP, 2, ride=down_halves[0], share=1
    )
    branch_first = to_tokens(branch_slots, own_pick_first)
    residual = tokens.astype(F32) + jnp.sum(own_gates_first[:, :, None] * branch_first, axis=0)

    square = grid_sum(jnp.sum(residual * residual, axis=1))
    inverse_second = lax.rsqrt(square / width_all + EPSILON)[:, None]
    normed_second = residual * inverse_second
    hidden_second = (normed_second * gain_second).astype(BF16)
    slots_second, down_last = gathered(
        to_slots(hidden_second, own_pick_second), 1, ride=down_halves[1], share=3
    )
    down_weight = [
        over_groups(half).reshape((groups * BLOCKS,) + half.shape[1:]) for half in (down_first, down_last)
    ]
    slots_second = slots_second.reshape(BLOCKS, CAP, width_all)
    gate_pre, up_pre, result, gate_slots_second, inner, grad_slots_second = expert_forward(
        slots_second,
        up_weight,
        down_weight,
        small,
        rank_second,
        jnp.pad(member_second.astype(BF16), ((6, 6), (0, 0))),
        grad_out_slots,
        4,
    )
    grad_slots_second = grad_slots_second.reshape(BLOCKS, CAP, width_all)
    grad_rows, grad_gate_up, grad_down_first, grad_down_last, result_slots, *landed = expert_backward(
        gate_pre, up_pre, grad_slots_second, gate_slots_second, up_weight, down_weight, inner, result,
        int(groups == 1), 5,
    )
    if groups > 1:
        grad_down = jnp.concatenate([grad_down_first, grad_down_last], axis=1)
        grad_down = group_sums(grad_down.reshape(groups, BLOCKS, own_rows, hidden_units))
        grad_down_first, grad_down_last = jnp.split(grad_down, 2, axis=1)
        landed = [exchanged(grad_down_first)]
    grad_down_first = landed[0]
    grad_up_first, grad_up, grad_rows, grad_down_last = expert_gradient(
        slots_second.reshape(-1, width_all), grad_gate_up, grad_rows, grad_down_last, 6
    )
    branch_second = to_tokens(result_slots, own_pick_second)

    grad_hidden_second = jnp.sum(to_tokens(grad_rows, own_pick_second), axis=0)
    grad_logits_second, inner_mean, own_gates_second = norm_sums(
        grad_hidden_second, normed_second * gain_second, router_second,
        jnp.sum(branch_second * grad_out[None], axis=2), width_all,
        hidden=hidden_second, member=own_member_second,
    )
    grad_hidden_second = grad_hidden_second + exact_first(
        grad_logits_second, router_second.astype(F32)
    )
    grad_normed = grad_hidden_second * gain_second
    grad_residual = grad_out + inverse_second * (grad_normed - normed_second * inner_mean)

    grad_up_first = return_gradients(grad_up_first.reshape(groups, BLOCKS, own_rows, EARLY))
    grad_slots_first = gathered(to_slots(grad_residual.astype(BF16), own_pick_first), 8)
    (
        grad_slots_first, grad_up_first, residual, own_gates_second, branch_second, hidden_second,
        grad_logits_second, grad_hidden_second, normed_second,
    ) = lax.optimization_barrier(
        (
            grad_slots_first, grad_up_first, residual, own_gates_second, branch_second, hidden_second,
            grad_logits_second, grad_hidden_second, normed_second,
        )
    )
    layer_output = residual + jnp.sum(own_gates_second[:, :, None] * branch_second, axis=0)
    layer_output = layer_output.astype(BF16)
    grad_router_second = exact(grad_logits_second, hidden_second.astype(F32))
    grad_gain_second = jnp.sum(grad_hidden_second * normed_second, axis=0)
    grad_slots_first = grad_slots_first.reshape(BLOCKS * CAP, -1)
    grad_up, grad_slots_first = lax.optimization_barrier((grad_up, grad_slots_first))
    grad_up = return_gradients(grad_up.reshape(groups, BLOCKS, own_rows, 2 * hidden_units - EARLY))
    grad_attended = gate_slots_first * dot(grad_slots_first, out_weight)
    grad_attended = grad_attended.astype(BF16)
    grad_query, grad_keys, grad_values = attention_backward(
        *attention_args, attended, lse, grad_attended, cosine, sine, head_width
    )
    grad_qkv = jnp.concatenate([grad_query, grad_keys, grad_values], axis=1)
    grad_hidden = contract_last(grad_qkv, qkv_weight).astype(BF16)
    grad_first, grad_hidden = closing(
        hidden_first, grad_query, grad_keys, grad_values, grad_slots_first, gated, grad_hidden, 3
    )
    grad_hidden = jnp.sum(grad_hidden.astype(F32), axis=0)
    grad_first, grad_up = lax.optimization_barrier((grad_first, grad_up))
    grad_first = return_gradients(grad_first.reshape(groups, BLOCKS, own_rows, 4 * span))
    expert_gate_up_grad = unpack_up(grad_up_first, grad_up)
    expert_down_grad = jnp.concatenate([grad_down_first, grad_down_last], axis=1)
    expert_down_grad = expert_down_grad.astype(F32).swapaxes(1, 2).reshape(expert_down.shape)

    own_normed = tokens.astype(F32) * own(inverse_first)
    own_hidden = (own_normed * gain_first).astype(BF16)
    grad_logits_first, inner_mean, _ = norm_sums(
        grad_hidden, own_normed * gain_first, router_first,
        jnp.sum(branch_first * grad_residual[None], axis=2), width_all, gates=own_gates_first,
    )
    grad_hidden_first = grad_hidden + exact_first(grad_logits_first, router_first.astype(F32))
    grad_router_first = exact(grad_logits_first, own_hidden.astype(F32))
    grad_gain_first = jnp.sum(grad_hidden_first * own_normed, axis=0)
    grad_normed = grad_hidden_first * gain_first
    input_grad = grad_residual + own(inverse_first) * (grad_normed - own_normed * inner_mean)

    small_grads = jnp.concatenate(
        [grad_gain_first[None], grad_gain_second[None], grad_router_first, grad_router_second],
        axis=0,
    )
    small_grads = lax.all_gather(small_grads, "grid", axis=1, tiled=True)
    if groups > 1:
        small_grads = lax.psum(small_grads, "t")
    small_grads = small_grads.reshape(-1, groups, BLOCKS, own_rows)
    small_grads = lax.dynamic_index_in_dim(small_grads, group, 1, keepdims=False).swapaxes(0, 1)
    small_grads = jnp.pad(small_grads, ((0, 0), (0, 6), (0, -own_rows % 128)))
    small_grads, expert_gate_up_grad, expert_down_grad = lax.optimization_barrier(
        (small_grads, expert_gate_up_grad, expert_down_grad)
    )
    (
        attention_query_grad, attention_kv_grad, attention_out_grad, gain_grad_first,
        gain_grad_second, router_grad_first, router_grad_second,
    ) = finish(
        grad_first, swapped(small_grads, 7), own_rows, span, attention_kv.shape[1], head_width
    )
    attention_out_grad = attention_out_grad.reshape(attention_out.shape)
    return (
        layer_output,
        input_grad.astype(BF16),
        gain_grad_first[0, :own_rows],
        attention_kv_grad,
        attention_query_grad.astype(F32),
        attention_out_grad.astype(F32),
        router_grad_first[:, :own_rows].T,
        gain_grad_second[0, :own_rows],
        router_grad_second[:, :own_rows].T,
        expert_gate_up_grad,
        expert_down_grad,
    )


def solution(mesh):
    groups = mesh.shape["wide"] // BLOCKS
    shape = (groups, PLANES, HALVES, mesh.shape["grid"])
    inner_mesh = Mesh(mesh.devices.reshape(shape), ("t", "z", "x", "grid"))
    wide = ("t", "z", "x")
    in_specs = (
        P(wide, "grid"),
        P(),
        P(wide, None),
        P(wide, None),
        P(wide),
        P(wide, "grid", None, None),
        P(None, wide, "grid", None),
        P(None, "grid", None, wide),
        P(wide, None),
        P(wide),
        P(wide, None),
        P(None, wide, None, "grid"),
        P(None, "grid", wide),
        P(wide, "grid"),
    )
    out_specs = (
        P(wide, "grid"),
        P(wide, "grid"),
        P(wide),
        P(wide, "grid", None, None),
        P(None, wide, "grid", None),
        P(None, "grid", None, wide),
        P(wide, None),
        P(wide),
        P(wide, None),
        P(None, wide, None, "grid"),
        P(None, "grid", wide),
    )
    return jax.shard_map(
        per_device, mesh=inner_mesh, in_specs=in_specs, out_specs=out_specs, check_vma=False
    )
```

```python
import functools
import math

import jax
import jax.numpy as jnp
import numpy as np
from jax import lax
from jax.experimental import pallas as pl
from jax.experimental.layout import Layout, with_layout_constraint
from jax.experimental.pallas import tpu as pltpu
from jax.sharding import Mesh, PartitionSpec as P

CAP = 320
PLANES = 4
HALVES = 2
BLOCKS = PLANES * HALVES
EPSILON = 1e-05
ROPE_BASE = 10000.0
NEGATIVE = -1e30
BF16 = jnp.bfloat16
F32 = jnp.float32
PLACES = ("z", "x")
MESH = pl.DeviceIdType.MESH
VMEM_BYTES = 56 * 1024 * 1024
EARLY = 128


def rope_tables(token_count, width):
    half = width // 2
    frequency = np.float32(ROPE_BASE) ** (-np.arange(half, dtype=np.float32) / np.float32(half))
    angles = np.arange(token_count, dtype=np.float32)[:, None] * frequency.astype(np.float32)[None, :]
    cosine, sine = np.cos(angles).astype(np.float32), np.sin(angles).astype(np.float32)
    return np.concatenate([cosine, cosine], axis=1), np.concatenate([-sine, sine], axis=1)


def turned(values, cosine, sine):
    return values * cosine + pltpu.roll(values, values.shape[1] // 2, 1) * sine


def dot(left, right):
    return jnp.dot(left, right, preferred_element_type=F32)


def contract_first(left, right):
    return lax.dot_general(left, right, (((0,), (0,)), ((), ())), preferred_element_type=F32)


def contract_last(left, right):
    return lax.dot_general(left, right, (((1,), (1,)), ((), ())), preferred_element_type=F32)


def exact(left, right):
    return jnp.dot(left, right, precision=lax.Precision.HIGHEST)


def project_kernel(
    tokens_ref, small_ref, query_weight_ref, shared_weight_ref, cos_ref, sin_ref,
    hidden_ref, q_ref, k_ref, v_ref, logits_ref, inverse_ref, *, head_width
):
    x = tokens_ref[0, 0].astype(F32)
    inverse = lax.rsqrt(jnp.mean(x * x, axis=1, keepdims=True) + EPSILON)
    inverse_ref[...] = inverse
    hidden = (x * inverse * small_ref[:1, :].astype(F32)).astype(BF16)
    hidden_ref[...] = hidden
    logits_ref[...] = contract_last(small_ref[...], hidden)
    queries = dot(hidden, query_weight_ref[...])
    shared = dot(hidden, shared_weight_ref[...])
    span = q_ref.shape[1]
    cosine, sine = cos_ref[...], sin_ref[...]
    for head in range(span // head_width):
        at = slice(head * head_width, (head + 1) * head_width)
        q_ref[:, at] = turned(queries[:, at], cosine, sine).astype(BF16)
        k_ref[:, at] = turned(shared[:, at], cosine, sine).astype(BF16)
    v_ref[...] = shared[:, span:].astype(BF16)


def project(tokens, rows, small, weight, cosine, sine, span, head_width):
    width = tokens.shape[-1]
    token_count = BLOCKS * rows
    whole = lambda b: (0, 0)
    block = lambda b: (b, 0)
    return pl.pallas_call(
        functools.partial(project_kernel, head_width=head_width),
        grid=(BLOCKS,),
        in_specs=[
            pl.BlockSpec((1, 1, rows, width), lambda b: (b // HALVES, b % HALVES, 0, 0)),
            pl.BlockSpec(small.shape, whole),
            pl.BlockSpec((width, span), lambda b: (0, 1)),
            pl.BlockSpec((width, 2 * span), lambda b: (0, 1)),
            pl.BlockSpec((rows, head_width), block),
            pl.BlockSpec((rows, head_width), block),
        ],
        out_specs=[
            pl.BlockSpec((rows, width), block),
            pl.BlockSpec((rows, span), block),
            pl.BlockSpec((rows, span), block),
            pl.BlockSpec((rows, span), block),
            pl.BlockSpec((small.shape[0], rows), lambda b: (0, b)),
            pl.BlockSpec((rows, 1), block),
        ],
        out_shape=[
            jax.ShapeDtypeStruct((token_count, width), BF16),
            jax.ShapeDtypeStruct((token_count, span), BF16),
            jax.ShapeDtypeStruct((token_count, span), BF16),
            jax.ShapeDtypeStruct((token_count, span), BF16),
            jax.ShapeDtypeStruct((small.shape[0], token_count), F32),
            jax.ShapeDtypeStruct((token_count, 1), F32),
        ],
        compiler_params=pltpu.CompilerParams(vmem_limit_bytes=VMEM_BYTES),
        name="project",
    )(tokens, small, weight, weight, cosine, sine)


def slots_of_block(rank_ref, table_ref, cap, block):
    rows = table_ref.shape[1]
    pick = (lax.broadcasted_iota(jnp.int32, (cap, rows), 0) == rank_ref[0]).astype(BF16)
    made = contract_last(pick, table_ref[...])
    base = block * rows
    filled = made[:, 4:5] > 0.5
    low = (64.0 * made[:, 2:3] + made[:, 3:4]).astype(jnp.int32)
    high = (64.0 * made[:, 0:1] + made[:, 1:2]).astype(jnp.int32)
    gate = made[:, 5:6] + made[:, 6:7] + made[:, 7:8]
    return pick, jnp.where(filled, low, base), jnp.where(filled, high, base), gate


def rows_of_block(rank_ref, table_ref, cap, block):
    rows = table_ref.shape[1]
    pick = (lax.broadcasted_iota(jnp.int32, (cap, rows), 0) == rank_ref[0]).astype(BF16)
    made = contract_last(table_ref[...], pick)
    filled = made[4:5] > 0.5
    low = (64.0 * made[2:3] + made[3:4]).astype(jnp.int32)
    high = (64.0 * made[0:1] + made[1:2]).astype(jnp.int32)
    return pick, jnp.where(filled, low, block * rows), jnp.where(filled, high, block * rows)


def token_table(position, document_start, gate):
    first = gate.astype(BF16).astype(F32)
    second = (gate - first).astype(BF16).astype(F32)
    rows = [
        position // 64, position % 64, document_start // 64, document_start % 64,
        jnp.ones_like(gate), first, second, gate - first - second,
    ]
    return jnp.pad(jnp.stack([row.astype(BF16) for row in rows]), ((0, 8), (0, 0)))


def attention_forward_kernel(
    begin_ref, q_ref, k_ref, v_ref, rank_ref, table_ref, out_ref, gated_ref, gate_ref, lse_ref, *,
    scaling, width
):
    block = pl.program_id(0)
    cap = out_ref.shape[0]
    tile_rows = q_ref.shape[0]
    heads = [slice(h * width, (h + 1) * width) for h in range(out_ref.shape[1] // width)]
    pick, low_bound, high_bound, gate = slots_of_block(rank_ref, table_ref, cap, block)
    queries = dot(pick, q_ref[...]).astype(BF16)

    def step(tile, carried):
        rows = pl.ds(pl.multiple_of(tile * tile_rows, tile_rows), tile_rows)
        column = tile * tile_rows + lax.broadcasted_iota(jnp.int32, (cap, tile_rows), 1)
        allowed = (column >= low_bound) & (column <= high_bound)
        made = []
        for at, (largest, total, summed) in zip(heads, carried):
            scores = contract_last(queries[:, at], k_ref[rows, at]) * scaling
            scores = jnp.where(allowed, scores, NEGATIVE)
            new_largest = jnp.maximum(largest, jnp.max(scores, axis=1, keepdims=True))
            weights = jnp.where(allowed, jnp.exp(scores - new_largest), 0.0)
            shrink = jnp.exp(largest - new_largest)
            made.append(
                (
                    new_largest,
                    total * shrink + jnp.sum(weights, axis=1, keepdims=True),
                    summed * shrink + dot(weights.astype(BF16), v_ref[rows, at]),
                )
            )
        return tuple(made)

    start = (
        jnp.full((cap, 1), NEGATIVE, F32), jnp.zeros((cap, 1), F32), jnp.zeros((cap, width), F32)
    )
    ended = lax.fori_loop(begin_ref[block], block + 1, step, (start,) * len(heads))
    gate_ref[...] = gate
    for h, (largest, total, summed) in enumerate(ended):
        attended = (summed / total).astype(BF16)
        out_ref[:, heads[h]] = attended
        gated_ref[:, heads[h]] = (gate * attended.astype(F32)).astype(BF16)
        lse_ref[h] = largest + jnp.log(total)


def attention_backward_kernel(
    begin_ref, q_ref, k_ref, v_ref, rank_ref, table_ref, out_ref, lse_ref, grad_ref,
    cos_ref, sin_ref, dq_ref, dk_ref, dv_ref, dk_sum, dv_sum, *, scaling, width
):
    block = pl.program_id(0)
    cap = out_ref.shape[0]
    tile_rows = q_ref.shape[0]
    heads = [slice(h * width, (h + 1) * width) for h in range(out_ref.shape[1] // width)]
    pick, low_bound, high_bound = rows_of_block(rank_ref, table_ref, cap, block)
    queries = dot(pick, q_ref[...]).astype(BF16)
    grads = grad_ref[...]
    product = grads.astype(F32) * out_ref[...].astype(F32)
    ones = jnp.ones((8, width), F32)
    deltas = [exact_last(ones, product[:, at])[:1] for at in heads]

    @pl.when(block == 0)
    def _():
        dk_sum[...] = jnp.zeros_like(dk_sum)
        dv_sum[...] = jnp.zeros_like(dv_sum)

    def step(tile, dq):
        rows = pl.ds(pl.multiple_of(tile * tile_rows, tile_rows), tile_rows)
        position = tile * tile_rows + lax.broadcasted_iota(jnp.int32, (tile_rows, cap), 0)
        allowed = (position >= low_bound) & (position <= high_bound)
        made = []
        for h, at in enumerate(heads):
            q, grad, keys = queries[:, at], grads[:, at], k_ref[rows, at]
            scores = contract_last(keys, q) * scaling
            chances = jnp.where(allowed, jnp.exp(scores - lse_ref[h, 0]), 0.0)
            dv_sum[rows, at] += dot(chances.astype(BF16), grad)
            grad_chances = contract_last(v_ref[rows, at], grad)
            grad_scores = (chances * (grad_chances - deltas[h])).astype(BF16)
            dk_sum[rows, at] += dot(grad_scores, q) * scaling
            made.append(dq[h] + contract_first(grad_scores, keys))
        return tuple(made)

    zero = jnp.zeros((cap, width), F32)
    dq = lax.fori_loop(begin_ref[block], block + 1, step, (zero,) * len(heads))
    own = pl.ds(pl.multiple_of(block * tile_rows, tile_rows), tile_rows)
    for h, at in enumerate(heads):
        scaled = dq[h] * scaling
        high = scaled.astype(BF16)
        rest = (scaled - high.astype(F32)).astype(BF16)
        dq_tokens = contract_first(pick, high) + contract_first(pick, rest)
        dq_ref[:, at] = turned(dq_tokens, cos_ref[own, :], -sin_ref[own, :]).astype(BF16)

    @pl.when(block == BLOCKS - 1)
    def _():
        def finish_tile(tile, nothing):
            rows = pl.ds(pl.multiple_of(tile * tile_rows, tile_rows), tile_rows)
            for at in heads:
                dk_ref[rows, at] = turned(
                    dk_sum[rows, at], cos_ref[rows, :], -sin_ref[rows, :]
                ).astype(BF16)
            dv_ref[rows, :] = dv_sum[rows, :].astype(BF16)
            return nothing

        lax.fori_loop(0, BLOCKS, finish_tile, 0)


def attention_forward(begin, q, k, v, rank, table, width):
    token_count, span = q.shape
    row_count = token_count // BLOCKS
    heads = span // width
    block = lambda b, s: (b, 0)
    tokens = pl.BlockSpec((row_count, span), block)
    keys = pl.BlockSpec((token_count, span), lambda b, s: (0, 0))
    slots = pl.BlockSpec((CAP, span), block)
    rows = [
        pl.BlockSpec((1, 1, row_count), lambda b, s: (b, 0, 0)),
        pl.BlockSpec((16, row_count), lambda b, s: (0, b)),
    ]
    return pl.pallas_call(
        functools.partial(
            attention_forward_kernel, scaling=1.0 / math.sqrt(width), width=width
        ),
        grid_spec=pltpu.PrefetchScalarGridSpec(
            num_scalar_prefetch=1,
            grid=(BLOCKS,),
            in_specs=[tokens, keys, keys] + rows,
            out_specs=[
                slots,
                slots,
                pl.BlockSpec((CAP, 1), block),
                pl.BlockSpec((heads, CAP, 1), lambda b, s: (0, b, 0)),
            ],
        ),
        out_shape=[
            jax.ShapeDtypeStruct((BLOCKS * CAP, span), BF16),
            jax.ShapeDtypeStruct((BLOCKS * CAP, span), BF16),
            jax.ShapeDtypeStruct((BLOCKS * CAP, 1), F32),
            jax.ShapeDtypeStruct((heads, BLOCKS * CAP, 1), F32),
        ],
        compiler_params=pltpu.CompilerParams(vmem_limit_bytes=VMEM_BYTES),
        name="attention_forward",
    )(begin, q, k, v, rank, table)


def attention_backward(begin, q, k, v, rank, table, out, lse, grad, cosine, sine, width):
    token_count, span = q.shape
    row_count = token_count // BLOCKS
    block = lambda b, s: (b, 0)
    whole = lambda b, s: (0, 0)
    tokens = pl.BlockSpec((row_count, span), block)
    keys = pl.BlockSpec((token_count, span), whole)
    slots = pl.BlockSpec((CAP, span), block)
    angles = pl.BlockSpec((token_count, width), whole)
    rows = [
        pl.BlockSpec((1, 1, row_count), lambda b, s: (b, 0, 0)),
        pl.BlockSpec((16, row_count), lambda b, s: (0, b)),
    ]
    sums = pl.BlockSpec((span // width, 1, 1, CAP), lambda b, s: (0, b, 0, 0))
    return pl.pallas_call(
        functools.partial(
            attention_backward_kernel, scaling=1.0 / math.sqrt(width), width=width
        ),
        grid_spec=pltpu.PrefetchScalarGridSpec(
            num_scalar_prefetch=1,
            grid=(BLOCKS,),
            in_specs=[tokens, keys, keys] + rows + [slots, sums, slots, angles, angles],
            out_specs=[tokens, keys, keys],
            scratch_shapes=[pltpu.VMEM((token_count, span), F32)] * 2,
        ),
        out_shape=[jax.ShapeDtypeStruct((token_count, span), BF16)] * 3,
        compiler_params=pltpu.CompilerParams(vmem_limit_bytes=VMEM_BYTES),
        name="attention_backward",
    )(begin, q, k, v, rank, table, out, lse, grad, cosine, sine)


def pack_up_kernel(weight_ref, pieces_ref):
    units = pieces_ref.shape[2] // 2
    both = weight_ref[0].astype(F32)
    gate, up = both[:, 0, :], both[:, 1, :]
    for half in range(HALVES):
        at = slice(half * units, (half + 1) * units)
        pieces_ref[half] = jnp.concatenate([gate[:, at], up[:, at]], axis=1).astype(BF16)


def pack_down_kernel(weight_ref, first_ref, last_ref):
    turned_rows = weight_ref[0].astype(F32).T.astype(BF16)
    middle = first_ref.shape[1]
    first_ref[0] = turned_rows[:middle]
    last_ref[0] = turned_rows[middle:]


def row_major(array):
    return with_layout_constraint(array, Layout(major_to_minor=tuple(range(array.ndim))))


def exchanged(pieces):
    return row_major(lax.all_to_all(row_major(pieces), PLACES, 0, 0, tiled=True))


def over_groups(landed):
    return lax.all_gather(landed, "t", axis=0, tiled=False)


def group_sums(pieces):
    return lax.psum_scatter(pieces, "t", scatter_dimension=0, tiled=False)


def return_gradients(pieces):
    return exchanged(group_sums(pieces))


def other_core(column):
    return column + 1 - 2 * (column % 2)


def crossed(plane, j):
    return (plane, plane + 1 - 2 * (plane % 2), (plane + 2) % 4, 3 - plane)[j]


def meet(peers):
    barrier = pltpu.get_barrier_semaphore()
    for peer in peers:
        pl.semaphore_signal(barrier, inc=1, device_id=peer, device_id_type=MESH)
    pl.semaphore_wait(barrier, len(peers))


def partners():
    plane, half, column = lax.axis_index("z"), lax.axis_index("x"), lax.axis_index("grid")
    planes = [{"z": crossed(plane, j)} for j in range(PLANES)]
    along_x, along_y = {"x": 1 - half}, {"grid": (column + 2) % 4}
    core = {"grid": other_core(column)}
    return plane, half, column, planes, along_x, along_y, core


class Moves:
    def __init__(self, send, recv):
        self.send, self.recv, self.made = send, recv, {}

    def add(self, index, source, target, peer):
        self.made[index] = (source, target, peer)

    def copy(self, index, source, target, peer):
        return pltpu.make_async_remote_copy(
            src_ref=source, dst_ref=target, send_sem=self.send.at[index],
            recv_sem=self.recv.at[index], device_id=peer, device_id_type=MESH,
        )

    def start(self, index):
        self.copy(index, *self.made[index]).start()

    def arrived(self, index, target, peer):
        self.copy(index, target, target, peer).wait_recv()

    def all_sent(self):
        for index in self.made:
            self.copy(index, *self.made[index]).wait_send()


class Ride:
    def __init__(self, pieces_ref, landed_ref, send, recv, local, columns=None):
        if columns is None:
            columns = pl.ds(0, pieces_ref.shape[2])
        rows = pl.ds(0, pieces_ref.shape[1])
        plane, half = lax.axis_index("z"), lax.axis_index("x")
        self.moves = Moves(send, recv)
        self.landings = {}
        own = plane * HALVES + half
        self.keep = pltpu.make_async_copy(pieces_ref.at[own], landed_ref.at[own], local)
        self.peers = []
        for dz in range(PLANES):
            for dx in range(HALVES):
                index = dz * HALVES + dx
                if index == 0:
                    continue
                at_half = 1 - half if dx else half
                peer = {"z": crossed(plane, dz), "x": at_half}
                other = crossed(plane, dz) * HALVES + at_half
                source = pieces_ref.at[other, rows, columns]
                self.moves.add(index, source, landed_ref.at[own, rows, columns], peer)
                self.landings[index] = (landed_ref.at[other, rows, columns], peer)
                if dz and dx:
                    self.peers.append(peer)

    def begin(self, first=(4, 6, 2)):
        self.keep.start()
        for index in first:
            self.moves.start(index)

    def go_on(self, number, plan=((5,), (7,), (3,), (1,))):
        for index in plan[number] if number < len(plan) else ():
            self.moves.start(index)

    def finish(self):
        for index, (landing, peer) in self.landings.items():
            self.moves.arrived(index, landing, peer)
        self.moves.all_sent()
        self.keep.wait()


RIDE_SCRATCH = (
    pltpu.SemaphoreType.DMA((8,)),
    pltpu.SemaphoreType.DMA((8,)),
    pltpu.SemaphoreType.DMA,
)


def run_with_ride(steps, ride):
    steps[0]()
    if ride is not None:
        ride.begin()
    for number, step in enumerate(steps[1:-1]):
        step()
        if ride is not None:
            ride.go_on(number)
    steps[-1]()
    if ride is not None:
        ride.finish()


def gather_parts(slots_ref, out_ref, send, recv, local, same, share=2, more=(), chain=None):
    plane, half, column, planes, along_x, along_y, core = partners()
    cap, width = slots_ref.shape[-2:]
    middle = cap * share // 64 * 16
    y_column, core_column = (column + 2) % 4, other_core(column)
    core_y = (core_column + 2) % 4
    sources = [crossed(plane, j) for j in range(PLANES)]
    moves = Moves(send, recv)

    def piece(source, at_half, at_column, first=0, count=cap):
        columns = pl.ds(pl.multiple_of(at_column * width, width), width)
        return out_ref.at[source, at_half, pl.ds(first, count), columns]

    def slots_for(j):
        return slots_ref if same else slots_ref.at[sources[j]]

    keep = pltpu.make_async_copy(slots_for(0), piece(plane, half, column), local)
    for j in range(PLANES):
        source = sources[j]
        place = piece(source, half, column)
        if j and chain is None:
            moves.add(j, slots_for(j), piece(plane, half, column), planes[j])
        here = place if j else slots_for(0)
        moves.add(4 + j, here, place, along_x)
        moves.add(8 + j, here, place, along_y)
        moves.add(12 + j, here, place, core)
        from_x, from_y = piece(source, 1 - half, column), piece(source, half, y_column)
        first = piece(source, 1 - half, column, 0, middle)
        last = piece(source, half, y_column, middle, cap - middle)
        diagonal = piece(source, 1 - half, y_column)
        moves.add(16 + j, first, first, along_y)
        moves.add(20 + j, from_x, from_x, core)
        moves.add(24 + j, last, last, along_x)
        moves.add(28 + j, from_y, from_y, core)
        moves.add(32 + j, diagonal, diagonal, core)

    def begin():
        meet(planes[1:] + [along_x, along_y, core] + list(more))
        if chain is None:
            for j in (1, 3, 2):
                moves.start(j)
        else:
            chain.begin()
        keep.start()

    def spread(j):
        if j and chain is None:
            moves.arrived(j, piece(sources[j], half, column), planes[j])
        elif j:
            chain.arrived(j)
        for index in (4, 8, 12):
            moves.start(index + j)

    def forward(j):
        moves.arrived(4 + j, piece(sources[j], 1 - half, column), along_x)
        moves.start(16 + j)
        moves.start(20 + j)
        moves.arrived(8 + j, piece(sources[j], half, y_column), along_y)
        moves.start(24 + j)
        moves.start(28 + j)

    def cross(j):
        moves.arrived(16 + j, piece(sources[j], 1 - half, y_column, 0, middle), along_y)
        moves.arrived(24 + j, piece(sources[j], 1 - half, y_column, middle, cap - middle), along_x)
        moves.start(32 + j)

    def finish():
        for j in order:
            moves.arrived(12 + j, piece(sources[j], half, core_column), core)
            moves.arrived(20 + j, piece(sources[j], 1 - half, core_column), core)
            moves.arrived(28 + j, piece(sources[j], half, core_y), core)
            moves.arrived(32 + j, piece(sources[j], 1 - half, core_y), core)
        moves.all_sent()
        keep.wait()

    order = (0, 1, 3, 2)
    return begin, spread, forward, cross, finish, order


def gather_steps(*refs, **settings):
    begin, spread, forward, cross, finish, order = gather_parts(*refs, **settings)

    def step(number):
        if number < len(order):
            spread(order[number])
        if 0 <= number - 1 < len(order):
            forward(order[number - 1])
        if 0 <= number - 2 < len(order):
            cross(order[number - 2])

    return [begin] + [functools.partial(step, number) for number in range(len(order) + 2)] + [finish]


class Chain:
    def __init__(self, view, source, send, recv):
        plane = lax.axis_index("z")
        self.inner = (plane == 1) | (plane == 2)
        near, far = {"z": crossed(plane, 1)}, {"z": crossed(plane, 3)}
        self.views = [view(crossed(plane, j)) for j in range(PLANES)]
        self.send, self.recv = send, recv
        self.near_own = (0, 1, source, self.views[0], near)
        self.far_own = (1, 3, source, self.views[0], far)
        self.on_arrival = {
            1: (2, 2, self.views[1], self.views[1], far),
            3: (3, 2, self.views[3], self.views[3], near),
            2: (4, 3, self.views[2], self.views[2], near),
        }

    def copy(self, at_send, at_recv, source, target, peer):
        return pltpu.make_async_remote_copy(
            src_ref=source, dst_ref=target, send_sem=self.send.at[at_send],
            recv_sem=self.recv.at[at_recv], device_id=peer, device_id_type=MESH,
        )

    def begin(self):
        self.copy(*self.near_own).start()

        @pl.when(self.inner)
        def _():
            self.copy(*self.far_own).start()

    def arrived(self, j):
        place = self.views[j]
        self.copy(0, j, place, place, self.near_own[-1]).wait_recv()

        @pl.when(self.inner)
        def _():
            self.copy(*self.on_arrival[j]).start()

    def finish(self):
        self.copy(*self.near_own).wait_send()

        @pl.when(self.inner)
        def _():
            self.copy(*self.far_own).wait_send()
            for made in self.on_arrival.values():
                self.copy(*made).wait_send()


CHAIN_SCRATCH = (pltpu.SemaphoreType.DMA((5,)), pltpu.SemaphoreType.DMA((4,)))


def opening_kernel(
    tokens_ref, pieces_ref, up_ref, down_ref, out_ref, landed_ref, up_pieces_ref, first_ref,
    last_ref, send, recv, local, ride_send, ride_recv,
    ride_local, hop_send, hop_recv, *chain_sems, share
):
    plane, half, column = lax.axis_index("z"), lax.axis_index("x"), lax.axis_index("grid")
    width = tokens_ref.shape[1]
    middle = pieces_ref.shape[2] // 2
    left, right = pl.ds(0, middle), pl.ds(middle, middle)
    rows = pl.ds(0, pieces_ref.shape[1])
    along_x = {"x": 1 - half}

    def tokens_of(source):
        columns = pl.ds(pl.multiple_of(column * width, width), width)
        return out_ref.at[source, half, pl.ds(0, tokens_ref.shape[0]), columns]

    def shared_of(at_half):
        return lambda source: landed_ref.at[source * HALVES + at_half, rows, right]

    own = plane * HALVES + half
    tokens = Chain(tokens_of, tokens_ref, *chain_sems[:2])
    here = Chain(shared_of(half), pieces_ref.at[own, rows, right], *chain_sems[2:4])
    there = Chain(shared_of(1 - half), shared_of(1 - half)(plane), *chain_sems[4:])
    ride = Ride(pieces_ref, landed_ref, ride_send, ride_recv, ride_local, left)
    hop = pltpu.make_async_remote_copy(
        src_ref=pieces_ref.at[plane * HALVES + 1 - half, rows, right],
        dst_ref=landed_ref.at[own, rows, right],
        send_sem=hop_send, recv_sem=hop_recv, device_id=along_x, device_id_type=MESH,
    )
    landing = shared_of(1 - half)(plane)
    hop_here = pltpu.make_async_remote_copy(
        src_ref=landing, dst_ref=landing, send_sem=hop_send, recv_sem=hop_recv,
        device_id=along_x, device_id_type=MESH,
    )
    begin, spread, forward, cross, finish, _ = gather_parts(
        tokens_ref, out_ref, send, recv, local, True, share, ride.peers, tokens
    )

    def first():
        begin()
        ride.keep.start()
        spread(0)
        hop.start()
        here.begin()

    def second():
        spread(1)
        forward(0)
        ride.moves.start(2)

    def third():
        spread(3)
        forward(1)
        cross(0)
        hop_here.wait_recv()
        there.begin()
        here.arrived(1)

    def fourth():
        spread(2)
        forward(3)
        cross(1)
        ride.moves.start(6)
        ride.moves.start(4)
        here.arrived(3)
        there.arrived(1)

    def fifth():
        forward(2)
        cross(3)
        for index in (3, 7, 5, 1):
            ride.moves.start(index)
        here.arrived(2)
        there.arrived(3)
        cross(2)
        there.arrived(2)
        finish()
        ride.finish()
        hop.wait_send()
        for chain in (tokens, here, there):
            chain.finish()

    def compute():
        pack_up_kernel(up_ref, up_pieces_ref)
        pack_down_kernel(down_ref, first_ref, last_ref)

    carry([first], [second, third, fourth, fifth], (3, 6, 7, 7), compute)


def opened(tokens, pieces, up, down, collective_id, share):
    rows, width = tokens.shape
    experts, own_rows, _, units = up.shape
    places = experts * HALVES
    tile = own_rows // 2
    down_half = (places, own_rows // 2, units // HALVES)
    anywhere = pl.BlockSpec(memory_space=pl.ANY)
    half = pl.BlockSpec((1,) + down_half[1:], lambda p: (p, 0, 0))
    return pl.pallas_call(
        functools.partial(opening_kernel, share=share),
        grid=(places,),
        in_specs=[
            anywhere,
            anywhere,
            pl.BlockSpec((1, tile, 2, units), lambda p: (p // 2, p % 2, 0, 0)),
            pl.BlockSpec((1,) + down.shape[1:], lambda p: (p, 0, 0)),
        ],
        out_specs=[
            anywhere,
            anywhere,
            pl.BlockSpec((HALVES, tile, units), lambda p: (p // 2, p % 2, 0)),
            half,
            half,
        ],
        out_shape=[
            jax.ShapeDtypeStruct((PLANES, HALVES, rows, 4 * width), BF16),
            jax.ShapeDtypeStruct(pieces.shape, BF16),
            jax.ShapeDtypeStruct((places, own_rows, units), BF16),
            jax.ShapeDtypeStruct(down_half, BF16),
            jax.ShapeDtypeStruct(down_half, BF16),
        ],
        scratch_shapes=list(GATHER_SCRATCH) + list(RIDE_SCRATCH)
        + [pltpu.SemaphoreType.DMA, pltpu.SemaphoreType.DMA] + list(CHAIN_SCRATCH) * 3,
        compiler_params=pltpu.CompilerParams(
            collective_id=collective_id, has_side_effects=True, vmem_limit_bytes=VMEM_BYTES
        ),
        name="open_rows",
    )(tokens, pieces, up, down)


GATHER_SCRATCH = (
    pltpu.SemaphoreType.DMA((36,)),
    pltpu.SemaphoreType.DMA((36,)),
    pltpu.SemaphoreType.DMA,
)


def gather_kernel(*refs, same, share, rides):
    if rides:
        slots_ref, pieces_ref, out_ref, landed_ref = refs[:4]
        ride = Ride(pieces_ref, landed_ref, *refs[7:])
        scratch = refs[4:7]
    else:
        slots_ref, out_ref = refs[:2]
        ride, scratch = None, refs[2:]
    more = ride.peers if rides else ()
    run_with_ride(gather_steps(slots_ref, out_ref, *scratch, same, share, more), ride)


def gathered(slots, collective_id, ride=None, share=2):
    rows, width = slots.shape[-2:]
    rides = () if ride is None else (ride,)
    anywhere = pl.BlockSpec(memory_space=pl.ANY)
    out = pl.pallas_call(
        functools.partial(gather_kernel, same=slots.ndim == 2, share=share, rides=len(rides)),
        out_shape=[jax.ShapeDtypeStruct((PLANES, HALVES, rows, 4 * width), BF16)]
        + [jax.ShapeDtypeStruct(r.shape, BF16) for r in rides],
        in_specs=[anywhere] * (1 + len(rides)),
        out_specs=[anywhere] * (1 + len(rides)),
        scratch_shapes=list(GATHER_SCRATCH) + list(RIDE_SCRATCH) * len(rides),
        compiler_params=pltpu.CompilerParams(collective_id=collective_id, has_side_effects=True),
        name="gather_rows",
    )(slots, *rides)
    return out if rides else out[0]


def scatter_steps(
    partial_ref, out_ref, own, other, crossing, side, send, recv, load, share=2, more=()
):
    plane, half, column, planes, along_x, along_y, core = partners()
    cap, width = out_ref.shape[-2:]
    middle = cap * share // 64 * 16
    chunk = 32 if middle % 32 == 0 and cap % 32 == 0 else 16
    y_column, core_column = (column + 2) % 4, other_core(column)
    core_y = (core_column + 2) % 4
    halves = (half, 1 - half, half, 1 - half)
    own_columns = (column, column, y_column, y_column)
    core_columns = (core_column, core_column, core_y, core_y)
    moves = Moves(send, recv)
    first, last = pl.ds(0, middle), pl.ds(middle, cap - middle)

    def part(j, q, at_columns):
        columns = pl.ds(pl.multiple_of(at_columns[q] * width, width), width)
        return partial_ref.at[crossed(plane, j), halves[q], :, columns]

    def loading(j, q):
        return pltpu.make_async_copy(part(j, q, own_columns), own.at[j, q], load.at[4 * j + q])

    keep = pltpu.make_async_copy(own.at[0, 0], out_ref.at[plane], load.at[16])
    for j in range(PLANES):
        for q in range(4):
            moves.add(4 * j + q, part(j, q, core_columns), other.at[j, q], core)
        moves.add(16 + j, own.at[j, 3, first], crossing.at[j, first], along_x)
        moves.add(20 + j, own.at[j, 3, last], crossing.at[j, last], along_y)
        moves.add(24 + j, own.at[j, 2], side.at[j, 1], along_y)
        moves.add(28 + j, own.at[j, 1], side.at[j, 0], along_x)
        if j:
            moves.add(32 + j, own.at[j, 0], out_ref.at[plane], planes[j])

    def add(j, q, begin_row, count, terms):
        def step(i, nothing):
            rows = pl.ds(pl.multiple_of(begin_row + i * chunk, chunk), chunk)
            total = own[j, q, rows, :].astype(F32)
            for ref, index in terms:
                total = total + ref[index + (rows, slice(None))].astype(F32)
            own[j, q, rows, :] = total.astype(BF16)
            return nothing

        lax.fori_loop(0, count // chunk, step, 0)

    def chip_sum(j, q):
        moves.arrived(4 * j + q, other.at[j, q], core)
        loading(j, q).wait()
        add(j, q, 0, cap, [(other, (j, q))])

    def stage_one(j):
        chip_sum(j, 3)
        moves.start(16 + j)
        moves.start(20 + j)
        chip_sum(j, 2)
        chip_sum(j, 1)
        chip_sum(j, 0)

    def stage_two(j):
        moves.arrived(16 + j, crossing.at[j, first], along_x)
        add(j, 2, 0, middle, [(crossing, (j,))])
        moves.start(24 + j)
        moves.arrived(20 + j, crossing.at[j, last], along_y)
        add(j, 1, middle, cap - middle, [(crossing, (j,))])
        moves.start(28 + j)

    def stage_three(j):
        moves.arrived(24 + j, side.at[j, 1], along_y)
        moves.arrived(28 + j, side.at[j, 0], along_x)
        add(j, 0, 0, cap, [(side, (j, 0)), (side, (j, 1))])
        if j:
            moves.start(32 + j)
        else:
            keep.start()

    order = (2, 3, 1, 0)

    def begin():
        meet(planes[1:] + [along_x, along_y, core] + list(more))
        for j in order:
            for q in (3, 2, 1, 0):
                moves.start(4 * j + q)
                loading(j, q).start()

    def step(number):
        if number < len(order):
            stage_one(order[number])
        if 0 <= number - 1 < len(order):
            stage_two(order[number - 1])
        if 0 <= number - 2 < len(order):
            stage_three(order[number - 2])

    def finish():
        for j in range(1, PLANES):
            moves.arrived(32 + j, out_ref.at[crossed(plane, j)], planes[j])
        moves.all_sent()
        keep.wait()

    return [begin] + [functools.partial(step, number) for number in range(len(order) + 2)] + [finish]


def scatter_scratch(rows, width):
    return [
        pltpu.VMEM((PLANES, 4, rows, width), BF16),
        pltpu.VMEM((PLANES, 4, rows, width), BF16),
        pltpu.VMEM((PLANES, rows, width), BF16),
        pltpu.VMEM((PLANES, 2, rows, width), BF16),
        pltpu.SemaphoreType.DMA((36,)),
        pltpu.SemaphoreType.DMA((36,)),
        pltpu.SemaphoreType.DMA((17,)),
    ]


def scatter_kernel(*refs, share, rides):
    if rides:
        partial_ref, pieces_ref, out_ref, landed_ref = refs[:4]
        ride = Ride(pieces_ref, landed_ref, *refs[11:])
        scratch = refs[4:11]
    else:
        partial_ref, out_ref = refs[:2]
        ride, scratch = None, refs[2:]
    more = ride.peers if rides else ()
    run_with_ride(scatter_steps(partial_ref, out_ref, *scratch, share, more), ride)


def scattered(partial, rows, collective_id, ride=None, share=2):
    width = partial.shape[1] // 4
    rides = () if ride is None else (ride,)
    anywhere = pl.BlockSpec(memory_space=pl.ANY)
    out = pl.pallas_call(
        functools.partial(scatter_kernel, share=share, rides=len(rides)),
        out_shape=[jax.ShapeDtypeStruct((PLANES, rows, width), BF16)]
        + [jax.ShapeDtypeStruct(r.shape, BF16) for r in rides],
        in_specs=[anywhere] * (1 + len(rides)),
        out_specs=[anywhere] * (1 + len(rides)),
        scratch_shapes=scatter_scratch(rows, width) + list(RIDE_SCRATCH) * len(rides),
        compiler_params=pltpu.CompilerParams(
            collective_id=collective_id, has_side_effects=True, vmem_limit_bytes=VMEM_BYTES
        ),
        name="scatter_rows",
    )(partial.reshape(PLANES, HALVES, rows, 4 * width), *rides)
    return out if rides else out[0]


def carry(before, after, places, compute):
    number = pl.program_id(0)

    @pl.when(number == 0)
    def _():
        for step in before:
            step()

    compute()
    for at in sorted(set(places)):

        @pl.when(number == at)
        def _(at=at):
            for place, step in zip(places, after):
                if place == at:
                    step()


def join_halves(first_ref, last_ref, whole_ref):
    count, height, _ = first_ref.shape

    @pl.when(pl.program_id(0) == 0)
    def _():
        for place in range(count):
            whole_ref[2 * place * height : (2 * place + 1) * height, :] = first_ref[place]
            whole_ref[(2 * place + 1) * height : (2 * place + 2) * height, :] = last_ref[place]


def expert_forward_kernel(
    rows_ref, up_weight_ref, first_ref, last_ref, small_ref, rank_ref, member_ref, grad_ref,
    slope_ref, silu_ref, result_ref, share_ref, shared_ref, grad_rows_ref, down_weight_ref, *scratch
):
    join_halves(first_ref, last_ref, down_weight_ref)
    steps = gather_steps(grad_ref, grad_rows_ref, *scratch, False)
    units = slope_ref.shape[1]

    def compute():
        rows = rows_ref[0]
        made = dot(rows, up_weight_ref[...])
        gate, up = made[:, :units], made[:, units:]
        sigmoid = jax.nn.sigmoid(gate)
        silu = gate * sigmoid
        slope_ref[...] = up * sigmoid * (1.0 + gate * (1.0 - sigmoid))
        silu_ref[...] = silu
        inner = silu * up
        result_ref[0] = contract_last(inner.astype(BF16), down_weight_ref[...]).astype(BF16)
        cap, count = rows.shape[0], rank_ref.shape[2]
        pick = (lax.broadcasted_iota(jnp.int32, (cap, count), 0) == rank_ref[0]).astype(BF16)
        member = contract_last(pick, member_ref[...]) > 0.5
        logits = jnp.where(member, contract_last(rows, small_ref[...]), NEGATIVE)
        largest = jnp.max(logits, axis=1, keepdims=True)
        weights = jnp.where(member, jnp.exp(logits - largest), 0.0)
        mine = lax.broadcasted_iota(jnp.int32, weights.shape, 1) == 6 + lax.axis_index("z")
        total = jnp.sum(weights, axis=1, keepdims=True)
        own = jnp.sum(jnp.where(mine, weights, 0.0), axis=1, keepdims=True)
        share = own / jnp.where(total > 0.0, total, 1.0)
        share_ref[...] = share
        shared_ref[...] = (share * inner).astype(BF16)

    carry(steps[:2], steps[2:], (1, 3, 5, 6, 7, 7), compute)


def once(shape):
    return pl.BlockSpec(shape, lambda b: (0,) * len(shape), pipeline_mode=pl.Buffered(1))


def expert_forward(rows, up_weight, down_halves, small, rank, member, grad_slots, collective_id):
    _, cap, width = rows.shape
    units = down_halves[0].shape[2]
    count = BLOCKS * cap
    anywhere = pl.BlockSpec(memory_space=pl.ANY)
    block = lambda b: (b, 0)
    return pl.pallas_call(
        expert_forward_kernel,
        grid=(BLOCKS,),
        in_specs=[
            pl.BlockSpec((1, cap, width), lambda b: (b, 0, 0)),
            once(up_weight.shape),
            once(down_halves[0].shape),
            once(down_halves[1].shape),
            once(small.shape),
            pl.BlockSpec((1, 1, rank.shape[2]), lambda b: (b, 0, 0)),
            pl.BlockSpec((16, rank.shape[2]), lambda b: (0, b)),
            anywhere,
        ],
        out_specs=[
            pl.BlockSpec((cap, units), block),
            pl.BlockSpec((cap, units), block),
            pl.BlockSpec((1, cap, width), lambda b: (b, 0, 0)),
            pl.BlockSpec((cap, 1), block),
            pl.BlockSpec((cap, units), block),
            anywhere,
        ],
        out_shape=[
            jax.ShapeDtypeStruct((count, units), F32),
            jax.ShapeDtypeStruct((count, units), F32),
            jax.ShapeDtypeStruct((BLOCKS, cap, width), BF16),
            jax.ShapeDtypeStruct((count, 1), F32),
            jax.ShapeDtypeStruct((count, units), BF16),
            jax.ShapeDtypeStruct((PLANES, HALVES, cap, width), BF16),
        ],
        scratch_shapes=[pltpu.VMEM((width, units), BF16)] + list(GATHER_SCRATCH),
        compiler_params=pltpu.CompilerParams(
            collective_id=collective_id, has_side_effects=True, vmem_limit_bytes=VMEM_BYTES
        ),
        name="expert_forward",
    )(rows, up_weight, *down_halves, small, rank, member, grad_slots)


def expert_backward_kernel(
    slope_ref, silu_ref, grad_ref, share_ref, up_weight_ref, first_ref, last_ref, columns_ref,
    inner_ref, result_ref, *refs, rides
):
    count = 6 if rides else 5
    grad_rows_ref, grad_gate_up_ref, down_first_ref, down_last_ref, out_ref = refs[:5]
    down_weight_ref, kept_ref, scratch = refs[count], refs[count + 1], refs[count + 2 :]
    ride = Ride(kept_ref, refs[5], *scratch[7:]) if rides else None
    steps = scatter_steps(result_ref, out_ref, *scratch[:7], 1, ride.peers if rides else ())
    middle = down_first_ref.shape[1]
    number = pl.program_id(0)
    join_halves(first_ref, last_ref, down_weight_ref)

    def down_gradient():
        down_grad = contract_first(columns_ref[...], inner_ref[...]).astype(BF16)
        kept_ref[number] = down_grad[:middle]
        down_first_ref[0] = down_grad[:middle]
        down_last_ref[0] = down_grad[middle:]

    def rows_gradient():
        grad_inner = dot(grad_ref[0], down_weight_ref[...]) * share_ref[...]
        grad_gate_up = jnp.concatenate(
            [grad_inner * slope_ref[...], grad_inner * silu_ref[...]], axis=1
        ).astype(BF16)
        grad_gate_up_ref[...] = grad_gate_up
        grad_rows_ref[0] = contract_last(grad_gate_up, up_weight_ref[...]).astype(BF16)

    def compute():
        pl.when(number < BLOCKS)(down_gradient)
        pl.when(number >= BLOCKS)(rows_gradient)

    after, places = list(steps[1:]), [3, 7, 9, 11, 13, 15, 15]
    if rides:
        after += [ride.begin] + [functools.partial(ride.go_on, i) for i in range(4)] + [ride.finish]
        places += [7, 8, 9, 10, 12, 15]
    carry(steps[:1], after, places, compute)


def expert_backward(
    slope, silu, grad_rows, share, up_weight, down_halves, inner, result, rides, collective_id
):
    _, cap, width = grad_rows.shape
    count, units = slope.shape
    tile = width // BLOCKS
    anywhere = pl.BlockSpec(memory_space=pl.ANY)
    at_row = lambda b: jnp.maximum(b - BLOCKS, 0)
    at_tile = lambda b: jnp.minimum(b, BLOCKS - 1)
    block = lambda b: (at_row(b), 0)
    rows = pl.BlockSpec((1, cap, width), lambda b: (at_row(b), 0, 0))
    half = pl.BlockSpec((1, tile // 2, units), lambda b: (at_tile(b), 0, 0))
    half_shape = jax.ShapeDtypeStruct((BLOCKS, tile // 2, units), BF16)
    return pl.pallas_call(
        functools.partial(expert_backward_kernel, rides=rides),
        grid=(2 * BLOCKS,),
        in_specs=[
            pl.BlockSpec((cap, units), block),
            pl.BlockSpec((cap, units), block),
            rows,
            pl.BlockSpec((cap, 1), block),
            once(up_weight.shape),
            once(down_halves[0].shape),
            once(down_halves[1].shape),
            pl.BlockSpec((count, tile), lambda b: (0, at_tile(b))),
            once(inner.shape),
            anywhere,
        ],
        out_specs=[rows, pl.BlockSpec((cap, 2 * units), block), half, half, anywhere]
        + [anywhere] * rides,
        out_shape=[
            jax.ShapeDtypeStruct((BLOCKS, cap, width), BF16),
            jax.ShapeDtypeStruct((count, 2 * units), BF16),
            half_shape,
            half_shape,
            jax.ShapeDtypeStruct((PLANES, cap, width // 4), BF16),
        ]
        + [half_shape] * rides,
        scratch_shapes=[
            pltpu.VMEM((width, units), BF16),
            pltpu.VMEM((BLOCKS, tile // 2, units), BF16),
        ]
        + scatter_scratch(cap, width // 4)
        + list(RIDE_SCRATCH) * rides,
        compiler_params=pltpu.CompilerParams(
            collective_id=collective_id, has_side_effects=True, vmem_limit_bytes=VMEM_BYTES
        ),
        name="expert_backward",
    )(
        slope, silu, grad_rows, share, up_weight, *down_halves, grad_rows.reshape(count, width), inner,
        result.reshape(PLANES, HALVES, cap, width),
    )


def expert_gradient_kernel(
    rows_ref, grad_gate_up_ref, partial_ref, pieces_ref, up_first_ref, up_last_ref, out_ref,
    landed_ref, *scratch
):
    ride = Ride(pieces_ref, landed_ref, *scratch[7:])
    steps = scatter_steps(partial_ref, out_ref, *scratch[:7], 1, ride.peers)

    def compute():
        up_grad = contract_first(rows_ref[...], grad_gate_up_ref[...]).astype(BF16)
        up_first_ref[...] = up_grad[:, :EARLY]
        up_last_ref[...] = up_grad[:, EARLY:]

    def with_ride(number):
        steps[1 + number]()
        ride.go_on(number)

    after = [functools.partial(with_ride, number) for number in range(6)]
    carry([steps[0], ride.begin], after + [steps[-1], ride.finish], (0, 1, 3, 5, 6, 7, 7, 7), compute)


def expert_gradient(rows, grad_gate_up, partial, pieces, collective_id):
    count, width = rows.shape
    units = grad_gate_up.shape[1]
    cap, tile = count // BLOCKS, width // BLOCKS
    anywhere = pl.BlockSpec(memory_space=pl.ANY)
    return pl.pallas_call(
        expert_gradient_kernel,
        grid=(BLOCKS,),
        in_specs=[
            pl.BlockSpec((count, tile), lambda b: (0, b)),
            once((count, units)),
            anywhere,
            anywhere,
        ],
        out_specs=[
            pl.BlockSpec((tile, EARLY), lambda b: (b, 0)),
            pl.BlockSpec((tile, units - EARLY), lambda b: (b, 0)),
            anywhere,
            anywhere,
        ],
        out_shape=[
            jax.ShapeDtypeStruct((width, EARLY), BF16),
            jax.ShapeDtypeStruct((width, units - EARLY), BF16),
            jax.ShapeDtypeStruct((PLANES, cap, width // 4), BF16),
            jax.ShapeDtypeStruct(pieces.shape, BF16),
        ],
        scratch_shapes=scatter_scratch(cap, width // 4) + list(RIDE_SCRATCH),
        compiler_params=pltpu.CompilerParams(
            collective_id=collective_id, has_side_effects=True, vmem_limit_bytes=VMEM_BYTES
        ),
        name="expert_gradient",
    )(rows, grad_gate_up, partial.reshape(PLANES, HALVES, cap, width), pieces)


def closing_kernel(
    hidden_ref, q_ref, k_ref, v_ref, rows_ref, gated_ref, partial_ref, grad_ref, out_ref, *scratch
):
    steps = scatter_steps(partial_ref, out_ref, *scratch)
    span = q_ref.shape[1]

    def compute():
        hidden = hidden_ref[...]
        for place, ref in enumerate((q_ref, k_ref, v_ref)):
            at = slice(place * span, (place + 1) * span)
            grad_ref[:, at] = contract_first(hidden, ref[...]).astype(BF16)
        grad_ref[:, 3 * span :] = contract_first(rows_ref[...], gated_ref[...]).astype(BF16)

    carry(steps[:1], steps[1:], (1, 3, 6, 7, 7, 7, 7), compute)


def closing(hidden, q, k, v, rows, gated, partial, collective_id):
    count, width = hidden.shape
    slot_count, span = gated.shape
    tile, own_rows = width // BLOCKS, count // BLOCKS
    anywhere = pl.BlockSpec(memory_space=pl.ANY)
    return pl.pallas_call(
        closing_kernel,
        grid=(BLOCKS,),
        in_specs=[
            pl.BlockSpec((count, tile), lambda b: (0, b)),
            once((count, span)),
            once((count, span)),
            once((count, span)),
            pl.BlockSpec((slot_count, tile), lambda b: (0, b)),
            once((slot_count, span)),
            anywhere,
        ],
        out_specs=[pl.BlockSpec((tile, 4 * span), lambda b: (b, 0)), anywhere],
        out_shape=[
            jax.ShapeDtypeStruct((width, 4 * span), BF16),
            jax.ShapeDtypeStruct((PLANES, own_rows, width // 4), BF16),
        ],
        scratch_shapes=scatter_scratch(own_rows, width // 4),
        compiler_params=pltpu.CompilerParams(
            collective_id=collective_id, has_side_effects=True, vmem_limit_bytes=VMEM_BYTES
        ),
        name="closing",
    )(hidden, q, k, v, rows, gated, partial.reshape(PLANES, HALVES, own_rows, width))


def finish_kernel(
    query_ref, all_ref, small_ref, query_grad_ref, kv_grad_ref, out_grad_ref, gain_first_ref,
    gain_second_ref, router_first_ref, router_second_ref
):
    span = query_ref.shape[2] // 4
    head_width = query_grad_ref.shape[3]
    pair = span // head_width
    own_rows = query_grad_ref.shape[1]
    for half in range(HALVES):
        landed = query_ref[half, :own_rows, :].astype(F32)
        for head in range(pair):
            at = half * pair + head
            query_grad_ref[0, :, at, :] = landed[:, head * head_width : (head + 1) * head_width]
        out_grad_ref[half] = landed[:, 3 * span :].T

    @pl.when(pl.program_id(0) == 0)
    def _():
        for half in range(HALVES):
            total = sum(
                all_ref[z * HALVES + half, :own_rows, span : 3 * span].astype(F32)
                for z in range(PLANES)
            )
            for kind in range(2):
                for head in range(pair):
                    first = kind * span + head * head_width
                    kv_grad_ref[:, half * pair + head, kind, :] = total[:, first : first + head_width]

        total = sum(small_ref[place] for place in range(BLOCKS))
        gain_first_ref[...] = total[0:1]
        gain_second_ref[...] = total[1:2]
        router_first_ref[...] = total[2 : 2 + PLANES]
        router_second_ref[...] = total[2 + PLANES : 2 + 2 * PLANES]


def unpack_up_kernel(first_ref, last_ref, grad_ref):
    units = grad_ref.shape[3] // HALVES
    halves = [
        jnp.concatenate([first_ref[half], last_ref[half]], axis=1).astype(F32) for half in range(HALVES)
    ]
    for kind in range(2):
        at = slice(kind * units, (kind + 1) * units)
        grad_ref[0, :, kind, :] = jnp.concatenate([half[:, at] for half in halves], axis=1)


def unpack_up(first, last):
    places, own_rows, early = first.shape
    units = early + last.shape[2]
    tile = own_rows // 2
    return pl.pallas_call(
        unpack_up_kernel,
        grid=(places // HALVES, 2),
        in_specs=[
            pl.BlockSpec((HALVES, tile, early), lambda e, r: (e, r, 0)),
            pl.BlockSpec((HALVES, tile, units - early), lambda e, r: (e, r, 0)),
        ],
        out_specs=pl.BlockSpec((1, tile, 2, units), lambda e, r: (e, r, 0, 0)),
        out_shape=jax.ShapeDtypeStruct((places // HALVES, own_rows, 2, units), F32),
        compiler_params=pltpu.CompilerParams(vmem_limit_bytes=VMEM_BYTES),
        name="unpack_up",
    )(first, last)


def swap_kernel(pieces_ref, landed_ref, *scratch):
    ride = Ride(pieces_ref, landed_ref, *scratch)
    meet([peer for _, _, peer in ride.moves.made.values()])
    ride.begin(tuple(ride.moves.made))
    ride.finish()


def swapped(pieces, collective_id):
    whole = pl.BlockSpec(memory_space=pltpu.VMEM)
    return pl.pallas_call(
        swap_kernel,
        out_shape=jax.ShapeDtypeStruct(pieces.shape, pieces.dtype),
        in_specs=[whole],
        out_specs=whole,
        scratch_shapes=list(RIDE_SCRATCH),
        compiler_params=pltpu.CompilerParams(collective_id=collective_id, has_side_effects=True),
        name="swap_small",
    )(pieces)


def finish(landed, small, own_rows, span, heads, head_width):
    places, height, width = landed.shape
    return pl.pallas_call(
        finish_kernel,
        grid=(PLANES,),
        in_specs=[
            pl.BlockSpec((HALVES, height, width), lambda e: (e, 0, 0)),
            once((places, height, width)),
            once(small.shape),
        ],
        out_specs=[
            pl.BlockSpec((1, own_rows, heads, head_width), lambda e: (e, 0, 0, 0)),
            pl.BlockSpec((own_rows, heads, 2, head_width), lambda e: (0, 0, 0, 0)),
            pl.BlockSpec((HALVES, span, own_rows), lambda e: (e, 0, 0)),
            pl.BlockSpec((1, small.shape[2]), lambda e: (0, 0)),
            pl.BlockSpec((1, small.shape[2]), lambda e: (0, 0)),
            pl.BlockSpec((PLANES, small.shape[2]), lambda e: (0, 0)),
            pl.BlockSpec((PLANES, small.shape[2]), lambda e: (0, 0)),
        ],
        out_shape=[
            jax.ShapeDtypeStruct((PLANES, own_rows, heads, head_width), F32),
            jax.ShapeDtypeStruct((own_rows, heads, 2, head_width), F32),
            jax.ShapeDtypeStruct((places, span, own_rows), F32),
            jax.ShapeDtypeStruct((1, small.shape[2]), F32),
            jax.ShapeDtypeStruct((1, small.shape[2]), F32),
            jax.ShapeDtypeStruct((PLANES, small.shape[2]), F32),
            jax.ShapeDtypeStruct((PLANES, small.shape[2]), F32),
        ],
        compiler_params=pltpu.CompilerParams(vmem_limit_bytes=VMEM_BYTES),
        name="attention_weight_gradients",
    )(landed, landed, small)


def grid_sum(values):
    shape = values.shape
    return lax.all_gather(values.reshape(-1, 128), "grid", axis=0).sum(axis=0).reshape(shape)


def prefix_ranks(member):
    counted = member.astype(BF16)
    width = member.shape[-1]
    before = jnp.arange(width)[:, None] < jnp.arange(width)[None, :]
    return jnp.where(member, dot(counted, before.astype(BF16)).astype(jnp.int32), -1)


def picks(rank):
    return (jnp.arange(CAP, dtype=jnp.int32)[:, None] == rank[..., None, :]).astype(BF16)


def members(first, second):
    names = jnp.arange(PLANES, dtype=first.dtype).reshape((PLANES,) + (1,) * first.ndim)
    return (first[None] == names) | (second[None] == names)


def route_gates(logits, member):
    shown = jnp.where(member, logits, NEGATIVE)
    weights = jnp.where(member, jnp.exp(shown - jnp.max(shown, axis=0, keepdims=True)), 0.0)
    return weights / jnp.sum(weights, axis=0, keepdims=True)


def logits_grad(gates, grad_gates):
    return gates * (grad_gates - jnp.sum(gates * grad_gates, axis=0, keepdims=True))


def exact_first(left, right):
    return lax.dot_general(
        left, right, (((0,), (0,)), ((), ())), precision=lax.Precision.HIGHEST
    )


def exact_last(left, right):
    return lax.dot_general(
        left, right, (((1,), (1,)), ((), ())), precision=lax.Precision.HIGHEST
    )


def norm_sums(grad_hidden, scaled, router, grad_gates, width, gates=None, hidden=None, member=None):
    parts = [
        grad_gates,
        exact_last(router.astype(F32), scaled),
        jnp.sum(grad_hidden * scaled, axis=1)[None],
    ]
    if gates is None:
        parts.append(contract_last(router, hidden))
    parts = grid_sum(jnp.concatenate(parts, axis=0))
    if gates is None:
        gates = route_gates(parts[2 * PLANES + 1 :], member)
    grad_logits = logits_grad(gates, parts[:PLANES])
    inner = parts[2 * PLANES] + jnp.sum(grad_logits * parts[PLANES : 2 * PLANES], axis=0)
    return grad_logits, inner[:, None] / width, gates


def per_device(
    tokens, segment_ids, attention_routes, expert_routes, attention_gain, attention_kv,
    attention_query, attention_out, attention_router, feedforward_gain, feedforward_router,
    expert_gate_up, expert_down, output_grad,
):
    groups = lax.axis_size("t")
    grid_count = lax.axis_size("grid")
    group = lax.axis_index("t")
    plane = lax.axis_index("z")
    place = plane * HALVES + lax.axis_index("x")
    column = lax.axis_index("grid")
    rows, features = tokens.shape
    width_all = features * grid_count
    token_count = BLOCKS * rows
    own_rows = attention_gain.shape[0]
    head_width = attention_kv.shape[3]
    head_pair = attention_kv.shape[1] // HALVES
    span = head_pair * head_width
    hidden_units = expert_gate_up.shape[3] // HALVES

    def mine(array, axis=0):
        return lax.dynamic_slice_in_dim(array, column * features, features, axis)

    def own(array, axis=0):
        return lax.dynamic_slice_in_dim(array, place * rows, rows, axis)

    query_pieces = attention_query.reshape(PLANES, own_rows, HALVES, span).transpose(0, 2, 1, 3)
    kv_pieces = attention_kv.reshape(own_rows, HALVES, head_pair, 2, head_width)
    kv_pieces = kv_pieces.transpose(1, 0, 3, 2, 4).reshape(1, HALVES, own_rows, 2 * span)
    kv_pieces = jnp.broadcast_to(kv_pieces, (PLANES,) + kv_pieces.shape[1:])
    qkv_pieces = jnp.concatenate([query_pieces, kv_pieces], axis=-1)
    out_pieces = attention_out.reshape(BLOCKS, span, own_rows).swapaxes(1, 2)
    first_pieces = jnp.concatenate([out_pieces, qkv_pieces.reshape(BLOCKS, own_rows, 3 * span)], axis=2)
    own_routes = jnp.concatenate([attention_routes, expert_routes], axis=1)
    small = jnp.concatenate(
        [attention_gain[:, None], feedforward_gain[:, None], attention_router, feedforward_router],
        axis=1,
    )
    small = lax.all_gather(small, "t", axis=0).reshape(-1, small.shape[1])
    small = small.T.reshape(small.shape[1], -1)
    spare = jnp.zeros((small.shape[0], features - small.shape[1] % features), BF16)
    small = jnp.concatenate([small, spare], axis=1).reshape(-1, features)
    under = jnp.concatenate([own_routes.T.astype(BF16), small], axis=0)
    under = jnp.pad(under, ((0, -under.shape[0] % 16), (0, 0)))
    everything, first_weight, up_pieces, *down_halves = opened(
        jnp.concatenate([tokens, under], axis=0), first_pieces, expert_gate_up,
        expert_down.reshape(BLOCKS, hidden_units, own_rows), 0, 3,
    )
    first_weight = over_groups(first_weight).reshape(width_all, 4 * span)
    out_weight, qkv_weight = first_weight[:, :span], first_weight[:, span:]
    up_weight = over_groups(exchanged(up_pieces)).reshape(width_all, 2 * hidden_units)
    under = everything[:, :, rows:, :features].reshape(BLOCKS, -1, features).swapaxes(0, 1)
    small = under[4:, :, : groups * own_rows].reshape(-1, BLOCKS, groups, own_rows)
    small = jnp.pad(small.swapaxes(1, 2).reshape(-1, width_all), ((0, 4), (0, 0)))
    gain_first, gain_second = mine(small[0]).astype(F32), mine(small[1]).astype(F32)
    router_first, router_second = mine(small[2:6], 1), mine(small[6:10], 1)

    member_first, member_second = members(under[0], under[1]), members(under[2], under[3])
    own_member_first = lax.dynamic_index_in_dim(member_first, place, 1, keepdims=False)
    own_member_second = lax.dynamic_index_in_dim(member_second, place, 1, keepdims=False)
    rank = prefix_ranks(
        jnp.concatenate(
            [
                lax.dynamic_index_in_dim(member_first, plane, 0, keepdims=False),
                lax.dynamic_index_in_dim(member_second, plane, 0, keepdims=False),
                own_member_first,
                own_member_second,
            ],
            axis=0,
        )
    )
    rank_first, rank_second = rank[:BLOCKS, None], rank[BLOCKS : 2 * BLOCKS, None]
    own_pick_first = picks(rank[2 * BLOCKS : 2 * BLOCKS + PLANES])
    own_pick_second = picks(rank[2 * BLOCKS + PLANES :])
    member_first = member_first.reshape(PLANES, token_count)
    member_second = member_second.reshape(PLANES, token_count)

    def to_slots(values, pick):
        return jnp.einsum("est,tf->esf", pick, values, preferred_element_type=F32).astype(BF16)

    def to_tokens(slots, pick):
        return jnp.einsum("est,esf->etf", pick, slots, preferred_element_type=F32)

    grad_out = output_grad.astype(F32)
    cosine, sine = rope_tables(token_count, head_width)
    cosine, sine = jnp.asarray(cosine), jnp.asarray(sine)
    hidden_first, queries, keys, values, logits_first, inverse_first = project(
        everything, rows, small, first_weight, cosine, sine, span, head_width
    )
    gates_first = route_gates(logits_first[2 : 2 + PLANES], member_first)
    own_gates_first = own(gates_first, 1)
    position = jnp.arange(token_count, dtype=jnp.int32)
    segment = lax.dynamic_slice_in_dim(segment_ids, group * token_count, token_count, 0)
    opens = jnp.concatenate([jnp.ones((1,), jnp.bool_), segment[1:] != segment[:-1]])
    document_start = lax.cummax(jnp.where(opens, position, 0))
    begin = document_start.reshape(BLOCKS, rows)[:, 0] // rows
    table = token_table(
        position, document_start, lax.dynamic_index_in_dim(gates_first, plane, 0, keepdims=False)
    )
    attention_args = (begin, queries, keys, values, rank_first, table)
    attended, gated, gate_slots_first, lse = attention_forward(*attention_args, head_width)
    branch, grad_out_slots, lse = lax.optimization_barrier(
        (
            contract_last(attended, out_weight).astype(BF16),
            to_slots(output_grad, own_pick_second),
            lse.reshape(-1, BLOCKS, 1, CAP),
        )
    )
    branch_slots, down_first = scattered(
        branch, CAP, 2, ride=down_halves[0], share=1
    )
    branch_first = to_tokens(branch_slots, own_pick_first)
    residual = tokens.astype(F32) + jnp.sum(own_gates_first[:, :, None] * branch_first, axis=0)

    square = grid_sum(jnp.sum(residual * residual, axis=1))
    inverse_second = lax.rsqrt(square / width_all + EPSILON)[:, None]
    normed_second = residual * inverse_second
    hidden_second = (normed_second * gain_second).astype(BF16)
    slots_second, down_last = gathered(
        to_slots(hidden_second, own_pick_second), 1, ride=down_halves[1], share=3
    )
    down_weight = [
        over_groups(half).reshape((groups * BLOCKS,) + half.shape[1:]) for half in (down_first, down_last)
    ]
    slots_second = slots_second.reshape(BLOCKS, CAP, width_all)
    gate_pre, up_pre, result, gate_slots_second, inner, grad_slots_second = expert_forward(
        slots_second,
        up_weight,
        down_weight,
        small,
        rank_second,
        jnp.pad(member_second.astype(BF16), ((6, 6), (0, 0))),
        grad_out_slots,
        4,
    )
    grad_slots_second = grad_slots_second.reshape(BLOCKS, CAP, width_all)
    grad_rows, grad_gate_up, grad_down_first, grad_down_last, result_slots, *landed = expert_backward(
        gate_pre, up_pre, grad_slots_second, gate_slots_second, up_weight, down_weight, inner, result,
        int(groups == 1), 5,
    )
    if groups > 1:
        grad_down = jnp.concatenate([grad_down_first, grad_down_last], axis=1)
        grad_down = group_sums(grad_down.reshape(groups, BLOCKS, own_rows, hidden_units))
        grad_down_first, grad_down_last = jnp.split(grad_down, 2, axis=1)
        landed = [exchanged(grad_down_first)]
    grad_down_first = landed[0]
    grad_up_first, grad_up, grad_rows, grad_down_last = expert_gradient(
        slots_second.reshape(-1, width_all), grad_gate_up, grad_rows, grad_down_last, 6
    )
    branch_second = to_tokens(result_slots, own_pick_second)

    grad_hidden_second = jnp.sum(to_tokens(grad_rows, own_pick_second), axis=0)
    grad_logits_second, inner_mean, own_gates_second = norm_sums(
        grad_hidden_second, normed_second * gain_second, router_second,
        jnp.sum(branch_second * grad_out[None], axis=2), width_all,
        hidden=hidden_second, member=own_member_second,
    )
    grad_hidden_second = grad_hidden_second + exact_first(
        grad_logits_second, router_second.astype(F32)
    )
    grad_normed = grad_hidden_second * gain_second
    grad_residual = grad_out + inverse_second * (grad_normed - normed_second * inner_mean)

    grad_up_first = return_gradients(grad_up_first.reshape(groups, BLOCKS, own_rows, EARLY))
    grad_slots_first = gathered(to_slots(grad_residual.astype(BF16), own_pick_first), 8)
    (
        grad_slots_first, grad_up_first, residual, own_gates_second, branch_second, hidden_second,
        grad_logits_second, grad_hidden_second, normed_second,
    ) = lax.optimization_barrier(
        (
            grad_slots_first, grad_up_first, residual, own_gates_second, branch_second, hidden_second,
            grad_logits_second, grad_hidden_second, normed_second,
        )
    )
    layer_output = residual + jnp.sum(own_gates_second[:, :, None] * branch_second, axis=0)
    layer_output = layer_output.astype(BF16)
    grad_router_second = exact(grad_logits_second, hidden_second.astype(F32))
    grad_gain_second = jnp.sum(grad_hidden_second * normed_second, axis=0)
    grad_slots_first = grad_slots_first.reshape(BLOCKS * CAP, -1)
    grad_up, grad_slots_first = lax.optimization_barrier((grad_up, grad_slots_first))
    grad_up = return_gradients(grad_up.reshape(groups, BLOCKS, own_rows, 2 * hidden_units - EARLY))
    grad_attended = gate_slots_first * dot(grad_slots_first, out_weight)
    grad_attended = grad_attended.astype(BF16)
    grad_query, grad_keys, grad_values = attention_backward(
        *attention_args, attended, lse, grad_attended, cosine, sine, head_width
    )
    grad_qkv = jnp.concatenate([grad_query, grad_keys, grad_values], axis=1)
    grad_hidden = contract_last(grad_qkv, qkv_weight).astype(BF16)
    grad_first, grad_hidden = closing(
        hidden_first, grad_query, grad_keys, grad_values, grad_slots_first, gated, grad_hidden, 3
    )
    grad_hidden = jnp.sum(grad_hidden.astype(F32), axis=0)
    grad_first, grad_up = lax.optimization_barrier((grad_first, grad_up))
    grad_first = return_gradients(grad_first.reshape(groups, BLOCKS, own_rows, 4 * span))
    expert_gate_up_grad = unpack_up(grad_up_first, grad_up)
    expert_down_grad = jnp.concatenate([grad_down_first, grad_down_last], axis=1)
    expert_down_grad = expert_down_grad.astype(F32).swapaxes(1, 2).reshape(expert_down.shape)

    own_normed = tokens.astype(F32) * own(inverse_first)
    own_hidden = (own_normed * gain_first).astype(BF16)
    grad_logits_first, inner_mean, _ = norm_sums(
        grad_hidden, own_normed * gain_first, router_first,
        jnp.sum(branch_first * grad_residual[None], axis=2), width_all, gates=own_gates_first,
    )
    grad_hidden_first = grad_hidden + exact_first(grad_logits_first, router_first.astype(F32))
    grad_router_first = exact(grad_logits_first, own_hidden.astype(F32))
    grad_gain_first = jnp.sum(grad_hidden_first * own_normed, axis=0)
    grad_normed = grad_hidden_first * gain_first
    input_grad = grad_residual + own(inverse_first) * (grad_normed - own_normed * inner_mean)

    small_grads = jnp.concatenate(
        [grad_gain_first[None], grad_gain_second[None], grad_router_first, grad_router_second],
        axis=0,
    )
    small_grads = lax.all_gather(small_grads, "grid", axis=1, tiled=True)
    if groups > 1:
        small_grads = lax.psum(small_grads, "t")
    small_grads = small_grads.reshape(-1, groups, BLOCKS, own_rows)
    small_grads = lax.dynamic_index_in_dim(small_grads, group, 1, keepdims=False).swapaxes(0, 1)
    small_grads = jnp.pad(small_grads, ((0, 0), (0, 6), (0, -own_rows % 128)))
    small_grads, expert_gate_up_grad, expert_down_grad = lax.optimization_barrier(
        (small_grads, expert_gate_up_grad, expert_down_grad)
    )
    (
        attention_query_grad, attention_kv_grad, attention_out_grad, gain_grad_first,
        gain_grad_second, router_grad_first, router_grad_second,
    ) = finish(
        grad_first, swapped(small_grads, 7), own_rows, span, attention_kv.shape[1], head_width
    )
    attention_out_grad = attention_out_grad.reshape(attention_out.shape)
    return (
        layer_output,
        input_grad.astype(BF16),
        gain_grad_first[0, :own_rows],
        attention_kv_grad,
        attention_query_grad.astype(F32),
        attention_out_grad.astype(F32),
        router_grad_first[:, :own_rows].T,
        gain_grad_second[0, :own_rows],
        router_grad_second[:, :own_rows].T,
        expert_gate_up_grad,
        expert_down_grad,
    )


def solution(mesh):
    groups = mesh.shape["wide"] // BLOCKS
    shape = (groups, PLANES, HALVES, mesh.shape["grid"])
    inner_mesh = Mesh(mesh.devices.reshape(shape), ("t", "z", "x", "grid"))
    wide = ("t", "z", "x")
    in_specs = (
        P(wide, "grid"),
        P(),
        P(wide, None),
        P(wide, None),
        P(wide),
        P(wide, "grid", None, None),
        P(None, wide, "grid", None),
        P(None, "grid", None, wide),
        P(wide, None),
        P(wide),
        P(wide, None),
        P(None, wide, None, "grid"),
        P(None, "grid", wide),
        P(wide, "grid"),
    )
    out_specs = (
        P(wide, "grid"),
        P(wide, "grid"),
        P(wide),
        P(wide, "grid", None, None),
        P(None, wide, "grid", None),
        P(None, "grid", None, wide),
        P(wide, None),
        P(wide),
        P(wide, None),
        P(None, wide, None, "grid"),
        P(None, "grid", wide),
    )
    return jax.shard_map(
        per_device, mesh=inner_mesh, in_specs=in_specs, out_specs=out_specs, check_vma=False
    )
```
